32 devices in a mesh: grp: 2 (over x), dp: 8 (over z, y), tp: 2 (over core).
Axes of the slice: x: 2, y: 2, z: 4, core: 2. Of those that a mesh axis runs over, the one named last changes fastest.
Arguments:
- tokens: bfloat16 [8192, 8192], P(('grp', 'dp'), 'tp'), parts along dimension 0, may hold values from -5 to 7
- norm_gain: bfloat16 [8192], P('tp'), may hold values from 0.6 to 8
- lengths: int32 [16], P('grp'), parts along dimension 0, may hold values from 1 to 1536, 4096 in all
- w_query: bfloat16 [8192, 1024], P(None, 'tp'), may hold values from -0.049939416 to 0.049939416
- w_key: bfloat16 [8192, 128], replicated, may hold values from -0.049939416 to 0.049939416
- w_value: bfloat16 [8192, 128], replicated, may hold values from -0.0625 to 0.0625
- w_out: bfloat16 [1024, 8192], P('tp'), may hold values from -0.1875 to 0.1875
Outputs:
- mixed: bfloat16 [8192, 8192], P(('grp', 'dp'), 'tp'), parts along dimension 0
The draws below stay inside these ranges and needn't reach their ends.
There are 2 independent parts, one for each index of `grp`. The reference program is written for one: setup_inputs(seed, part) draws one part's arguments, and reference() takes and returns one part's arrays. A program takes and returns all parts, laid end to end along the dimension named above; an argument that names none is the same for every part. Nothing has to cross between parts.
All inputs are finite; a program needn't handle non-finite values.
Results may differ from the reference program's by a relative error of at most 0.012.
The reference program's roundings to bfloat16 on the way count: a program that leaves them out, or rounds other values in their place, can miss the bound.
Values may be sent and summed in bfloat16 or wider, within the bound.
No kernel may reach another device: no remote copies, remote signals or barrier semaphores. Data moves between devices by JAX's collectives and lax.ppermute only.
A program may use at most 128 MiB of HBM per device.

```python
import math
import jax
import jax.numpy as jnp
import numpy as np
from jax import lax

D = 8192
HEAD = 128
HEADS_Q = 8
TOKENS = 4096
MOST = 1536
NDOCS = 8
N_TP = 2


def draw_norm_gain(key, part):
    key = jax.random.fold_in(key, 11)
    values = jax.random.uniform(key, (D,), jnp.float32, 0.6, 1.4)
    return values.astype(jnp.bfloat16)


def draw_tokens(key, part):
    key = jax.random.fold_in(key, 31)
    noise = jax.random.normal(key, (TOKENS, D), jnp.float32)
    values = jnp.clip(noise, -5.0, 5.0)
    return values.astype(jnp.bfloat16)


def draw_w_key(key, part):
    key = jax.random.fold_in(key, 23)
    base = jax.random.normal(key, (D, HEAD), jnp.float32)
    return (jnp.clip(base, -4.5, 4.5) / math.sqrt(D)).astype(jnp.bfloat16)


def draw_w_query(key, part):
    key = jax.random.fold_in(key, 29)
    own = jax.random.normal(key, (D, HEADS_Q * HEAD), jnp.float32)
    return (jnp.clip(own, -4.5, 4.5) / math.sqrt(D)).astype(jnp.bfloat16)


def block_scale(key, dims, split, low, largest):
    gain = 1.0
    for position, blocks in split:
        steps = jax.random.uniform(jax.random.fold_in(jax.random.fold_in(key, 6), position), (blocks,), jnp.float32, low / len(split), largest / len(split))
        gain = gain * jnp.repeat(jnp.exp(steps), dims[position] // blocks).reshape((-1,) + (1,) * (len(dims) - 1 - position))
    return gain


def split_up(amount, total, bound, lean):
    weights = [(1 << 20) // math.isqrt(grade ** lean) + 1 for grade in range(2, amount + 1)]
    surplus, holding = total - bound - (amount - 1), [1] * (amount - 1)
    while surplus > 0:
        candidates = [i for i in range(amount - 1) if holding[i] < bound]
        mass, left = sum([weights[i] for i in candidates]), surplus
        for i in candidates:
            more = min(bound - holding[i], max(1, left * weights[i] // mass), surplus)
            holding[i] = holding[i] + more
            surplus = surplus - more
    return np.array([bound] + holding)


def ragged_sizes(own_key, number_of, total, reach, skew):
    if number_of == 2:
        one = jax.random.randint(own_key, (), max(1, total - reach), min(reach, total - 1) + 1)
        return jnp.stack([one, total - one])
    tallies = jnp.asarray(split_up(number_of, total, reach, skew), jnp.int32)
    couples = (number_of - 1) // 2
    source_of, sink = tallies[1:1 + 2 * couples:2], tallies[2:2 + 2 * couples:2]
    margin = jnp.minimum(source_of - 1, reach - sink)
    passed = jax.random.randint(jax.random.fold_in(own_key, 1), (couples,), 0, 1 << 20) % (margin + 1)
    tallies = tallies.at[1:1 + 2 * couples:2].set(source_of - passed).at[2:2 + 2 * couples:2].set(sink + passed)
    return tallies[jax.random.permutation(jax.random.fold_in(own_key, 2), number_of)]


def scatter_about(stream_key, extent, deviation, bound, split=(), held_as=jnp.bfloat16):
    factor_of = block_scale(stream_key, extent, split, -0.22, 0.18) if split else 1.0
    entries = jax.random.normal(stream_key, extent, jnp.float32) * deviation * factor_of
    return jnp.minimum(jnp.maximum(entries, -bound), bound).astype(held_as)


def setup_inputs(seed: int = 0, part: int = 0) -> dict:
    key_list = jax.random.split(jax.random.key(seed), 8)
    own_keys = jax.random.split(jax.random.fold_in(key_list[7], part), 8)
    return {
        "tokens": draw_tokens(jax.random.fold_in(jax.random.fold_in(key_list[7], part), 71), part),
        "norm_gain": draw_norm_gain(jax.random.fold_in(key_list[7], 71), part),
        "lengths": ragged_sizes(own_keys[2], NDOCS, TOKENS, MOST, 2).astype(jnp.int32),
        "w_query": draw_w_query(jax.random.fold_in(key_list[7], 71), part),
        "w_key": draw_w_key(jax.random.fold_in(key_list[7], 71), part),
        "w_value": scatter_about(key_list[5], (D, HEAD), D ** -0.5, 0.0625),
        "w_out": scatter_about(key_list[6], (HEADS_Q * HEAD, D), (HEADS_Q * HEAD) ** -0.5, 0.1875, ((0, 2),)),
    }


def locate(lengths, places):
    doc_ends = jnp.cumsum(lengths).astype(jnp.int32)
    doc_starts = (doc_ends - lengths).astype(jnp.int32)
    doc_ids = lax.optimization_barrier(jnp.sum((places[:, None] >= doc_ends[None, :]).astype(jnp.int32), axis=1)).astype(jnp.int32)
    numbers = jnp.arange(lengths.shape[0], dtype=jnp.int32)
    first_rows = lax.optimization_barrier(jnp.sum(jnp.where(doc_ids[:, None] == numbers[None, :], doc_starts[None, :], 0), axis=1)).astype(jnp.int32)
    return (doc_ids, (places - first_rows).astype(jnp.int32))

def rotate(heads, within):
    half_width = heads.shape[-1] // 2
    frequency = 500000.0 ** (-jnp.arange(half_width, dtype=jnp.float32) * 2.0 / heads.shape[-1])
    angles = within.astype(jnp.float32)[:, None] * frequency[None, :]
    cosine = jnp.cos(angles)[:, None, :]
    sine_part = jnp.sin(angles)[:, None, :]
    lower_half = heads[..., :half_width]
    upper_half = heads[..., half_width:]
    return jnp.concatenate([lower_half * cosine - upper_half * sine_part, upper_half * cosine + lower_half * sine_part], axis=-1)

def reference(tokens, norm_gain, lengths, w_query, w_key, w_value, w_out):
    wide_tokens = tokens.astype(jnp.float32)
    inverse = lax.rsqrt(lax.optimization_barrier(jnp.mean(wide_tokens * wide_tokens, axis=-1, keepdims=True)) + 1e-05)
    normed = (wide_tokens * inverse * norm_gain.astype(jnp.float32)).astype(jnp.bfloat16)
    places = jnp.arange(TOKENS, dtype=jnp.int32)
    doc_ids, within = locate(lengths, places)
    queries = jnp.dot(normed, w_query, preferred_element_type=jnp.float32).reshape(TOKENS, HEADS_Q, HEAD)
    queries = rotate(queries, within).astype(jnp.bfloat16)
    keys_here = jnp.dot(normed, w_key, preferred_element_type=jnp.float32)
    keys_here = rotate(keys_here[:, None, :], within)[:, 0, :].astype(jnp.bfloat16)
    values_here = jnp.dot(normed, w_value, preferred_element_type=jnp.float32).astype(jnp.bfloat16)
    allowed = (doc_ids[None, :] == doc_ids[:, None]) & (places[None, :] <= places[:, None])
    score_scale = 1.0 / HEAD ** 0.5

    def attend_head(head_queries):
        scores = jnp.dot(head_queries, keys_here.T, preferred_element_type=jnp.float32) * score_scale
        masked = jnp.where(allowed, scores, -1e+30)
        running_max = lax.optimization_barrier(jnp.max(masked, axis=-1, keepdims=True))
        weights = jnp.where(allowed, jnp.exp(masked - running_max), 0.0)
        totals = lax.optimization_barrier(jnp.sum(weights, axis=-1, keepdims=True))
        rounded_weights = weights.astype(jnp.bfloat16)
        return jnp.dot(rounded_weights, values_here, preferred_element_type=jnp.float32) / totals
    context = lax.map(attend_head, jnp.transpose(queries, (1, 0, 2)))
    context = jnp.transpose(context, (1, 0, 2)).reshape(TOKENS, HEADS_Q * HEAD).astype(jnp.bfloat16)
    group_width = HEADS_Q * HEAD // N_TP
    mixed_rows = wide_tokens
    for head_group in range(N_TP):
        head_term = jnp.dot(context[:, head_group * group_width:(head_group + 1) * group_width], w_out[head_group * group_width:(head_group + 1) * group_width], preferred_element_type=jnp.float32)
        rounded_term = lax.optimization_barrier(head_term.astype(jnp.bfloat16))
        mixed_rows = mixed_rows + rounded_term.astype(jnp.float32)
    return mixed_rows.astype(jnp.bfloat16)
```

```python
import functools
import math

import jax
import jax.numpy as jnp
from jax import lax
from jax.experimental import pallas as pl
from jax.experimental.pallas import tpu as pltpu
from jax.sharding import PartitionSpec as P

HEAD = 128
MOST = 1536
LANES = 128
SWAP = [(0, 1), (1, 0)]
VMEM_LIMIT = 48 * 1024 * 1024
EXP2_SCALE = math.log2(math.e) / HEAD**0.5


def params(**kw):
    return pltpu.CompilerParams(vmem_limit_bytes=VMEM_LIMIT, **kw)


def vmem_spec(shape, index_map):
    return pl.BlockSpec(shape, index_map)


def squares_kernel(tokens_ref, gain_ref, out_ref):
    rows = tokens_ref.shape[0]

    @pl.when(pl.program_id(0) == 0)
    def _():
        out_ref[0:rows, :] = jnp.zeros((rows, LANES), jnp.float32)
        out_ref[rows:, :] = gain_ref[...].astype(jnp.float32)

    total = out_ref[0:rows, :]
    for j in range(tokens_ref.shape[1] // LANES):
        wide = tokens_ref[:, j * LANES : (j + 1) * LANES].astype(jnp.float32)
        total = total + wide * wide
    out_ref[0:rows, :] = total


def squares(tokens, gain):
    rows, width = tokens.shape
    step = 1024
    gain_rows = gain.shape[0]
    return pl.pallas_call(
        squares_kernel,
        grid=(width // step,),
        in_specs=[
            pl.BlockSpec((rows, step), lambda k: (0, k)),
            pl.BlockSpec((gain_rows, LANES), lambda k: (0, 0)),
        ],
        out_specs=pl.BlockSpec((rows + gain_rows, LANES), lambda k: (0, 0)),
        out_shape=jax.ShapeDtypeStruct((rows + gain_rows, LANES), jnp.float32),
        compiler_params=params(),
        cost_estimate=pl.CostEstimate(flops=rows * width * 2, bytes_accessed=rows * width * 2, transcendentals=0),
        name="squares",
    )(tokens, gain)


def project_kernel(first, model, tp_ref, tokens_ref, mine_ref, other_ref, wq_ref, wk_ref, wv_ref, *rest):
    k = pl.program_id(0)
    steps = pl.num_programs(0)
    rows, step = tokens_ref.shape
    if first:
        acc_out, acc, inv = rest
    else:
        acc_in, cos_ref, sin_ref, q_ref, kv_ref, acc, inv = rest

    @pl.when(k == 0)
    def _():
        sums = mine_ref[0:rows, :] + other_ref[0:rows, :]
        mean = jnp.sum(sums, axis=1, keepdims=True) * (1.0 / model)
        inv[...] = jnp.broadcast_to(lax.rsqrt(mean + 1e-05), (rows, LANES))
        acc[...] = jnp.zeros(acc.shape, jnp.float32) if first else acc_in[...]

    gains = mine_ref if first else other_ref
    inverse = inv[...]
    normed = []
    for j in range(step // LANES):
        wide = tokens_ref[:, j * LANES : (j + 1) * LANES].astype(jnp.float32)
        gain = gains[pl.ds(rows + k * (step // LANES) + j, 1), :]
        normed.append((wide * inverse * gain).astype(jnp.bfloat16))
    normed = jnp.concatenate(normed, axis=1)
    wkv = jnp.concatenate([wk_ref[...], wv_ref[...]], axis=1)
    nq = wq_ref.shape[1]
    acc[:, nq:] += jnp.dot(normed, wkv, preferred_element_type=jnp.float32)
    acc[:, :nq] += jnp.dot(normed, wq_ref[...], preferred_element_type=jnp.float32)

    @pl.when(k == steps - 1)
    def _():
        if first:
            acc_out[...] = acc[...]
        else:
            cosine = cos_ref[...]
            sine = sin_ref[...]
            for h in range(nq // HEAD + 1):
                x = acc[:, h * HEAD : (h + 1) * HEAD]
                turned = (x * cosine + pltpu.roll(x, HEAD // 2, 1) * sine).astype(jnp.bfloat16)
                if h < nq // HEAD:
                    q_ref[:, h * HEAD : (h + 1) * HEAD] = turned
                else:
                    kv_ref[:, :HEAD] = turned
            kv_ref[:, HEAD:] = acc[:, nq + HEAD :].astype(jnp.bfloat16)


def project(half, tokens, mine, other, wq, wk, wv, partial=None, tables=None):
    rows, width = tokens.shape
    step = 512
    steps = width // step
    nq = wq.shape[1]
    wide = nq + 2 * HEAD
    first = partial is None
    weight_map = lambda k, s: (s[0] * steps + k, 0)
    whole = lambda k, s: (0, 0)
    in_specs = [
        pl.BlockSpec((rows, step), lambda k, s: (0, k)),
        pl.BlockSpec(mine.shape, whole),
        pl.BlockSpec(other.shape, whole),
        pl.BlockSpec((step, nq), weight_map),
        pl.BlockSpec((step, HEAD), weight_map),
        pl.BlockSpec((step, HEAD), weight_map),
    ]
    args = [half, tokens, mine, other, wq, wk, wv]
    if first:
        out_specs = pl.BlockSpec((rows, wide), whole)
        out_shape = jax.ShapeDtypeStruct((rows, wide), jnp.float32)
    else:
        in_specs += [pl.BlockSpec((rows, wide), whole), pl.BlockSpec((rows, HEAD), whole), pl.BlockSpec((rows, HEAD), whole)]
        args += [partial, *tables]
        out_specs = [pl.BlockSpec((rows, nq), whole), pl.BlockSpec((rows, 2 * HEAD), whole)]
        out_shape = [
            jax.ShapeDtypeStruct((rows, nq), jnp.bfloat16),
            jax.ShapeDtypeStruct((rows, 2 * HEAD), jnp.bfloat16),
        ]
    return pl.pallas_call(
        functools.partial(project_kernel, first, 2 * width),
        grid_spec=pltpu.PrefetchScalarGridSpec(
            num_scalar_prefetch=1,
            grid=(steps,),
            in_specs=in_specs,
            out_specs=out_specs,
            scratch_shapes=[pltpu.VMEM((rows, wide), jnp.float32), pltpu.VMEM((rows, LANES), jnp.float32)],
        ),
        out_shape=out_shape,
        compiler_params=params(),
        cost_estimate=pl.CostEstimate(
            flops=2 * rows * width * wide, bytes_accessed=(rows + wide) * width * 2 + rows * wide * 4, transcendentals=0
        ),
        name="project_own" if first else "project_other",
    )(*args)


def attend_kernel(reach, starts_ref, q_ref, *rest):
    blocks = rest[: reach + 1]
    ctx_ref, keys, values, scores, acc, tops, sums = rest[reach + 1 :]
    rows = q_ref.shape[0]
    tile_rows = ctx_ref.shape[0]
    heads = q_ref.shape[1] // HEAD
    span = scores.shape[2]
    t = pl.program_id(0)

    @pl.when(t == 0)
    def _():
        for b, block in enumerate(blocks):
            keys[b * rows : (b + 1) * rows, :] = block[:, :HEAD]
            values[b * rows : (b + 1) * rows, :] = block[:, HEAD:]

    first_row = reach * rows + t * tile_rows
    row = first_row + lax.broadcasted_iota(jnp.int32, (tile_rows, span), 0)
    begin = jnp.zeros((tile_rows, span), jnp.int32)
    lowest = jnp.int32(0)
    for d in range(starts_ref.shape[0]):
        start = starts_ref[d]
        begin = jnp.where(row >= start, jnp.maximum(begin, start), begin)
        lowest = jnp.where(first_row >= start, jnp.maximum(lowest, start), lowest)
    lane = lax.broadcasted_iota(jnp.int32, (tile_rows, span), 1)
    low = lowest // span
    high = (first_row + tile_rows - 1) // span + 1
    q_rows = pl.ds(pl.multiple_of(t * tile_rows, tile_rows), tile_rows)

    tops[...] = jnp.full(tops.shape, -1e30, jnp.float32)
    sums[...] = jnp.zeros(sums.shape, jnp.float32)
    acc[...] = jnp.zeros(acc.shape, jnp.float32)

    def score(i, carry):
        place = lane + i * span
        allowed = (place >= begin) & (place <= row)
        block_keys = keys[pl.ds(pl.multiple_of(i * span, span), span), :]
        for h in range(heads):
            s = lax.dot_general(
                q_ref[q_rows, h * HEAD : (h + 1) * HEAD],
                block_keys,
                (((1,), (1,)), ((), ())),
                preferred_element_type=jnp.float32,
            )
            s = jnp.where(allowed, s, -1e30)
            scores[i, h * tile_rows : (h + 1) * tile_rows, :] = s
            top = tops[h * tile_rows : (h + 1) * tile_rows, :]
            for j in range(span // LANES):
                top = jnp.maximum(top, s[:, j * LANES : (j + 1) * LANES])
            tops[h * tile_rows : (h + 1) * tile_rows, :] = top
        return carry

    lax.fori_loop(low, high, score, 0)
    top = jnp.max(tops[...], axis=1, keepdims=True)
    tops[...] = jnp.broadcast_to(top * EXP2_SCALE, tops.shape)

    def weigh(i, carry):
        block_values = values[pl.ds(pl.multiple_of(i * span, span), span), :]
        for h in range(heads):
            part = slice(h * tile_rows, (h + 1) * tile_rows)
            top = tops[part, :]
            total = sums[part, :]
            rounded = []
            for j in range(span // LANES):
                w = jnp.exp2(scores[i, part, j * LANES : (j + 1) * LANES] * EXP2_SCALE - top)
                total = total + w
                rounded.append(w.astype(jnp.bfloat16))
            sums[part, :] = total
            acc[part, :] += jnp.dot(
                jnp.concatenate(rounded, axis=1), block_values, preferred_element_type=jnp.float32
            )
        return carry

    lax.fori_loop(low, high, weigh, 0)
    for h in range(heads):
        part = slice(h * tile_rows, (h + 1) * tile_rows)
        total = jnp.sum(sums[part, :], axis=1, keepdims=True)
        ctx_ref[:, h * HEAD : (h + 1) * HEAD] = (acc[part, :] / total).astype(jnp.bfloat16)


def attend(starts, queries, blocks):
    rows, width = queries.shape
    reach = len(blocks) - 1
    tile_rows, span = 128, 256
    heads = width // HEAD
    places = (reach + 1) * rows
    whole = lambda t, s: (0, 0)
    return pl.pallas_call(
        functools.partial(attend_kernel, reach),
        grid_spec=pltpu.PrefetchScalarGridSpec(
            num_scalar_prefetch=1,
            grid=(rows // tile_rows,),
            in_specs=[pl.BlockSpec((rows, width), whole)] + [pl.BlockSpec((rows, 2 * HEAD), whole)] * (reach + 1),
            out_specs=pl.BlockSpec((tile_rows, width), lambda t, s: (t, 0)),
            scratch_shapes=[
                pltpu.VMEM((places, HEAD), jnp.bfloat16),
                pltpu.VMEM((places, HEAD), jnp.bfloat16),
                pltpu.VMEM((places // span, heads * tile_rows, span), jnp.float32),
                pltpu.VMEM((heads * tile_rows, HEAD), jnp.float32),
                pltpu.VMEM((heads * tile_rows, LANES), jnp.float32),
                pltpu.VMEM((heads * tile_rows, LANES), jnp.float32),
            ],
        ),
        out_shape=jax.ShapeDtypeStruct((rows, width), jnp.bfloat16),
        compiler_params=params(),
        cost_estimate=pl.CostEstimate(
            flops=4 * rows * width * places, bytes_accessed=rows * width * 8, transcendentals=rows * heads * places
        ),
        name="attend",
    )(starts, queries, *blocks)


def output_kernel(tp_ref, tokens_ref, mine_ref, other_ref, w_mine_ref, w_other_ref, out_ref):
    mine = jnp.dot(mine_ref[...], w_mine_ref[...], preferred_element_type=jnp.float32).astype(jnp.bfloat16)
    other = jnp.dot(other_ref[...], w_other_ref[...], preferred_element_type=jnp.float32).astype(jnp.bfloat16)
    out = tokens_ref[...].astype(jnp.float32) + mine.astype(jnp.float32) + other.astype(jnp.float32)
    out_ref[...] = out.astype(jnp.bfloat16)


def output(half, tokens, mine, other, w_out, w_other):
    rows, width = tokens.shape
    depth = mine.shape[1]
    step = 512
    steps = width // step
    whole = lambda j, s: (0, 0)
    here = lambda j, s: (0, j)
    return pl.pallas_call(
        output_kernel,
        grid_spec=pltpu.PrefetchScalarGridSpec(
            num_scalar_prefetch=1,
            grid=(steps,),
            in_specs=[
                pl.BlockSpec((rows, step), here),
                pl.BlockSpec((rows, depth), whole),
                pl.BlockSpec((rows, depth), whole),
                pl.BlockSpec((depth, step), lambda j, s: (0, s[0] * steps + j)),
                pl.BlockSpec((depth, step), here),
            ],
            out_specs=pl.BlockSpec((rows, step), here),
        ),
        out_shape=jax.ShapeDtypeStruct((rows, width), jnp.bfloat16),
        compiler_params=params(),
        cost_estimate=pl.CostEstimate(
            flops=4 * rows * width * depth, bytes_accessed=(4 * rows + 4 * depth) * width, transcendentals=0
        ),
        name="output",
    )(half, tokens, mine, other, w_out, w_other)


def shift(value, axis, steps):
    count = lax.axis_size(axis)
    return lax.ppermute(value, axis, [(source, source + steps) for source in range(count - steps)])


def rotary_tables(lengths, places):
    doc_ends = jnp.cumsum(lengths)
    first_rows = jnp.max(jnp.where(places[:, None] >= doc_ends[None, :], doc_ends[None, :], 0), axis=1)
    within = places - first_rows
    half = HEAD // 2
    frequency = 500000.0 ** (-jnp.arange(half, dtype=jnp.float32) * 2.0 / HEAD)
    frequency = jnp.concatenate([frequency, frequency])
    angles = within.astype(jnp.float32)[:, None] * frequency[None, :]
    sign = jnp.where(jnp.arange(HEAD) < half, -1.0, 1.0)
    return jnp.cos(angles), jnp.sin(angles) * sign[None, :]


def local(tokens, norm_gain, lengths, w_query, w_key, w_value, w_out):
    rows, width = tokens.shape
    me = lax.axis_index("tp")
    mine_half = me[None].astype(jnp.int32)
    other_half = 1 - mine_half
    first_here = lax.axis_index("dp") * rows
    reach = (rows + MOST - 2) // rows

    tokens_other = lax.ppermute(tokens, "tp", SWAP)
    sums = squares(tokens, norm_gain.reshape(-1, LANES))
    sums_other = lax.ppermute(sums, "tp", SWAP)
    tables = rotary_tables(lengths, first_here + jnp.arange(rows, dtype=jnp.int32))
    partial = project(mine_half, tokens, sums, sums_other, w_query, w_key, w_value)
    w_send = lax.dynamic_slice_in_dim(w_out, (1 - me) * width, width, axis=1)
    w_other = lax.ppermute(w_send, "tp", SWAP)
    queries, kv = project(other_half, tokens_other, sums, sums_other, w_query, w_key, w_value, partial, tables)
    blocks = [shift(kv, "dp", d) for d in range(reach, 0, -1)] + [kv]
    starts = jnp.cumsum(lengths) - lengths - first_here + reach * rows
    context = attend(starts.astype(jnp.int32), queries, blocks)
    context_other = lax.ppermute(context, "tp", SWAP)
    return output(mine_half, tokens, context, context_other, w_out, w_other)


def solution(mesh):
    placed = (P(("grp", "dp"), "tp"), P("tp"), P("grp"), P(None, "tp"), P(), P(), P("tp", None))
    return jax.shard_map(
        local, mesh=mesh, in_specs=placed, out_specs=P(("grp", "dp"), "tp"), check_vma=False
    )
```

```python
import functools
import math

import jax
import jax.numpy as jnp
from jax import lax
from jax.experimental import pallas as pl
from jax.experimental.pallas import tpu as pltpu
from jax.sharding import PartitionSpec as P

HEAD = 128
MOST = 1536
LANES = 128
SWAP = [(0, 1), (1, 0)]
MIB = 1024 * 1024
EXP2_SCALE = math.log2(math.e) / HEAD**0.5


def in_hbm(*arrays):
    return [pltpu.with_memory_space_constraint(array, pltpu.HBM) for array in arrays]


def params(mib):
    return pltpu.CompilerParams(vmem_limit_bytes=mib * MIB)


SCALAR = pl.BlockSpec(memory_space=pltpu.SMEM)
WHOLE = pl.BlockSpec(memory_space=pltpu.VMEM)


def prepare_kernel(gain_ref, tokens_hbm, wk_hbm, wv_hbm, wq_hbm, sums_ref, tokens_ref, wkv_ref, wq_ref, sems):
    rows, width = tokens_ref.shape
    step = 1024
    chunks = width // step
    loads = [
        pltpu.make_async_copy(tokens_hbm.at[:, c * step : (c + 1) * step], tokens_ref.at[:, c * step : (c + 1) * step], sems.at[c])
        for c in range(chunks)
    ]
    loads += [
        pltpu.make_async_copy(wk_hbm, wkv_ref.at[:, :HEAD], sems.at[chunks]),
        pltpu.make_async_copy(wv_hbm, wkv_ref.at[:, HEAD:], sems.at[chunks + 1]),
        pltpu.make_async_copy(wq_hbm, wq_ref, sems.at[chunks + 2]),
    ]
    for load in loads:
        load.start()
    sums_ref[rows:, :] = gain_ref[...].astype(jnp.float32)
    for c in range(chunks):
        loads[c].wait()
        total = sums_ref[0:rows, :] if c else jnp.zeros((rows, LANES), jnp.float32)
        for j in range(c * step // LANES, (c + 1) * step // LANES):
            wide = tokens_ref[:, j * LANES : (j + 1) * LANES].astype(jnp.float32)
            total = total + wide * wide
        sums_ref[0:rows, :] = total
    for load in loads[chunks:]:
        load.wait()


def prepare(tokens, gain, wk, wv, wq):
    rows, width = tokens.shape
    gain_rows = gain.shape[0]
    hbm = pl.BlockSpec(memory_space=pltpu.HBM)
    return pl.pallas_call(
        prepare_kernel,
        in_specs=[WHOLE] + [hbm] * 4,
        out_specs=[WHOLE] * 4,
        out_shape=[
            jax.ShapeDtypeStruct((rows + gain_rows, LANES), jnp.float32),
            jax.ShapeDtypeStruct(tokens.shape, tokens.dtype),
            jax.ShapeDtypeStruct((wk.shape[0], 2 * HEAD), wk.dtype),
            jax.ShapeDtypeStruct(wq.shape, wq.dtype),
        ],
        scratch_shapes=[pltpu.SemaphoreType.DMA((width // 1024 + 3,))],
        compiler_params=params(8),
        cost_estimate=pl.CostEstimate(flops=rows * width * 2, bytes_accessed=16 * MIB, transcendentals=0),
        name="prepare",
    )(gain, *in_hbm(tokens, wk, wv, wq))


def inverse_norm(mine, other, model):
    mean = jnp.sum(mine + other, axis=1, keepdims=True) * (1.0 / model)
    return jnp.broadcast_to(lax.rsqrt(mean + 1e-05), mine.shape)


def normalize(block, inverse, gains_ref, gain_row):
    parts = []
    for j in range(block.shape[1] // LANES):
        wide = block[:, j * LANES : (j + 1) * LANES].astype(jnp.float32)
        gain = gains_ref[gain_row + j : gain_row + j + 1, :]
        parts.append((wide * inverse * gain).astype(jnp.bfloat16))
    return jnp.concatenate(parts, axis=1)


def turn(x, cosine, sine):
    return (x * cosine + pltpu.roll(x, HEAD // 2, 1) * sine).astype(jnp.bfloat16)


def keys_kernel(
    half_ref, mine_ref, other_ref, smine_ref, sother_ref, cos_ref, sin_ref, wkv_ref, wout_ref, kv_ref, wsend_ref, sem
):
    rows, width = mine_ref.shape
    part_rows = rows // 2
    step = 1024
    me = half_ref[0]
    send_start = pl.multiple_of((1 - me) * width, width)
    send = pltpu.make_async_copy(wout_ref.at[:, pl.ds(send_start, width)], wsend_ref, sem)
    send.start()
    here = pl.ds(pl.multiple_of(me * part_rows, part_rows), part_rows)
    inverse = inverse_norm(smine_ref[here, :], sother_ref[here, :], 2 * width)
    total = jnp.zeros((part_rows, 2 * HEAD), jnp.float32)
    for part in range(2):
        tokens_ref, sums_ref = ((mine_ref, smine_ref), (other_ref, sother_ref))[part]
        base = (me if part == 0 else 1 - me) * width
        for c in range(width // step):
            block = tokens_ref[here, c * step : (c + 1) * step]
            normed = normalize(block, inverse, sums_ref, rows + c * (step // LANES))
            depth = pl.ds(pl.multiple_of(base + c * step, step), step)
            total = total + jnp.dot(normed, wkv_ref[depth, :], preferred_element_type=jnp.float32)
    kv_ref[:, :HEAD] = turn(total[:, :HEAD], cos_ref[here, :], sin_ref[here, :])
    kv_ref[:, HEAD:] = total[:, HEAD:].astype(jnp.bfloat16)
    send.wait()


def keys_values(half, tokens, tokens_other, sums, sums_other, tables, wkv, w_out):
    rows, width = tokens.shape
    part = rows // 2
    hbm = pl.BlockSpec(memory_space=pltpu.HBM)
    return pl.pallas_call(
        keys_kernel,
        in_specs=[SCALAR] + [WHOLE] * 7 + [hbm],
        out_specs=[WHOLE, WHOLE],
        out_shape=[
            jax.ShapeDtypeStruct((part, 2 * HEAD), jnp.bfloat16),
            jax.ShapeDtypeStruct((w_out.shape[0], width), w_out.dtype),
        ],
        scratch_shapes=[pltpu.SemaphoreType.DMA],
        compiler_params=params(8),
        cost_estimate=pl.CostEstimate(
            flops=4 * rows * width * HEAD * 2, bytes_accessed=rows * width * 2, transcendentals=0
        ),
        name="keys_values",
    )(half, tokens, tokens_other, sums, sums_other, *tables, wkv, *in_hbm(w_out))


def queries_kernel(half_ref, mine_ref, other_ref, smine_ref, sother_ref, cos_ref, sin_ref, wq_ref, wout_ref, q_ref, wkeep_ref, acc, sem):
    rows, width = mine_ref.shape
    step = 1024
    me = half_ref[0]
    keep = pltpu.make_async_copy(wout_ref.at[:, pl.ds(pl.multiple_of(me * width, width), width)], wkeep_ref, sem)
    keep.start()
    inverse = inverse_norm(smine_ref[0:rows, :], sother_ref[0:rows, :], 2 * width)
    for part in range(2):
        tokens_ref, sums_ref = ((mine_ref, smine_ref), (other_ref, sother_ref))[part]
        base = (me if part == 0 else 1 - me) * width
        for c in range(width // step):
            normed = normalize(tokens_ref[:, c * step : (c + 1) * step], inverse, sums_ref, rows + c * (step // LANES))
            depth = pl.ds(pl.multiple_of(base + c * step, step), step)
            term = jnp.dot(normed, wq_ref[depth, :], preferred_element_type=jnp.float32)
            if part == 0 and c == 0:
                acc[...] = term
            else:
                acc[...] += term
    for h in range(q_ref.shape[1] // HEAD):
        lanes = slice(h * HEAD, (h + 1) * HEAD)
        q_ref[:, lanes] = turn(acc[:, lanes], cos_ref[...], sin_ref[...])
    keep.wait()


def project_queries(half, tokens, tokens_other, sums, sums_other, tables, wq, w_out):
    rows, width = tokens.shape
    nq = wq.shape[1]
    return pl.pallas_call(
        queries_kernel,
        in_specs=[SCALAR] + [WHOLE] * 7 + [pl.BlockSpec(memory_space=pltpu.HBM)],
        out_specs=[WHOLE, WHOLE],
        out_shape=[
            jax.ShapeDtypeStruct((rows, nq), jnp.bfloat16),
            jax.ShapeDtypeStruct((w_out.shape[0], width), w_out.dtype),
        ],
        scratch_shapes=[pltpu.VMEM((rows, nq), jnp.float32), pltpu.SemaphoreType.DMA],
        compiler_params=params(8),
        cost_estimate=pl.CostEstimate(flops=4 * rows * width * nq, bytes_accessed=rows * width * 4, transcendentals=0),
        name="queries",
    )(half, tokens, tokens_other, sums, sums_other, *tables, wq, *in_hbm(w_out))


def attend_kernel(reach, half_ref, starts_ref, q_ref, *rest):
    blocks = rest[: 2 * (reach + 1)]
    ctx_ref, keys, values, scores, acc, tops, sums = rest[2 * (reach + 1) :]
    rows = q_ref.shape[0]
    tile_rows = ctx_ref.shape[0]
    heads = q_ref.shape[1] // HEAD
    span = scores.shape[2]
    t = pl.program_id(0)

    @pl.when(t == 0)
    def _():
        part = rows // 2
        for b, block in enumerate(blocks):
            which = half_ref[0] if b % 2 == 0 else 1 - half_ref[0]
            at = pl.ds(pl.multiple_of((b // 2) * rows + which * part, part), part)
            keys[at, :] = block[:, :HEAD]
            values[at, :] = block[:, HEAD:]

    first_row = reach * rows + t * tile_rows
    row = first_row + lax.broadcasted_iota(jnp.int32, (tile_rows, span), 0)
    begin = jnp.zeros((tile_rows, span), jnp.int32)
    lowest = jnp.int32(0)
    for d in range(starts_ref.shape[0]):
        start = starts_ref[d]
        begin = jnp.where(row >= start, jnp.maximum(begin, start), begin)
        lowest = jnp.where(first_row >= start, jnp.maximum(lowest, start), lowest)
    lane = lax.broadcasted_iota(jnp.int32, (tile_rows, span), 1)
    low = lowest // span
    high = (first_row + tile_rows - 1) // span + 1
    q_rows = pl.ds(pl.multiple_of(t * tile_rows, tile_rows), tile_rows)

    tops[...] = jnp.full(tops.shape, -1e30, jnp.float32)
    sums[...] = jnp.zeros(sums.shape, jnp.float32)
    acc[...] = jnp.zeros(acc.shape, jnp.float32)

    def score(i, carry):
        place = lane + i * span
        allowed = (place >= begin) & (place <= row)
        block_keys = keys[pl.ds(pl.multiple_of(i * span, span), span), :]
        for h in range(heads):
            s = lax.dot_general(
                q_ref[q_rows, h * HEAD : (h + 1) * HEAD],
                block_keys,
                (((1,), (1,)), ((), ())),
                preferred_element_type=jnp.float32,
            )
            s = jnp.where(allowed, s, -1e30)
            scores[i, h * tile_rows : (h + 1) * tile_rows, :] = s
            top = tops[h * tile_rows : (h + 1) * tile_rows, :]
            for j in range(span // LANES):
                top = jnp.maximum(top, s[:, j * LANES : (j + 1) * LANES])
            tops[h * tile_rows : (h + 1) * tile_rows, :] = top
        return carry

    lax.fori_loop(low, high, score, 0)
    top = jnp.max(tops[...], axis=1, keepdims=True)
    tops[...] = jnp.broadcast_to(top * EXP2_SCALE, tops.shape)

    def weigh(i, carry):
        block_values = values[pl.ds(pl.multiple_of(i * span, span), span), :]
        for h in range(heads):
            part = slice(h * tile_rows, (h + 1) * tile_rows)
            top = tops[part, :]
            total = sums[part, :]
            rounded = []
            for j in range(span // LANES):
                w = jnp.exp2(scores[i, part, j * LANES : (j + 1) * LANES] * EXP2_SCALE - top)
                total = total + w
                rounded.append(w.astype(jnp.bfloat16))
            sums[part, :] = total
            acc[part, :] += jnp.dot(
                jnp.concatenate(rounded, axis=1), block_values, preferred_element_type=jnp.float32
            )
        return carry

    lax.fori_loop(low, high, weigh, 0)
    for h in range(heads):
        part = slice(h * tile_rows, (h + 1) * tile_rows)
        total = jnp.sum(sums[part, :], axis=1, keepdims=True)
        ctx_ref[:, h * HEAD : (h + 1) * HEAD] = (acc[part, :] / total).astype(jnp.bfloat16)


def attend(half, starts, queries, blocks):
    rows, width = queries.shape
    reach = len(blocks) // 2 - 1
    tile_rows, span = 128, 256
    heads = width // HEAD
    places = (reach + 1) * rows
    whole = lambda t, s, u: (0, 0)
    return pl.pallas_call(
        functools.partial(attend_kernel, reach),
        grid_spec=pltpu.PrefetchScalarGridSpec(
            num_scalar_prefetch=2,
            grid=(rows // tile_rows,),
            in_specs=[pl.BlockSpec((rows, width), whole)] + [pl.BlockSpec((rows // 2, 2 * HEAD), whole)] * len(blocks),
            out_specs=pl.BlockSpec((tile_rows, width), lambda t, s, u: (t, 0)),
            scratch_shapes=[
                pltpu.VMEM((places, HEAD), jnp.bfloat16),
                pltpu.VMEM((places, HEAD), jnp.bfloat16),
                pltpu.VMEM((places // span, heads * tile_rows, span), jnp.float32),
                pltpu.VMEM((heads * tile_rows, HEAD), jnp.float32),
                pltpu.VMEM((heads * tile_rows, LANES), jnp.float32),
                pltpu.VMEM((heads * tile_rows, LANES), jnp.float32),
            ],
        ),
        out_shape=jax.ShapeDtypeStruct((rows, width), jnp.bfloat16),
        compiler_params=params(16),
        cost_estimate=pl.CostEstimate(
            flops=4 * rows * width * places, bytes_accessed=rows * width * 8, transcendentals=rows * heads * places
        ),
        name="attend",
    )(half, starts, queries, *blocks)


def output_kernel(tokens_ref, mine_ref, other_ref, w_mine_ref, w_other_ref, out_ref):
    step = out_ref.shape[1]
    here = pl.ds(pl.multiple_of(pl.program_id(0) * step, step), step)
    mine = jnp.dot(mine_ref[...], w_mine_ref[:, here], preferred_element_type=jnp.float32).astype(jnp.bfloat16)
    other = jnp.dot(other_ref[...], w_other_ref[:, here], preferred_element_type=jnp.float32).astype(jnp.bfloat16)
    out = tokens_ref[:, here].astype(jnp.float32) + mine.astype(jnp.float32) + other.astype(jnp.float32)
    out_ref[...] = out.astype(jnp.bfloat16)


def output(tokens, mine, other, w_mine, w_other):
    rows, width = tokens.shape
    depth = mine.shape[1]
    step = 512
    return pl.pallas_call(
        output_kernel,
        grid=(width // step,),
        in_specs=[WHOLE] * 5,
        out_specs=pl.BlockSpec((rows, step), lambda j: (0, j)),
        out_shape=jax.ShapeDtypeStruct((rows, width), jnp.bfloat16),
        compiler_params=params(16),
        cost_estimate=pl.CostEstimate(
            flops=4 * rows * width * depth, bytes_accessed=(4 * rows + 4 * depth) * width, transcendentals=0
        ),
        name="output",
    )(tokens, mine, other, w_mine, w_other)


def shift(value, axis, steps):
    count = lax.axis_size(axis)
    return lax.ppermute(value, axis, [(source, source + steps) for source in range(count - steps)])


def rotary_tables(lengths, places):
    doc_ends = jnp.cumsum(lengths)
    first_rows = jnp.max(jnp.where(places[:, None] >= doc_ends[None, :], doc_ends[None, :], 0), axis=1)
    within = places - first_rows
    half = HEAD // 2
    frequency = 500000.0 ** (-jnp.arange(half, dtype=jnp.float32) * 2.0 / HEAD)
    frequency = jnp.concatenate([frequency, frequency])
    angles = within.astype(jnp.float32)[:, None] * frequency[None, :]
    sign = jnp.where(jnp.arange(HEAD) < half, -1.0, 1.0)
    return jnp.cos(angles), jnp.sin(angles) * sign[None, :]


def local(tokens, norm_gain, lengths, w_query, w_key, w_value, w_out):
    rows, width = tokens.shape
    me = lax.axis_index("tp")
    mine_half = me[None].astype(jnp.int32)
    first_here = lax.axis_index("dp") * rows
    reach = (rows + MOST - 2) // rows

    tokens_other = lax.ppermute(tokens, "tp", SWAP)
    sums, tokens, wkv, wq = prepare(tokens, norm_gain.reshape(-1, LANES), w_key, w_value, w_query)
    sums_other = lax.ppermute(sums, "tp", SWAP)
    tables = rotary_tables(lengths, first_here + jnp.arange(rows, dtype=jnp.int32))

    kv, w_send = keys_values(mine_half, tokens, tokens_other, sums, sums_other, tables, wkv, w_out)
    parts = [shift(kv, "dp", d) for d in range(reach, 0, -1)]
    own_other = lax.ppermute(kv, "tp", SWAP)
    w_other = lax.ppermute(w_send, "tp", SWAP)
    queries, w_mine = project_queries(mine_half, tokens, tokens_other, sums, sums_other, tables, wq, w_out)
    parts, queries = lax.optimization_barrier((parts, queries))
    blocks = []
    for part in parts:
        blocks += [part, lax.ppermute(part, "tp", SWAP)]
    blocks += [kv, own_other]
    starts = jnp.cumsum(lengths) - lengths - first_here + reach * rows
    context = attend(mine_half, starts.astype(jnp.int32), queries, blocks)
    context_other = lax.ppermute(context, "tp", SWAP)
    return output(tokens, context, context_other, w_mine, w_other)


def solution(mesh):
    placed = (P(("grp", "dp"), "tp"), P("tp"), P("grp"), P(None, "tp"), P(), P(), P("tp", None))
    return jax.shard_map(
        local, mesh=mesh, in_specs=placed, out_specs=P(("grp", "dp"), "tp"), check_vma=False
    )
```

```python
import functools
import math

import jax
import jax.numpy as jnp
from jax import lax
from jax.experimental import pallas as pl
from jax.experimental.pallas import tpu as pltpu
from jax.sharding import PartitionSpec as P

HEAD = 128
MOST = 1536
LANES = 128
SWAP = [(0, 1), (1, 0)]
MIB = 1024 * 1024
EXP2_SCALE = math.log2(math.e) / HEAD**0.5


def in_hbm(*arrays):
    return [pltpu.with_memory_space_constraint(array, pltpu.HBM) for array in arrays]


def params(mib):
    return pltpu.CompilerParams(vmem_limit_bytes=mib * MIB)


SCALAR = pl.BlockSpec(memory_space=pltpu.SMEM)
WHOLE = pl.BlockSpec(memory_space=pltpu.VMEM)


def first_of_document(info_ref, row):
    begin = jnp.full(row.shape, info_ref[1], jnp.int32)
    for d in range(2, info_ref.shape[0]):
        begin = jnp.where(row >= info_ref[d], info_ref[d], begin)
    return begin


def prepare_kernel(
    info_ref, gain_ref, frequency_ref, tokens_hbm, wk_hbm, wv_hbm, wq_hbm, sums_ref, tokens_ref, wkv_ref, wq_ref, cos_ref, sin_ref, sems
):
    rows, width = tokens_ref.shape
    step = 1024
    chunks = width // step
    loads = [
        pltpu.make_async_copy(tokens_hbm.at[:, c * step : (c + 1) * step], tokens_ref.at[:, c * step : (c + 1) * step], sems.at[c])
        for c in range(chunks)
    ]
    loads += [
        pltpu.make_async_copy(wk_hbm, wkv_ref.at[:, :HEAD], sems.at[chunks]),
        pltpu.make_async_copy(wv_hbm, wkv_ref.at[:, HEAD:], sems.at[chunks + 1]),
        pltpu.make_async_copy(wq_hbm, wq_ref, sems.at[chunks + 2]),
    ]
    for load in loads:
        load.start()
    sums_ref[rows:, :] = gain_ref[...].astype(jnp.float32)
    for c in range(chunks):
        loads[c].wait()
        total = sums_ref[0:rows, :] if c else jnp.zeros((rows, LANES), jnp.float32)
        for j in range(c * step // LANES, (c + 1) * step // LANES):
            wide = tokens_ref[:, j * LANES : (j + 1) * LANES].astype(jnp.float32)
            total = total + wide * wide
        sums_ref[0:rows, :] = total
    row = lax.broadcasted_iota(jnp.int32, (rows, HEAD), 0)
    begin = first_of_document(info_ref, row)
    angles = (row - begin).astype(jnp.float32) * frequency_ref[...]
    lane = lax.broadcasted_iota(jnp.int32, (rows, HEAD), 1)
    cos_ref[...] = jnp.cos(angles)
    sine = jnp.sin(angles)
    sin_ref[...] = jnp.where(lane < HEAD // 2, -sine, sine)
    for load in loads[chunks:]:
        load.wait()


def prepare(info, gain, frequency, tokens, wk, wv, wq):
    rows, width = tokens.shape
    gain_rows = gain.shape[0]
    hbm = pl.BlockSpec(memory_space=pltpu.HBM)
    return pl.pallas_call(
        prepare_kernel,
        in_specs=[SCALAR, WHOLE, WHOLE] + [hbm] * 4,
        out_specs=[WHOLE] * 6,
        out_shape=[
            jax.ShapeDtypeStruct((rows + gain_rows, LANES), jnp.float32),
            jax.ShapeDtypeStruct(tokens.shape, tokens.dtype),
            jax.ShapeDtypeStruct((wk.shape[0], 2 * HEAD), wk.dtype),
            jax.ShapeDtypeStruct(wq.shape, wq.dtype),
            jax.ShapeDtypeStruct((rows, HEAD), jnp.float32),
            jax.ShapeDtypeStruct((rows, HEAD), jnp.float32),
        ],
        scratch_shapes=[pltpu.SemaphoreType.DMA((width // 1024 + 3,))],
        compiler_params=params(20),
        cost_estimate=pl.CostEstimate(flops=rows * width * 2, bytes_accessed=16 * MIB, transcendentals=0),
        name="prepare",
    )(info, gain, frequency, *in_hbm(tokens, wk, wv, wq))


def inverse_norm(mine, other, model):
    mean = jnp.sum(mine + other, axis=1, keepdims=True) * (1.0 / model)
    return jnp.broadcast_to(lax.rsqrt(mean + 1e-05), mine.shape)


def normalize(block, inverse, gains_ref, gain_row):
    parts = []
    for j in range(block.shape[1] // LANES):
        wide = block[:, j * LANES : (j + 1) * LANES].astype(jnp.float32)
        gain = gains_ref[gain_row + j : gain_row + j + 1, :]
        parts.append((wide * inverse * gain).astype(jnp.bfloat16))
    return jnp.concatenate(parts, axis=1)


def turn(x, cosine, sine):
    return (x * cosine + pltpu.roll(x, HEAD // 2, 1) * sine).astype(jnp.bfloat16)


def keys_kernel(
    info_ref, mine_ref, other_ref, smine_ref, sother_ref, cos_ref, sin_ref, wkv_ref, wout_ref, kv_ref, wsend_ref, sem
):
    rows, width = mine_ref.shape
    part_rows = rows // 2
    step = 1024
    me = info_ref[0]
    send_start = pl.multiple_of((1 - me) * width, width)
    send = pltpu.make_async_copy(wout_ref.at[:, pl.ds(send_start, width)], wsend_ref, sem)
    send.start()
    here = pl.ds(pl.multiple_of(me * part_rows, part_rows), part_rows)
    inverse = inverse_norm(smine_ref[here, :], sother_ref[here, :], 2 * width)
    totals = [jnp.zeros((part_rows, 2 * HEAD), jnp.float32)] * 2
    for c in range(width // step):
        for part in range(2):
            tokens_ref, sums_ref = ((mine_ref, smine_ref), (other_ref, sother_ref))[part]
            base = (me if part == 0 else 1 - me) * width
            block = tokens_ref[here, c * step : (c + 1) * step]
            normed = normalize(block, inverse, sums_ref, rows + c * (step // LANES))
            depth = pl.ds(pl.multiple_of(base + c * step, step), step)
            totals[part] = totals[part] + jnp.dot(normed, wkv_ref[depth, :], preferred_element_type=jnp.float32)
    total = totals[0] + totals[1]
    kv_ref[:, :HEAD] = turn(total[:, :HEAD], cos_ref[here, :], sin_ref[here, :])
    kv_ref[:, HEAD:] = total[:, HEAD:].astype(jnp.bfloat16)
    send.wait()


def keys_values(info, tokens, tokens_other, sums, sums_other, tables, wkv, w_out):
    rows, width = tokens.shape
    part = rows // 2
    hbm = pl.BlockSpec(memory_space=pltpu.HBM)
    return pl.pallas_call(
        keys_kernel,
        in_specs=[SCALAR] + [WHOLE] * 7 + [hbm],
        out_specs=[WHOLE, WHOLE],
        out_shape=[
            jax.ShapeDtypeStruct((part, 2 * HEAD), jnp.bfloat16),
            jax.ShapeDtypeStruct((w_out.shape[0], width), w_out.dtype),
        ],
        scratch_shapes=[pltpu.SemaphoreType.DMA],
        compiler_params=params(20),
        cost_estimate=pl.CostEstimate(
            flops=4 * rows * width * HEAD * 2, bytes_accessed=rows * width * 2, transcendentals=0
        ),
        name="keys_values",
    )(info, tokens, tokens_other, sums, sums_other, *tables, wkv, *in_hbm(w_out))


def queries_kernel(info_ref, mine_ref, other_ref, smine_ref, sother_ref, cos_ref, sin_ref, wq_ref, wout_ref, q_ref, wkeep_ref, acc, sem):
    rows, width = mine_ref.shape
    step = 1024
    me = info_ref[0]
    keep = pltpu.make_async_copy(wout_ref.at[:, pl.ds(pl.multiple_of(me * width, width), width)], wkeep_ref, sem)
    keep.start()
    inverse = inverse_norm(smine_ref[0:rows, :], sother_ref[0:rows, :], 2 * width)
    for c in range(width // step):
        for part in range(2):
            tokens_ref, sums_ref = ((mine_ref, smine_ref), (other_ref, sother_ref))[part]
            base = (me if part == 0 else 1 - me) * width
            normed = normalize(tokens_ref[:, c * step : (c + 1) * step], inverse, sums_ref, rows + c * (step // LANES))
            depth = pl.ds(pl.multiple_of(base + c * step, step), step)
            term = jnp.dot(normed, wq_ref[depth, :], preferred_element_type=jnp.float32)
            if c == 0:
                acc[part] = term
            else:
                acc[part] += term
    for h in range(q_ref.shape[1] // HEAD):
        lanes = slice(h * HEAD, (h + 1) * HEAD)
        q_ref[:, lanes] = turn(acc[0, :, lanes] + acc[1, :, lanes], cos_ref[...], sin_ref[...])
    keep.wait()


def project_queries(info, tokens, tokens_other, sums, sums_other, tables, wq, w_out):
    rows, width = tokens.shape
    nq = wq.shape[1]
    return pl.pallas_call(
        queries_kernel,
        in_specs=[SCALAR] + [WHOLE] * 7 + [pl.BlockSpec(memory_space=pltpu.HBM)],
        out_specs=[WHOLE, WHOLE],
        out_shape=[
            jax.ShapeDtypeStruct((rows, nq), jnp.bfloat16),
            jax.ShapeDtypeStruct((w_out.shape[0], width), w_out.dtype),
        ],
        scratch_shapes=[pltpu.VMEM((2, rows, nq), jnp.float32), pltpu.SemaphoreType.DMA],
        compiler_params=params(20),
        cost_estimate=pl.CostEstimate(flops=4 * rows * width * nq, bytes_accessed=rows * width * 4, transcendentals=0),
        name="queries",
    )(info, tokens, tokens_other, sums, sums_other, *tables, wq, *in_hbm(w_out))


def attend_kernel(reach, info_ref, q_ref, *rest):
    blocks = rest[: 2 * (reach + 1)]
    ctx_ref, keys, values, stacked, scores, acc, tops, sums = rest[2 * (reach + 1) :]
    rows = q_ref.shape[0]
    tile_rows = ctx_ref.shape[0]
    heads = q_ref.shape[1] // HEAD
    span = scores.shape[2]
    t = pl.program_id(0)

    @pl.when(t == 0)
    def _():
        part = rows // 2
        for b, block in enumerate(blocks):
            which = info_ref[0] if b % 2 == 0 else 1 - info_ref[0]
            at = pl.ds(pl.multiple_of((b // 2) * rows + which * part, part), part)
            keys[at, :] = block[:, :HEAD]
            values[at, :] = block[:, HEAD:]

    behind = reach * rows
    first_row = t * tile_rows
    row = first_row + lax.broadcasted_iota(jnp.int32, (tile_rows, span), 0)
    begin = first_of_document(info_ref, row) + behind
    row = row + behind
    lowest = info_ref[1]
    for d in range(2, info_ref.shape[0]):
        lowest = jnp.where(first_row >= info_ref[d], info_ref[d], lowest)
    lane = lax.broadcasted_iota(jnp.int32, (tile_rows, span), 1)
    low = (lowest + behind) // span
    high = (first_row + behind + tile_rows - 1) // span + 1
    q_rows = pl.ds(pl.multiple_of(first_row, tile_rows), tile_rows)
    for h in range(heads):
        stacked[h * tile_rows : (h + 1) * tile_rows, :] = q_ref[q_rows, h * HEAD : (h + 1) * HEAD]

    tops[...] = jnp.full(tops.shape, -1e30, jnp.float32)
    sums[...] = jnp.zeros(sums.shape, jnp.float32)
    acc[...] = jnp.zeros(acc.shape, jnp.float32)

    def score(i, carry):
        place = lane + i * span
        allowed = (place >= begin) & (place <= row)
        s = lax.dot_general(
            stacked[...],
            keys[pl.ds(pl.multiple_of(i * span, span), span), :],
            (((1,), (1,)), ((), ())),
            preferred_element_type=jnp.float32,
        )
        for h in range(heads):
            part = slice(h * tile_rows, (h + 1) * tile_rows)
            masked = jnp.where(allowed, s[part, :], -1e30)
            scores[i, part, :] = masked
            top = tops[part, :]
            for j in range(span // LANES):
                top = jnp.maximum(top, masked[:, j * LANES : (j + 1) * LANES])
            tops[part, :] = top
        return carry

    lax.fori_loop(low, high, score, 0)
    top = jnp.max(tops[...], axis=1, keepdims=True)
    tops[...] = jnp.broadcast_to(top * EXP2_SCALE, tops.shape)

    def weigh(i, carry):
        top = tops[...]
        total = sums[...]
        rounded = []
        for j in range(span // LANES):
            w = jnp.exp2(scores[i, :, j * LANES : (j + 1) * LANES] * EXP2_SCALE - top)
            total = total + w
            rounded.append(w.astype(jnp.bfloat16))
        sums[...] = total
        acc[...] += jnp.dot(
            jnp.concatenate(rounded, axis=1),
            values[pl.ds(pl.multiple_of(i * span, span), span), :],
            preferred_element_type=jnp.float32,
        )
        return carry

    lax.fori_loop(low, high, weigh, 0)
    for h in range(heads):
        part = slice(h * tile_rows, (h + 1) * tile_rows)
        total = jnp.sum(sums[part, :], axis=1, keepdims=True)
        ctx_ref[:, h * HEAD : (h + 1) * HEAD] = (acc[part, :] / total).astype(jnp.bfloat16)


def attend(info, queries, blocks):
    rows, width = queries.shape
    reach = len(blocks) // 2 - 1
    tile_rows, span = 128, 512
    heads = width // HEAD
    places = (reach + 1) * rows
    tall = heads * tile_rows
    return pl.pallas_call(
        functools.partial(attend_kernel, reach),
        grid=(rows // tile_rows,),
        in_specs=[SCALAR] + [WHOLE] * (1 + len(blocks)),
        out_specs=pl.BlockSpec((tile_rows, width), lambda t: (t, 0)),
        scratch_shapes=[
            pltpu.VMEM((places, HEAD), jnp.bfloat16),
            pltpu.VMEM((places, HEAD), jnp.bfloat16),
            pltpu.VMEM((tall, HEAD), jnp.bfloat16),
            pltpu.VMEM((places // span, tall, span), jnp.float32),
            pltpu.VMEM((tall, HEAD), jnp.float32),
            pltpu.VMEM((tall, LANES), jnp.float32),
            pltpu.VMEM((tall, LANES), jnp.float32),
        ],
        out_shape=jax.ShapeDtypeStruct((rows, width), jnp.bfloat16),
        compiler_params=params(20),
        cost_estimate=pl.CostEstimate(
            flops=4 * rows * width * places, bytes_accessed=rows * width * 8, transcendentals=rows * heads * places
        ),
        name="attend",
    )(info, queries, *blocks)


def output_kernel(tokens_ref, mine_ref, other_ref, w_mine_ref, w_other_ref, out_ref):
    step = out_ref.shape[1]
    here = pl.ds(pl.multiple_of(pl.program_id(0) * step, step), step)
    mine = jnp.dot(mine_ref[...], w_mine_ref[:, here], preferred_element_type=jnp.float32).astype(jnp.bfloat16)
    other = jnp.dot(other_ref[...], w_other_ref[:, here], preferred_element_type=jnp.float32).astype(jnp.bfloat16)
    out = tokens_ref[:, here].astype(jnp.float32) + mine.astype(jnp.float32) + other.astype(jnp.float32)
    out_ref[...] = out.astype(jnp.bfloat16)


def output(tokens, mine, other, w_mine, w_other):
    rows, width = tokens.shape
    depth = mine.shape[1]
    step = 1024
    return pl.pallas_call(
        output_kernel,
        grid=(width // step,),
        in_specs=[WHOLE] * 5,
        out_specs=pl.BlockSpec((rows, step), lambda j: (0, j)),
        out_shape=jax.ShapeDtypeStruct((rows, width), jnp.bfloat16),
        compiler_params=params(20),
        cost_estimate=pl.CostEstimate(
            flops=4 * rows * width * depth, bytes_accessed=(4 * rows + 4 * depth) * width, transcendentals=0
        ),
        name="output",
    )(tokens, mine, other, w_mine, w_other)


def shift(value, axis, steps):
    count = lax.axis_size(axis)
    return lax.ppermute(value, axis, [(source, source + steps) for source in range(count - steps)])


def local(tokens, norm_gain, lengths, w_query, w_key, w_value, w_out):
    rows = tokens.shape[0]
    first_here = lax.axis_index("dp") * rows
    reach = (rows + MOST - 2) // rows
    half = HEAD // 2
    frequency = 500000.0 ** (-jnp.arange(half, dtype=jnp.float32) * 2.0 / HEAD)
    frequency = jnp.concatenate([frequency, frequency])[None, :]
    starts = jnp.cumsum(lengths) - lengths - first_here
    info = jnp.concatenate([lax.axis_index("tp")[None], starts]).astype(jnp.int32)

    tokens_other = lax.ppermute(tokens, "tp", SWAP)
    sums, tokens, wkv, wq, *tables = prepare(
        info, norm_gain.reshape(-1, LANES), frequency, tokens, w_key, w_value, w_query
    )
    sums_other = lax.ppermute(sums, "tp", SWAP)

    kv, w_send = keys_values(info, tokens, tokens_other, sums, sums_other, tables, wkv, w_out)
    parts = [shift(kv, "dp", d) for d in range(reach, 0, -1)]
    own_other = lax.ppermute(kv, "tp", SWAP)
    w_other = lax.ppermute(w_send, "tp", SWAP)
    queries, w_mine = project_queries(info, tokens, tokens_other, sums, sums_other, tables, wq, w_out)
    parts, queries = lax.optimization_barrier((parts, queries))
    blocks = []
    for part in parts:
        blocks += [part, lax.ppermute(part, "tp", SWAP)]
    blocks += [kv, own_other]
    context = attend(info, queries, blocks)
    context_other = lax.ppermute(context, "tp", SWAP)
    return output(tokens, context, context_other, w_mine, w_other)


def solution(mesh):
    placed = (P(("grp", "dp"), "tp"), P("tp"), P("grp"), P(None, "tp"), P(), P(), P("tp", None))
    return jax.shard_map(
        local, mesh=mesh, in_specs=placed, out_specs=P(("grp", "dp"), "tp"), check_vma=False
    )
```

```python
import functools
import math

import jax
import jax.numpy as jnp
from jax import lax
from jax.experimental import pallas as pl
from jax.experimental.pallas import tpu as pltpu
from jax.sharding import PartitionSpec as P

HEAD = 128
MOST = 1536
LANES = 128
SWAP = [(0, 1), (1, 0)]
MIB = 1024 * 1024
EXP2_SCALE = math.log2(math.e) / HEAD**0.5

SCALAR = pl.BlockSpec(memory_space=pltpu.SMEM)
WHOLE = pl.BlockSpec(memory_space=pltpu.VMEM)
HBM = pl.BlockSpec(memory_space=pltpu.HBM)


def in_hbm(*arrays):
    return [pltpu.with_memory_space_constraint(array, pltpu.HBM) for array in arrays]


def params(mib):
    return pltpu.CompilerParams(vmem_limit_bytes=mib * MIB)


def cost(flops, moved):
    return pl.CostEstimate(flops=flops, bytes_accessed=moved, transcendentals=0)


def shaped(shape, dtype):
    return jax.ShapeDtypeStruct(shape, dtype)


def first_of_document(place_ref, lengths_ref, row):
    start = -place_ref[1]
    begin = jnp.full(row.shape, start, jnp.int32)
    for d in range(lengths_ref.shape[0] - 1):
        start = start + lengths_ref[d]
        begin = jnp.where(row >= start, start, begin)
    return begin


def squares_kernel(place_ref, frequency_ref, gain_ref, tokens_hbm, sums_ref, tokens_ref, sems):
    rows, width = tokens_ref.shape
    chunks = sems.shape[0]
    step = width // chunks
    loads = []
    for c in range(chunks):
        part = (slice(None), slice(c * step, (c + 1) * step))
        loads.append(pltpu.make_async_copy(tokens_hbm.at[part], tokens_ref.at[part], sems.at[c]))
        loads[c].start()
    sums_ref[rows:, :] = gain_ref[...].astype(jnp.float32)
    for c in range(chunks):
        loads[c].wait()
        total = sums_ref[0:rows, :] if c else jnp.zeros((rows, LANES), jnp.float32)
        for j in range(c * step // LANES, (c + 1) * step // LANES):
            wide = tokens_ref[:, j * LANES : (j + 1) * LANES].astype(jnp.float32)
            total = total + wide * wide
        sums_ref[0:rows, :] = total


def squares(place, frequency, gain, tokens):
    rows, width = tokens.shape
    return pl.pallas_call(
        squares_kernel,
        in_specs=[SCALAR, WHOLE, WHOLE, HBM],
        out_specs=[WHOLE] * 2,
        out_shape=[shaped((rows + gain.shape[0], LANES), jnp.float32), shaped(tokens.shape, tokens.dtype)],
        scratch_shapes=[pltpu.SemaphoreType.DMA((4,))],
        compiler_params=params(16),
        cost_estimate=cost(rows * width * 2, rows * width * 2),
        name="squares",
    )(place, frequency, gain, *in_hbm(tokens))


def tables_kernel(place_ref, lengths_ref, frequency_ref, wk_hbm, wv_hbm, wkv_ref, cos_ref, sin_ref, sems):
    loads = [
        pltpu.make_async_copy(wk_hbm, wkv_ref.at[:, :HEAD], sems.at[0]),
        pltpu.make_async_copy(wv_hbm, wkv_ref.at[:, HEAD:], sems.at[1]),
    ]
    for load in loads:
        load.start()
    row = lax.broadcasted_iota(jnp.int32, cos_ref.shape, 0)
    lane = lax.broadcasted_iota(jnp.int32, cos_ref.shape, 1)
    angles = (row - first_of_document(place_ref, lengths_ref, row)).astype(jnp.float32) * frequency_ref[...]
    cos_ref[...] = jnp.cos(angles)
    sine = jnp.sin(angles)
    sin_ref[...] = jnp.where(lane < HEAD // 2, -sine, sine)
    for load in loads:
        load.wait()


def tables_and_weights(place, lengths, frequency, wk, wv, rows):
    return pl.pallas_call(
        tables_kernel,
        in_specs=[SCALAR, SCALAR, WHOLE, HBM, HBM],
        out_specs=[WHOLE] * 3,
        out_shape=[
            shaped((wk.shape[0], 2 * HEAD), wk.dtype),
            shaped((rows, HEAD), jnp.float32),
            shaped((rows, HEAD), jnp.float32),
        ],
        scratch_shapes=[pltpu.SemaphoreType.DMA((2,))],
        compiler_params=params(16),
        cost_estimate=cost(rows * HEAD * 100, wk.shape[0] * HEAD * 4),
        name="tables",
    )(place, lengths, frequency, *in_hbm(wk, wv))


def normalize(block, inverse, gains_ref, gain_row):
    parts = []
    for j in range(block.shape[1] // LANES):
        wide = block[:, j * LANES : (j + 1) * LANES].astype(jnp.float32)
        gain = gains_ref[gain_row + j : gain_row + j + 1, :]
        parts.append((wide * inverse * gain).astype(jnp.bfloat16))
    return jnp.concatenate(parts, axis=1)


def turn(x, cosine, sine):
    return (x * cosine + pltpu.roll(x, HEAD // 2, 1) * sine).astype(jnp.bfloat16)


def partial_kernel(
    place_ref, tokens_ref, mine_ref, other_ref, wkv_ref, wq_hbm, normed_ref, inverse_ref, keep_ref, send_ref, wq_ref, acc, sem
):
    rows, width = tokens_ref.shape
    half = rows // 2
    step = 1024
    me = place_ref[0]
    load = pltpu.make_async_copy(wq_hbm, wq_ref, sem)
    load.start()
    mean = jnp.sum(mine_ref[0:rows, :] + other_ref[0:rows, :], axis=1, keepdims=True) * (0.5 / width)
    inverse_ref[...] = jnp.broadcast_to(lax.rsqrt(mean + 1e-05), inverse_ref.shape)
    inverse = inverse_ref[...]
    for c in range(width // step):
        columns = slice(c * step, (c + 1) * step)
        normed = normalize(tokens_ref[:, columns], inverse, mine_ref, rows + c * (step // LANES))
        normed_ref[:, columns] = normed
        depth = pl.ds(pl.multiple_of(me * width + c * step, step), step)
        term = jnp.dot(normed, wkv_ref[depth, :], preferred_element_type=jnp.float32)
        if c == 0:
            acc[...] = term
        else:
            acc[...] += term
    keep_ref[...] = acc[pl.ds(pl.multiple_of(me * half, half), half), :]
    send_ref[...] = acc[pl.ds(pl.multiple_of((1 - me) * half, half), half), :]
    load.wait()


def partial_keys(place, tokens, mine, other, wkv, wq):
    rows, width = tokens.shape
    both = 2 * HEAD
    return pl.pallas_call(
        partial_kernel,
        in_specs=[SCALAR] + [WHOLE] * 4 + [HBM],
        out_specs=[WHOLE] * 5,
        out_shape=[
            shaped(tokens.shape, jnp.bfloat16),
            shaped((rows, LANES), jnp.float32),
            shaped((rows // 2, both), jnp.float32),
            shaped((rows // 2, both), jnp.float32),
            shaped(wq.shape, wq.dtype),
        ],
        scratch_shapes=[pltpu.VMEM((rows, both), jnp.float32), pltpu.SemaphoreType.DMA],
        compiler_params=params(16),
        cost_estimate=cost(2 * rows * width * both, wq.size * 2),
        name="partial_keys",
    )(place, tokens, mine, other, wkv, *in_hbm(wq))


def keys_kernel(place_ref, mine_ref, other_ref, cos_ref, sin_ref, kv_ref):
    half = mine_ref.shape[0]
    here = pl.ds(pl.multiple_of(place_ref[0] * half, half), half)
    total = mine_ref[...] + other_ref[...]
    kv_ref[:, :HEAD] = turn(total[:, :HEAD], cos_ref[here, :], sin_ref[here, :])
    kv_ref[:, HEAD:] = total[:, HEAD:].astype(jnp.bfloat16)


def finish_keys(place, mine, other, tables):
    return pl.pallas_call(
        keys_kernel,
        in_specs=[SCALAR] + [WHOLE] * 4,
        out_specs=WHOLE,
        out_shape=shaped(mine.shape, jnp.bfloat16),
        compiler_params=params(8),
        cost_estimate=cost(mine.size * 8, mine.size * 8),
        name="keys",
    )(place, mine, other, *tables)


def queries_own_kernel(place_ref, normed_ref, wq_ref, wout_hbm, acc_ref, wsend_ref, sem):
    width = normed_ref.shape[1]
    me = place_ref[0]
    start = pl.multiple_of((1 - me) * width, width)
    load = pltpu.make_async_copy(wout_hbm.at[:, pl.ds(start, width)], wsend_ref, sem)
    load.start()
    depth = pl.ds(pl.multiple_of(me * width, width), width)
    acc_ref[...] = jnp.dot(normed_ref[...], wq_ref[depth, :], preferred_element_type=jnp.float32)
    load.wait()


def queries_own(place, normed, wq, w_out):
    rows, width = normed.shape
    nq = wq.shape[1]
    return pl.pallas_call(
        queries_own_kernel,
        in_specs=[SCALAR, WHOLE, WHOLE, HBM],
        out_specs=[WHOLE, WHOLE],
        out_shape=[shaped((rows, nq), jnp.float32), shaped((w_out.shape[0], width), w_out.dtype)],
        scratch_shapes=[pltpu.SemaphoreType.DMA],
        compiler_params=params(16),
        cost_estimate=cost(2 * rows * width * nq, w_out.size * 2),
        name="queries_own",
    )(place, normed, wq, *in_hbm(w_out))


def queries_kernel(
    place_ref, acc_ref, tokens_ref, gains_ref, inverse_ref, cos_ref, sin_ref, wq_ref, wout_hbm, q_ref, wkeep_ref, acc, sem
):
    rows, width = tokens_ref.shape
    step = 1024
    me = place_ref[0]
    load = pltpu.make_async_copy(wout_hbm.at[:, pl.ds(pl.multiple_of(me * width, width), width)], wkeep_ref, sem)
    load.start()
    inverse = inverse_ref[...]
    for c in range(width // step):
        normed = normalize(tokens_ref[:, c * step : (c + 1) * step], inverse, gains_ref, rows + c * (step // LANES))
        depth = pl.ds(pl.multiple_of((1 - me) * width + c * step, step), step)
        term = jnp.dot(normed, wq_ref[depth, :], preferred_element_type=jnp.float32)
        if c == 0:
            acc[...] = acc_ref[...] + term
        else:
            acc[...] += term
    for h in range(q_ref.shape[1] // HEAD):
        lanes = slice(h * HEAD, (h + 1) * HEAD)
        q_ref[:, lanes] = turn(acc[:, lanes], cos_ref[...], sin_ref[...])
    load.wait()


def finish_queries(place, acc, tokens_other, sums_other, inverse, tables, wq, w_out):
    rows, width = tokens_other.shape
    nq = wq.shape[1]
    return pl.pallas_call(
        queries_kernel,
        in_specs=[SCALAR] + [WHOLE] * 7 + [HBM],
        out_specs=[WHOLE, WHOLE],
        out_shape=[shaped((rows, nq), jnp.bfloat16), shaped((w_out.shape[0], width), w_out.dtype)],
        scratch_shapes=[pltpu.VMEM((rows, nq), jnp.float32), pltpu.SemaphoreType.DMA],
        compiler_params=params(16),
        cost_estimate=cost(2 * rows * width * nq, w_out.size * 2),
        name="queries",
    )(place, acc, tokens_other, sums_other, inverse, *tables, wq, *in_hbm(w_out))


def attend_kernel(reach, own, place_ref, lengths_ref, q_ref, *rest):
    count = 2 if own else 2 * reach
    blocks = rest[:count]
    rest = rest[count:]
    if own:
        acc, tops, sums, keys, values, stacked, scores = rest
    else:
        acc_ref, tops_ref, sums_ref, ctx_ref, keys, values, stacked, scores, acc, tops, sums = rest
    rows = q_ref.shape[0]
    tall = stacked.shape[0]
    heads = q_ref.shape[1] // HEAD
    tile_rows = tall // heads
    span = scores.shape[2]
    t = pl.program_id(0)

    @pl.when(t == 0)
    def _():
        part = rows // 2
        for b, block in enumerate(blocks):
            which = place_ref[0] if b % 2 == 0 else 1 - place_ref[0]
            at = pl.ds(pl.multiple_of((b // 2) * rows + which * part, part), part)
            keys[at, :] = block[:, :HEAD]
            values[at, :] = block[:, HEAD:]

    behind = 0 if own else reach * rows
    first_row = t * tile_rows
    row = first_row + lax.broadcasted_iota(jnp.int32, (tile_rows, span), 0)
    begin = first_of_document(place_ref, lengths_ref, row) + behind
    row = row + behind
    start = -place_ref[1]
    lowest = start
    for d in range(lengths_ref.shape[0] - 1):
        start = start + lengths_ref[d]
        lowest = jnp.where(first_row >= start, start, lowest)
    lane = lax.broadcasted_iota(jnp.int32, (tile_rows, span), 1)
    if own:
        low = jnp.maximum(lowest, 0) // span
        high = (first_row + tile_rows - 1) // span + 1
    else:
        low = jnp.minimum(lowest + behind, behind) // span
        high = behind // span
    q_rows = pl.ds(pl.multiple_of(first_row, tile_rows), tile_rows)
    for h in range(heads):
        stacked[h * tile_rows : (h + 1) * tile_rows, :] = q_ref[q_rows, h * HEAD : (h + 1) * HEAD]

    if own:
        tops[...] = jnp.full(tops.shape, -1e30, jnp.float32)
        sums[...] = jnp.zeros(sums.shape, jnp.float32)
        acc[...] = jnp.zeros(acc.shape, jnp.float32)
    else:
        tops[...] = tops_ref[...]

    def score(i, carry):
        place = lane + i * span
        allowed = place >= begin
        if own:
            allowed = allowed & (place <= row)
        s = lax.dot_general(
            stacked[...],
            keys[pl.ds(pl.multiple_of(i * span, span), span), :],
            (((1,), (1,)), ((), ())),
            preferred_element_type=jnp.float32,
        )
        for h in range(heads):
            part = slice(h * tile_rows, (h + 1) * tile_rows)
            masked = jnp.where(allowed, s[part, :], -1e30)
            scores[i, part, :] = masked
            top = tops[part, :]
            for j in range(span // LANES):
                top = jnp.maximum(top, masked[:, j * LANES : (j + 1) * LANES])
            tops[part, :] = top
        return carry

    lax.fori_loop(low, high, score, 0)
    top = jnp.max(tops[...], axis=1, keepdims=True)
    tops[...] = jnp.broadcast_to(top, tops.shape)
    if not own:
        rescale = jnp.exp2((tops_ref[...] - tops[...]) * EXP2_SCALE)
        acc[...] = acc_ref[...] * rescale
        sums[...] = sums_ref[...] * rescale

    def weigh(i, carry):
        top = tops[...] * EXP2_SCALE
        total = sums[...]
        rounded = []
        for j in range(span // LANES):
            w = jnp.exp2(scores[i, :, j * LANES : (j + 1) * LANES] * EXP2_SCALE - top)
            total = total + w
            rounded.append(w.astype(jnp.bfloat16))
        sums[...] = total
        acc[...] += jnp.dot(
            jnp.concatenate(rounded, axis=1),
            values[pl.ds(pl.multiple_of(i * span, span), span), :],
            preferred_element_type=jnp.float32,
        )
        return carry

    lax.fori_loop(low, high, weigh, 0)
    if not own:
        for h in range(heads):
            part = slice(h * tile_rows, (h + 1) * tile_rows)
            total = jnp.sum(sums[part, :], axis=1, keepdims=True)
            ctx_ref[:, h * HEAD : (h + 1) * HEAD] = (acc[part, :] / total).astype(jnp.bfloat16)


def attend(place, lengths, queries, blocks, state=None):
    rows, width = queries.shape
    own = state is None
    count = len(blocks) // 2
    tile_rows, span = 128, 512 if not own else 256
    heads = width // HEAD
    places = count * rows
    tall = heads * tile_rows
    state_spec = pl.BlockSpec((tall, LANES), lambda t: (t, 0))
    scratch = [
        pltpu.VMEM((places, HEAD), jnp.bfloat16),
        pltpu.VMEM((places, HEAD), jnp.bfloat16),
        pltpu.VMEM((tall, HEAD), jnp.bfloat16),
        pltpu.VMEM((places // span, tall, span), jnp.float32),
    ]
    in_specs = [SCALAR, SCALAR, WHOLE] + [WHOLE] * len(blocks)
    if own:
        out_specs = [state_spec] * 3
        out_shape = [shaped((heads * rows, LANES), jnp.float32)] * 3
    else:
        in_specs += [state_spec] * 3
        out_specs = pl.BlockSpec((tile_rows, width), lambda t: (t, 0))
        out_shape = shaped((rows, width), jnp.bfloat16)
        scratch += [pltpu.VMEM((tall, LANES), jnp.float32)] * 3
    return pl.pallas_call(
        functools.partial(attend_kernel, count, own),
        grid=(rows // tile_rows,),
        in_specs=in_specs,
        out_specs=out_specs,
        scratch_shapes=scratch,
        out_shape=out_shape,
        compiler_params=params(20),
        cost_estimate=cost(4 * rows * width * places, rows * width * 8),
        name="attend_own" if own else "attend",
    )(place, lengths, queries, *blocks, *(state or ()))


def term_kernel(context_ref, w_ref, term_ref):
    step = 1024
    for c in range(w_ref.shape[1] // step):
        part = slice(c * step, (c + 1) * step)
        term_ref[:, part] = jnp.dot(context_ref[...], w_ref[:, part], preferred_element_type=jnp.float32).astype(jnp.bfloat16)


def group_term(context, w):
    rows, depth = context.shape
    width = w.shape[1]
    return pl.pallas_call(
        term_kernel,
        in_specs=[WHOLE] * 2,
        out_specs=WHOLE,
        out_shape=shaped((rows, width), jnp.bfloat16),
        compiler_params=params(16),
        cost_estimate=cost(2 * rows * depth * width, rows * width * 2),
        name="own_term",
    )(context, w)


def output_kernel(tokens_ref, term_ref, context_ref, w_ref, out_ref):
    step = out_ref.shape[1]
    here = pl.ds(pl.multiple_of(pl.program_id(0) * step, step), step)
    other = jnp.dot(context_ref[...], w_ref[:, here], preferred_element_type=jnp.float32).astype(jnp.bfloat16)
    out = tokens_ref[:, here].astype(jnp.float32) + term_ref[:, here].astype(jnp.float32) + other.astype(jnp.float32)
    out_ref[...] = out.astype(jnp.bfloat16)


def output(tokens, term, context, w):
    rows, width = tokens.shape
    depth = context.shape[1]
    step = 1024
    return pl.pallas_call(
        output_kernel,
        grid=(width // step,),
        in_specs=[WHOLE] * 4,
        out_specs=pl.BlockSpec((rows, step), lambda j: (0, j)),
        out_shape=shaped((rows, width), jnp.bfloat16),
        compiler_params=params(20),
        cost_estimate=cost(2 * rows * width * depth, rows * width * 4),
        name="output",
    )(tokens, term, context, w)


def shift(value, axis, steps):
    count = lax.axis_size(axis)
    return lax.ppermute(value, axis, [(source, source + steps) for source in range(count - steps)])


def swap(value):
    return lax.ppermute(value, "tp", SWAP)


def local(tokens, norm_gain, lengths, w_query, w_key, w_value, w_out):
    rows = tokens.shape[0]
    reach = (rows + MOST - 2) // rows
    place = jnp.stack([lax.axis_index("tp"), lax.axis_index("dp") * rows]).astype(jnp.int32)
    frequency = 500000.0 ** (-jnp.arange(HEAD // 2, dtype=jnp.float32) * 2.0 / HEAD)
    frequency = jnp.concatenate([frequency, frequency])[None, :]

    sums, tokens = squares(place, frequency, norm_gain.reshape(-1, LANES), tokens)
    sums_other = swap(sums)
    wkv, *tables = tables_and_weights(place, lengths, frequency, w_key, w_value, rows)
    normed, inverse, kv_keep, kv_send, wq = partial_keys(place, tokens, sums, sums_other, wkv, w_query)
    kv_come = swap(kv_send)
    tokens, kv_come = lax.optimization_barrier((tokens, kv_come))
    tokens_other = swap(tokens)
    kv = finish_keys(place, kv_keep, kv_come, tables)
    kv, normed = lax.optimization_barrier((kv, normed))
    parts = [shift(kv, "dp", d) for d in range(reach, 0, -1)]
    kv_other = swap(kv)
    acc, w_send = queries_own(place, normed, wq, w_out)
    queries, w_mine = finish_queries(place, acc, tokens_other, sums_other, inverse, tables, wq, w_out)
    state = attend(place, lengths, queries, [kv, kv_other])
    parts, state = lax.optimization_barrier((parts, state))
    blocks = []
    for part in parts:
        blocks += [part, swap(part)]
    w_send, blocks = lax.optimization_barrier((w_send, blocks))
    w_other = swap(w_send)
    context = attend(place, lengths, queries, blocks, state)
    context_other = swap(context)
    term = group_term(context, w_mine)
    return output(tokens, term, context_other, w_other)


def solution(mesh):
    placed = (P(("grp", "dp"), "tp"), P("tp"), P("grp"), P(None, "tp"), P(), P(), P("tp", None))
    return jax.shard_map(
        local, mesh=mesh, in_specs=placed, out_specs=P(("grp", "dp"), "tp"), check_vma=False
    )
```

```python
import functools
import math

import jax
import jax.numpy as jnp
from jax import lax
from jax.experimental import pallas as pl
from jax.experimental.pallas import tpu as pltpu
from jax.sharding import PartitionSpec as P

HEAD = 128
MOST = 1536
LANES = 128
SWAP = [(0, 1), (1, 0)]
MIB = 1024 * 1024
EXP2_SCALE = math.log2(math.e) / HEAD**0.5

SCALAR = pl.BlockSpec(memory_space=pltpu.SMEM)
WHOLE = pl.BlockSpec(memory_space=pltpu.VMEM)
HBM = pl.BlockSpec(memory_space=pltpu.HBM)


def in_hbm(*arrays):
    return [pltpu.with_memory_space_constraint(array, pltpu.HBM) for array in arrays]


def params(mib):
    return pltpu.CompilerParams(vmem_limit_bytes=mib * MIB)


def cost(flops, moved):
    return pl.CostEstimate(flops=flops, bytes_accessed=moved, transcendentals=0)


def shaped(shape, dtype):
    return jax.ShapeDtypeStruct(shape, dtype)


def first_of_document(place_ref, lengths_ref, row):
    start = -place_ref[1]
    begin = jnp.full(row.shape, start, jnp.int32)
    for d in range(lengths_ref.shape[0] - 1):
        start = start + lengths_ref[d]
        begin = jnp.where(row >= start, start, begin)
    return begin


def squares_kernel(place_ref, frequency_ref, gain_ref, tokens_hbm, sums_ref, tokens_ref, sems):
    rows, width = tokens_ref.shape
    chunks = sems.shape[0]
    step = width // chunks
    loads = []
    for c in range(chunks):
        part = (slice(None), slice(c * step, (c + 1) * step))
        loads.append(pltpu.make_async_copy(tokens_hbm.at[part], tokens_ref.at[part], sems.at[c]))
        loads[c].start()
    sums_ref[rows:, :] = gain_ref[...].astype(jnp.float32)
    for c in range(chunks):
        loads[c].wait()
        total = sums_ref[0:rows, :] if c else jnp.zeros((rows, LANES), jnp.float32)
        for j in range(c * step // LANES, (c + 1) * step // LANES):
            wide = tokens_ref[:, j * LANES : (j + 1) * LANES].astype(jnp.float32)
            total = total + wide * wide
        sums_ref[0:rows, :] = total


def squares(place, frequency, gain, tokens):
    rows, width = tokens.shape
    return pl.pallas_call(
        squares_kernel,
        in_specs=[SCALAR, WHOLE, WHOLE, HBM],
        out_specs=[WHOLE] * 2,
        out_shape=[shaped((rows + gain.shape[0], LANES), jnp.float32), shaped(tokens.shape, tokens.dtype)],
        scratch_shapes=[pltpu.SemaphoreType.DMA((4,))],
        compiler_params=params(16),
        cost_estimate=cost(rows * width * 2, rows * width * 2),
        name="squares",
    )(place, frequency, gain, *in_hbm(tokens))


def tables_kernel(
    place_ref, lengths_ref, frequency_ref, wk_hbm, wv_hbm, wout_hbm, wkv_ref, wsend_ref, cos_ref, sin_ref, sems
):
    width = wsend_ref.shape[1]
    start = pl.multiple_of((1 - place_ref[0]) * width, width)
    loads = [
        pltpu.make_async_copy(wk_hbm, wkv_ref.at[:, :HEAD], sems.at[0]),
        pltpu.make_async_copy(wv_hbm, wkv_ref.at[:, HEAD:], sems.at[1]),
        pltpu.make_async_copy(wout_hbm.at[:, pl.ds(start, width)], wsend_ref, sems.at[2]),
    ]
    for load in loads:
        load.start()
    row = lax.broadcasted_iota(jnp.int32, cos_ref.shape, 0)
    lane = lax.broadcasted_iota(jnp.int32, cos_ref.shape, 1)
    angles = (row - first_of_document(place_ref, lengths_ref, row)).astype(jnp.float32) * frequency_ref[...]
    cos_ref[...] = jnp.cos(angles)
    sine = jnp.sin(angles)
    sin_ref[...] = jnp.where(lane < HEAD // 2, -sine, sine)
    for load in loads:
        load.wait()


def tables_and_weights(place, lengths, frequency, wk, wv, w_out, rows, width):
    return pl.pallas_call(
        tables_kernel,
        in_specs=[SCALAR, SCALAR, WHOLE, HBM, HBM, HBM],
        out_specs=[WHOLE] * 4,
        out_shape=[
            shaped((wk.shape[0], 2 * HEAD), wk.dtype),
            shaped((w_out.shape[0], width), w_out.dtype),
            shaped((rows, HEAD), jnp.float32),
            shaped((rows, HEAD), jnp.float32),
        ],
        scratch_shapes=[pltpu.SemaphoreType.DMA((3,))],
        compiler_params=params(16),
        cost_estimate=cost(rows * HEAD * 100, wk.size * 4 + w_out.size),
        name="tables",
    )(place, lengths, frequency, *in_hbm(wk, wv, w_out))


STEP = 1024


def normalize(out_ref, out_rows, out_column, tokens_ref, rows, column, inverse, gains_ref):
    for j in range(0, STEP, LANES):
        wide = tokens_ref[rows, column + j : column + j + LANES].astype(jnp.float32)
        gain_row = tokens_ref.shape[0] + (column + j) // LANES
        gain = gains_ref[gain_row : gain_row + 1, :]
        out_ref[out_rows, out_column + j : out_column + j + LANES] = (wide * inverse * gain).astype(jnp.bfloat16)


def inverse_norm(mine_ref, other_ref, rows, width):
    mean = jnp.sum(mine_ref[rows, :] + other_ref[rows, :], axis=1, keepdims=True) * (0.5 / width)
    return jnp.broadcast_to(lax.rsqrt(mean + 1e-05), (rows.size, LANES))


def turn(x, cosine, sine):
    return (x * cosine + pltpu.roll(x, HEAD // 2, 1) * sine).astype(jnp.bfloat16)


def keys_kernel(
    place_ref, tokens_ref, tokens_other_ref, mine_ref, other_ref, cos_ref, sin_ref, wkv_ref, wq_hbm, kv_ref, normed_ref, wq_ref, acc, sem
):
    rows, width = tokens_ref.shape
    half = rows // 2
    me = place_ref[0]
    load = pltpu.make_async_copy(wq_hbm, wq_ref, sem)
    load.start()
    here = pl.ds(pl.multiple_of(me * half, half), half)
    inverse = inverse_norm(mine_ref, other_ref, here, width)
    chunks = [
        (tokens, gains, base, column)
        for column in range(0, width, STEP)
        for tokens, gains, base in ((tokens_ref, mine_ref, me), (tokens_other_ref, other_ref, 1 - me))
    ]
    every = slice(None)

    def ready(c):
        tokens, gains, _, column = chunks[c]
        normalize(normed_ref, every, c * STEP, tokens, here, column, inverse, gains)

    ready(0)
    for c, (_, _, base, column) in enumerate(chunks):
        if c + 1 < len(chunks):
            ready(c + 1)
        depth = pl.ds(pl.multiple_of(base * width + column, STEP), STEP)
        term = jnp.dot(normed_ref[:, c * STEP : (c + 1) * STEP], wkv_ref[depth, :], preferred_element_type=jnp.float32)
        if c < 2:
            acc[c] = term
        else:
            acc[c % 2] += term
    total = acc[0] + acc[1]
    kv_ref[:, :HEAD] = turn(total[:, :HEAD], cos_ref[here, :], sin_ref[here, :])
    kv_ref[:, HEAD:] = total[:, HEAD:].astype(jnp.bfloat16)
    load.wait()


def keys_values(place, tokens, tokens_other, sums, sums_other, tables, wkv, wq):
    rows, width = tokens.shape
    half = rows // 2
    both = 2 * HEAD
    return pl.pallas_call(
        keys_kernel,
        in_specs=[SCALAR] + [WHOLE] * 7 + [HBM],
        out_specs=[WHOLE] * 3,
        out_shape=[
            shaped((half, both), jnp.bfloat16),
            shaped((half, 2 * width), jnp.bfloat16),
            shaped(wq.shape, wq.dtype),
        ],
        scratch_shapes=[pltpu.VMEM((2, half, both), jnp.float32), pltpu.SemaphoreType.DMA],
        compiler_params=params(16),
        cost_estimate=cost(2 * rows * width * both, wq.size * 2),
        name="keys",
    )(place, tokens, tokens_other, sums, sums_other, *tables, wkv, *in_hbm(wq))


def queries_kernel(
    place_ref,
    tokens_ref,
    tokens_other_ref,
    mine_ref,
    other_ref,
    normed_ref,
    cos_ref,
    sin_ref,
    wq_ref,
    wout_hbm,
    q_ref,
    wkeep_ref,
    even,
    odd,
    acc,
    sem,
):
    rows, width = tokens_ref.shape
    half = rows // 2
    me = place_ref[0]
    load = pltpu.make_async_copy(wout_hbm.at[:, pl.ds(pl.multiple_of(me * width, width), width)], wkeep_ref, sem)
    load.start()
    here = pl.ds(pl.multiple_of(me * half, half), half)
    there = pl.ds(pl.multiple_of((1 - me) * half, half), half)
    inverse = inverse_norm(mine_ref, other_ref, there, width)
    chunks = [
        (tokens, gains, base, column)
        for column in range(0, width, STEP)
        for tokens, gains, base in ((tokens_ref, mine_ref, me), (tokens_other_ref, other_ref, 1 - me))
    ]
    buffers = (even, odd)

    def ready(c):
        tokens, gains, _, column = chunks[c]
        buffer = buffers[c % 2]
        buffer[:half, :] = normed_ref[:, c * STEP : (c + 1) * STEP]
        normalize(buffer, slice(half, rows), 0, tokens, there, column, inverse, gains)

    ready(0)
    for c, (_, _, base, column) in enumerate(chunks):
        if c + 1 < len(chunks):
            ready(c + 1)
        depth = pl.ds(pl.multiple_of(base * width + column, STEP), STEP)
        term = jnp.dot(buffers[c % 2][...], wq_ref[depth, :], preferred_element_type=jnp.float32)
        if c == 0:
            acc[...] = term
        else:
            acc[...] += term
    for at, part in ((here, slice(0, half)), (there, slice(half, rows))):
        for h in range(q_ref.shape[1] // HEAD):
            lanes = slice(h * HEAD, (h + 1) * HEAD)
            q_ref[at, lanes] = turn(acc[part, lanes], cos_ref[at, :], sin_ref[at, :])
    load.wait()


def project_queries(place, tokens, tokens_other, sums, sums_other, normed, tables, wq, w_out):
    rows, width = tokens.shape
    nq = wq.shape[1]
    return pl.pallas_call(
        queries_kernel,
        in_specs=[SCALAR] + [WHOLE] * 8 + [HBM],
        out_specs=[WHOLE, WHOLE],
        out_shape=[shaped((rows, nq), jnp.bfloat16), shaped((w_out.shape[0], width), w_out.dtype)],
        scratch_shapes=[pltpu.VMEM((rows, STEP), jnp.bfloat16)] * 2
        + [pltpu.VMEM((rows, nq), jnp.float32), pltpu.SemaphoreType.DMA],
        compiler_params=params(16),
        cost_estimate=cost(4 * rows * width * nq, w_out.size),
        name="queries",
    )(place, tokens, tokens_other, sums, sums_other, normed, *tables, wq, *in_hbm(w_out))


TILE = 128


def attend_kernel(own, place_ref, lengths_ref, q_ref, *rest):
    if own:
        blocks, (acc_out, tops_out, sums_out, keys, values, stacked, scores) = rest[:2], rest[2:]
    else:
        blocks, (acc_in, tops_in, sums_in, ctx_ref, keys, values, stacked, scores, acc, tops, sums) = rest[:-11], rest[-11:]
    rows = q_ref.shape[0]
    heads = q_ref.shape[1] // HEAD
    tall = heads * TILE
    span = scores.shape[2]
    part = rows // 2
    for b, block in enumerate(blocks):
        which = place_ref[0] if b % 2 == 0 else 1 - place_ref[0]
        at = pl.ds(pl.multiple_of((b // 2) * rows + which * part, part), part)
        keys[at, :] = block[:, :HEAD]
        values[at, :] = block[:, HEAD:]
    behind = 0 if own else len(blocks) // 2 * rows
    lane = lax.broadcasted_iota(jnp.int32, (TILE, span), 1)

    def tile(t, carry):
        first_row = t * TILE
        state = pl.ds(pl.multiple_of(t * tall, tall), tall)
        q_rows = pl.ds(pl.multiple_of(first_row, TILE), TILE)
        row = first_row + lax.broadcasted_iota(jnp.int32, (TILE, span), 0)
        begin = first_of_document(place_ref, lengths_ref, row) + behind
        row = row + behind
        start = -place_ref[1]
        lowest = start
        for d in range(lengths_ref.shape[0] - 1):
            start = start + lengths_ref[d]
            lowest = jnp.where(first_row >= start, start, lowest)
        if own:
            acc, tops, sums = acc_out.at[state, :], tops_out.at[state, :], sums_out.at[state, :]
            low = jnp.maximum(lowest, 0) // span
            high = (first_row + TILE - 1) // span + 1
            tops[...] = jnp.full((tall, LANES), -1e30, jnp.float32)
            sums[...] = jnp.zeros((tall, LANES), jnp.float32)
            acc[...] = jnp.zeros((tall, HEAD), jnp.float32)
        else:
            acc, tops, sums = rest[-3:]
            low = jnp.minimum(lowest + behind, behind) // span
            high = behind // span

        def score(i, carry):
            place = lane + i * span
            allowed = place >= begin
            if own:
                allowed = allowed & (place <= row)
            s = lax.dot_general(
                stacked[...],
                keys[pl.ds(pl.multiple_of(i * span, span), span), :],
                (((1,), (1,)), ((), ())),
                preferred_element_type=jnp.float32,
            )
            for h in range(heads):
                block = slice(h * TILE, (h + 1) * TILE)
                masked = jnp.where(allowed, s[block, :], -1e30)
                scores[i, block, :] = masked
                top = tops[block, :]
                for j in range(0, span, LANES):
                    top = jnp.maximum(top, masked[:, j : j + LANES])
                tops[block, :] = top
            return carry

        def weigh(i, carry):
            top = tops[...] * EXP2_SCALE
            total = sums[...]
            rounded = []
            for j in range(0, span, LANES):
                w = jnp.exp2(scores[i, :, j : j + LANES] * EXP2_SCALE - top)
                total = total + w
                rounded.append(w.astype(jnp.bfloat16))
            sums[...] = total
            acc[...] += jnp.dot(
                jnp.concatenate(rounded, axis=1),
                values[pl.ds(pl.multiple_of(i * span, span), span), :],
                preferred_element_type=jnp.float32,
            )
            return carry

        def finish(acc_ref, sums_ref):
            for h in range(heads):
                block = slice(h * TILE, (h + 1) * TILE)
                total = jnp.sum(sums_ref[block, :], axis=1, keepdims=True)
                ctx_ref[q_rows, h * HEAD : (h + 1) * HEAD] = (acc_ref[block, :] / total).astype(jnp.bfloat16)

        def work():
            for h in range(heads):
                stacked[h * TILE : (h + 1) * TILE, :] = q_ref[q_rows, h * HEAD : (h + 1) * HEAD]
            if not own:
                tops[...] = tops_in[state, :]
            lax.fori_loop(low, high, score, 0)
            top = jnp.max(tops[...], axis=1, keepdims=True)
            tops[...] = jnp.broadcast_to(top, (tall, LANES))
            if not own:
                rescale = jnp.exp2((tops_in[state, :] - tops[...]) * EXP2_SCALE)
                acc[...] = acc_in[state, :] * rescale
                sums[...] = sums_in[state, :] * rescale
            lax.fori_loop(low, high, weigh, 0)

        if own:
            work()
        else:

            @pl.when(low < high)
            def _():
                work()
                finish(acc, sums)

            @pl.when(low >= high)
            def _():
                finish(acc_in.at[state, :], sums_in.at[state, :])

        return carry

    lax.fori_loop(0, rows // TILE, tile, 0)


def attend(place, lengths, queries, blocks, state=None):
    rows, width = queries.shape
    own = state is None
    places = len(blocks) // 2 * rows
    span = 256 if own else 512
    heads = width // HEAD
    tall = heads * TILE
    scratch = [
        pltpu.VMEM((places, HEAD), jnp.bfloat16),
        pltpu.VMEM((places, HEAD), jnp.bfloat16),
        pltpu.VMEM((tall, HEAD), jnp.bfloat16),
        pltpu.VMEM((places // span, tall, span), jnp.float32),
    ]
    if own:
        out_shape = [shaped((heads * rows, LANES), jnp.float32)] * 3
    else:
        out_shape = shaped((rows, width), jnp.bfloat16)
        scratch += [pltpu.VMEM((tall, LANES), jnp.float32)] * 3
    return pl.pallas_call(
        functools.partial(attend_kernel, own),
        in_specs=[SCALAR, SCALAR] + [WHOLE] * (1 + len(blocks) + (0 if own else 3)),
        out_specs=[WHOLE] * 3 if own else WHOLE,
        scratch_shapes=scratch,
        out_shape=out_shape,
        compiler_params=params(20),
        cost_estimate=cost(4 * rows * width * places, rows * width * 8),
        name="attend_own" if own else "attend",
    )(place, lengths, queries, *blocks, *(state or ()))


def term_kernel(context_ref, w_ref, term_ref):
    step = 1024
    for c in range(w_ref.shape[1] // step):
        part = slice(c * step, (c + 1) * step)
        term_ref[:, part] = jnp.dot(context_ref[...], w_ref[:, part], preferred_element_type=jnp.float32).astype(jnp.bfloat16)


def group_term(context, w):
    rows, depth = context.shape
    width = w.shape[1]
    return pl.pallas_call(
        term_kernel,
        in_specs=[WHOLE] * 2,
        out_specs=WHOLE,
        out_shape=shaped((rows, width), jnp.bfloat16),
        compiler_params=params(16),
        cost_estimate=cost(2 * rows * depth * width, rows * width * 2),
        name="own_term",
    )(context, w)


def output_kernel(tokens_ref, term_ref, context_ref, w_ref, out_ref):
    step = out_ref.shape[1]
    here = pl.ds(pl.multiple_of(pl.program_id(0) * step, step), step)
    other = jnp.dot(context_ref[...], w_ref[:, here], preferred_element_type=jnp.float32).astype(jnp.bfloat16)
    out = tokens_ref[:, here].astype(jnp.float32) + term_ref[:, here].astype(jnp.float32) + other.astype(jnp.float32)
    out_ref[...] = out.astype(jnp.bfloat16)


def output(tokens, term, context, w):
    rows, width = tokens.shape
    depth = context.shape[1]
    step = 1024
    return pl.pallas_call(
        output_kernel,
        grid=(width // step,),
        in_specs=[WHOLE] * 4,
        out_specs=pl.BlockSpec((rows, step), lambda j: (0, j)),
        out_shape=shaped((rows, width), jnp.bfloat16),
        compiler_params=params(20),
        cost_estimate=cost(2 * rows * width * depth, rows * width * 4),
        name="output",
    )(tokens, term, context, w)


def shift(value, axis, steps):
    count = lax.axis_size(axis)
    return lax.ppermute(value, axis, [(source, source + steps) for source in range(count - steps)])


def swap(value):
    return lax.ppermute(value, "tp", SWAP)


def local(tokens, norm_gain, lengths, w_query, w_key, w_value, w_out):
    rows = tokens.shape[0]
    reach = (rows + MOST - 2) // rows
    place = jnp.stack([lax.axis_index("tp"), lax.axis_index("dp") * rows]).astype(jnp.int32)
    frequency = 500000.0 ** (-jnp.arange(HEAD // 2, dtype=jnp.float32) * 2.0 / HEAD)
    frequency = jnp.concatenate([frequency, frequency])[None, :]

    tokens_other = swap(tokens)
    sums, tokens = squares(place, frequency, norm_gain.reshape(-1, LANES), tokens)
    sums_other = swap(sums)
    wkv, w_send, *tables = tables_and_weights(place, lengths, frequency, w_key, w_value, w_out, rows, tokens.shape[1])
    kv, normed, wq = keys_values(place, tokens, tokens_other, sums, sums_other, tables, wkv, w_query)
    kv, normed = lax.optimization_barrier((kv, normed))
    parts = [shift(kv, "dp", d) for d in range(reach, 0, -1)]
    kv_other = swap(kv)
    queries, w_mine = project_queries(place, tokens, tokens_other, sums, sums_other, normed, tables, wq, w_out)
    state = attend(place, lengths, queries, [kv, kv_other])
    parts, state = lax.optimization_barrier((parts, state))
    blocks = []
    for part in parts:
        blocks += [part, swap(part)]
    blocks, w_send = lax.optimization_barrier((blocks, w_send))
    w_other = swap(w_send)
    context = attend(place, lengths, queries, blocks, state)
    context_other = swap(context)
    term = group_term(context, w_mine)
    return output(tokens, term, context_other, w_other)


def solution(mesh):
    placed = (P(("grp", "dp"), "tp"), P("tp"), P("grp"), P(None, "tp"), P(), P(), P("tp", None))
    return jax.shard_map(
        local, mesh=mesh, in_specs=placed, out_specs=P(("grp", "dp"), "tp"), check_vma=False
    )
```

```python
import functools
import math

import jax
import jax.numpy as jnp
from jax import lax
from jax.experimental import pallas as pl
from jax.experimental.pallas import tpu as pltpu
from jax.sharding import PartitionSpec as P

HEAD = 128
MOST = 1536
LANES = 128
SWAP = [(0, 1), (1, 0)]
MIB = 1024 * 1024
EXP2_SCALE = math.log2(math.e) / HEAD**0.5

SCALAR = pl.BlockSpec(memory_space=pltpu.SMEM)
WHOLE = pl.BlockSpec(memory_space=pltpu.VMEM)
HBM = pl.BlockSpec(memory_space=pltpu.HBM)


def in_hbm(*arrays):
    return [pltpu.with_memory_space_constraint(array, pltpu.HBM) for array in arrays]


def params(mib):
    return pltpu.CompilerParams(vmem_limit_bytes=mib * MIB)


def cost(flops, moved):
    return pl.CostEstimate(flops=flops, bytes_accessed=moved, transcendentals=0)


def shaped(shape, dtype):
    return jax.ShapeDtypeStruct(shape, dtype)


def first_of_document(place_ref, lengths_ref, row):
    start = -place_ref[1]
    begin = jnp.full(row.shape, start, jnp.int32)
    for d in range(lengths_ref.shape[0] - 1):
        start = start + lengths_ref[d]
        begin = jnp.where(row >= start, start, begin)
    return begin


ROWS = 64


def block_rows(start, r):
    return pl.ds(pl.multiple_of(start + r * ROWS, ROWS), ROWS)


def load_kernel(
    place_ref, lengths_ref, frequency_ref, gain_ref, tokens_hbm, wk_hbm, wv_hbm,
    sums_ref, tokens_ref, wkv_ref, cos_ref, sin_ref, sems,
):
    rows, width = tokens_ref.shape
    half = rows // 2
    chunks = sems.shape[0] - 2
    height = rows // chunks
    loads = [
        pltpu.make_async_copy(
            tokens_hbm.at[c * height : (c + 1) * height], tokens_ref.at[c * height : (c + 1) * height], sems.at[c]
        )
        for c in range(chunks)
    ]
    loads += [
        pltpu.make_async_copy(wk_hbm, wkv_ref.at[:, :HEAD], sems.at[chunks]),
        pltpu.make_async_copy(wv_hbm, wkv_ref.at[:, HEAD:], sems.at[chunks + 1]),
    ]
    for load in loads:
        load.start()
    sums_ref[rows:, :] = gain_ref[...].astype(jnp.float32)

    lane = lax.broadcasted_iota(jnp.int32, (half, HEAD), 1)
    row = lax.broadcasted_iota(jnp.int32, (half, HEAD), 0) + jnp.where(lane < HEAD // 2, 0, half)
    angles = (row - first_of_document(place_ref, lengths_ref, row)).astype(jnp.float32) * frequency_ref[...]
    for table_ref, table, sign in ((cos_ref, jnp.cos(angles), 1.0), (sin_ref, jnp.sin(angles), -1.0)):
        turned = pltpu.roll(table, HEAD // 2, 1)
        low = lane < HEAD // 2
        table_ref[:half, :] = jnp.where(low, sign * table, turned)
        table_ref[half:, :] = jnp.where(low, sign * turned, table)

    for c in range(chunks):
        loads[c].wait()
        for r in range(height // ROWS):
            at = slice(c * height + r * ROWS, c * height + (r + 1) * ROWS)
            total = jnp.zeros((ROWS, LANES), jnp.float32)
            for j in range(0, width, LANES):
                wide = tokens_ref[at, j : j + LANES].astype(jnp.float32)
                total = total + wide * wide
            sums_ref[at, :] = total
    for load in loads[chunks:]:
        load.wait()


def load_own(place, lengths, frequency, gain, tokens, wk, wv):
    rows, width = tokens.shape
    return pl.pallas_call(
        load_kernel,
        in_specs=[SCALAR, SCALAR, WHOLE, WHOLE, HBM, HBM, HBM],
        out_specs=[WHOLE] * 5,
        out_shape=[
            shaped((rows + gain.shape[0], LANES), jnp.float32),
            shaped(tokens.shape, tokens.dtype),
            shaped((wk.shape[0], 2 * HEAD), wk.dtype),
            shaped((rows, HEAD), jnp.float32),
            shaped((rows, HEAD), jnp.float32),
        ],
        scratch_shapes=[pltpu.SemaphoreType.DMA((4 + 2,))],
        compiler_params=params(16),
        cost_estimate=cost(rows * width * 2, rows * width * 2 + wk.size * 4),
        name="load_own",
    )(place, lengths, frequency, gain, *in_hbm(tokens, wk, wv))


def normalize(out_ref, out_start, tokens_ref, start, count, inverse_ref, gains_ref):
    rows, width = tokens_ref.shape

    def block(r, carry):
        at = block_rows(start, r)
        out_at = block_rows(out_start, r)
        inverse = inverse_ref[at, :]
        for j in range(0, width, LANES):
            wide = tokens_ref[at, j : j + LANES].astype(jnp.float32)
            gain = gains_ref[rows + j // LANES : rows + j // LANES + 1, :]
            out_ref[out_at, j : j + LANES] = (wide * inverse * gain).astype(jnp.bfloat16)
        return carry

    lax.fori_loop(0, count // ROWS, block, 0)


def turn(x, cosine, sine):
    return (x * cosine + pltpu.roll(x, HEAD // 2, 1) * sine).astype(jnp.bfloat16)


def own_rows(place_ref, rows):
    half = rows // 2
    return pl.ds(pl.multiple_of(place_ref[0] * half, half), half)


def features(place_ref, width, other):
    which = 1 - place_ref[0] if other else place_ref[0]
    return pl.ds(pl.multiple_of(which * width, width), width)


def keys_own_kernel(
    place_ref, tokens_ref, mine_ref, other_ref, wkv_ref, wq_hbm, normed_ref, inverse_ref, acc_ref, wq_ref, sem
):
    rows, width = tokens_ref.shape
    load = pltpu.make_async_copy(wq_hbm, wq_ref, sem)
    load.start()
    mean = jnp.sum(mine_ref[0:rows, :] + other_ref[0:rows, :], axis=1, keepdims=True) * (0.5 / width)
    inverse_ref[...] = jnp.broadcast_to(lax.rsqrt(mean + 1e-05), (rows, LANES))
    normalize(normed_ref, 0, tokens_ref, 0, rows, inverse_ref, mine_ref)
    acc_ref[...] = jnp.dot(
        normed_ref[own_rows(place_ref, rows), :],
        wkv_ref[features(place_ref, width, False), :],
        preferred_element_type=jnp.float32,
    )
    load.wait()


def keys_own(place, tokens, sums, sums_other, wkv, wq):
    rows, width = tokens.shape
    return pl.pallas_call(
        keys_own_kernel,
        in_specs=[SCALAR] + [WHOLE] * 4 + [HBM],
        out_specs=[WHOLE] * 4,
        out_shape=[
            shaped(tokens.shape, jnp.bfloat16),
            shaped((rows, LANES), jnp.float32),
            shaped((rows // 2, 2 * HEAD), jnp.float32),
            shaped(wq.shape, wq.dtype),
        ],
        scratch_shapes=[pltpu.SemaphoreType.DMA],
        compiler_params=params(16),
        cost_estimate=cost(2 * rows * width * HEAD, wq.size * 2),
        name="keys_own",
    )(place, tokens, sums, sums_other, wkv, *in_hbm(wq))


def keys_kernel(place_ref, tokens_ref, gains_ref, inverse_ref, acc_ref, wkv_ref, cos_ref, sin_ref, kv_ref, normed_ref):
    rows, width = tokens_ref.shape
    half = rows // 2
    here = own_rows(place_ref, rows)
    normalize(normed_ref, 0, tokens_ref, place_ref[0] * half, half, inverse_ref, gains_ref)
    total = acc_ref[...] + jnp.dot(
        normed_ref[...], wkv_ref[features(place_ref, width, True), :], preferred_element_type=jnp.float32
    )
    kv_ref[:, :HEAD] = turn(total[:, :HEAD], cos_ref[here, :], sin_ref[here, :])
    kv_ref[:, HEAD:] = total[:, HEAD:].astype(jnp.bfloat16)


def finish_keys(place, tokens_other, sums_other, inverse, acc, wkv, tables):
    rows, width = tokens_other.shape
    return pl.pallas_call(
        keys_kernel,
        in_specs=[SCALAR] + [WHOLE] * 7,
        out_specs=[WHOLE] * 2,
        out_shape=[shaped(acc.shape, jnp.bfloat16), shaped((rows // 2, width), jnp.bfloat16)],
        compiler_params=params(16),
        cost_estimate=cost(2 * rows * width * HEAD, rows * width),
        name="keys",
    )(place, tokens_other, sums_other, inverse, acc, wkv, *tables)


def queries_own_kernel(place_ref, normed_ref, wq_ref, acc_ref):
    width = normed_ref.shape[1]
    acc_ref[...] = jnp.dot(
        normed_ref[...], wq_ref[features(place_ref, width, False), :], preferred_element_type=jnp.float32
    )


def queries_own(place, normed, wq):
    rows, width = normed.shape
    nq = wq.shape[1]
    return pl.pallas_call(
        queries_own_kernel,
        in_specs=[SCALAR, WHOLE, WHOLE],
        out_specs=WHOLE,
        out_shape=shaped((rows, nq), jnp.float32),
        compiler_params=params(12),
        cost_estimate=cost(2 * rows * width * nq, rows * nq * 4),
        name="queries_own",
    )(place, normed, wq)


def queries_kernel(
    place_ref, tokens_ref, gains_ref, inverse_ref, acc_ref, wq_ref, cos_ref, sin_ref, ready_ref, wout_hbm,
    q_ref, wsend_ref, wkeep_ref, normed_ref, acc, sems,
):
    rows, width = tokens_ref.shape
    half = rows // 2
    loads = [
        pltpu.make_async_copy(wout_hbm.at[:, features(place_ref, width, True)], wsend_ref, sems.at[0]),
        pltpu.make_async_copy(wout_hbm.at[:, features(place_ref, width, False)], wkeep_ref, sems.at[1]),
    ]
    for load in loads:
        load.start()
    normed_ref[own_rows(place_ref, rows), :] = ready_ref[...]
    normalize(normed_ref, (1 - place_ref[0]) * half, tokens_ref, (1 - place_ref[0]) * half, half, inverse_ref, gains_ref)
    acc[...] = acc_ref[...] + jnp.dot(
        normed_ref[...], wq_ref[features(place_ref, width, True), :], preferred_element_type=jnp.float32
    )
    for h in range(q_ref.shape[1] // HEAD):
        lanes = slice(h * HEAD, (h + 1) * HEAD)
        q_ref[:, lanes] = turn(acc[:, lanes], cos_ref[...], sin_ref[...])
    for load in loads:
        load.wait()


def finish_queries(place, tokens_other, sums_other, inverse, acc, wq, tables, normed, w_out):
    rows, width = tokens_other.shape
    nq = wq.shape[1]
    half_out = shaped((w_out.shape[0], width), w_out.dtype)
    return pl.pallas_call(
        queries_kernel,
        in_specs=[SCALAR] + [WHOLE] * 8 + [HBM],
        out_specs=[WHOLE] * 3,
        out_shape=[shaped((rows, nq), jnp.bfloat16), half_out, half_out],
        scratch_shapes=[
            pltpu.VMEM((rows, width), jnp.bfloat16),
            pltpu.VMEM((rows, nq), jnp.float32),
            pltpu.SemaphoreType.DMA((2,)),
        ],
        compiler_params=params(16),
        cost_estimate=cost(2 * rows * width * nq, rows * width * 4),
        name="queries",
    )(place, tokens_other, sums_other, inverse, acc, wq, *tables, normed, *in_hbm(w_out))


TILE = 128


def attend_kernel(own, place_ref, lengths_ref, q_ref, *rest):
    if own:
        blocks, (acc_out, tops_out, sums_out, keys, values, stacked, scores) = rest[:2], rest[2:]
    else:
        blocks, (acc_in, tops_in, sums_in, ctx_ref, keys, values, stacked, scores, acc, tops, sums) = rest[:-11], rest[-11:]
    rows = q_ref.shape[0]
    heads = q_ref.shape[1] // HEAD
    tall = heads * TILE
    span = scores.shape[2]
    part = rows // 2
    for b, block in enumerate(blocks):
        which = place_ref[0] if b % 2 == 0 else 1 - place_ref[0]
        at = pl.ds(pl.multiple_of((b // 2) * rows + which * part, part), part)
        keys[at, :] = block[:, :HEAD]
        values[at, :] = block[:, HEAD:]
    behind = 0 if own else len(blocks) // 2 * rows
    lane = lax.broadcasted_iota(jnp.int32, (TILE, span), 1)

    def tile(t, carry):
        first_row = t * TILE
        state = pl.ds(pl.multiple_of(t * tall, tall), tall)
        q_rows = pl.ds(pl.multiple_of(first_row, TILE), TILE)
        row = first_row + lax.broadcasted_iota(jnp.int32, (TILE, span), 0)
        begin = first_of_document(place_ref, lengths_ref, row) + behind
        row = row + behind
        start = -place_ref[1]
        lowest = start
        for d in range(lengths_ref.shape[0] - 1):
            start = start + lengths_ref[d]
            lowest = jnp.where(first_row >= start, start, lowest)
        if own:
            acc, tops, sums = acc_out.at[state, :], tops_out.at[state, :], sums_out.at[state, :]
            low = jnp.maximum(lowest, 0) // span
            high = (first_row + TILE - 1) // span + 1
            tops[...] = jnp.full((tall, LANES), -1e30, jnp.float32)
            sums[...] = jnp.zeros((tall, LANES), jnp.float32)
            acc[...] = jnp.zeros((tall, HEAD), jnp.float32)
        else:
            acc, tops, sums = rest[-3:]
            low = jnp.minimum(lowest + behind, behind) // span
            high = behind // span

        def score(i, carry):
            place = lane + i * span
            allowed = place >= begin
            if own:
                allowed = allowed & (place <= row)
            s = lax.dot_general(
                stacked[...],
                keys[pl.ds(pl.multiple_of(i * span, span), span), :],
                (((1,), (1,)), ((), ())),
                preferred_element_type=jnp.float32,
            )
            for h in range(heads):
                block = slice(h * TILE, (h + 1) * TILE)
                masked = jnp.where(allowed, s[block, :], -1e30)
                scores[i, block, :] = masked
                top = tops[block, :]
                for j in range(0, span, LANES):
                    top = jnp.maximum(top, masked[:, j : j + LANES])
                tops[block, :] = top
            return carry

        def weigh(i, carry):
            top = tops[...] * EXP2_SCALE
            total = sums[...]
            rounded = []
            for j in range(0, span, LANES):
                w = jnp.exp2(scores[i, :, j : j + LANES] * EXP2_SCALE - top)
                total = total + w
                rounded.append(w.astype(jnp.bfloat16))
            sums[...] = total
            acc[...] += jnp.dot(
                jnp.concatenate(rounded, axis=1),
                values[pl.ds(pl.multiple_of(i * span, span), span), :],
                preferred_element_type=jnp.float32,
            )
            return carry

        def finish(acc_ref, sums_ref):
            for h in range(heads):
                block = slice(h * TILE, (h + 1) * TILE)
                total = jnp.sum(sums_ref[block, :], axis=1, keepdims=True)
                ctx_ref[q_rows, h * HEAD : (h + 1) * HEAD] = (acc_ref[block, :] / total).astype(jnp.bfloat16)

        def work():
            for h in range(heads):
                stacked[h * TILE : (h + 1) * TILE, :] = q_ref[q_rows, h * HEAD : (h + 1) * HEAD]
            if not own:
                tops[...] = tops_in[state, :]
            lax.fori_loop(low, high, score, 0)
            top = jnp.max(tops[...], axis=1, keepdims=True)
            tops[...] = jnp.broadcast_to(top, (tall, LANES))
            if not own:
                rescale = jnp.exp2((tops_in[state, :] - tops[...]) * EXP2_SCALE)
                acc[...] = acc_in[state, :] * rescale
                sums[...] = sums_in[state, :] * rescale
            lax.fori_loop(low, high, weigh, 0)

        if own:
            work()
        else:

            @pl.when(low < high)
            def _():
                work()
                finish(acc, sums)

            @pl.when(low >= high)
            def _():
                finish(acc_in.at[state, :], sums_in.at[state, :])

        return carry

    lax.fori_loop(0, rows // TILE, tile, 0)


def attend(place, lengths, queries, blocks, state=None):
    rows, width = queries.shape
    own = state is None
    places = len(blocks) // 2 * rows
    span = 256 if own else 512
    heads = width // HEAD
    tall = heads * TILE
    scratch = [
        pltpu.VMEM((places, HEAD), jnp.bfloat16),
        pltpu.VMEM((places, HEAD), jnp.bfloat16),
        pltpu.VMEM((tall, HEAD), jnp.bfloat16),
        pltpu.VMEM((places // span, tall, span), jnp.float32),
    ]
    if own:
        out_shape = [shaped((heads * rows, LANES), jnp.float32)] * 3
    else:
        out_shape = shaped((rows, width), jnp.bfloat16)
        scratch += [pltpu.VMEM((tall, LANES), jnp.float32)] * 3
    return pl.pallas_call(
        functools.partial(attend_kernel, own),
        in_specs=[SCALAR, SCALAR] + [WHOLE] * (1 + len(blocks) + (0 if own else 3)),
        out_specs=[WHOLE] * 3 if own else WHOLE,
        scratch_shapes=scratch,
        out_shape=out_shape,
        compiler_params=params(20),
        cost_estimate=cost(4 * rows * width * places, rows * width * 8),
        name="attend_own" if own else "attend",
    )(place, lengths, queries, *blocks, *(state or ()))


def term_kernel(context_ref, w_ref, term_ref):
    step = 1024
    for c in range(w_ref.shape[1] // step):
        part = slice(c * step, (c + 1) * step)
        term_ref[:, part] = jnp.dot(context_ref[...], w_ref[:, part], preferred_element_type=jnp.float32).astype(jnp.bfloat16)


def group_term(context, w):
    rows, depth = context.shape
    width = w.shape[1]
    return pl.pallas_call(
        term_kernel,
        in_specs=[WHOLE] * 2,
        out_specs=WHOLE,
        out_shape=shaped((rows, width), jnp.bfloat16),
        compiler_params=params(16),
        cost_estimate=cost(2 * rows * depth * width, rows * width * 2),
        name="own_term",
    )(context, w)


def output_kernel(tokens_ref, term_ref, context_ref, w_ref, out_ref):
    step = out_ref.shape[1]
    here = pl.ds(pl.multiple_of(pl.program_id(0) * step, step), step)
    other = jnp.dot(context_ref[...], w_ref[:, here], preferred_element_type=jnp.float32).astype(jnp.bfloat16)
    out = tokens_ref[:, here].astype(jnp.float32) + term_ref[:, here].astype(jnp.float32) + other.astype(jnp.float32)
    out_ref[...] = out.astype(jnp.bfloat16)


def output(tokens, term, context, w):
    rows, width = tokens.shape
    depth = context.shape[1]
    step = 1024
    return pl.pallas_call(
        output_kernel,
        grid=(width // step,),
        in_specs=[WHOLE] * 4,
        out_specs=pl.BlockSpec((rows, step), lambda j: (0, j)),
        out_shape=shaped((rows, width), jnp.bfloat16),
        compiler_params=params(20),
        cost_estimate=cost(2 * rows * width * depth, rows * width * 4),
        name="output",
    )(tokens, term, context, w)


def shift(value, axis, steps):
    count = lax.axis_size(axis)
    return lax.ppermute(value, axis, [(source, source + steps) for source in range(count - steps)])


def swap(value):
    return lax.ppermute(value, "tp", SWAP)


def local(tokens, norm_gain, lengths, w_query, w_key, w_value, w_out):
    rows = tokens.shape[0]
    reach = (rows + MOST - 2) // rows
    place = jnp.stack([lax.axis_index("tp"), lax.axis_index("dp") * rows]).astype(jnp.int32)
    frequency = 500000.0 ** (-jnp.arange(HEAD // 2, dtype=jnp.float32) * 2.0 / HEAD)
    frequency = jnp.concatenate([frequency, frequency])[None, :]

    sums, tokens, wkv, *tables = load_own(
        place, lengths, frequency, norm_gain.reshape(-1, LANES), tokens, w_key, w_value
    )
    sums_other = swap(sums)
    tokens, sums_other = lax.optimization_barrier((tokens, sums_other))
    tokens_other = swap(tokens)
    normed, inverse, kv_partial, wq = keys_own(place, tokens, sums, sums_other, wkv, w_query)
    partial = queries_own(place, normed, wq)
    tokens_other, partial = lax.optimization_barrier((tokens_other, partial))
    kv, normed = finish_keys(place, tokens_other, sums_other, inverse, kv_partial, wkv, tables)
    kv, normed = lax.optimization_barrier((kv, normed))
    parts = [shift(kv, "dp", d) for d in range(reach, 0, -1)]
    kv_other = swap(kv)
    queries, w_send, w_mine = finish_queries(
        place, tokens_other, sums_other, inverse, partial, wq, tables, normed, w_out
    )
    state = attend(place, lengths, queries, [kv, kv_other])
    parts, state = lax.optimization_barrier((parts, state))
    blocks = []
    for part in parts:
        blocks += [part, swap(part)]
    blocks, w_send = lax.optimization_barrier((blocks, w_send))
    w_other = swap(w_send)
    context = attend(place, lengths, queries, blocks, state)
    context_other = swap(context)
    term = group_term(context, w_mine)
    return output(tokens, term, context_other, w_other)


def solution(mesh):
    placed = (P(("grp", "dp"), "tp"), P("tp"), P("grp"), P(None, "tp"), P(), P(), P("tp", None))
    return jax.shard_map(
        local, mesh=mesh, in_specs=placed, out_specs=P(("grp", "dp"), "tp"), check_vma=False
    )
```

```python
import functools
import math

import jax
import jax.numpy as jnp
from jax import lax
from jax.experimental import pallas as pl
from jax.experimental.pallas import tpu as pltpu
from jax.sharding import PartitionSpec as P

HEAD = 128
MOST = 1536
LANES = 128
SWAP = [(0, 1), (1, 0)]
MIB = 1024 * 1024
EXP2_SCALE = math.log2(math.e) / HEAD**0.5

SCALAR = pl.BlockSpec(memory_space=pltpu.SMEM)
WHOLE = pl.BlockSpec(memory_space=pltpu.VMEM)
HBM = pl.BlockSpec(memory_space=pltpu.HBM)


def in_hbm(*arrays):
    return [pltpu.with_memory_space_constraint(array, pltpu.HBM) for array in arrays]


def params(mib):
    return pltpu.CompilerParams(vmem_limit_bytes=mib * MIB)


def cost(flops, moved):
    return pl.CostEstimate(flops=flops, bytes_accessed=moved, transcendentals=0)


SMALL = cost(1, 1)


def shaped(shape, dtype):
    return jax.ShapeDtypeStruct(shape, dtype)


def first_of_document(place_ref, row):
    start = -place_ref[1]
    begin = jnp.full(jnp.shape(row), start, jnp.int32)
    for d in range(2, place_ref.shape[0] - 1):
        start = start + place_ref[d]
        begin = jnp.where(row >= start, start, begin)
    return begin


ROWS = 64
WIDE = 256


def block_rows(start, r):
    return pl.ds(pl.multiple_of(start + r * ROWS, ROWS), ROWS)


def wide_slice(ref, at, j):
    wide = ref[at, j : j + WIDE].astype(jnp.float32)
    return [wide[:, i : i + LANES] for i in range(0, WIDE, LANES)]


def squares_kernel(place_ref, frequency_ref, gain_hbm, tokens_hbm, sums_ref, tokens_ref, gain_ref, sems):
    rows, width = tokens_ref.shape
    chunks = sems.shape[0] - 1
    height = rows // chunks
    loads = [
        pltpu.make_async_copy(
            tokens_hbm.at[c * height : (c + 1) * height], tokens_ref.at[c * height : (c + 1) * height], sems.at[c]
        )
        for c in range(chunks)
    ]
    loads.append(pltpu.make_async_copy(gain_hbm, gain_ref, sems.at[chunks]))
    for load in loads:
        load.start()
    for c in range(chunks):
        loads[c].wait()
        for r in range(height // ROWS):
            at = slice(c * height + r * ROWS, c * height + (r + 1) * ROWS)
            total = jnp.zeros((ROWS, LANES), jnp.float32)
            for j in range(0, width, WIDE):
                for wide in wide_slice(tokens_ref, at, j):
                    total = total + wide * wide
            sums_ref[at, :] = total
    loads[chunks].wait()
    sums_ref[rows:, :] = gain_ref[...].astype(jnp.float32)


def squares(place, frequency, gain, tokens):
    rows, width = tokens.shape
    return pl.pallas_call(
        squares_kernel,
        in_specs=[SCALAR, WHOLE, HBM, HBM],
        out_specs=[WHOLE] * 2,
        out_shape=[shaped((rows + gain.shape[0], LANES), jnp.float32), shaped(tokens.shape, tokens.dtype)],
        scratch_shapes=[pltpu.VMEM(gain.shape, gain.dtype), pltpu.SemaphoreType.DMA((8 + 1,))],
        compiler_params=params(16),
        cost_estimate=cost(rows * width * 2, rows * width * 2),
        name="squares",
    )(place, frequency, *in_hbm(gain, tokens))


def tables_kernel(place_ref, frequency_ref, wk_hbm, wv_hbm, wkv_ref, cos_ref, sin_ref, sems):
    rows = cos_ref.shape[0]
    half = rows // 2
    loads = [
        pltpu.make_async_copy(wk_hbm, wkv_ref.at[:, :HEAD], sems.at[0]),
        pltpu.make_async_copy(wv_hbm, wkv_ref.at[:, HEAD:], sems.at[1]),
    ]
    for load in loads:
        load.start()
    lane = lax.broadcasted_iota(jnp.int32, (half, HEAD), 1)
    row = lax.broadcasted_iota(jnp.int32, (half, HEAD), 0) + jnp.where(lane < HEAD // 2, 0, half)
    angles = (row - first_of_document(place_ref, row)).astype(jnp.float32) * frequency_ref[...]
    for table_ref, table, sign in ((cos_ref, jnp.cos(angles), 1.0), (sin_ref, jnp.sin(angles), -1.0)):
        turned = pltpu.roll(table, HEAD // 2, 1)
        low = lane < HEAD // 2
        table_ref[:half, :] = jnp.where(low, sign * table, turned)
        table_ref[half:, :] = jnp.where(low, sign * turned, table)
    for load in loads:
        load.wait()


def tables_and_weights(place, frequency, wk, wv, rows):
    return pl.pallas_call(
        tables_kernel,
        in_specs=[SCALAR, WHOLE, HBM, HBM],
        out_specs=[WHOLE] * 3,
        out_shape=[
            shaped((wk.shape[0], 2 * HEAD), wk.dtype),
            shaped((rows, HEAD), jnp.float32),
            shaped((rows, HEAD), jnp.float32),
        ],
        scratch_shapes=[pltpu.SemaphoreType.DMA((2,))],
        compiler_params=params(16),
        cost_estimate=cost(rows * HEAD * 100, wk.size * 4),
        name="tables",
    )(place, frequency, *in_hbm(wk, wv))


def normalize(out_ref, out_start, tokens_ref, start, count, inverse_ref, gains_ref):
    rows, width = tokens_ref.shape

    def block(r, carry):
        at = block_rows(start, r)
        out_at = block_rows(out_start, r)
        inverse = inverse_ref[at, :]
        for j in range(0, width, WIDE):
            normed = []
            for i, wide in enumerate(wide_slice(tokens_ref, at, j)):
                gain_row = rows + j // LANES + i
                normed.append(wide * inverse * gains_ref[gain_row : gain_row + 1, :])
            out_ref[out_at, j : j + WIDE] = jnp.concatenate(normed, axis=1).astype(jnp.bfloat16)
        return carry

    lax.fori_loop(0, count // ROWS, block, 0)


def turn(x, cosine, sine):
    return (x * cosine + pltpu.roll(x, HEAD // 2, 1) * sine).astype(jnp.bfloat16)


def own_rows(place_ref, rows):
    half = rows // 2
    return pl.ds(pl.multiple_of(place_ref[0] * half, half), half)


def features(place_ref, width, other):
    which = 1 - place_ref[0] if other else place_ref[0]
    return pl.ds(pl.multiple_of(which * width, width), width)


def keys_own_kernel(
    place_ref, tokens_ref, mine_ref, other_ref, wkv_ref, wq_hbm, normed_ref, inverse_ref, acc_ref, wq_ref, sem
):
    rows, width = tokens_ref.shape
    load = pltpu.make_async_copy(wq_hbm, wq_ref, sem)
    load.start()
    mean = jnp.sum(mine_ref[0:rows, :] + other_ref[0:rows, :], axis=1, keepdims=True) * (0.5 / width)
    inverse_ref[...] = jnp.broadcast_to(lax.rsqrt(mean + 1e-05), (rows, LANES))
    normalize(normed_ref, 0, tokens_ref, 0, rows, inverse_ref, mine_ref)
    acc_ref[...] = jnp.dot(
        normed_ref[own_rows(place_ref, rows), :],
        wkv_ref[features(place_ref, width, False), :],
        preferred_element_type=jnp.float32,
    )
    load.wait()


def keys_own(place, tokens, sums, sums_other, wkv, wq):
    rows, width = tokens.shape
    return pl.pallas_call(
        keys_own_kernel,
        in_specs=[SCALAR] + [WHOLE] * 4 + [HBM],
        out_specs=[WHOLE] * 4,
        out_shape=[
            shaped(tokens.shape, jnp.bfloat16),
            shaped((rows, LANES), jnp.float32),
            shaped((rows // 2, 2 * HEAD), jnp.float32),
            shaped(wq.shape, wq.dtype),
        ],
        scratch_shapes=[pltpu.SemaphoreType.DMA],
        compiler_params=params(16),
        cost_estimate=cost(2 * rows * width * HEAD, wq.size * 2),
        name="keys_own",
    )(place, tokens, sums, sums_other, wkv, *in_hbm(wq))


def keys_kernel(place_ref, tokens_ref, gains_ref, inverse_ref, acc_ref, wkv_ref, cos_ref, sin_ref, kv_ref, normed_ref):
    rows, width = tokens_ref.shape
    half = rows // 2
    here = own_rows(place_ref, rows)
    normalize(normed_ref, 0, tokens_ref, place_ref[0] * half, half, inverse_ref, gains_ref)
    total = acc_ref[...] + jnp.dot(
        normed_ref[...], wkv_ref[features(place_ref, width, True), :], preferred_element_type=jnp.float32
    )
    kv_ref[:, :HEAD] = turn(total[:, :HEAD], cos_ref[here, :], sin_ref[here, :])
    kv_ref[:, HEAD:] = total[:, HEAD:].astype(jnp.bfloat16)


def finish_keys(place, tokens_other, sums_other, inverse, acc, wkv, tables):
    rows, width = tokens_other.shape
    return pl.pallas_call(
        keys_kernel,
        in_specs=[SCALAR] + [WHOLE] * 7,
        out_specs=[WHOLE] * 2,
        out_shape=[shaped(acc.shape, jnp.bfloat16), shaped((rows // 2, width), jnp.bfloat16)],
        compiler_params=params(16),
        cost_estimate=cost(2 * rows * width * HEAD, rows * width),
        name="keys",
    )(place, tokens_other, sums_other, inverse, acc, wkv, *tables)


def join_kernel(place_ref, mine_ref, other_ref, out_ref):
    half = mine_ref.shape[0]
    for block, which in ((mine_ref, place_ref[0]), (other_ref, 1 - place_ref[0])):
        out_ref[pl.ds(pl.multiple_of(which * half, half), half), :] = block[...]


def join(place, mine, other):
    half, width = mine.shape
    return pl.pallas_call(
        join_kernel,
        in_specs=[SCALAR] + [WHOLE] * 2,
        out_specs=WHOLE,
        out_shape=shaped((2 * half, width), mine.dtype),
        compiler_params=params(8),
        cost_estimate=SMALL,
        name="join",
    )(place, mine, other)


def queries_own_kernel(place_ref, normed_ref, wq_ref, acc_ref):
    width = normed_ref.shape[1]
    acc_ref[...] = jnp.dot(
        normed_ref[...], wq_ref[features(place_ref, width, False), :], preferred_element_type=jnp.float32
    )


def queries_own(place, normed, wq):
    rows, width = normed.shape
    nq = wq.shape[1]
    return pl.pallas_call(
        queries_own_kernel,
        in_specs=[SCALAR, WHOLE, WHOLE],
        out_specs=WHOLE,
        out_shape=shaped((rows, nq), jnp.float32),
        compiler_params=params(12),
        cost_estimate=cost(2 * rows * width * nq, rows * nq * 4),
        name="queries_own",
    )(place, normed, wq)


def queries_kernel(
    place_ref, tokens_ref, gains_ref, inverse_ref, acc_ref, wq_ref, cos_ref, sin_ref, ready_ref, wout_hbm,
    q_ref, wsend_ref, wlater_ref, wkeep_ref, normed_ref, acc, sems,
):
    rows, width = tokens_ref.shape
    half = rows // 2
    send = pl.multiple_of((1 - place_ref[0]) * width, width)
    loads = [
        pltpu.make_async_copy(wout_hbm.at[:, pl.ds(send, width // 2)], wsend_ref, sems.at[0]),
        pltpu.make_async_copy(wout_hbm.at[:, pl.ds(send + width // 2, width // 2)], wlater_ref, sems.at[1]),
        pltpu.make_async_copy(wout_hbm.at[:, features(place_ref, width, False)], wkeep_ref, sems.at[2]),
    ]
    for load in loads:
        load.start()
    normed_ref[own_rows(place_ref, rows), :] = ready_ref[...]
    normalize(normed_ref, (1 - place_ref[0]) * half, tokens_ref, (1 - place_ref[0]) * half, half, inverse_ref, gains_ref)
    acc[...] = acc_ref[...] + jnp.dot(
        normed_ref[...], wq_ref[features(place_ref, width, True), :], preferred_element_type=jnp.float32
    )
    for h in range(q_ref.shape[1] // HEAD):
        lanes = slice(h * HEAD, (h + 1) * HEAD)
        q_ref[:, lanes] = turn(acc[:, lanes], cos_ref[...], sin_ref[...])
    for load in loads:
        load.wait()


def finish_queries(place, tokens_other, sums_other, inverse, acc, wq, tables, normed, w_out):
    rows, width = tokens_other.shape
    nq = wq.shape[1]
    depth = w_out.shape[0]
    return pl.pallas_call(
        queries_kernel,
        in_specs=[SCALAR] + [WHOLE] * 8 + [HBM],
        out_specs=[WHOLE] * 4,
        out_shape=[
            shaped((rows, nq), jnp.bfloat16),
            shaped((depth, width // 2), w_out.dtype),
            shaped((depth, width // 2), w_out.dtype),
            shaped((depth, width), w_out.dtype),
        ],
        scratch_shapes=[
            pltpu.VMEM((rows, width), jnp.bfloat16),
            pltpu.VMEM((rows, nq), jnp.float32),
            pltpu.SemaphoreType.DMA((3,)),
        ],
        compiler_params=params(16),
        cost_estimate=cost(2 * rows * width * nq, rows * width * 4),
        name="queries",
    )(place, tokens_other, sums_other, inverse, acc, wq, *tables, normed, *in_hbm(w_out))


TILE = 128


def attend_kernel(own, place_ref, q_ref, *rest):
    rows = q_ref.shape[0]
    half = rows // 2
    if own:
        blocks, (acc_out, tops_out, sums_out, keys, values, stacked, scores) = rest[:2], rest[2:]
    else:
        blocks, (acc_in, tops_in, sums_in, ctx_ref, keys, values, stacked, scores, acc, tops, sums) = rest[:-11], rest[-11:]
    heads = q_ref.shape[1] // HEAD
    tall = heads * TILE
    span = scores.shape[2]
    me = place_ref[0]
    places = [me * half, (1 - me) * half]
    if not own:
        places += [rows * (2 - me), rows * (1 + me)]
    for block, start in zip(blocks, places, strict=True):
        at = pl.ds(pl.multiple_of(start, half), block.shape[0])
        keys[at, :] = block[:, :HEAD]
        values[at, :] = block[:, HEAD:]
    behind = 0 if own else keys.shape[0]
    lane = lax.broadcasted_iota(jnp.int32, (TILE, span), 1)

    def tile(t, carry):
        first_row = t * TILE
        state = pl.ds(pl.multiple_of(t * tall, tall), tall)
        q_rows = pl.ds(pl.multiple_of(first_row, TILE), TILE)
        row = first_row + lax.broadcasted_iota(jnp.int32, (TILE, span), 0)
        begin = first_of_document(place_ref, row) + behind
        row = row + behind
        lowest = first_of_document(place_ref, first_row)
        if own:
            acc, tops, sums = acc_out.at[state, :], tops_out.at[state, :], sums_out.at[state, :]
            low = jnp.maximum(lowest, 0) // span
            high = (first_row + TILE - 1) // span + 1
            tops[...] = jnp.full((tall, LANES), -1e30, jnp.float32)
            sums[...] = jnp.zeros((tall, LANES), jnp.float32)
            acc[...] = jnp.zeros((tall, HEAD), jnp.float32)
        else:
            acc, tops, sums = rest[-3:]
            low = jnp.minimum(lowest + behind, behind) // span
            high = behind // span

        def score(i, carry):
            place = lane + i * span
            allowed = place >= begin
            if own:
                allowed = allowed & (place <= row)
            s = lax.dot_general(
                stacked[...],
                keys[pl.ds(pl.multiple_of(i * span, span), span), :],
                (((1,), (1,)), ((), ())),
                preferred_element_type=jnp.float32,
            )
            for h in range(heads):
                block = slice(h * TILE, (h + 1) * TILE)
                masked = jnp.where(allowed, s[block, :], -1e30)
                scores[i, block, :] = masked
                top = tops[block, :]
                for j in range(0, span, LANES):
                    top = jnp.maximum(top, masked[:, j : j + LANES])
                tops[block, :] = top
            return carry

        def weigh(i, carry):
            top = tops[...] * EXP2_SCALE
            total = sums[...]
            rounded = []
            for j in range(0, span, LANES):
                w = jnp.exp2(scores[i, :, j : j + LANES] * EXP2_SCALE - top)
                total = total + w
                rounded.append(w.astype(jnp.bfloat16))
            sums[...] = total
            acc[...] += jnp.dot(
                jnp.concatenate(rounded, axis=1),
                values[pl.ds(pl.multiple_of(i * span, span), span), :],
                preferred_element_type=jnp.float32,
            )
            return carry

        def finish(acc_ref, sums_ref):
            for h in range(heads):
                block = slice(h * TILE, (h + 1) * TILE)
                total = jnp.sum(sums_ref[block, :], axis=1, keepdims=True)
                ctx_ref[q_rows, h * HEAD : (h + 1) * HEAD] = (acc_ref[block, :] / total).astype(jnp.bfloat16)

        def work():
            for h in range(heads):
                stacked[h * TILE : (h + 1) * TILE, :] = q_ref[q_rows, h * HEAD : (h + 1) * HEAD]
            if not own:
                tops[...] = tops_in[state, :]
            lax.fori_loop(low, high, score, 0)
            top = jnp.max(tops[...], axis=1, keepdims=True)
            tops[...] = jnp.broadcast_to(top, (tall, LANES))
            if not own:
                rescale = jnp.exp2((tops_in[state, :] - tops[...]) * EXP2_SCALE)
                acc[...] = acc_in[state, :] * rescale
                sums[...] = sums_in[state, :] * rescale
            lax.fori_loop(low, high, weigh, 0)

        if own:
            work()
        else:

            @pl.when(low < high)
            def _():
                work()
                finish(acc, sums)

            @pl.when(low >= high)
            def _():
                finish(acc_in.at[state, :], sums_in.at[state, :])

        return carry

    lax.fori_loop(0, rows // TILE, tile, 0)


def attend(place, queries, blocks, state=None):
    rows, width = queries.shape
    own = state is None
    places = sum(block.shape[0] for block in blocks)
    span = 256 if own else 512
    heads = width // HEAD
    tall = heads * TILE
    scratch = [
        pltpu.VMEM((places, HEAD), jnp.bfloat16),
        pltpu.VMEM((places, HEAD), jnp.bfloat16),
        pltpu.VMEM((tall, HEAD), jnp.bfloat16),
        pltpu.VMEM((places // span, tall, span), jnp.float32),
    ]
    if own:
        out_shape = [shaped((heads * rows, LANES), jnp.float32)] * 3
    else:
        out_shape = shaped((rows, width), jnp.bfloat16)
        scratch += [pltpu.VMEM((tall, LANES), jnp.float32)] * 3
    return pl.pallas_call(
        functools.partial(attend_kernel, own),
        in_specs=[SCALAR] + [WHOLE] * (1 + len(blocks) + (0 if own else 3)),
        out_specs=[WHOLE] * 3 if own else WHOLE,
        scratch_shapes=scratch,
        out_shape=out_shape,
        compiler_params=params(20),
        cost_estimate=cost(4 * rows * width * places, rows * width * 8),
        name="attend_own" if own else "attend",
    )(place, queries, *blocks, *(state or ()))


def term_kernel(context_ref, w_ref, term_ref):
    step = 1024
    for c in range(w_ref.shape[1] // step):
        part = slice(c * step, (c + 1) * step)
        term_ref[:, part] = jnp.dot(context_ref[...], w_ref[:, part], preferred_element_type=jnp.float32).astype(jnp.bfloat16)


def group_term(context, w):
    rows, depth = context.shape
    width = w.shape[1]
    return pl.pallas_call(
        term_kernel,
        in_specs=[WHOLE] * 2,
        out_specs=WHOLE,
        out_shape=shaped((rows, width), jnp.bfloat16),
        compiler_params=params(16),
        cost_estimate=cost(2 * rows * depth * width, rows * width * 2),
        name="own_term",
    )(context, w)


def output_kernel(tokens_ref, term_ref, context_ref, w_ref, w_later_ref, out_ref):
    step = out_ref.shape[1]
    j = pl.program_id(0)
    here = pl.ds(pl.multiple_of(j * step, step), step)

    def work(weights_ref, first):
        part = pl.ds(pl.multiple_of((j - first) * step, step), step)
        other = jnp.dot(context_ref[...], weights_ref[:, part], preferred_element_type=jnp.float32).astype(jnp.bfloat16)
        out = tokens_ref[:, here].astype(jnp.float32) + term_ref[:, here].astype(jnp.float32) + other.astype(jnp.float32)
        out_ref[...] = out.astype(jnp.bfloat16)

    middle = w_ref.shape[1] // step
    pl.when(j < middle)(lambda: work(w_ref, 0))
    pl.when(j >= middle)(lambda: work(w_later_ref, middle))


def output(tokens, term, context, w, w_later):
    rows, width = tokens.shape
    depth = context.shape[1]
    step = 1024
    return pl.pallas_call(
        output_kernel,
        grid=(width // step,),
        in_specs=[WHOLE] * 5,
        out_specs=pl.BlockSpec((rows, step), lambda j: (0, j)),
        out_shape=shaped((rows, width), jnp.bfloat16),
        compiler_params=params(20),
        cost_estimate=cost(2 * rows * width * depth, rows * width * 4),
        name="output",
    )(tokens, term, context, w, w_later)


def swap(value):
    return lax.ppermute(value, "tp", SWAP)


def onward(value, distances):
    count, cores = lax.axis_size("dp"), len(distances)
    pairs = [
        (source * cores + core, (source + distance) * cores + core)
        for core, distance in enumerate(distances)
        for source in range(count - distance)
    ]
    return lax.ppermute(value, ("dp", "tp"), pairs)


def local(tokens, norm_gain, lengths, w_query, w_key, w_value, w_out):
    rows = tokens.shape[0]
    first_here = lax.axis_index("dp") * rows
    place = jnp.concatenate([lax.axis_index("tp")[None], first_here[None], lengths]).astype(jnp.int32)
    frequency = 500000.0 ** (-jnp.arange(HEAD // 2, dtype=jnp.float32) * 2.0 / HEAD)
    frequency = jnp.concatenate([frequency, frequency])[None, :]

    sums, tokens = squares(place, frequency, norm_gain.reshape(-1, LANES), tokens)
    sums_other = swap(sums)
    wkv, *tables = tables_and_weights(place, frequency, w_key, w_value, rows)
    tokens, sums_other, wkv = lax.optimization_barrier((tokens, sums_other, wkv))
    tokens_other = swap(tokens)
    normed, inverse, kv_partial, wq = keys_own(place, tokens, sums, sums_other, wkv, w_query)
    partial = queries_own(place, normed, wq)
    tokens_other, partial = lax.optimization_barrier((tokens_other, partial))
    kv, normed = finish_keys(place, tokens_other, sums_other, inverse, kv_partial, wkv, tables)
    assert (rows + MOST - 2) // rows == 3
    kv_other = swap(kv)
    third = onward(kv, (3, 3))
    block = onward(join(place, kv, kv_other), (1, 2))
    queries, w_send, w_later, w_mine = finish_queries(
        place, tokens_other, sums_other, inverse, partial, wq, tables, normed, w_out
    )
    w_other = swap(w_send)
    state = attend(place, queries, [kv, kv_other])
    third, block, state = lax.optimization_barrier((third, block, state))
    blocks = [third, swap(third), block, swap(block)]
    blocks, w_later = lax.optimization_barrier((blocks, w_later))
    w_other_later = swap(w_later)
    context = attend(place, queries, blocks, state)
    context_other = swap(context)
    term = group_term(context, w_mine)
    return output(tokens, term, context_other, w_other, w_other_later)


def solution(mesh):
    placed = (P(("grp", "dp"), "tp"), P("tp"), P("grp"), P(None, "tp"), P(), P(), P("tp", None))
    return jax.shard_map(
        local, mesh=mesh, in_specs=placed, out_specs=P(("grp", "dp"), "tp"), check_vma=False
    )
```

```python
import functools
import math

import jax
import jax.numpy as jnp
from jax import lax
from jax.experimental import pallas as pl
from jax.experimental.pallas import tpu as pltpu
from jax.sharding import PartitionSpec as P

HEAD = 128
MOST = 1536
LANES = 128
SWAP = [(0, 1), (1, 0)]
MIB = 1024 * 1024
EXP2_SCALE = math.log2(math.e) / HEAD**0.5

SCALAR = pl.BlockSpec(memory_space=pltpu.SMEM)
WHOLE = pl.BlockSpec(memory_space=pltpu.VMEM)
HBM = pl.BlockSpec(memory_space=pltpu.HBM)


def in_hbm(*arrays):
    return [pltpu.with_memory_space_constraint(array, pltpu.HBM) for array in arrays]


def params(mib):
    return pltpu.CompilerParams(vmem_limit_bytes=mib * MIB)


def cost(flops, moved):
    return pl.CostEstimate(flops=flops, bytes_accessed=moved, transcendentals=0)


SMALL = cost(1, 1)


def shaped(shape, dtype):
    return jax.ShapeDtypeStruct(shape, dtype)


def first_of_document(place_ref, row):
    start = -place_ref[1]
    begin = jnp.full(jnp.shape(row), start, jnp.int32)
    for d in range(2, place_ref.shape[0] - 1):
        start = start + place_ref[d]
        begin = jnp.where(row >= start, start, begin)
    return begin


ROWS = 64
WIDE = 256


def block_rows(start, r):
    return pl.ds(pl.multiple_of(start + r * ROWS, ROWS), ROWS)


def wide_slice(ref, at, j):
    wide = ref[at, j : j + WIDE].astype(jnp.float32)
    return [wide[:, i : i + LANES] for i in range(0, WIDE, LANES)]


def squares_kernel(place_ref, frequency_ref, gain_hbm, tokens_hbm, sums_ref, tokens_ref, gain_ref, sems):
    rows, width = tokens_ref.shape
    chunks = sems.shape[0] - 1
    height = rows // chunks
    loads = [
        pltpu.make_async_copy(
            tokens_hbm.at[c * height : (c + 1) * height], tokens_ref.at[c * height : (c + 1) * height], sems.at[c]
        )
        for c in range(chunks)
    ]
    loads.append(pltpu.make_async_copy(gain_hbm, gain_ref, sems.at[chunks]))
    for load in loads:
        load.start()
    for c in range(chunks):
        loads[c].wait()
        for r in range(height // ROWS):
            at = slice(c * height + r * ROWS, c * height + (r + 1) * ROWS)
            total = jnp.zeros((ROWS, LANES), jnp.float32)
            for j in range(0, width, WIDE):
                for wide in wide_slice(tokens_ref, at, j):
                    total = total + wide * wide
            sums_ref[at, :] = total
    loads[chunks].wait()
    sums_ref[rows:, :] = gain_ref[...].astype(jnp.float32)


def squares(place, frequency, gain, tokens):
    rows, width = tokens.shape
    return pl.pallas_call(
        squares_kernel,
        in_specs=[SCALAR, WHOLE, HBM, HBM],
        out_specs=[WHOLE] * 2,
        out_shape=[shaped((rows + gain.shape[0], LANES), jnp.float32), shaped(tokens.shape, tokens.dtype)],
        scratch_shapes=[pltpu.VMEM(gain.shape, gain.dtype), pltpu.SemaphoreType.DMA((8 + 1,))],
        compiler_params=params(16),
        cost_estimate=cost(rows * width * 2, rows * width * 2),
        name="squares",
    )(place, frequency, *in_hbm(gain, tokens))


def tables_kernel(place_ref, frequency_ref, wk_hbm, wv_hbm, wk_ref, wv_ref, cos_ref, sin_ref, sems):
    rows = cos_ref.shape[0]
    half = rows // 2
    loads = [
        pltpu.make_async_copy(wk_hbm, wk_ref, sems.at[0]),
        pltpu.make_async_copy(wv_hbm, wv_ref, sems.at[1]),
    ]
    for load in loads:
        load.start()
    lane = lax.broadcasted_iota(jnp.int32, (half, HEAD), 1)
    row = lax.broadcasted_iota(jnp.int32, (half, HEAD), 0) + jnp.where(lane < HEAD // 2, 0, half)
    angles = (row - first_of_document(place_ref, row)).astype(jnp.float32) * frequency_ref[...]
    for table_ref, table, sign in ((cos_ref, jnp.cos(angles), 1.0), (sin_ref, jnp.sin(angles), -1.0)):
        turned = pltpu.roll(table, HEAD // 2, 1)
        low = lane < HEAD // 2
        table_ref[:half, :] = jnp.where(low, sign * table, turned)
        table_ref[half:, :] = jnp.where(low, sign * turned, table)
    for load in loads:
        load.wait()


def tables_and_weights(place, frequency, wk, wv, rows):
    return pl.pallas_call(
        tables_kernel,
        in_specs=[SCALAR, WHOLE, HBM, HBM],
        out_specs=[WHOLE] * 4,
        out_shape=[
            shaped(wk.shape, wk.dtype),
            shaped(wv.shape, wv.dtype),
            shaped((rows, HEAD), jnp.float32),
            shaped((rows, HEAD), jnp.float32),
        ],
        scratch_shapes=[pltpu.SemaphoreType.DMA((2,))],
        compiler_params=params(16),
        cost_estimate=cost(rows * HEAD * 100, wk.size * 4),
        name="tables",
    )(place, frequency, *in_hbm(wk, wv))


def normalize(out_ref, out_start, tokens_ref, start, count, inverse_ref, gains_ref):
    rows, width = tokens_ref.shape

    def block(r, carry):
        at = block_rows(start, r)
        out_at = block_rows(out_start, r)
        inverse = inverse_ref[at, :]
        for j in range(0, width, WIDE):
            normed = []
            for i, wide in enumerate(wide_slice(tokens_ref, at, j)):
                gain_row = rows + j // LANES + i
                normed.append(wide * inverse * gains_ref[gain_row : gain_row + 1, :])
            out_ref[out_at, j : j + WIDE] = jnp.concatenate(normed, axis=1).astype(jnp.bfloat16)
        return carry

    lax.fori_loop(0, count // ROWS, block, 0)


def turn(x, cosine, sine):
    return (x * cosine + pltpu.roll(x, HEAD // 2, 1) * sine).astype(jnp.bfloat16)


def own_rows(rows):
    half = rows // 2
    return pl.ds(pl.multiple_of(lax.axis_index("tp") * half, half), half)


def features(width, other):
    me = lax.axis_index("tp")
    which = 1 - me if other else me
    return pl.ds(pl.multiple_of(which * width, width), width)


def keys_own_kernel(
    tokens_ref, mine_ref, other_ref, wk_ref, wv_ref, wq_hbm, normed_ref, inverse_ref, acc_ref, wq_ref, sem
):
    rows, width = tokens_ref.shape
    load = pltpu.make_async_copy(wq_hbm, wq_ref, sem)
    load.start()
    mean = jnp.sum(mine_ref[0:rows, :] + other_ref[0:rows, :], axis=1, keepdims=True) * (0.5 / width)
    inverse_ref[...] = jnp.broadcast_to(lax.rsqrt(mean + 1e-05), (rows, LANES))
    normalize(normed_ref, 0, tokens_ref, 0, rows, inverse_ref, mine_ref)
    acc_ref[...] = jnp.dot(
        normed_ref[own_rows(rows), :],
        both_weights(wk_ref, wv_ref, features(width, False)),
        preferred_element_type=jnp.float32,
    )
    load.wait()


def keys_own(tokens, sums, sums_other, wk, wv, wq):
    rows, width = tokens.shape
    return pl.pallas_call(
        keys_own_kernel,
        in_specs=[WHOLE] * 5 + [HBM],
        out_specs=[WHOLE] * 4,
        out_shape=[
            shaped(tokens.shape, jnp.bfloat16),
            shaped((rows, LANES), jnp.float32),
            shaped((rows // 2, 2 * HEAD), jnp.float32),
            shaped(wq.shape, wq.dtype),
        ],
        scratch_shapes=[pltpu.SemaphoreType.DMA],
        compiler_params=params(16),
        cost_estimate=cost(2 * rows * width * HEAD, wq.size * 2),
        name="keys_own",
    )(tokens, sums, sums_other, wk, wv, *in_hbm(wq))


def both_weights(wk_ref, wv_ref, depth):
    return jnp.concatenate([wk_ref[depth, :], wv_ref[depth, :]], axis=1)


def keys_kernel(tokens_ref, gains_ref, inverse_ref, acc_ref, wk_ref, wv_ref, cos_ref, sin_ref, kv_ref, normed_ref):
    rows, width = tokens_ref.shape
    half = rows // 2
    here = own_rows(rows)
    normalize(normed_ref, 0, tokens_ref, lax.axis_index("tp") * half, half, inverse_ref, gains_ref)
    total = acc_ref[...] + jnp.dot(
        normed_ref[...], both_weights(wk_ref, wv_ref, features(width, True)), preferred_element_type=jnp.float32
    )
    kv_ref[:, :HEAD] = turn(total[:, :HEAD], cos_ref[here, :], sin_ref[here, :])
    kv_ref[:, HEAD:] = total[:, HEAD:].astype(jnp.bfloat16)


def finish_keys(tokens_other, sums_other, inverse, acc, wk, wv, tables):
    rows, width = tokens_other.shape
    return pl.pallas_call(
        keys_kernel,
        in_specs=[WHOLE] * 8,
        out_specs=[WHOLE] * 2,
        out_shape=[shaped(acc.shape, jnp.bfloat16), shaped((rows // 2, width), jnp.bfloat16)],
        compiler_params=params(16),
        cost_estimate=cost(2 * rows * width * HEAD, rows * width),
        name="keys",
    )(tokens_other, sums_other, inverse, acc, wk, wv, *tables)


def join_kernel(mine_ref, other_ref, out_ref):
    half = mine_ref.shape[0]
    me = lax.axis_index("tp")
    for block, which in ((mine_ref, me), (other_ref, 1 - me)):
        out_ref[pl.ds(pl.multiple_of(which * half, half), half), :] = block[...]


def join(mine, other):
    half, width = mine.shape
    return pl.pallas_call(
        join_kernel,
        in_specs=[WHOLE] * 2,
        out_specs=WHOLE,
        out_shape=shaped((2 * half, width), mine.dtype),
        compiler_params=params(8),
        cost_estimate=SMALL,
        name="join",
    )(mine, other)


def queries_own_kernel(normed_ref, wq_ref, acc_ref):
    width = normed_ref.shape[1]
    acc_ref[...] = jnp.dot(
        normed_ref[...], wq_ref[features(width, False), :], preferred_element_type=jnp.float32
    )


def queries_own(normed, wq):
    rows, width = normed.shape
    nq = wq.shape[1]
    return pl.pallas_call(
        queries_own_kernel,
        in_specs=[WHOLE, WHOLE],
        out_specs=WHOLE,
        out_shape=shaped((rows, nq), jnp.float32),
        compiler_params=params(12),
        cost_estimate=cost(2 * rows * width * nq, rows * nq * 4),
        name="queries_own",
    )(normed, wq)


def queries_kernel(
    tokens_ref, gains_ref, inverse_ref, acc_ref, wq_ref, cos_ref, sin_ref, ready_ref, wout_hbm,
    q_ref, wsend_ref, wlater_ref, wkeep_ref, normed_ref, acc, sems,
):
    rows, width = tokens_ref.shape
    half = rows // 2
    send = pl.multiple_of((1 - lax.axis_index("tp")) * width, width)
    loads = [
        pltpu.make_async_copy(wout_hbm.at[:, pl.ds(send, width // 2)], wsend_ref, sems.at[0]),
        pltpu.make_async_copy(wout_hbm.at[:, pl.ds(send + width // 2, width // 2)], wlater_ref, sems.at[1]),
        pltpu.make_async_copy(wout_hbm.at[:, features(width, False)], wkeep_ref, sems.at[2]),
    ]
    for load in loads:
        load.start()
    normed_ref[own_rows(rows), :] = ready_ref[...]
    there = (1 - lax.axis_index("tp")) * half
    normalize(normed_ref, there, tokens_ref, there, half, inverse_ref, gains_ref)
    acc[...] = acc_ref[...] + jnp.dot(
        normed_ref[...], wq_ref[features(width, True), :], preferred_element_type=jnp.float32
    )
    for h in range(q_ref.shape[1] // HEAD):
        lanes = slice(h * HEAD, (h + 1) * HEAD)
        q_ref[:, lanes] = turn(acc[:, lanes], cos_ref[...], sin_ref[...])
    for load in loads:
        load.wait()


def finish_queries(tokens_other, sums_other, inverse, acc, wq, tables, normed, w_out):
    rows, width = tokens_other.shape
    nq = wq.shape[1]
    depth = w_out.shape[0]
    return pl.pallas_call(
        queries_kernel,
        in_specs=[WHOLE] * 8 + [HBM],
        out_specs=[WHOLE] * 4,
        out_shape=[
            shaped((rows, nq), jnp.bfloat16),
            shaped((depth, width // 2), w_out.dtype),
            shaped((depth, width // 2), w_out.dtype),
            shaped((depth, width), w_out.dtype),
        ],
        scratch_shapes=[
            pltpu.VMEM((rows, width), jnp.bfloat16),
            pltpu.VMEM((rows, nq), jnp.float32),
            pltpu.SemaphoreType.DMA((3,)),
        ],
        compiler_params=params(16),
        cost_estimate=cost(2 * rows * width * nq, rows * width * 4),
        name="queries",
    )(tokens_other, sums_other, inverse, acc, wq, *tables, normed, *in_hbm(w_out))


TILE = 128
SPAN = 512


def place_blocks(blocks, starts, keys, values):
    for block, start in zip(blocks, starts, strict=True):
        at = pl.ds(pl.multiple_of(start, block.shape[0]), block.shape[0])
        keys[at, :] = block[:, :HEAD]
        values[at, :] = block[:, HEAD:]


def lanes_max(x):
    return jnp.broadcast_to(jnp.max(x, axis=1, keepdims=True), x.shape)


def weigh(scores, probs, at, first, count, top):
    scaled = top * EXP2_SCALE
    total = jnp.zeros((ROWS, LANES), jnp.float32)
    for j in range(0, count, WIDE):
        weights = []
        for i in range(j, j + WIDE, LANES):
            w = jnp.exp2(scores[at, first + i : first + i + LANES] * EXP2_SCALE - scaled)
            total = total + w
            weights.append(w)
        probs[at, first + j : first + j + WIDE] = jnp.concatenate(weights, axis=1).astype(jnp.bfloat16)
    return total


def attend_own_kernel(place_ref, q_ref, mine_ref, other_ref, acc_ref, tops_ref, sums_ref, keys, values, bias, scores, probs):
    rows = q_ref.shape[0]
    half = rows // 2
    me = lax.axis_index("tp")
    place_blocks([mine_ref, other_ref], [me * half, (1 - me) * half], keys, values)
    row = lax.broadcasted_iota(jnp.int32, (rows, LANES), 0)
    lane = lax.broadcasted_iota(jnp.int32, (rows, LANES), 1)
    begin = first_of_document(place_ref, row)
    for j in range(0, rows, LANES):
        allowed = (lane + j >= begin) & (lane + j <= row)
        bias[:, j : j + LANES] = jnp.where(allowed, 0.0, -1e30)
    for h in range(q_ref.shape[1] // HEAD):
        for first, count in ((0, half), (half, rows)):
            scores[:, :count] = lax.dot_general(
                q_ref[first : first + half, h * HEAD : (h + 1) * HEAD],
                keys[:count, :],
                (((1,), (1,)), ((), ())),
                preferred_element_type=jnp.float32,
            )
            out = h * rows + first

            def block(r, carry):
                at = block_rows(0, r)
                out_at = block_rows(out, r)
                top = jnp.full((ROWS, LANES), -1e30, jnp.float32)
                for j in range(0, count, LANES):
                    s = scores[at, j : j + LANES] + bias[block_rows(first, r), j : j + LANES]
                    scores[at, j : j + LANES] = s
                    top = jnp.maximum(top, s)
                top = lanes_max(top)
                tops_ref[out_at, :] = top
                sums_ref[out_at, :] = weigh(scores, probs, at, 0, count, top)
                return carry

            lax.fori_loop(0, half // ROWS, block, 0, unroll=True)
            acc_ref[out : out + half, :] = jnp.dot(
                probs[:, :count], values[:count, :], preferred_element_type=jnp.float32
            )


def attend_kernel(
    place_ref, q_ref, third_ref, third_other_ref, block_ref, block_other_ref, acc_in, tops_in, sums_in,
    ctx_ref, keys, values, stacked, scores, probs, acc, sums,
):
    rows = q_ref.shape[0]
    half = rows // 2
    heads = q_ref.shape[1] // HEAD
    tall = heads * TILE
    behind = keys.shape[0]
    me = lax.axis_index("tp")
    place_blocks(
        [third_ref, third_other_ref, block_ref, block_other_ref],
        [me * half, (1 - me) * half, rows * (2 - me), rows * (1 + me)],
        keys,
        values,
    )
    start = -place_ref[1]
    begin, end = start, jnp.int32(rows)
    for d in range(2, place_ref.shape[0] - 1):
        start = start + place_ref[d]
        begin = jnp.where(start <= 0, start, begin)
        end = jnp.where(start > 0, jnp.minimum(end, start), end)
    low = begin + behind
    lane = lax.broadcasted_iota(jnp.int32, (ROWS, LANES), 1)
    line = lax.broadcasted_iota(jnp.int32, (ROWS, LANES), 0)

    def alone(at, q_at, h):
        total = jnp.sum(sums_in[at, :], axis=1, keepdims=True)
        ctx_ref[q_at, h * HEAD : (h + 1) * HEAD] = (acc_in[at, :] / total).astype(jnp.bfloat16)

    def tile(t, carry):
        reached = (t * TILE < end) & (low < behind)

        @pl.when(jnp.logical_not(reached))
        def _():
            for h in range(heads):
                for r in range(TILE // ROWS):
                    alone(block_rows(h * rows + t * TILE, r), block_rows(t * TILE, r), h)

        def merge(first):
            for h in range(heads):
                stacked[h * TILE : (h + 1) * TILE, :] = q_ref[
                    pl.ds(pl.multiple_of(t * TILE, TILE), TILE), h * HEAD : (h + 1) * HEAD
                ]
            scores[:, first:] = lax.dot_general(
                stacked[...], keys[first:, :], (((1,), (1,)), ((), ())), preferred_element_type=jnp.float32
            )
            for h in range(heads):
                for r in range(TILE // ROWS):
                    at = slice(h * TILE + r * ROWS, h * TILE + (r + 1) * ROWS)
                    state = block_rows(h * rows + t * TILE, r)
                    own_top = tops_in[state, :]
                    top = own_top
                    for j in range(first, behind, LANES):
                        s = scores[at, j : j + LANES]
                        if j < first + SPAN:
                            s = jnp.where(lane + j >= low, s, -1e30)
                            scores[at, j : j + LANES] = s
                        top = jnp.maximum(top, s)
                    top = lanes_max(top)
                    rescale = jnp.exp2((own_top - top) * EXP2_SCALE)
                    acc[at, :] = acc_in[state, :] * rescale
                    sums[at, :] = sums_in[state, :] * rescale + weigh(scores, probs, at, first, behind - first, top)
            acc[...] += jnp.dot(probs[:, first:], values[first:, :], preferred_element_type=jnp.float32)
            for h in range(heads):
                for r in range(TILE // ROWS):
                    at = slice(h * TILE + r * ROWS, h * TILE + (r + 1) * ROWS)
                    state = block_rows(h * rows + t * TILE, r)
                    merged = line + (t * TILE + r * ROWS) < end
                    total = jnp.sum(jnp.where(merged, sums[at, :], sums_in[state, :]), axis=1, keepdims=True)
                    context = jnp.where(merged, acc[at, :], acc_in[state, :]) / total
                    ctx_ref[block_rows(t * TILE, r), h * HEAD : (h + 1) * HEAD] = context.astype(jnp.bfloat16)

        for first in range(0, behind, SPAN):
            inside = (low >= first) & (low < first + SPAN)
            pl.when(reached & inside)(functools.partial(merge, first))
        return carry

    lax.fori_loop(0, rows // TILE, tile, 0)


def attend_own(place, queries, blocks):
    rows, width = queries.shape
    half = rows // 2
    heads = width // HEAD
    return pl.pallas_call(
        attend_own_kernel,
        in_specs=[SCALAR] + [WHOLE] * 3,
        out_specs=[WHOLE] * 3,
        scratch_shapes=[
            pltpu.VMEM((rows, HEAD), jnp.bfloat16),
            pltpu.VMEM((rows, HEAD), jnp.bfloat16),
            pltpu.VMEM((rows, rows), jnp.float32),
            pltpu.VMEM((half, rows), jnp.float32),
            pltpu.VMEM((half, rows), jnp.bfloat16),
        ],
        out_shape=[shaped((heads * rows, LANES), jnp.float32)] * 3,
        compiler_params=params(16),
        cost_estimate=cost(4 * rows * width * rows, rows * width * 8),
        name="attend_own",
    )(place, queries, *blocks)


def attend(place, queries, blocks, state):
    rows, width = queries.shape
    heads = width // HEAD
    tall = heads * TILE
    places = sum(block.shape[0] for block in blocks)
    return pl.pallas_call(
        attend_kernel,
        in_specs=[SCALAR] + [WHOLE] * (1 + len(blocks) + len(state)),
        out_specs=WHOLE,
        scratch_shapes=[
            pltpu.VMEM((places, HEAD), jnp.bfloat16),
            pltpu.VMEM((places, HEAD), jnp.bfloat16),
            pltpu.VMEM((tall, HEAD), jnp.bfloat16),
            pltpu.VMEM((tall, places), jnp.float32),
            pltpu.VMEM((tall, places), jnp.bfloat16),
            pltpu.VMEM((tall, HEAD), jnp.float32),
            pltpu.VMEM((tall, LANES), jnp.float32),
        ],
        out_shape=shaped((rows, width), jnp.bfloat16),
        compiler_params=params(20),
        cost_estimate=cost(4 * rows * width * places, rows * width * 8),
        name="attend",
    )(place, queries, *blocks, *state)


def term_kernel(context_ref, w_ref, term_ref):
    step = 1024
    for c in range(w_ref.shape[1] // step):
        part = slice(c * step, (c + 1) * step)
        term_ref[:, part] = jnp.dot(context_ref[...], w_ref[:, part], preferred_element_type=jnp.float32).astype(jnp.bfloat16)


def group_term(context, w):
    rows, depth = context.shape
    width = w.shape[1]
    return pl.pallas_call(
        term_kernel,
        in_specs=[WHOLE] * 2,
        out_specs=WHOLE,
        out_shape=shaped((rows, width), jnp.bfloat16),
        compiler_params=params(16),
        cost_estimate=cost(2 * rows * depth * width, rows * width * 2),
        name="own_term",
    )(context, w)


def output_kernel(tokens_ref, term_ref, context_ref, w_ref, w_later_ref, out_ref):
    step = out_ref.shape[1]
    j = pl.program_id(0)
    here = pl.ds(pl.multiple_of(j * step, step), step)

    def work(weights_ref, first):
        part = pl.ds(pl.multiple_of((j - first) * step, step), step)
        other = jnp.dot(context_ref[...], weights_ref[:, part], preferred_element_type=jnp.float32).astype(jnp.bfloat16)
        out = tokens_ref[:, here].astype(jnp.float32) + term_ref[:, here].astype(jnp.float32) + other.astype(jnp.float32)
        out_ref[...] = out.astype(jnp.bfloat16)

    middle = w_ref.shape[1] // step
    pl.when(j < middle)(lambda: work(w_ref, 0))
    pl.when(j >= middle)(lambda: work(w_later_ref, middle))


def output(tokens, term, context, w, w_later):
    rows, width = tokens.shape
    depth = context.shape[1]
    step = 1024
    return pl.pallas_call(
        output_kernel,
        grid=(width // step,),
        in_specs=[WHOLE] * 5,
        out_specs=pl.BlockSpec((rows, step), lambda j: (0, j)),
        out_shape=shaped((rows, width), jnp.bfloat16),
        compiler_params=params(20),
        cost_estimate=cost(2 * rows * width * depth, rows * width * 4),
        name="output",
    )(tokens, term, context, w, w_later)


def swap(value):
    return lax.ppermute(value, "tp", SWAP)


def onward(value, distances):
    count, cores = lax.axis_size("dp"), len(distances)
    pairs = [
        (source * cores + core, (source + distance) * cores + core)
        for core, distance in enumerate(distances)
        for source in range(count - distance)
    ]
    return lax.ppermute(value, ("dp", "tp"), pairs)


def local(tokens, norm_gain, lengths, w_query, w_key, w_value, w_out):
    rows = tokens.shape[0]
    first_here = lax.axis_index("dp") * rows
    place = jnp.concatenate([lax.axis_index("tp")[None], first_here[None], lengths]).astype(jnp.int32)
    frequency = 500000.0 ** (-jnp.arange(HEAD // 2, dtype=jnp.float32) * 2.0 / HEAD)
    frequency = jnp.concatenate([frequency, frequency])[None, :]

    sums, tokens = squares(place, frequency, norm_gain.reshape(-1, LANES), tokens)
    sums_other = swap(sums)
    wk, wv, *tables = tables_and_weights(place, frequency, w_key, w_value, rows)
    tokens, sums_other, wk = lax.optimization_barrier((tokens, sums_other, wk))
    tokens_other = swap(tokens)
    normed, inverse, kv_partial, wq = keys_own(tokens, sums, sums_other, wk, wv, w_query)
    partial = queries_own(normed, wq)
    tokens_other, partial = lax.optimization_barrier((tokens_other, partial))
    kv, normed = finish_keys(tokens_other, sums_other, inverse, kv_partial, wk, wv, tables)
    assert (rows + MOST - 2) // rows == 3
    kv_other = swap(kv)
    third = onward(kv, (3, 3))
    block = onward(join(kv, kv_other), (1, 2))
    queries, w_send, w_later, w_mine = finish_queries(
        tokens_other, sums_other, inverse, partial, wq, tables, normed, w_out
    )
    w_other = swap(w_send)
    state = attend_own(place, queries, [kv, kv_other])
    third, block, state = lax.optimization_barrier((third, block, state))
    blocks = [third, swap(third), block, swap(block)]
    blocks, w_later = lax.optimization_barrier((blocks, w_later))
    w_other_later = swap(w_later)
    context = attend(place, queries, blocks, state)
    context_other = swap(context)
    term = group_term(context, w_mine)
    return output(tokens, term, context_other, w_other, w_other_later)


def solution(mesh):
    placed = (P(("grp", "dp"), "tp"), P("tp"), P("grp"), P(None, "tp"), P(), P(), P("tp", None))
    return jax.shard_map(
        local, mesh=mesh, in_specs=placed, out_specs=P(("grp", "dp"), "tp"), check_vma=False
    )
```

```python
import functools
import math

import jax
import jax.numpy as jnp
from jax import lax
from jax.experimental import pallas as pl
from jax.experimental.pallas import tpu as pltpu
from jax.sharding import PartitionSpec as P

HEAD = 128
MOST = 1536
LANES = 128
SWAP = [(0, 1), (1, 0)]
MIB = 1024 * 1024
EXP2_SCALE = math.log2(math.e) / HEAD**0.5

WHOLE = pl.BlockSpec(memory_space=pltpu.VMEM)
HBM = pl.BlockSpec(memory_space=pltpu.HBM)


def in_hbm(*arrays):
    return [pltpu.with_memory_space_constraint(array, pltpu.HBM) for array in arrays]


def params(mib):
    return pltpu.CompilerParams(vmem_limit_bytes=mib * MIB)


def cost(flops, moved):
    return pl.CostEstimate(flops=flops, bytes_accessed=moved, transcendentals=0)


SMALL = cost(1, 1)


def shaped(shape, dtype):
    return jax.ShapeDtypeStruct(shape, dtype)


def first_of_document(lengths_ref, first_here, row):
    start = -first_here
    begin = jnp.full(jnp.shape(row), start, jnp.int32)
    for d in range(lengths_ref.shape[0] - 1):
        start = start + lengths_ref[d]
        begin = jnp.where(row >= start, start, begin)
    return begin


ROWS = 64
WIDE = 256


def block_rows(start, r):
    return pl.ds(pl.multiple_of(start + r * ROWS, ROWS), ROWS)


def wide_slice(ref, at, j):
    wide = ref[at, j : j + WIDE].astype(jnp.float32)
    return [wide[:, i : i + LANES] for i in range(0, WIDE, LANES)]


def squares_kernel(frequency_ref, gain_hbm, tokens_hbm, sums_ref, gain_ref, tokens_ref, narrow, sems):
    rows, width = tokens_ref.shape
    chunks = sems.shape[0] - 1
    height = rows // chunks
    loads = [
        pltpu.make_async_copy(
            tokens_hbm.at[c * height : (c + 1) * height], tokens_ref.at[c * height : (c + 1) * height], sems.at[c]
        )
        for c in range(chunks)
    ]
    loads.append(pltpu.make_async_copy(gain_hbm, narrow, sems.at[chunks]))
    for load in loads:
        load.start()
    for c in range(chunks):
        loads[c].wait()
        for r in range(height // ROWS):
            at = slice(c * height + r * ROWS, c * height + (r + 1) * ROWS)
            total = jnp.zeros((ROWS, LANES), jnp.float32)
            for j in range(0, width, WIDE):
                for wide in wide_slice(tokens_ref, at, j):
                    total = total + wide * wide
            sums_ref[at, :] = total
    loads[chunks].wait()
    gain_ref[...] = narrow[...].astype(jnp.float32)


def squares(frequency, gain, tokens):
    rows, width = tokens.shape
    return pl.pallas_call(
        squares_kernel,
        in_specs=[WHOLE, HBM, HBM],
        out_specs=[WHOLE] * 3,
        out_shape=[
            shaped((rows, LANES), jnp.float32),
            shaped(gain.shape, jnp.float32),
            shaped(tokens.shape, tokens.dtype),
        ],
        scratch_shapes=[pltpu.VMEM(gain.shape, gain.dtype), pltpu.SemaphoreType.DMA((8 + 1,))],
        compiler_params=params(16),
        cost_estimate=cost(rows * width * 2, rows * width * 2),
        name="squares",
    )(frequency, *in_hbm(gain, tokens))


def sine_and_cosine(x):
    turns = jnp.floor(x * (2.0 / math.pi) + 0.5)
    r = ((x - turns * 1.5703125) - turns * 4.837512969970703125e-4) - turns * 7.54978995489188e-8
    z = r * r
    s = ((-1.9515295891e-4 * z + 8.3321608736e-3) * z - 1.6666654611e-1) * z * r + r
    c = ((2.443315711809948e-5 * z - 1.388731625493765e-3) * z + 4.166664568298827e-2) * z * z - 0.5 * z + 1.0
    quadrant = turns.astype(jnp.int32)
    odd = (quadrant & 1) == 1
    sine = jnp.where(odd, c, s)
    cosine = jnp.where(odd, s, c)
    sine = jnp.where((quadrant & 2) == 2, -sine, sine)
    cosine = jnp.where(((quadrant + 1) & 2) == 2, -cosine, cosine)
    return sine, cosine


def tables_kernel(frequency_ref, lengths_hbm, cos_ref, sin_ref, lengths_ref, sem):
    rows = cos_ref.shape[0]
    half = rows // 2
    load = pltpu.make_async_copy(lengths_hbm, lengths_ref, sem)
    load.start()
    lane = lax.broadcasted_iota(jnp.int32, (half, HEAD), 1)
    row = lax.broadcasted_iota(jnp.int32, (half, HEAD), 0) + jnp.where(lane < HEAD // 2, 0, half)
    low = lane < HEAD // 2
    load.wait()
    begin = first_of_document(lengths_ref, lax.axis_index("dp") * rows, row)
    sine, cosine = sine_and_cosine((row - begin).astype(jnp.float32) * frequency_ref[...])
    for table_ref, table, sign in ((cos_ref, cosine, 1.0), (sin_ref, sine, -1.0)):
        turned = pltpu.roll(table, HEAD // 2, 1)
        table_ref[:half, :] = jnp.where(low, sign * table, turned)
        table_ref[half:, :] = jnp.where(low, sign * turned, table)


def rotary_tables(frequency, lengths, rows):
    return pl.pallas_call(
        tables_kernel,
        in_specs=[WHOLE, HBM],
        out_specs=[WHOLE] * 2,
        out_shape=[shaped((rows, HEAD), jnp.float32)] * 2,
        scratch_shapes=[pltpu.SMEM(lengths.shape, lengths.dtype), pltpu.SemaphoreType.DMA],
        compiler_params=params(16),
        cost_estimate=cost(rows * HEAD * 100, rows * HEAD * 8),
        name="tables",
    )(frequency, *in_hbm(lengths))


def normalize(out_ref, tokens_ref, start, inverse_ref, gains_ref):
    count, width = out_ref.shape

    def block(r, carry):
        at = block_rows(start, r)
        inverse = inverse_ref[at, :]
        for j in range(0, width, WIDE):
            normed = []
            for i, wide in enumerate(wide_slice(tokens_ref, at, j)):
                gain_row = j // LANES + i
                normed.append(wide * inverse * gains_ref[gain_row : gain_row + 1, :])
            out_ref[block_rows(0, r), j : j + WIDE] = jnp.concatenate(normed, axis=1).astype(jnp.bfloat16)
        return carry

    lax.fori_loop(0, count // ROWS, block, 0)


def turn(x, cosine, sine):
    return (x * cosine + pltpu.roll(x, HEAD // 2, 1) * sine).astype(jnp.bfloat16)


def half_rows(rows, other):
    me = lax.axis_index("tp")
    half = rows // 2
    return pl.ds(pl.multiple_of((1 - me if other else me) * half, half), half)


def features(width, other):
    me = lax.axis_index("tp")
    return pl.ds(pl.multiple_of((1 - me if other else me) * width, width), width)


def both_weights(wk_ref, wv_ref, depth):
    return jnp.concatenate([wk_ref[depth, :], wv_ref[depth, :]], axis=1)


def normalize_other_kernel(
    tokens_ref, mine_ref, other_ref, gain_ref, wk_hbm, wv_hbm, normed_ref, inverse_ref, wk_ref, wv_ref, sems
):
    rows, width = tokens_ref.shape
    loads = [
        pltpu.make_async_copy(wk_hbm, wk_ref, sems.at[0]),
        pltpu.make_async_copy(wv_hbm, wv_ref, sems.at[1]),
    ]
    for load in loads:
        load.start()
    mean = jnp.sum(mine_ref[...] + other_ref[...], axis=1, keepdims=True) * (0.5 / width)
    inverse_ref[...] = jnp.broadcast_to(lax.rsqrt(mean + 1e-05), (rows, LANES))
    normalize(normed_ref, tokens_ref, half_rows(rows, True).start, inverse_ref, gain_ref)
    for load in loads:
        load.wait()


def normalize_other(tokens, sums, sums_other, gain, wk, wv):
    rows, width = tokens.shape
    return pl.pallas_call(
        normalize_other_kernel,
        in_specs=[WHOLE] * 4 + [HBM] * 2,
        out_specs=[WHOLE] * 4,
        out_shape=[
            shaped((rows // 2, width), jnp.bfloat16),
            shaped((rows, LANES), jnp.float32),
            shaped(wk.shape, wk.dtype),
            shaped(wv.shape, wv.dtype),
        ],
        scratch_shapes=[pltpu.SemaphoreType.DMA((2,))],
        compiler_params=params(12),
        cost_estimate=cost(rows * width * 2, wk.size * 4),
        name="normalize_other",
    )(tokens, sums, sums_other, gain, *in_hbm(wk, wv))


def normalize_own_kernel(tokens_ref, gain_ref, inverse_ref, wk_ref, wv_ref, wq_hbm, normed_ref, acc_ref, wq_ref, sem):
    rows, width = tokens_ref.shape
    load = pltpu.make_async_copy(wq_hbm, wq_ref, sem)
    load.start()
    normalize(normed_ref, tokens_ref, half_rows(rows, False).start, inverse_ref, gain_ref)
    acc_ref[...] = jnp.dot(
        normed_ref[...], both_weights(wk_ref, wv_ref, features(width, False)), preferred_element_type=jnp.float32
    )
    load.wait()


def normalize_own(tokens, gain, inverse, wk, wv, wq):
    rows, width = tokens.shape
    return pl.pallas_call(
        normalize_own_kernel,
        in_specs=[WHOLE] * 5 + [HBM],
        out_specs=[WHOLE] * 3,
        out_shape=[
            shaped((rows // 2, width), jnp.bfloat16),
            shaped((rows // 2, 2 * HEAD), jnp.float32),
            shaped(wq.shape, wq.dtype),
        ],
        scratch_shapes=[pltpu.SemaphoreType.DMA],
        compiler_params=params(12),
        cost_estimate=cost(2 * rows * width * HEAD, wq.size * 2),
        name="normalize_own",
    )(tokens, gain, inverse, wk, wv, *in_hbm(wq))


def keys_kernel(normed_ref, acc_ref, wk_ref, wv_ref, cos_ref, sin_ref, kv_ref):
    half, width = normed_ref.shape
    here = half_rows(2 * half, False)
    total = acc_ref[...] + jnp.dot(
        normed_ref[...], both_weights(wk_ref, wv_ref, features(width, True)), preferred_element_type=jnp.float32
    )
    kv_ref[:, :HEAD] = turn(total[:, :HEAD], cos_ref[here, :], sin_ref[here, :])
    kv_ref[:, HEAD:] = total[:, HEAD:].astype(jnp.bfloat16)


def finish_keys(normed_come, acc, wk, wv, tables):
    return pl.pallas_call(
        keys_kernel,
        in_specs=[WHOLE] * 6,
        out_specs=WHOLE,
        out_shape=shaped(acc.shape, jnp.bfloat16),
        compiler_params=params(12),
        cost_estimate=cost(normed_come.size * 4 * HEAD, acc.size * 4),
        name="keys",
    )(normed_come, acc, wk, wv, *tables)


def join_kernel(mine_ref, other_ref, out_ref):
    rows = out_ref.shape[0]
    out_ref[half_rows(rows, False), :] = mine_ref[...]
    out_ref[half_rows(rows, True), :] = other_ref[...]


def join(mine, other):
    half, width = mine.shape
    return pl.pallas_call(
        join_kernel,
        in_specs=[WHOLE] * 2,
        out_specs=WHOLE,
        out_shape=shaped((2 * half, width), mine.dtype),
        compiler_params=params(8),
        cost_estimate=SMALL,
        name="join",
    )(mine, other)


def queries_own_kernel(mine_ref, other_ref, wq_ref, acc_ref):
    half, width = mine_ref.shape
    weights = wq_ref[features(width, False), :]
    acc_ref[:half, :] = jnp.dot(mine_ref[...], weights, preferred_element_type=jnp.float32)
    acc_ref[half:, :] = jnp.dot(other_ref[...], weights, preferred_element_type=jnp.float32)


def queries_own(mine, other, wq):
    half, width = mine.shape
    nq = wq.shape[1]
    return pl.pallas_call(
        queries_own_kernel,
        in_specs=[WHOLE] * 3,
        out_specs=WHOLE,
        out_shape=shaped((2 * half, nq), jnp.float32),
        compiler_params=params(12),
        cost_estimate=cost(4 * half * width * nq, half * nq * 8),
        name="queries_own",
    )(mine, other, wq)


def queries_kernel(
    mine_ref, other_ref, acc_ref, wq_ref, cos_ref, sin_ref, wout_hbm, q_ref, wsend_ref, wlater_ref, wkeep_ref, acc, sems
):
    half, width = mine_ref.shape
    send = features(width, True).start
    loads = [
        pltpu.make_async_copy(wout_hbm.at[:, pl.ds(send, width // 2)], wsend_ref, sems.at[0]),
        pltpu.make_async_copy(wout_hbm.at[:, pl.ds(send + width // 2, width // 2)], wlater_ref, sems.at[1]),
        pltpu.make_async_copy(wout_hbm.at[:, features(width, False)], wkeep_ref, sems.at[2]),
    ]
    for load in loads:
        load.start()
    weights = wq_ref[features(width, True), :]
    for part, normed_ref, other in ((slice(0, half), mine_ref, False), (slice(half, 2 * half), other_ref, True)):
        acc[part, :] = acc_ref[part, :] + jnp.dot(normed_ref[...], weights, preferred_element_type=jnp.float32)
        at = half_rows(2 * half, other)
        for h in range(q_ref.shape[1] // HEAD):
            lanes = slice(h * HEAD, (h + 1) * HEAD)
            q_ref[at, lanes] = turn(acc[part, lanes], cos_ref[at, :], sin_ref[at, :])
    for load in loads:
        load.wait()


def finish_queries(mine, other, acc, wq, tables, w_out):
    half, width = mine.shape
    nq = wq.shape[1]
    depth = w_out.shape[0]
    return pl.pallas_call(
        queries_kernel,
        in_specs=[WHOLE] * 6 + [HBM],
        out_specs=[WHOLE] * 4,
        out_shape=[
            shaped((2 * half, nq), jnp.bfloat16),
            shaped((depth, width // 2), w_out.dtype),
            shaped((depth, width // 2), w_out.dtype),
            shaped((depth, width), w_out.dtype),
        ],
        scratch_shapes=[pltpu.VMEM((2 * half, nq), jnp.float32), pltpu.SemaphoreType.DMA((3,))],
        compiler_params=params(12),
        cost_estimate=cost(4 * half * width * nq, w_out.size * 2),
        name="queries",
    )(mine, other, acc, wq, *tables, *in_hbm(w_out))


TILE = 128
SPAN = 512


def place_blocks(blocks, starts, keys, values):
    for block, start in zip(blocks, starts, strict=True):
        at = pl.ds(pl.multiple_of(start, block.shape[0]), block.shape[0])
        keys[at, :] = block[:, :HEAD]
        values[at, :] = block[:, HEAD:]


def lanes_max(x):
    return jnp.broadcast_to(jnp.max(x, axis=1, keepdims=True), x.shape)


def weigh(scores, probs, at, first, count, top):
    scaled = top * EXP2_SCALE
    total = jnp.zeros((ROWS, LANES), jnp.float32)
    for j in range(0, count, WIDE):
        weights = []
        for i in range(j, j + WIDE, LANES):
            w = jnp.exp2(scores[at, first + i : first + i + LANES] * EXP2_SCALE - scaled)
            total = total + w
            weights.append(w)
        probs[at, first + j : first + j + WIDE] = jnp.concatenate(weights, axis=1).astype(jnp.bfloat16)
    return total


def attend_own_kernel(
    lengths_hbm, q_ref, mine_ref, other_ref, acc_ref, tops_ref, sums_ref, keys, values, bias, scores, probs, lengths_ref, sem
):
    load = pltpu.make_async_copy(lengths_hbm, lengths_ref, sem)
    load.start()
    rows = q_ref.shape[0]
    half = rows // 2
    me = lax.axis_index("tp")
    place_blocks([mine_ref, other_ref], [me * half, (1 - me) * half], keys, values)
    load.wait()
    row = lax.broadcasted_iota(jnp.int32, (rows, LANES), 0)
    lane = lax.broadcasted_iota(jnp.int32, (rows, LANES), 1)
    begin = first_of_document(lengths_ref, lax.axis_index("dp") * rows, row)
    for j in range(0, rows, LANES):
        allowed = (lane + j >= begin) & (lane + j <= row)
        bias[:, j : j + LANES] = jnp.where(allowed, 0.0, -1e30)
    for h in range(q_ref.shape[1] // HEAD):
        for first, count in ((0, half), (half, rows)):
            scores[:, :count] = lax.dot_general(
                q_ref[first : first + half, h * HEAD : (h + 1) * HEAD],
                keys[:count, :],
                (((1,), (1,)), ((), ())),
                preferred_element_type=jnp.float32,
            )
            out = h * rows + first

            def block(r, carry):
                at = block_rows(0, r)
                out_at = block_rows(out, r)
                top = jnp.full((ROWS, LANES), -1e30, jnp.float32)
                for j in range(0, count, LANES):
                    s = scores[at, j : j + LANES] + bias[block_rows(first, r), j : j + LANES]
                    scores[at, j : j + LANES] = s
                    top = jnp.maximum(top, s)
                top = lanes_max(top)
                tops_ref[out_at, :] = top
                sums_ref[out_at, :] = weigh(scores, probs, at, 0, count, top)
                return carry

            lax.fori_loop(0, half // ROWS, block, 0, unroll=True)
            acc_ref[out : out + half, :] = jnp.dot(
                probs[:, :count], values[:count, :], preferred_element_type=jnp.float32
            )


def attend_kernel(
    lengths_hbm, q_ref, third_ref, third_other_ref, block_ref, block_other_ref, acc_in, tops_in, sums_in,
    ctx_ref, keys, values, stacked, scores, probs, acc, sums, lengths_ref, sem,
):
    load = pltpu.make_async_copy(lengths_hbm, lengths_ref, sem)
    load.start()
    rows = q_ref.shape[0]
    half = rows // 2
    heads = q_ref.shape[1] // HEAD
    behind = keys.shape[0]
    me = lax.axis_index("tp")
    place_blocks(
        [third_ref, third_other_ref, block_ref, block_other_ref],
        [me * half, (1 - me) * half, rows * (2 - me), rows * (1 + me)],
        keys,
        values,
    )
    load.wait()
    start = -lax.axis_index("dp") * rows
    begin, end = start, jnp.int32(rows)
    for d in range(lengths_ref.shape[0] - 1):
        start = start + lengths_ref[d]
        begin = jnp.where(start <= 0, start, begin)
        end = jnp.where(start > 0, jnp.minimum(end, start), end)
    low = begin + behind
    lane = lax.broadcasted_iota(jnp.int32, (ROWS, LANES), 1)
    line = lax.broadcasted_iota(jnp.int32, (ROWS, LANES), 0)

    def alone(at, q_at, h):
        total = jnp.sum(sums_in[at, :], axis=1, keepdims=True)
        ctx_ref[q_at, h * HEAD : (h + 1) * HEAD] = (acc_in[at, :] / total).astype(jnp.bfloat16)

    def tile(t, carry):
        reached = (t * TILE < end) & (low < behind)

        @pl.when(jnp.logical_not(reached))
        def _():
            for h in range(heads):
                for r in range(TILE // ROWS):
                    alone(block_rows(h * rows + t * TILE, r), block_rows(t * TILE, r), h)

        def merge(first):
            for h in range(heads):
                stacked[h * TILE : (h + 1) * TILE, :] = q_ref[
                    pl.ds(pl.multiple_of(t * TILE, TILE), TILE), h * HEAD : (h + 1) * HEAD
                ]
            scores[:, first:] = lax.dot_general(
                stacked[...], keys[first:, :], (((1,), (1,)), ((), ())), preferred_element_type=jnp.float32
            )
            for h in range(heads):
                for r in range(TILE // ROWS):
                    at = slice(h * TILE + r * ROWS, h * TILE + (r + 1) * ROWS)
                    state = block_rows(h * rows + t * TILE, r)
                    own_top = tops_in[state, :]
                    top = own_top
                    for j in range(first, behind, LANES):
                        s = scores[at, j : j + LANES]
                        if j < first + SPAN:
                            s = jnp.where(lane + j >= low, s, -1e30)
                            scores[at, j : j + LANES] = s
                        top = jnp.maximum(top, s)
                    top = lanes_max(top)
                    rescale = jnp.exp2((own_top - top) * EXP2_SCALE)
                    acc[at, :] = acc_in[state, :] * rescale
                    sums[at, :] = sums_in[state, :] * rescale + weigh(scores, probs, at, first, behind - first, top)
            acc[...] += jnp.dot(probs[:, first:], values[first:, :], preferred_element_type=jnp.float32)
            for h in range(heads):
                for r in range(TILE // ROWS):
                    at = slice(h * TILE + r * ROWS, h * TILE + (r + 1) * ROWS)
                    state = block_rows(h * rows + t * TILE, r)
                    merged = line + (t * TILE + r * ROWS) < end
                    total = jnp.sum(jnp.where(merged, sums[at, :], sums_in[state, :]), axis=1, keepdims=True)
                    context = jnp.where(merged, acc[at, :], acc_in[state, :]) / total
                    ctx_ref[block_rows(t * TILE, r), h * HEAD : (h + 1) * HEAD] = context.astype(jnp.bfloat16)

        for first in range(0, behind, SPAN):
            inside = (low >= first) & (low < first + SPAN)
            pl.when(reached & inside)(functools.partial(merge, first))
        return carry

    lax.fori_loop(0, rows // TILE, tile, 0)


def attend_own(lengths, queries, blocks):
    rows, width = queries.shape
    half = rows // 2
    heads = width // HEAD
    return pl.pallas_call(
        attend_own_kernel,
        in_specs=[HBM] + [WHOLE] * 3,
        out_specs=[WHOLE] * 3,
        scratch_shapes=[
            pltpu.VMEM((rows, HEAD), jnp.bfloat16),
            pltpu.VMEM((rows, HEAD), jnp.bfloat16),
            pltpu.VMEM((rows, rows), jnp.float32),
            pltpu.VMEM((half, rows), jnp.float32),
            pltpu.VMEM((half, rows), jnp.bfloat16),
            pltpu.SMEM(lengths.shape, lengths.dtype),
            pltpu.SemaphoreType.DMA,
        ],
        out_shape=[shaped((heads * rows, LANES), jnp.float32)] * 3,
        compiler_params=params(16),
        cost_estimate=cost(4 * rows * width * rows, rows * width * 8),
        name="attend_own",
    )(*in_hbm(lengths), queries, *blocks)


def attend(lengths, queries, blocks, state):
    rows, width = queries.shape
    heads = width // HEAD
    tall = heads * TILE
    places = sum(block.shape[0] for block in blocks)
    return pl.pallas_call(
        attend_kernel,
        in_specs=[HBM] + [WHOLE] * (1 + len(blocks) + len(state)),
        out_specs=WHOLE,
        scratch_shapes=[
            pltpu.VMEM((places, HEAD), jnp.bfloat16),
            pltpu.VMEM((places, HEAD), jnp.bfloat16),
            pltpu.VMEM((tall, HEAD), jnp.bfloat16),
            pltpu.VMEM((tall, places), jnp.float32),
            pltpu.VMEM((tall, places), jnp.bfloat16),
            pltpu.VMEM((tall, HEAD), jnp.float32),
            pltpu.VMEM((tall, LANES), jnp.float32),
            pltpu.SMEM(lengths.shape, lengths.dtype),
            pltpu.SemaphoreType.DMA,
        ],
        out_shape=shaped((rows, width), jnp.bfloat16),
        compiler_params=params(20),
        cost_estimate=cost(4 * rows * width * places, rows * width * 8),
        name="attend",
    )(*in_hbm(lengths), queries, *blocks, *state)


def term_kernel(context_ref, w_ref, term_ref):
    step = 1024
    for c in range(w_ref.shape[1] // step):
        part = slice(c * step, (c + 1) * step)
        term_ref[:, part] = jnp.dot(context_ref[...], w_ref[:, part], preferred_element_type=jnp.float32).astype(jnp.bfloat16)


def group_term(context, w):
    rows, depth = context.shape
    width = w.shape[1]
    return pl.pallas_call(
        term_kernel,
        in_specs=[WHOLE] * 2,
        out_specs=WHOLE,
        out_shape=shaped((rows, width), jnp.bfloat16),
        compiler_params=params(16),
        cost_estimate=cost(2 * rows * depth * width, rows * width * 2),
        name="own_term",
    )(context, w)


def output_kernel(tokens_ref, term_ref, context_ref, w_ref, w_later_ref, out_ref):
    step = out_ref.shape[1]
    j = pl.program_id(0)
    here = pl.ds(pl.multiple_of(j * step, step), step)

    def work(weights_ref, first):
        part = pl.ds(pl.multiple_of((j - first) * step, step), step)
        other = jnp.dot(context_ref[...], weights_ref[:, part], preferred_element_type=jnp.float32).astype(jnp.bfloat16)
        out = tokens_ref[:, here].astype(jnp.float32) + term_ref[:, here].astype(jnp.float32) + other.astype(jnp.float32)
        out_ref[...] = out.astype(jnp.bfloat16)

    middle = w_ref.shape[1] // step
    pl.when(j < middle)(lambda: work(w_ref, 0))
    pl.when(j >= middle)(lambda: work(w_later_ref, middle))


def output(tokens, term, context, w, w_later):
    rows, width = tokens.shape
    depth = context.shape[1]
    step = 1024
    return pl.pallas_call(
        output_kernel,
        grid=(width // step,),
        in_specs=[WHOLE] * 5,
        out_specs=pl.BlockSpec((rows, step), lambda j: (0, j)),
        out_shape=shaped((rows, width), jnp.bfloat16),
        compiler_params=params(20),
        cost_estimate=cost(2 * rows * width * depth, rows * width * 4),
        name="output",
    )(tokens, term, context, w, w_later)


def swap(value):
    return lax.ppermute(value, "tp", SWAP)


def onward(value, distances):
    count, cores = lax.axis_size("dp"), len(distances)
    pairs = [
        (source * cores + core, (source + distance) * cores + core)
        for core, distance in enumerate(distances)
        for source in range(count - distance)
    ]
    return lax.ppermute(value, ("dp", "tp"), pairs)


def local(tokens, norm_gain, lengths, w_query, w_key, w_value, w_out):
    rows = tokens.shape[0]
    frequency = 500000.0 ** (-jnp.arange(HEAD // 2, dtype=jnp.float32) * 2.0 / HEAD)
    frequency = jnp.concatenate([frequency, frequency])[None, :]

    sums, gain, tokens = squares(frequency, norm_gain.reshape(-1, LANES), tokens)
    sums_other = swap(sums)
    tables = rotary_tables(frequency, lengths, rows)
    sums_other, tables = lax.optimization_barrier((sums_other, tables))
    normed_other, inverse, wk, wv = normalize_other(tokens, sums, sums_other, gain, w_key, w_value)
    come_mine = swap(normed_other)
    normed_mine, kv_partial, wq = normalize_own(tokens, gain, inverse, wk, wv, w_query)
    come_other = swap(normed_mine)
    come_mine, kv_partial = lax.optimization_barrier((come_mine, kv_partial))
    kv = finish_keys(come_mine, kv_partial, wk, wv, tables)
    assert (rows + MOST - 2) // rows == 3
    kv, normed_mine = lax.optimization_barrier((kv, normed_mine))
    third = onward(kv, (3, 3))
    kv_other = swap(kv)
    block = onward(join(kv, kv_other), (1, 2))
    partial = queries_own(normed_mine, normed_other, wq)
    queries, w_send, w_later, w_mine = finish_queries(come_mine, come_other, partial, wq, tables, w_out)
    w_other = swap(w_send)
    state = attend_own(lengths, queries, [kv, kv_other])
    third, block, state = lax.optimization_barrier((third, block, state))
    blocks = [third, swap(third), block, swap(block)]
    blocks, w_later = lax.optimization_barrier((blocks, w_later))
    w_other_later = swap(w_later)
    context = attend(lengths, queries, blocks, state)
    context_other = swap(context)
    term = group_term(context, w_mine)
    return output(tokens, term, context_other, w_other, w_other_later)


def solution(mesh):
    placed = (P(("grp", "dp"), "tp"), P("tp"), P("grp"), P(None, "tp"), P(), P(), P("tp", None))
    return jax.shard_map(
        local, mesh=mesh, in_specs=placed, out_specs=P(("grp", "dp"), "tp"), check_vma=False
    )
```

```python
import functools
import math

import jax
import jax.numpy as jnp
from jax import lax
from jax.experimental import pallas as pl
from jax.experimental.pallas import tpu as pltpu
from jax.sharding import PartitionSpec as P

HEAD = 128
MOST = 1536
LANES = 128
SWAP = [(0, 1), (1, 0)]
MIB = 1024 * 1024
EXP2_SCALE = math.log2(math.e) / HEAD**0.5

WHOLE = pl.BlockSpec(memory_space=pltpu.VMEM)
HBM = pl.BlockSpec(memory_space=pltpu.HBM)


def in_hbm(*arrays):
    return [pltpu.with_memory_space_constraint(array, pltpu.HBM) for array in arrays]


def params(mib):
    return pltpu.CompilerParams(vmem_limit_bytes=mib * MIB)


def cost(flops, moved):
    return pl.CostEstimate(flops=flops, bytes_accessed=moved, transcendentals=0)


SMALL = cost(1, 1)


def shaped(shape, dtype):
    return jax.ShapeDtypeStruct(shape, dtype)


def first_of_document(lengths_ref, first_here, row):
    start = -first_here
    begin = jnp.full(jnp.shape(row), start, jnp.int32)
    for d in range(lengths_ref.shape[0] - 1):
        start = start + lengths_ref[d]
        begin = jnp.where(row >= start, start, begin)
    return begin


ROWS = 64
WIDE = 256


def block_rows(start, r):
    return pl.ds(pl.multiple_of(start + r * ROWS, ROWS), ROWS)


def wide_slice(ref, at, j):
    wide = ref[at, j : j + WIDE].astype(jnp.float32)
    return [wide[:, i : i + LANES] for i in range(0, WIDE, LANES)]


def squares_kernel(frequency_ref, gain_hbm, tokens_hbm, sums_ref, gain_ref, tokens_ref, narrow, sems):
    rows, width = tokens_ref.shape
    chunks = sems.shape[0] - 1
    height = rows // chunks
    loads = [
        pltpu.make_async_copy(
            tokens_hbm.at[c * height : (c + 1) * height], tokens_ref.at[c * height : (c + 1) * height], sems.at[c]
        )
        for c in range(chunks)
    ]
    loads.append(pltpu.make_async_copy(gain_hbm, narrow, sems.at[chunks]))
    for load in loads:
        load.start()
    for c in range(chunks):
        loads[c].wait()
        for r in range(height // ROWS):
            at = slice(c * height + r * ROWS, c * height + (r + 1) * ROWS)
            total = jnp.zeros((ROWS, LANES), jnp.float32)
            for j in range(0, width, WIDE):
                for wide in wide_slice(tokens_ref, at, j):
                    total = total + wide * wide
            sums_ref[at, :] = total
    loads[chunks].wait()
    gain_ref[...] = narrow[...].astype(jnp.float32)


def squares(frequency, gain, tokens):
    rows, width = tokens.shape
    return pl.pallas_call(
        squares_kernel,
        in_specs=[WHOLE, HBM, HBM],
        out_specs=[WHOLE] * 3,
        out_shape=[
            shaped((rows, LANES), jnp.float32),
            shaped(gain.shape, jnp.float32),
            shaped(tokens.shape, tokens.dtype),
        ],
        scratch_shapes=[pltpu.VMEM(gain.shape, gain.dtype), pltpu.SemaphoreType.DMA((8 + 1,))],
        compiler_params=params(16),
        cost_estimate=cost(rows * width * 2, rows * width * 2),
        name="squares",
    )(frequency, *in_hbm(gain, tokens))


def sine_and_cosine(x):
    turns = jnp.floor(x * (2.0 / math.pi) + 0.5)
    r = ((x - turns * 1.5703125) - turns * 4.837512969970703125e-4) - turns * 7.54978995489188e-8
    z = r * r
    s = ((-1.9515295891e-4 * z + 8.3321608736e-3) * z - 1.6666654611e-1) * z * r + r
    c = ((2.443315711809948e-5 * z - 1.388731625493765e-3) * z + 4.166664568298827e-2) * z * z - 0.5 * z + 1.0
    quadrant = turns.astype(jnp.int32)
    odd = (quadrant & 1) == 1
    sine = jnp.where(odd, c, s)
    cosine = jnp.where(odd, s, c)
    sine = jnp.where((quadrant & 2) == 2, -sine, sine)
    cosine = jnp.where(((quadrant + 1) & 2) == 2, -cosine, cosine)
    return sine, cosine


def tables_kernel(frequency_ref, lengths_hbm, cos_ref, sin_ref, lengths_ref, sem):
    rows = cos_ref.shape[0]
    half = rows // 2
    load = pltpu.make_async_copy(lengths_hbm, lengths_ref, sem)
    load.start()
    lane = lax.broadcasted_iota(jnp.int32, (half, HEAD), 1)
    row = lax.broadcasted_iota(jnp.int32, (half, HEAD), 0) + jnp.where(lane < HEAD // 2, 0, half)
    low = lane < HEAD // 2
    load.wait()
    begin = first_of_document(lengths_ref, lax.axis_index("dp") * rows, row)
    sine, cosine = sine_and_cosine((row - begin).astype(jnp.float32) * frequency_ref[...])
    for table_ref, table, sign in ((cos_ref, cosine, 1.0), (sin_ref, sine, -1.0)):
        turned = pltpu.roll(table, HEAD // 2, 1)
        table_ref[:half, :] = jnp.where(low, sign * table, turned)
        table_ref[half:, :] = jnp.where(low, sign * turned, table)


def rotary_tables(frequency, lengths, rows):
    return pl.pallas_call(
        tables_kernel,
        in_specs=[WHOLE, HBM],
        out_specs=[WHOLE] * 2,
        out_shape=[shaped((rows, HEAD), jnp.float32)] * 2,
        scratch_shapes=[pltpu.SMEM(lengths.shape, lengths.dtype), pltpu.SemaphoreType.DMA],
        compiler_params=params(16),
        cost_estimate=cost(rows * HEAD * 100, rows * HEAD * 8),
        name="tables",
    )(frequency, *in_hbm(lengths))


def normalize(out_ref, tokens_ref, start, inverse_ref, gains_ref):
    count, width = out_ref.shape

    def block(r, carry):
        at = block_rows(start, r)
        inverse = inverse_ref[at, :]
        for j in range(0, width, WIDE):
            normed = []
            for i, wide in enumerate(wide_slice(tokens_ref, at, j)):
                gain_row = j // LANES + i
                normed.append(wide * inverse * gains_ref[gain_row : gain_row + 1, :])
            out_ref[block_rows(0, r), j : j + WIDE] = jnp.concatenate(normed, axis=1).astype(jnp.bfloat16)
        return carry

    lax.fori_loop(0, count // ROWS, block, 0)


def turn(x, cosine, sine):
    return (x * cosine + pltpu.roll(x, HEAD // 2, 1) * sine).astype(jnp.bfloat16)


def half_rows(rows, other):
    me = lax.axis_index("tp")
    half = rows // 2
    return pl.ds(pl.multiple_of((1 - me if other else me) * half, half), half)


def features(width, other):
    me = lax.axis_index("tp")
    return pl.ds(pl.multiple_of((1 - me if other else me) * width, width), width)


def both_weights(wk_ref, wv_ref, depth):
    return jnp.concatenate([wk_ref[depth, :], wv_ref[depth, :]], axis=1)


def normalize_other_kernel(tokens_ref, mine_ref, other_ref, gain_ref, normed_ref, inverse_ref):
    rows, width = tokens_ref.shape
    mean = jnp.sum(mine_ref[...] + other_ref[...], axis=1, keepdims=True) * (0.5 / width)
    inverse_ref[...] = jnp.broadcast_to(lax.rsqrt(mean + 1e-05), (rows, LANES))
    normalize(normed_ref, tokens_ref, half_rows(rows, True).start, inverse_ref, gain_ref)


def normalize_other(tokens, sums, sums_other, gain):
    rows, width = tokens.shape
    return pl.pallas_call(
        normalize_other_kernel,
        in_specs=[WHOLE] * 4,
        out_specs=[WHOLE] * 2,
        out_shape=[shaped((rows // 2, width), jnp.bfloat16), shaped((rows, LANES), jnp.float32)],
        compiler_params=params(12),
        cost_estimate=cost(rows * width * 2, rows * width * 2),
        name="normalize_other",
    )(tokens, sums, sums_other, gain)


def normalize_own_kernel(tokens_ref, gain_ref, inverse_ref, wk_hbm, wv_hbm, normed_ref, acc_ref, wk_ref, wv_ref, sems):
    rows, width = tokens_ref.shape
    loads = [
        pltpu.make_async_copy(wk_hbm, wk_ref, sems.at[0]),
        pltpu.make_async_copy(wv_hbm, wv_ref, sems.at[1]),
    ]
    for load in loads:
        load.start()
    normalize(normed_ref, tokens_ref, half_rows(rows, False).start, inverse_ref, gain_ref)
    for load in loads:
        load.wait()
    acc_ref[...] = jnp.dot(
        normed_ref[...], both_weights(wk_ref, wv_ref, features(width, False)), preferred_element_type=jnp.float32
    )


def normalize_own(tokens, gain, inverse, wk, wv):
    rows, width = tokens.shape
    return pl.pallas_call(
        normalize_own_kernel,
        in_specs=[WHOLE] * 3 + [HBM] * 2,
        out_specs=[WHOLE] * 4,
        out_shape=[
            shaped((rows // 2, width), jnp.bfloat16),
            shaped((rows // 2, 2 * HEAD), jnp.float32),
            shaped(wk.shape, wk.dtype),
            shaped(wv.shape, wv.dtype),
        ],
        scratch_shapes=[pltpu.SemaphoreType.DMA((2,))],
        compiler_params=params(12),
        cost_estimate=cost(2 * rows * width * HEAD, wk.size * 4),
        name="normalize_own",
    )(tokens, gain, inverse, *in_hbm(wk, wv))


def keys_kernel(normed_ref, acc_ref, wk_ref, wv_ref, cos_ref, sin_ref, kv_ref):
    half, width = normed_ref.shape
    here = half_rows(2 * half, False)
    total = acc_ref[...] + jnp.dot(
        normed_ref[...], both_weights(wk_ref, wv_ref, features(width, True)), preferred_element_type=jnp.float32
    )
    kv_ref[:, :HEAD] = turn(total[:, :HEAD], cos_ref[here, :], sin_ref[here, :])
    kv_ref[:, HEAD:] = total[:, HEAD:].astype(jnp.bfloat16)


def finish_keys(normed_come, acc, wk, wv, tables):
    return pl.pallas_call(
        keys_kernel,
        in_specs=[WHOLE] * 6,
        out_specs=WHOLE,
        out_shape=shaped(acc.shape, jnp.bfloat16),
        compiler_params=params(12),
        cost_estimate=cost(normed_come.size * 4 * HEAD, acc.size * 4),
        name="keys",
    )(normed_come, acc, wk, wv, *tables)


def join_kernel(mine_ref, other_ref, out_ref):
    rows = out_ref.shape[0]
    out_ref[half_rows(rows, False), :] = mine_ref[...]
    out_ref[half_rows(rows, True), :] = other_ref[...]


def join(mine, other):
    half, width = mine.shape
    return pl.pallas_call(
        join_kernel,
        in_specs=[WHOLE] * 2,
        out_specs=WHOLE,
        out_shape=shaped((2 * half, width), mine.dtype),
        compiler_params=params(8),
        cost_estimate=SMALL,
        name="join",
    )(mine, other)


def queries_own_kernel(mine_ref, other_ref, wq_ref, acc_ref):
    half, width = mine_ref.shape
    weights = wq_ref[features(width, False), :]
    acc_ref[:half, :] = jnp.dot(mine_ref[...], weights, preferred_element_type=jnp.float32)
    acc_ref[half:, :] = jnp.dot(other_ref[...], weights, preferred_element_type=jnp.float32)


def queries_own(mine, other, wq):
    half, width = mine.shape
    nq = wq.shape[1]
    return pl.pallas_call(
        queries_own_kernel,
        in_specs=[WHOLE] * 3,
        out_specs=WHOLE,
        out_shape=shaped((2 * half, nq), jnp.float32),
        compiler_params=params(12),
        cost_estimate=cost(4 * half * width * nq, half * nq * 8),
        name="queries_own",
    )(mine, other, wq)


def queries_kernel(mine_ref, other_ref, acc_ref, wq_ref, cos_ref, sin_ref, wout_hbm, q_ref, wsend_ref, wlater_ref, acc, sems):
    half, width = mine_ref.shape
    send = features(width, True).start
    loads = [
        pltpu.make_async_copy(wout_hbm.at[:, pl.ds(send, width // 2)], wsend_ref, sems.at[0]),
        pltpu.make_async_copy(wout_hbm.at[:, pl.ds(send + width // 2, width // 2)], wlater_ref, sems.at[1]),
    ]
    for load in loads:
        load.start()
    weights = wq_ref[features(width, True), :]
    acc[:half, :] = jnp.dot(mine_ref[...], weights, preferred_element_type=jnp.float32)
    acc[half:, :] = jnp.dot(other_ref[...], weights, preferred_element_type=jnp.float32)
    for part, other in ((slice(0, half), False), (slice(half, 2 * half), True)):
        at = half_rows(2 * half, other)
        for h in range(q_ref.shape[1] // HEAD):
            lanes = slice(h * HEAD, (h + 1) * HEAD)
            q_ref[at, lanes] = turn(acc_ref[part, lanes] + acc[part, lanes], cos_ref[at, :], sin_ref[at, :])
    for load in loads:
        load.wait()


def finish_queries(mine, other, acc, wq, tables, w_out):
    half, width = mine.shape
    nq = wq.shape[1]
    depth = w_out.shape[0]
    return pl.pallas_call(
        queries_kernel,
        in_specs=[WHOLE] * 6 + [HBM],
        out_specs=[WHOLE] * 3,
        out_shape=[
            shaped((2 * half, nq), jnp.bfloat16),
            shaped((depth, width // 2), w_out.dtype),
            shaped((depth, width // 2), w_out.dtype),
        ],
        scratch_shapes=[pltpu.VMEM((2 * half, nq), jnp.float32), pltpu.SemaphoreType.DMA((2,))],
        compiler_params=params(12),
        cost_estimate=cost(4 * half * width * nq, w_out.size),
        name="queries",
    )(mine, other, acc, wq, *tables, *in_hbm(w_out))


TILE = 128
SPAN = 512


def place_blocks(blocks, starts, keys, values):
    for block, start in zip(blocks, starts, strict=True):
        at = pl.ds(pl.multiple_of(start, block.shape[0]), block.shape[0])
        keys[at, :] = block[:, :HEAD]
        values[at, :] = block[:, HEAD:]


def lanes_max(x):
    return jnp.broadcast_to(jnp.max(x, axis=1, keepdims=True), x.shape)


def weigh(scores, probs, at, first, count, top):
    scaled = top * EXP2_SCALE
    total = jnp.zeros((ROWS, LANES), jnp.float32)
    for j in range(0, count, WIDE):
        weights = []
        for i in range(j, j + WIDE, LANES):
            w = jnp.exp2(scores[at, first + i : first + i + LANES] * EXP2_SCALE - scaled)
            total = total + w
            weights.append(w)
        probs[at, first + j : first + j + WIDE] = jnp.concatenate(weights, axis=1).astype(jnp.bfloat16)
    return total


def attend_own_kernel(
    lengths_hbm, q_ref, mine_ref, other_ref, wout_hbm, acc_ref, tops_ref, sums_ref, wkeep_ref,
    keys, values, bias, scores, probs, lengths_ref, sems,
):
    load = pltpu.make_async_copy(lengths_hbm, lengths_ref, sems.at[0])
    load.start()
    keep = pltpu.make_async_copy(wout_hbm.at[:, features(wkeep_ref.shape[1], False)], wkeep_ref, sems.at[1])
    keep.start()
    rows = q_ref.shape[0]
    half = rows // 2
    me = lax.axis_index("tp")
    place_blocks([mine_ref, other_ref], [me * half, (1 - me) * half], keys, values)
    load.wait()
    row = lax.broadcasted_iota(jnp.int32, (rows, LANES), 0)
    lane = lax.broadcasted_iota(jnp.int32, (rows, LANES), 1)
    begin = first_of_document(lengths_ref, lax.axis_index("dp") * rows, row)
    for j in range(0, rows, LANES):
        allowed = (lane + j >= begin) & (lane + j <= row)
        bias[:, j : j + LANES] = jnp.where(allowed, 0.0, -1e30)
    for h in range(q_ref.shape[1] // HEAD):
        for first, count in ((0, half), (half, rows)):
            scores[:, :count] = lax.dot_general(
                q_ref[first : first + half, h * HEAD : (h + 1) * HEAD],
                keys[:count, :],
                (((1,), (1,)), ((), ())),
                preferred_element_type=jnp.float32,
            )
            out = h * rows + first

            def block(r, carry):
                at = block_rows(0, r)
                out_at = block_rows(out, r)
                top = jnp.full((ROWS, LANES), -1e30, jnp.float32)
                for j in range(0, count, LANES):
                    s = scores[at, j : j + LANES] + bias[block_rows(first, r), j : j + LANES]
                    scores[at, j : j + LANES] = s
                    top = jnp.maximum(top, s)
                top = lanes_max(top)
                tops_ref[out_at, :] = top
                sums_ref[out_at, :] = weigh(scores, probs, at, 0, count, top)
                return carry

            lax.fori_loop(0, half // ROWS, block, 0, unroll=True)
            acc_ref[out : out + half, :] = jnp.dot(
                probs[:, :count], values[:count, :], preferred_element_type=jnp.float32
            )
    keep.wait()


def attend_kernel(
    lengths_hbm, q_ref, third_ref, third_other_ref, block_ref, block_other_ref, acc_in, tops_in, sums_in,
    ctx_ref, keys, values, stacked, scores, probs, acc, sums, lengths_ref, sem,
):
    load = pltpu.make_async_copy(lengths_hbm, lengths_ref, sem)
    load.start()
    rows = q_ref.shape[0]
    half = rows // 2
    heads = q_ref.shape[1] // HEAD
    behind = keys.shape[0]
    me = lax.axis_index("tp")
    place_blocks(
        [third_ref, third_other_ref, block_ref, block_other_ref],
        [me * half, (1 - me) * half, rows * (2 - me), rows * (1 + me)],
        keys,
        values,
    )
    load.wait()
    start = -lax.axis_index("dp") * rows
    begin, end = start, jnp.int32(rows)
    for d in range(lengths_ref.shape[0] - 1):
        start = start + lengths_ref[d]
        begin = jnp.where(start <= 0, start, begin)
        end = jnp.where(start > 0, jnp.minimum(end, start), end)
    low = begin + behind
    lane = lax.broadcasted_iota(jnp.int32, (ROWS, LANES), 1)
    line = lax.broadcasted_iota(jnp.int32, (ROWS, LANES), 0)

    def alone(at, q_at, h):
        total = jnp.sum(sums_in[at, :], axis=1, keepdims=True)
        ctx_ref[q_at, h * HEAD : (h + 1) * HEAD] = (acc_in[at, :] / total).astype(jnp.bfloat16)

    def tile(t, carry):
        reached = (t * TILE < end) & (low < behind)

        @pl.when(jnp.logical_not(reached))
        def _():
            for h in range(heads):
                for r in range(TILE // ROWS):
                    alone(block_rows(h * rows + t * TILE, r), block_rows(t * TILE, r), h)

        def merge(first):
            for h in range(heads):
                stacked[h * TILE : (h + 1) * TILE, :] = q_ref[
                    pl.ds(pl.multiple_of(t * TILE, TILE), TILE), h * HEAD : (h + 1) * HEAD
                ]
            scores[:, first:] = lax.dot_general(
                stacked[...], keys[first:, :], (((1,), (1,)), ((), ())), preferred_element_type=jnp.float32
            )
            for h in range(heads):
                for r in range(TILE // ROWS):
                    at = slice(h * TILE + r * ROWS, h * TILE + (r + 1) * ROWS)
                    state = block_rows(h * rows + t * TILE, r)
                    own_top = tops_in[state, :]
                    top = own_top
                    for j in range(first, behind, LANES):
                        s = scores[at, j : j + LANES]
                        if j < first + SPAN:
                            s = jnp.where(lane + j >= low, s, -1e30)
                            scores[at, j : j + LANES] = s
                        top = jnp.maximum(top, s)
                    top = lanes_max(top)
                    rescale = jnp.exp2((own_top - top) * EXP2_SCALE)
                    acc[at, :] = acc_in[state, :] * rescale
                    sums[at, :] = sums_in[state, :] * rescale + weigh(scores, probs, at, first, behind - first, top)
            acc[...] += jnp.dot(probs[:, first:], values[first:, :], preferred_element_type=jnp.float32)
            for h in range(heads):
                for r in range(TILE // ROWS):
                    at = slice(h * TILE + r * ROWS, h * TILE + (r + 1) * ROWS)
                    state = block_rows(h * rows + t * TILE, r)
                    merged = line + (t * TILE + r * ROWS) < end
                    total = jnp.sum(jnp.where(merged, sums[at, :], sums_in[state, :]), axis=1, keepdims=True)
                    context = jnp.where(merged, acc[at, :], acc_in[state, :]) / total
                    ctx_ref[block_rows(t * TILE, r), h * HEAD : (h + 1) * HEAD] = context.astype(jnp.bfloat16)

        for first in range(0, behind, SPAN):
            inside = (low >= first) & (low < first + SPAN)
            pl.when(reached & inside)(functools.partial(merge, first))
        return carry

    lax.fori_loop(0, rows // TILE, tile, 0)


def attend_own(lengths, queries, blocks, w_out):
    rows, width = queries.shape
    half = rows // 2
    heads = width // HEAD
    return pl.pallas_call(
        attend_own_kernel,
        in_specs=[HBM] + [WHOLE] * 3 + [HBM],
        out_specs=[WHOLE] * 4,
        scratch_shapes=[
            pltpu.VMEM((rows, HEAD), jnp.bfloat16),
            pltpu.VMEM((rows, HEAD), jnp.bfloat16),
            pltpu.VMEM((rows, rows), jnp.float32),
            pltpu.VMEM((half, rows), jnp.float32),
            pltpu.VMEM((half, rows), jnp.bfloat16),
            pltpu.SMEM(lengths.shape, lengths.dtype),
            pltpu.SemaphoreType.DMA((2,)),
        ],
        out_shape=[shaped((heads * rows, LANES), jnp.float32)] * 3
        + [shaped((w_out.shape[0], w_out.shape[1] // 2), w_out.dtype)],
        compiler_params=params(16),
        cost_estimate=cost(4 * rows * width * rows, rows * width * 8),
        name="attend_own",
    )(*in_hbm(lengths), queries, *blocks, *in_hbm(w_out))


def attend(lengths, queries, blocks, state):
    rows, width = queries.shape
    heads = width // HEAD
    tall = heads * TILE
    places = sum(block.shape[0] for block in blocks)
    return pl.pallas_call(
        attend_kernel,
        in_specs=[HBM] + [WHOLE] * (1 + len(blocks) + len(state)),
        out_specs=WHOLE,
        scratch_shapes=[
            pltpu.VMEM((places, HEAD), jnp.bfloat16),
            pltpu.VMEM((places, HEAD), jnp.bfloat16),
            pltpu.VMEM((tall, HEAD), jnp.bfloat16),
            pltpu.VMEM((tall, places), jnp.float32),
            pltpu.VMEM((tall, places), jnp.bfloat16),
            pltpu.VMEM((tall, HEAD), jnp.float32),
            pltpu.VMEM((tall, LANES), jnp.float32),
            pltpu.SMEM(lengths.shape, lengths.dtype),
            pltpu.SemaphoreType.DMA,
        ],
        out_shape=shaped((rows, width), jnp.bfloat16),
        compiler_params=params(20),
        cost_estimate=cost(4 * rows * width * places, rows * width * 8),
        name="attend",
    )(*in_hbm(lengths), queries, *blocks, *state)


def term_kernel(context_ref, w_ref, term_ref):
    step = 1024
    for c in range(w_ref.shape[1] // step):
        part = slice(c * step, (c + 1) * step)
        term_ref[:, part] = jnp.dot(context_ref[...], w_ref[:, part], preferred_element_type=jnp.float32).astype(jnp.bfloat16)


def group_term(context, w):
    rows, depth = context.shape
    width = w.shape[1]
    return pl.pallas_call(
        term_kernel,
        in_specs=[WHOLE] * 2,
        out_specs=WHOLE,
        out_shape=shaped((rows, width), jnp.bfloat16),
        compiler_params=params(16),
        cost_estimate=cost(2 * rows * depth * width, rows * width * 2),
        name="own_term",
    )(context, w)


def output_kernel(tokens_ref, term_ref, context_ref, w_ref, w_later_ref, out_hbm, out, sems):
    width = out.shape[1]
    half = width // 2
    chunks = sems.shape[0]
    step = width // chunks
    stores = []
    for c in range(chunks):
        here = slice(c * step, (c + 1) * step)
        weights = w_ref[:, here] if c < chunks // 2 else w_later_ref[:, c * step - half : (c + 1) * step - half]
        other = jnp.dot(context_ref[...], weights, preferred_element_type=jnp.float32).astype(jnp.bfloat16)
        total = tokens_ref[:, here].astype(jnp.float32) + term_ref[:, here].astype(jnp.float32) + other.astype(jnp.float32)
        out[:, here] = total.astype(jnp.bfloat16)
        stores.append(pltpu.make_async_copy(out.at[:, here], out_hbm.at[:, here], sems.at[c]))
        stores[c].start()
    for store in stores:
        store.wait()


def output(tokens, term, context, w, w_later):
    rows, width = tokens.shape
    depth = context.shape[1]
    return pl.pallas_call(
        output_kernel,
        in_specs=[WHOLE] * 5,
        out_specs=HBM,
        out_shape=shaped((rows, width), jnp.bfloat16),
        scratch_shapes=[pltpu.VMEM((rows, width), jnp.bfloat16), pltpu.SemaphoreType.DMA((8,))],
        compiler_params=params(20),
        cost_estimate=cost(2 * rows * width * depth, rows * width * 4),
        name="output",
    )(tokens, term, context, w, w_later)


def swap(value):
    return lax.ppermute(value, "tp", SWAP)


def onward(value, distances):
    count, cores = lax.axis_size("dp"), len(distances)
    pairs = [
        (source * cores + core, (source + distance) * cores + core)
        for core, distance in enumerate(distances)
        for source in range(count - distance)
    ]
    return lax.ppermute(value, ("dp", "tp"), pairs)


def local(tokens, norm_gain, lengths, w_query, w_key, w_value, w_out):
    rows = tokens.shape[0]
    frequency = 500000.0 ** (-jnp.arange(HEAD // 2, dtype=jnp.float32) * 2.0 / HEAD)
    frequency = jnp.concatenate([frequency, frequency])[None, :]

    sums, gain, tokens = squares(frequency, norm_gain.reshape(-1, LANES), tokens)
    sums_other = swap(sums)
    tables = rotary_tables(frequency, lengths, rows)
    sums_other, tables = lax.optimization_barrier((sums_other, tables))
    normed_other, inverse = normalize_other(tokens, sums, sums_other, gain)
    come_mine = swap(normed_other)
    normed_mine, kv_partial, wk, wv = normalize_own(tokens, gain, inverse, w_key, w_value)
    come_other = swap(normed_mine)
    come_mine, kv_partial = lax.optimization_barrier((come_mine, kv_partial))
    kv = finish_keys(come_mine, kv_partial, wk, wv, tables)
    assert (rows + MOST - 2) // rows == 3
    kv, normed_mine = lax.optimization_barrier((kv, normed_mine))
    third = onward(kv, (3, 3))
    kv_other = swap(kv)
    block = onward(join(kv, kv_other), (1, 2))
    partial = queries_own(normed_mine, normed_other, w_query)
    queries, w_send, w_later = finish_queries(come_mine, come_other, partial, w_query, tables, w_out)
    w_other = swap(w_send)
    *state, w_mine = attend_own(lengths, queries, [kv, kv_other], w_out)
    third, block, state = lax.optimization_barrier((third, block, state))
    blocks = [third, swap(third), block, swap(block)]
    blocks, w_later = lax.optimization_barrier((blocks, w_later))
    w_other_later = swap(w_later)
    context = attend(lengths, queries, blocks, state)
    context_other = swap(context)
    term = group_term(context, w_mine)
    return output(tokens, term, context_other, w_other, w_other_later)


def solution(mesh):
    placed = (P(("grp", "dp"), "tp"), P("tp"), P("grp"), P(None, "tp"), P(), P(), P("tp", None))
    return jax.shard_map(
        local, mesh=mesh, in_specs=placed, out_specs=P(("grp", "dp"), "tp"), check_vma=False
    )
```

```python
import functools
import math

import jax
import jax.numpy as jnp
from jax import lax
from jax.experimental import pallas as pl
from jax.experimental.pallas import tpu as pltpu
from jax.sharding import PartitionSpec as P

HEAD = 128
MOST = 1536
LANES = 128
SWAP = [(0, 1), (1, 0)]
MIB = 1024 * 1024
EXP2_SCALE = math.log2(math.e) / HEAD**0.5

WHOLE = pl.BlockSpec(memory_space=pltpu.VMEM)
HBM = pl.BlockSpec(memory_space=pltpu.HBM)


def in_hbm(*arrays):
    return [pltpu.with_memory_space_constraint(array, pltpu.HBM) for array in arrays]


def params(mib):
    return pltpu.CompilerParams(vmem_limit_bytes=mib * MIB)


def cost(flops, moved):
    return pl.CostEstimate(flops=flops, bytes_accessed=moved, transcendentals=0)


SMALL = cost(1, 1)


def shaped(shape, dtype):
    return jax.ShapeDtypeStruct(shape, dtype)


def first_of_document(lengths_ref, first_here, row):
    start = -first_here
    begin = jnp.full(jnp.shape(row), start, jnp.int32)
    for d in range(lengths_ref.shape[0] - 1):
        start = start + lengths_ref[d]
        begin = jnp.where(row >= start, start, begin)
    return begin


ROWS = 64
WIDE = 256


def block_rows(start, r):
    return pl.ds(pl.multiple_of(start + r * ROWS, ROWS), ROWS)


def wide_slice(ref, at, j):
    wide = ref[at, j : j + WIDE].astype(jnp.float32)
    return [wide[:, i : i + LANES] for i in range(0, WIDE, LANES)]


def squares_kernel(frequency_ref, gain_hbm, tokens_hbm, sums_ref, gain_ref, tokens_ref, narrow, sems):
    rows, width = tokens_ref.shape
    chunks = sems.shape[0] - 1
    height = rows // chunks
    loads = [
        pltpu.make_async_copy(
            tokens_hbm.at[c * height : (c + 1) * height], tokens_ref.at[c * height : (c + 1) * height], sems.at[c]
        )
        for c in range(chunks)
    ]
    loads.append(pltpu.make_async_copy(gain_hbm, narrow, sems.at[chunks]))
    for load in loads:
        load.start()
    for c in range(chunks):
        loads[c].wait()
        for r in range(height // ROWS):
            at = slice(c * height + r * ROWS, c * height + (r + 1) * ROWS)
            total = jnp.zeros((ROWS, LANES), jnp.float32)
            for j in range(0, width, WIDE):
                for wide in wide_slice(tokens_ref, at, j):
                    total = total + wide * wide
            sums_ref[at, :] = total
    loads[chunks].wait()
    gain_ref[...] = narrow[...].astype(jnp.float32)


def squares(frequency, gain, tokens):
    rows, width = tokens.shape
    return pl.pallas_call(
        squares_kernel,
        in_specs=[WHOLE, HBM, HBM],
        out_specs=[WHOLE] * 3,
        out_shape=[
            shaped((rows, LANES), jnp.float32),
            shaped(gain.shape, jnp.float32),
            shaped(tokens.shape, tokens.dtype),
        ],
        scratch_shapes=[pltpu.VMEM(gain.shape, gain.dtype), pltpu.SemaphoreType.DMA((8 + 1,))],
        compiler_params=params(16),
        cost_estimate=cost(rows * width * 2, rows * width * 2),
        name="squares",
    )(frequency, *in_hbm(gain, tokens))


def sine_and_cosine(x):
    turns = jnp.floor(x * (2.0 / math.pi) + 0.5)
    r = ((x - turns * 1.5703125) - turns * 4.837512969970703125e-4) - turns * 7.54978995489188e-8
    z = r * r
    s = ((-1.9515295891e-4 * z + 8.3321608736e-3) * z - 1.6666654611e-1) * z * r + r
    c = ((2.443315711809948e-5 * z - 1.388731625493765e-3) * z + 4.166664568298827e-2) * z * z - 0.5 * z + 1.0
    quadrant = turns.astype(jnp.int32)
    odd = (quadrant & 1) == 1
    sine = jnp.where(odd, c, s)
    cosine = jnp.where(odd, s, c)
    sine = jnp.where((quadrant & 2) == 2, -sine, sine)
    cosine = jnp.where(((quadrant + 1) & 2) == 2, -cosine, cosine)
    return sine, cosine


def tables_kernel(frequency_ref, lengths_hbm, cos_ref, sin_ref, lengths_ref, sem):
    rows = cos_ref.shape[0]
    half = rows // 2
    load = pltpu.make_async_copy(lengths_hbm, lengths_ref, sem)
    load.start()
    lane = lax.broadcasted_iota(jnp.int32, (half, HEAD), 1)
    row = lax.broadcasted_iota(jnp.int32, (half, HEAD), 0) + jnp.where(lane < HEAD // 2, 0, half)
    low = lane < HEAD // 2
    load.wait()
    begin = first_of_document(lengths_ref, lax.axis_index("dp") * rows, row)
    sine, cosine = sine_and_cosine((row - begin).astype(jnp.float32) * frequency_ref[...])
    for table_ref, table, sign in ((cos_ref, cosine, 1.0), (sin_ref, sine, -1.0)):
        turned = pltpu.roll(table, HEAD // 2, 1)
        table_ref[:half, :] = jnp.where(low, sign * table, turned)
        table_ref[half:, :] = jnp.where(low, sign * turned, table)


def rotary_tables(frequency, lengths, rows):
    return pl.pallas_call(
        tables_kernel,
        in_specs=[WHOLE, HBM],
        out_specs=[WHOLE] * 2,
        out_shape=[shaped((rows, HEAD), jnp.float32)] * 2,
        scratch_shapes=[pltpu.SMEM(lengths.shape, lengths.dtype), pltpu.SemaphoreType.DMA],
        compiler_params=params(16),
        cost_estimate=cost(rows * HEAD * 100, rows * HEAD * 8),
        name="tables",
    )(frequency, *in_hbm(lengths))


def normalize(out_ref, tokens_ref, start, inverse_ref, gains_ref):
    count, width = out_ref.shape

    def block(r, carry):
        at = block_rows(start, r)
        inverse = inverse_ref[at, :]
        for j in range(0, width, WIDE):
            normed = []
            for i, wide in enumerate(wide_slice(tokens_ref, at, j)):
                gain_row = j // LANES + i
                normed.append(wide * inverse * gains_ref[gain_row : gain_row + 1, :])
            out_ref[block_rows(0, r), j : j + WIDE] = jnp.concatenate(normed, axis=1).astype(jnp.bfloat16)
        return carry

    lax.fori_loop(0, count // ROWS, block, 0)


def turn(x, cosine, sine):
    return (x * cosine + pltpu.roll(x, HEAD // 2, 1) * sine).astype(jnp.bfloat16)


def half_rows(rows, other):
    me = lax.axis_index("tp")
    half = rows // 2
    return pl.ds(pl.multiple_of((1 - me if other else me) * half, half), half)


def features(width, other):
    me = lax.axis_index("tp")
    return pl.ds(pl.multiple_of((1 - me if other else me) * width, width), width)


def both_weights(wk_ref, wv_ref, depth):
    return jnp.concatenate([wk_ref[depth, :], wv_ref[depth, :]], axis=1)


def normalize_other_kernel(tokens_ref, mine_ref, other_ref, gain_ref, normed_ref, inverse_ref):
    rows, width = tokens_ref.shape
    mean = jnp.sum(mine_ref[...] + other_ref[...], axis=1, keepdims=True) * (0.5 / width)
    inverse_ref[...] = jnp.broadcast_to(lax.rsqrt(mean + 1e-05), (rows, LANES))
    normalize(normed_ref, tokens_ref, half_rows(rows, True).start, inverse_ref, gain_ref)


def normalize_other(tokens, sums, sums_other, gain):
    rows, width = tokens.shape
    return pl.pallas_call(
        normalize_other_kernel,
        in_specs=[WHOLE] * 4,
        out_specs=[WHOLE] * 2,
        out_shape=[shaped((rows // 2, width), jnp.bfloat16), shaped((rows, LANES), jnp.float32)],
        compiler_params=params(12),
        cost_estimate=cost(rows * width * 2, rows * width * 2),
        name="normalize_other",
    )(tokens, sums, sums_other, gain)


def normalize_own_kernel(tokens_ref, gain_ref, inverse_ref, wk_hbm, wv_hbm, normed_ref, acc_ref, wk_ref, wv_ref, sems):
    rows, width = tokens_ref.shape
    loads = [
        pltpu.make_async_copy(wk_hbm, wk_ref, sems.at[0]),
        pltpu.make_async_copy(wv_hbm, wv_ref, sems.at[1]),
    ]
    for load in loads:
        load.start()
    normalize(normed_ref, tokens_ref, half_rows(rows, False).start, inverse_ref, gain_ref)
    for load in loads:
        load.wait()
    acc_ref[...] = jnp.dot(
        normed_ref[...], both_weights(wk_ref, wv_ref, features(width, False)), preferred_element_type=jnp.float32
    )


def normalize_own(tokens, gain, inverse, wk, wv):
    rows, width = tokens.shape
    return pl.pallas_call(
        normalize_own_kernel,
        in_specs=[WHOLE] * 3 + [HBM] * 2,
        out_specs=[WHOLE] * 4,
        out_shape=[
            shaped((rows // 2, width), jnp.bfloat16),
            shaped((rows // 2, 2 * HEAD), jnp.float32),
            shaped(wk.shape, wk.dtype),
            shaped(wv.shape, wv.dtype),
        ],
        scratch_shapes=[pltpu.SemaphoreType.DMA((2,))],
        compiler_params=params(12),
        cost_estimate=cost(2 * rows * width * HEAD, wk.size * 4),
        name="normalize_own",
    )(tokens, gain, inverse, *in_hbm(wk, wv))


def keys_kernel(normed_ref, acc_ref, wk_ref, wv_ref, cos_ref, sin_ref, kv_ref):
    half, width = normed_ref.shape
    here = half_rows(2 * half, False)
    total = acc_ref[...] + jnp.dot(
        normed_ref[...], both_weights(wk_ref, wv_ref, features(width, True)), preferred_element_type=jnp.float32
    )
    kv_ref[:, :HEAD] = turn(total[:, :HEAD], cos_ref[here, :], sin_ref[here, :])
    kv_ref[:, HEAD:] = total[:, HEAD:].astype(jnp.bfloat16)


def finish_keys(normed_come, acc, wk, wv, tables):
    return pl.pallas_call(
        keys_kernel,
        in_specs=[WHOLE] * 6,
        out_specs=WHOLE,
        out_shape=shaped(acc.shape, jnp.bfloat16),
        compiler_params=params(12),
        cost_estimate=cost(normed_come.size * 4 * HEAD, acc.size * 4),
        name="keys",
    )(normed_come, acc, wk, wv, *tables)


def join_kernel(mine_ref, other_ref, out_ref):
    rows = out_ref.shape[0]
    out_ref[half_rows(rows, False), :] = mine_ref[...]
    out_ref[half_rows(rows, True), :] = other_ref[...]


def join(mine, other):
    half, width = mine.shape
    return pl.pallas_call(
        join_kernel,
        in_specs=[WHOLE] * 2,
        out_specs=WHOLE,
        out_shape=shaped((2 * half, width), mine.dtype),
        compiler_params=params(8),
        cost_estimate=SMALL,
        name="join",
    )(mine, other)


def queries_own_kernel(mine_ref, other_ref, wq_ref, wout_hbm, acc_ref, wsend_ref, wlater_ref, sems):
    half, width = mine_ref.shape
    send = features(width, True).start
    loads = [
        pltpu.make_async_copy(wout_hbm.at[:, pl.ds(send, width // 2)], wsend_ref, sems.at[0]),
        pltpu.make_async_copy(wout_hbm.at[:, pl.ds(send + width // 2, width // 2)], wlater_ref, sems.at[1]),
    ]
    for load in loads:
        load.start()
    weights = wq_ref[features(width, False), :]
    acc_ref[:half, :] = jnp.dot(mine_ref[...], weights, preferred_element_type=jnp.float32)
    acc_ref[half:, :] = jnp.dot(other_ref[...], weights, preferred_element_type=jnp.float32)
    for load in loads:
        load.wait()


def queries_own(mine, other, wq, w_out):
    half, width = mine.shape
    nq = wq.shape[1]
    depth = w_out.shape[0]
    return pl.pallas_call(
        queries_own_kernel,
        in_specs=[WHOLE] * 3 + [HBM],
        out_specs=[WHOLE] * 3,
        out_shape=[
            shaped((2 * half, nq), jnp.float32),
            shaped((depth, width // 2), w_out.dtype),
            shaped((depth, width // 2), w_out.dtype),
        ],
        scratch_shapes=[pltpu.SemaphoreType.DMA((2,))],
        compiler_params=params(12),
        cost_estimate=cost(4 * half * width * nq, w_out.size),
        name="queries_own",
    )(mine, other, wq, *in_hbm(w_out))


def queries_kernel(mine_ref, other_ref, acc_ref, wq_ref, cos_ref, sin_ref, q_ref, acc):
    half, width = mine_ref.shape
    weights = wq_ref[features(width, True), :]
    acc[:half, :] = jnp.dot(mine_ref[...], weights, preferred_element_type=jnp.float32)
    acc[half:, :] = jnp.dot(other_ref[...], weights, preferred_element_type=jnp.float32)

    def finish(me):
        for part, which in ((slice(0, half), me), (slice(half, 2 * half), 1 - me)):
            at = slice(which * half, (which + 1) * half)
            for h in range(q_ref.shape[1] // HEAD):
                lanes = slice(h * HEAD, (h + 1) * HEAD)
                q_ref[at, lanes] = turn(acc_ref[part, lanes] + acc[part, lanes], cos_ref[at, :], sin_ref[at, :])

    for core in range(2):
        pl.when(lax.axis_index("tp") == core)(functools.partial(finish, core))


def finish_queries(mine, other, acc, wq, tables):
    half, width = mine.shape
    nq = wq.shape[1]
    return pl.pallas_call(
        queries_kernel,
        in_specs=[WHOLE] * 6,
        out_specs=WHOLE,
        out_shape=shaped((2 * half, nq), jnp.bfloat16),
        scratch_shapes=[pltpu.VMEM((2 * half, nq), jnp.float32)],
        compiler_params=params(12),
        cost_estimate=cost(4 * half * width * nq, half * nq * 16),
        name="queries",
    )(mine, other, acc, wq, *tables)


TILE = 128
SPAN = 512


def place_blocks(blocks, starts, keys, values):
    for block, start in zip(blocks, starts, strict=True):
        at = pl.ds(pl.multiple_of(start, block.shape[0]), block.shape[0])
        keys[:, at] = block[:, :HEAD].T
        values[at, :] = block[:, HEAD:]


def lanes_max(x):
    return jnp.broadcast_to(jnp.max(x, axis=1, keepdims=True), x.shape)


def weigh(scores, probs, at, first, count, top):
    scaled = top * EXP2_SCALE
    total = jnp.zeros((ROWS, LANES), jnp.float32)
    for j in range(0, count, WIDE):
        weights = []
        for i in range(j, j + WIDE, LANES):
            w = jnp.exp2(scores[at, first + i : first + i + LANES] * EXP2_SCALE - scaled)
            total = total + w
            weights.append(w)
        probs[at, first + j : first + j + WIDE] = jnp.concatenate(weights, axis=1).astype(jnp.bfloat16)
    return total


def attend_own_kernel(
    lengths_hbm, q_ref, mine_ref, other_ref, wout_hbm, acc_ref, tops_ref, sums_ref, wkeep_ref,
    keys, values, stacked, bias, scores, probs, lengths_ref, sems,
):
    load = pltpu.make_async_copy(lengths_hbm, lengths_ref, sems.at[0])
    load.start()
    keep = pltpu.make_async_copy(wout_hbm.at[:, features(wkeep_ref.shape[1], False)], wkeep_ref, sems.at[1])
    keep.start()
    rows = q_ref.shape[0]
    half = rows // 2
    me = lax.axis_index("tp")
    place_blocks([mine_ref, other_ref], [me * half, (1 - me) * half], keys, values)
    load.wait()
    row = lax.broadcasted_iota(jnp.int32, (rows, LANES), 0)
    lane = lax.broadcasted_iota(jnp.int32, (rows, LANES), 1)
    begin = first_of_document(lengths_ref, lax.axis_index("dp") * rows, row)
    for j in range(0, rows, LANES):
        allowed = (lane + j >= begin) & (lane + j <= row)
        bias[:, j : j + LANES] = jnp.where(allowed, 0.0, -1e30)
    heads = q_ref.shape[1] // HEAD
    for first, count in ((0, half), (half, rows)):
        for h in range(heads):
            stacked[h * half : (h + 1) * half, :] = q_ref[first : first + half, h * HEAD : (h + 1) * HEAD]
        scores[:, :count] = jnp.dot(stacked[...], keys[:, :count], preferred_element_type=jnp.float32)

        def block(r, carry):
            h, within = r // (half // ROWS), lax.rem(r, half // ROWS)
            at = block_rows(0, r)
            out_at = block_rows(h * rows + first, within)
            top = jnp.full((ROWS, LANES), -1e30, jnp.float32)
            for j in range(0, count, LANES):
                s = scores[at, j : j + LANES] + bias[block_rows(first, within), j : j + LANES]
                scores[at, j : j + LANES] = s
                top = jnp.maximum(top, s)
            top = lanes_max(top)
            tops_ref[out_at, :] = top
            sums_ref[out_at, :] = weigh(scores, probs, at, 0, count, top)
            return carry

        lax.fori_loop(0, heads * half // ROWS, block, 0, unroll=4)
        term = jnp.dot(probs[:, :count], values[:count, :], preferred_element_type=jnp.float32)
        for h in range(heads):
            acc_ref[h * rows + first : h * rows + first + half, :] = term[h * half : (h + 1) * half, :]
    keep.wait()


def attend_kernel(
    lengths_hbm, q_ref, third_ref, third_other_ref, block_ref, block_other_ref, acc_in, tops_in, sums_in,
    ctx_ref, keys, values, stacked, scores, probs, acc, sums, lengths_ref, sem,
):
    load = pltpu.make_async_copy(lengths_hbm, lengths_ref, sem)
    load.start()
    rows = q_ref.shape[0]
    half = rows // 2
    heads = q_ref.shape[1] // HEAD
    behind = keys.shape[1]
    me = lax.axis_index("tp")
    place_blocks(
        [third_ref, third_other_ref, block_ref, block_other_ref],
        [me * half, (1 - me) * half, rows * (2 - me), rows * (1 + me)],
        keys,
        values,
    )
    load.wait()
    start = -lax.axis_index("dp") * rows
    begin, end = start, jnp.int32(rows)
    for d in range(lengths_ref.shape[0] - 1):
        start = start + lengths_ref[d]
        begin = jnp.where(start <= 0, start, begin)
        end = jnp.where(start > 0, jnp.minimum(end, start), end)
    low = begin + behind
    lane = lax.broadcasted_iota(jnp.int32, (ROWS, LANES), 1)
    line = lax.broadcasted_iota(jnp.int32, (ROWS, LANES), 0)

    def alone(at, q_at, h):
        total = jnp.sum(sums_in[at, :], axis=1, keepdims=True)
        ctx_ref[q_at, h * HEAD : (h + 1) * HEAD] = (acc_in[at, :] / total).astype(jnp.bfloat16)

    def tile(t, carry):
        reached = (t * TILE < end) & (low < behind)

        @pl.when(jnp.logical_not(reached))
        def _():
            for h in range(heads):
                for r in range(TILE // ROWS):
                    alone(block_rows(h * rows + t * TILE, r), block_rows(t * TILE, r), h)

        def merge(first):
            for h in range(heads):
                stacked[h * TILE : (h + 1) * TILE, :] = q_ref[
                    pl.ds(pl.multiple_of(t * TILE, TILE), TILE), h * HEAD : (h + 1) * HEAD
                ]
            scores[:, first:] = jnp.dot(stacked[...], keys[:, first:], preferred_element_type=jnp.float32)
            for h in range(heads):
                for r in range(TILE // ROWS):
                    at = slice(h * TILE + r * ROWS, h * TILE + (r + 1) * ROWS)
                    state = block_rows(h * rows + t * TILE, r)
                    own_top = tops_in[state, :]
                    top = own_top
                    for j in range(first, behind, LANES):
                        s = scores[at, j : j + LANES]
                        if j < first + SPAN:
                            s = jnp.where(lane + j >= low, s, -1e30)
                            scores[at, j : j + LANES] = s
                        top = jnp.maximum(top, s)
                    top = lanes_max(top)
                    rescale = jnp.exp2((own_top - top) * EXP2_SCALE)
                    acc[at, :] = acc_in[state, :] * rescale
                    sums[at, :] = sums_in[state, :] * rescale + weigh(scores, probs, at, first, behind - first, top)
            acc[...] += jnp.dot(probs[:, first:], values[first:, :], preferred_element_type=jnp.float32)
            for h in range(heads):
                for r in range(TILE // ROWS):
                    at = slice(h * TILE + r * ROWS, h * TILE + (r + 1) * ROWS)
                    state = block_rows(h * rows + t * TILE, r)
                    merged = line + (t * TILE + r * ROWS) < end
                    total = jnp.sum(jnp.where(merged, sums[at, :], sums_in[state, :]), axis=1, keepdims=True)
                    context = jnp.where(merged, acc[at, :], acc_in[state, :]) / total
                    ctx_ref[block_rows(t * TILE, r), h * HEAD : (h + 1) * HEAD] = context.astype(jnp.bfloat16)

        for first in range(0, behind, SPAN):
            inside = (low >= first) & (low < first + SPAN)
            pl.when(reached & inside)(functools.partial(merge, first))
        return carry

    lax.fori_loop(0, rows // TILE, tile, 0)


def attend_own(lengths, queries, blocks, w_out):
    rows, width = queries.shape
    half = rows // 2
    heads = width // HEAD
    return pl.pallas_call(
        attend_own_kernel,
        in_specs=[HBM] + [WHOLE] * 3 + [HBM],
        out_specs=[WHOLE] * 4,
        scratch_shapes=[
            pltpu.VMEM((HEAD, rows), jnp.bfloat16),
            pltpu.VMEM((rows, HEAD), jnp.bfloat16),
            pltpu.VMEM((heads * half, HEAD), jnp.bfloat16),
            pltpu.VMEM((rows, rows), jnp.float32),
            pltpu.VMEM((heads * half, rows), jnp.float32),
            pltpu.VMEM((heads * half, rows), jnp.bfloat16),
            pltpu.SMEM(lengths.shape, lengths.dtype),
            pltpu.SemaphoreType.DMA((2,)),
        ],
        out_shape=[shaped((heads * rows, LANES), jnp.float32)] * 3
        + [shaped((w_out.shape[0], w_out.shape[1] // 2), w_out.dtype)],
        compiler_params=params(16),
        cost_estimate=cost(4 * rows * width * rows, rows * width * 8),
        name="attend_own",
    )(*in_hbm(lengths), queries, *blocks, *in_hbm(w_out))


def attend(lengths, queries, blocks, state):
    rows, width = queries.shape
    heads = width // HEAD
    tall = heads * TILE
    places = sum(block.shape[0] for block in blocks)
    return pl.pallas_call(
        attend_kernel,
        in_specs=[HBM] + [WHOLE] * (1 + len(blocks) + len(state)),
        out_specs=WHOLE,
        scratch_shapes=[
            pltpu.VMEM((HEAD, places), jnp.bfloat16),
            pltpu.VMEM((places, HEAD), jnp.bfloat16),
            pltpu.VMEM((tall, HEAD), jnp.bfloat16),
            pltpu.VMEM((tall, places), jnp.float32),
            pltpu.VMEM((tall, places), jnp.bfloat16),
            pltpu.VMEM((tall, HEAD), jnp.float32),
            pltpu.VMEM((tall, LANES), jnp.float32),
            pltpu.SMEM(lengths.shape, lengths.dtype),
            pltpu.SemaphoreType.DMA,
        ],
        out_shape=shaped((rows, width), jnp.bfloat16),
        compiler_params=params(20),
        cost_estimate=cost(4 * rows * width * places, rows * width * 8),
        name="attend",
    )(*in_hbm(lengths), queries, *blocks, *state)


def term_kernel(context_ref, w_ref, term_ref):
    step = 1024
    for c in range(w_ref.shape[1] // step):
        part = slice(c * step, (c + 1) * step)
        term_ref[:, part] = jnp.dot(context_ref[...], w_ref[:, part], preferred_element_type=jnp.float32).astype(jnp.bfloat16)


def group_term(context, w):
    rows, depth = context.shape
    width = w.shape[1]
    return pl.pallas_call(
        term_kernel,
        in_specs=[WHOLE] * 2,
        out_specs=WHOLE,
        out_shape=shaped((rows, width), jnp.bfloat16),
        compiler_params=params(16),
        cost_estimate=cost(2 * rows * depth * width, rows * width * 2),
        name="own_term",
    )(context, w)


def output_kernel(tokens_ref, term_ref, context_ref, w_ref, w_later_ref, out_hbm, out, sems):
    width = out.shape[1]
    half = width // 2
    chunks = sems.shape[0]
    step = width // chunks
    stores = []
    for c in range(chunks):
        here = slice(c * step, (c + 1) * step)
        weights = w_ref[:, here] if c < chunks // 2 else w_later_ref[:, c * step - half : (c + 1) * step - half]
        other = jnp.dot(context_ref[...], weights, preferred_element_type=jnp.float32).astype(jnp.bfloat16)
        total = tokens_ref[:, here].astype(jnp.float32) + term_ref[:, here].astype(jnp.float32) + other.astype(jnp.float32)
        out[:, here] = total.astype(jnp.bfloat16)
        stores.append(pltpu.make_async_copy(out.at[:, here], out_hbm.at[:, here], sems.at[c]))
        stores[c].start()
    for store in stores:
        store.wait()


def output(tokens, term, context, w, w_later):
    rows, width = tokens.shape
    depth = context.shape[1]
    return pl.pallas_call(
        output_kernel,
        in_specs=[WHOLE] * 5,
        out_specs=HBM,
        out_shape=shaped((rows, width), jnp.bfloat16),
        scratch_shapes=[pltpu.VMEM((rows, width), jnp.bfloat16), pltpu.SemaphoreType.DMA((8,))],
        compiler_params=params(20),
        cost_estimate=cost(2 * rows * width * depth, rows * width * 4),
        name="output",
    )(tokens, term, context, w, w_later)


def swap(value):
    return lax.ppermute(value, "tp", SWAP)


def onward(value, distances):
    count, cores = lax.axis_size("dp"), len(distances)
    pairs = [
        (source * cores + core, (source + distance) * cores + core)
        for core, distance in enumerate(distances)
        for source in range(count - distance)
    ]
    return lax.ppermute(value, ("dp", "tp"), pairs)


def local(tokens, norm_gain, lengths, w_query, w_key, w_value, w_out):
    rows = tokens.shape[0]
    frequency = 500000.0 ** (-jnp.arange(HEAD // 2, dtype=jnp.float32) * 2.0 / HEAD)
    frequency = jnp.concatenate([frequency, frequency])[None, :]

    sums, gain, tokens = squares(frequency, norm_gain.reshape(-1, LANES), tokens)
    sums_other = swap(sums)
    tables = rotary_tables(frequency, lengths, rows)
    sums_other, tables = lax.optimization_barrier((sums_other, tables))
    normed_other, inverse = normalize_other(tokens, sums, sums_other, gain)
    come_mine = swap(normed_other)
    normed_mine, kv_partial, wk, wv = normalize_own(tokens, gain, inverse, w_key, w_value)
    come_other = swap(normed_mine)
    come_mine, kv_partial = lax.optimization_barrier((come_mine, kv_partial))
    kv = finish_keys(come_mine, kv_partial, wk, wv, tables)
    assert (rows + MOST - 2) // rows == 3
    kv, normed_mine = lax.optimization_barrier((kv, normed_mine))
    third = onward(kv, (3, 3))
    kv_other = swap(kv)
    block = onward(join(kv, kv_other), (1, 2))
    partial, w_send, w_later = queries_own(normed_mine, normed_other, w_query, w_out)
    queries = finish_queries(come_mine, come_other, partial, w_query, tables)
    w_other = swap(w_send)
    *state, w_mine = attend_own(lengths, queries, [kv, kv_other], w_out)
    third, block, state = lax.optimization_barrier((third, block, state))
    blocks = [third, swap(third), block, swap(block)]
    blocks, w_later = lax.optimization_barrier((blocks, w_later))
    w_other_later = swap(w_later)
    context = attend(lengths, queries, blocks, state)
    context_other = swap(context)
    term = group_term(context, w_mine)
    return output(tokens, term, context_other, w_other, w_other_later)


def solution(mesh):
    placed = (P(("grp", "dp"), "tp"), P("tp"), P("grp"), P(None, "tp"), P(), P(), P("tp", None))
    return jax.shard_map(
        local, mesh=mesh, in_specs=placed, out_specs=P(("grp", "dp"), "tp"), check_vma=False
    )
```

```python
import functools
import math

import jax
import jax.numpy as jnp
from jax import lax
from jax.experimental import pallas as pl
from jax.experimental.pallas import tpu as pltpu
from jax.sharding import PartitionSpec as P

HEAD = 128
MOST = 1536
LANES = 128
SWAP = [(0, 1), (1, 0)]
MIB = 1024 * 1024
PIECES = 8
EXP2_SCALE = math.log2(math.e) / HEAD**0.5

WHOLE = pl.BlockSpec(memory_space=pltpu.VMEM)
HBM = pl.BlockSpec(memory_space=pltpu.HBM)


def in_hbm(*arrays):
    return [pltpu.with_memory_space_constraint(array, pltpu.HBM) for array in arrays]


def params(mib):
    return pltpu.CompilerParams(vmem_limit_bytes=mib * MIB)


def cost(flops, moved):
    return pl.CostEstimate(flops=flops, bytes_accessed=moved, transcendentals=0)


SMALL = cost(1, 1)


def load_rows(source, destination, sems, count):
    rows = destination.shape[0] // count
    loads = [
        pltpu.make_async_copy(source.at[i * rows : (i + 1) * rows], destination.at[i * rows : (i + 1) * rows], sems.at[i])
        for i in range(count)
    ]
    for load in loads:
        load.start()
    return loads


def shaped(shape, dtype):
    return jax.ShapeDtypeStruct(shape, dtype)


def first_of_document(lengths_ref, first_here, row):
    start = -first_here
    begin = jnp.full(jnp.shape(row), start, jnp.int32)
    for d in range(lengths_ref.shape[0] - 1):
        start = start + lengths_ref[d]
        begin = jnp.where(row >= start, start, begin)
    return begin


ROWS = 64
WIDE = 256


def block_rows(start, r):
    return pl.ds(pl.multiple_of(start + r * ROWS, ROWS), ROWS)


def wide_slice(ref, at, j):
    wide = ref[at, j : j + WIDE].astype(jnp.float32)
    return [wide[:, i : i + LANES] for i in range(0, WIDE, LANES)]


def squares_kernel(frequency_ref, gain_hbm, tokens_hbm, sums_ref, gain_ref, tokens_ref, narrow, sems):
    rows, width = tokens_ref.shape
    chunks = sems.shape[0] - 1
    height = rows // chunks
    loads = [
        pltpu.make_async_copy(
            tokens_hbm.at[c * height : (c + 1) * height], tokens_ref.at[c * height : (c + 1) * height], sems.at[c]
        )
        for c in range(chunks)
    ]
    loads.append(pltpu.make_async_copy(gain_hbm, narrow, sems.at[chunks]))
    for load in loads:
        load.start()
    for c in range(chunks):
        loads[c].wait()
        for r in range(height // ROWS):
            at = slice(c * height + r * ROWS, c * height + (r + 1) * ROWS)
            total = jnp.zeros((ROWS, LANES), jnp.float32)
            for j in range(0, width, WIDE):
                for wide in wide_slice(tokens_ref, at, j):
                    total = total + wide * wide
            sums_ref[at, :] = total
    loads[chunks].wait()
    gain_ref[...] = narrow[...].astype(jnp.float32)


def squares(frequency, gain, tokens):
    rows, width = tokens.shape
    return pl.pallas_call(
        squares_kernel,
        in_specs=[WHOLE, HBM, HBM],
        out_specs=[WHOLE] * 3,
        out_shape=[
            shaped((rows, LANES), jnp.float32),
            shaped(gain.shape, jnp.float32),
            shaped(tokens.shape, tokens.dtype),
        ],
        scratch_shapes=[pltpu.VMEM(gain.shape, gain.dtype), pltpu.SemaphoreType.DMA((8 + 1,))],
        compiler_params=params(16),
        cost_estimate=cost(rows * width * 2, rows * width * 2),
        name="squares",
    )(frequency, *in_hbm(gain, tokens))


def sine_and_cosine(x):
    turns = jnp.floor(x * (2.0 / math.pi) + 0.5)
    r = ((x - turns * 1.5703125) - turns * 4.837512969970703125e-4) - turns * 7.54978995489188e-8
    z = r * r
    s = ((-1.9515295891e-4 * z + 8.3321608736e-3) * z - 1.6666654611e-1) * z * r + r
    c = ((2.443315711809948e-5 * z - 1.388731625493765e-3) * z + 4.166664568298827e-2) * z * z - 0.5 * z + 1.0
    quadrant = turns.astype(jnp.int32)
    odd = (quadrant & 1) == 1
    sine = jnp.where(odd, c, s)
    cosine = jnp.where(odd, s, c)
    sine = jnp.where((quadrant & 2) == 2, -sine, sine)
    cosine = jnp.where(((quadrant + 1) & 2) == 2, -cosine, cosine)
    return sine, cosine


def tables_kernel(frequency_ref, lengths_hbm, cos_ref, sin_ref, lengths_ref, sem):
    rows = cos_ref.shape[0]
    half = rows // 2
    load = pltpu.make_async_copy(lengths_hbm, lengths_ref, sem)
    load.start()
    lane = lax.broadcasted_iota(jnp.int32, (half, HEAD), 1)
    row = lax.broadcasted_iota(jnp.int32, (half, HEAD), 0) + jnp.where(lane < HEAD // 2, 0, half)
    low = lane < HEAD // 2
    load.wait()
    begin = first_of_document(lengths_ref, lax.axis_index("dp") * rows, row)
    sine, cosine = sine_and_cosine((row - begin).astype(jnp.float32) * frequency_ref[...])
    for table_ref, table, sign in ((cos_ref, cosine, 1.0), (sin_ref, sine, -1.0)):
        turned = pltpu.roll(table, HEAD // 2, 1)
        table_ref[:half, :] = jnp.where(low, sign * table, turned)
        table_ref[half:, :] = jnp.where(low, sign * turned, table)


def rotary_tables(frequency, lengths, rows):
    return pl.pallas_call(
        tables_kernel,
        in_specs=[WHOLE, HBM],
        out_specs=[WHOLE] * 2,
        out_shape=[shaped((rows, HEAD), jnp.float32)] * 2,
        scratch_shapes=[pltpu.SMEM(lengths.shape, lengths.dtype), pltpu.SemaphoreType.DMA],
        compiler_params=params(16),
        cost_estimate=cost(rows * HEAD * 100, rows * HEAD * 8),
        name="tables",
    )(frequency, *in_hbm(lengths))


def normalize(out_ref, tokens_ref, start, inverse_ref, gains_ref):
    count, width = out_ref.shape

    def block(r, carry):
        at = block_rows(start, r)
        inverse = inverse_ref[at, :]
        for j in range(0, width, WIDE):
            normed = []
            for i, wide in enumerate(wide_slice(tokens_ref, at, j)):
                gain_row = j // LANES + i
                normed.append(wide * inverse * gains_ref[gain_row : gain_row + 1, :])
            out_ref[block_rows(0, r), j : j + WIDE] = jnp.concatenate(normed, axis=1).astype(jnp.bfloat16)
        return carry

    lax.fori_loop(0, count // ROWS, block, 0)


def turn(x, cosine, sine):
    return (x * cosine + pltpu.roll(x, HEAD // 2, 1) * sine).astype(jnp.bfloat16)


def half_rows(rows, other):
    me = lax.axis_index("tp")
    half = rows // 2
    return pl.ds(pl.multiple_of((1 - me if other else me) * half, half), half)


def features(width, other):
    me = lax.axis_index("tp")
    return pl.ds(pl.multiple_of((1 - me if other else me) * width, width), width)


def both_weights(wk_ref, wv_ref, depth):
    return jnp.concatenate([wk_ref[depth, :], wv_ref[depth, :]], axis=1)


def normalize_other_kernel(tokens_ref, mine_ref, other_ref, gain_ref, normed_ref, inverse_ref):
    rows, width = tokens_ref.shape
    mean = jnp.sum(mine_ref[...] + other_ref[...], axis=1, keepdims=True) * (0.5 / width)
    inverse_ref[...] = jnp.broadcast_to(lax.rsqrt(mean + 1e-05), (rows, LANES))
    normalize(normed_ref, tokens_ref, half_rows(rows, True).start, inverse_ref, gain_ref)


def normalize_other(tokens, sums, sums_other, gain):
    rows, width = tokens.shape
    return pl.pallas_call(
        normalize_other_kernel,
        in_specs=[WHOLE] * 4,
        out_specs=[WHOLE] * 2,
        out_shape=[shaped((rows // 2, width), jnp.bfloat16), shaped((rows, LANES), jnp.float32)],
        compiler_params=params(12),
        cost_estimate=cost(rows * width * 2, rows * width * 2),
        name="normalize_other",
    )(tokens, sums, sums_other, gain)


def normalize_own_kernel(tokens_ref, gain_ref, inverse_ref, wk_hbm, wv_hbm, normed_ref, acc_ref, wk_ref, wv_ref, sems):
    rows, width = tokens_ref.shape
    loads = load_rows(wk_hbm, wk_ref, sems.at[0], PIECES) + load_rows(wv_hbm, wv_ref, sems.at[1], PIECES)
    normalize(normed_ref, tokens_ref, half_rows(rows, False).start, inverse_ref, gain_ref)
    for load in loads:
        load.wait()
    acc_ref[...] = jnp.dot(
        normed_ref[...], both_weights(wk_ref, wv_ref, features(width, False)), preferred_element_type=jnp.float32
    )


def normalize_own(tokens, gain, inverse, wk, wv):
    rows, width = tokens.shape
    return pl.pallas_call(
        normalize_own_kernel,
        in_specs=[WHOLE] * 3 + [HBM] * 2,
        out_specs=[WHOLE] * 4,
        out_shape=[
            shaped((rows // 2, width), jnp.bfloat16),
            shaped((rows // 2, 2 * HEAD), jnp.float32),
            shaped(wk.shape, wk.dtype),
            shaped(wv.shape, wv.dtype),
        ],
        scratch_shapes=[pltpu.SemaphoreType.DMA((2, PIECES))],
        compiler_params=params(12),
        cost_estimate=cost(2 * rows * width * HEAD, wk.size * 4),
        name="normalize_own",
    )(tokens, gain, inverse, *in_hbm(wk, wv))


def keys_kernel(normed_ref, acc_ref, wk_ref, wv_ref, cos_ref, sin_ref, kv_ref):
    half, width = normed_ref.shape
    here = half_rows(2 * half, False)
    total = acc_ref[...] + jnp.dot(
        normed_ref[...], both_weights(wk_ref, wv_ref, features(width, True)), preferred_element_type=jnp.float32
    )
    kv_ref[:, :HEAD] = turn(total[:, :HEAD], cos_ref[here, :], sin_ref[here, :])
    kv_ref[:, HEAD:] = total[:, HEAD:].astype(jnp.bfloat16)


def finish_keys(normed_come, acc, wk, wv, tables):
    return pl.pallas_call(
        keys_kernel,
        in_specs=[WHOLE] * 6,
        out_specs=WHOLE,
        out_shape=shaped(acc.shape, jnp.bfloat16),
        compiler_params=params(12),
        cost_estimate=cost(normed_come.size * 4 * HEAD, acc.size * 4),
        name="keys",
    )(normed_come, acc, wk, wv, *tables)


def join_kernel(mine_ref, other_ref, out_ref):
    rows = out_ref.shape[0]
    out_ref[half_rows(rows, False), :] = mine_ref[...]
    out_ref[half_rows(rows, True), :] = other_ref[...]


def join(mine, other):
    half, width = mine.shape
    return pl.pallas_call(
        join_kernel,
        in_specs=[WHOLE] * 2,
        out_specs=WHOLE,
        out_shape=shaped((2 * half, width), mine.dtype),
        compiler_params=params(8),
        cost_estimate=SMALL,
        name="join",
    )(mine, other)


def queries_own_kernel(mine_ref, other_ref, wq_ref, acc_ref):
    half, width = mine_ref.shape
    weights = wq_ref[features(width, False), :]
    acc_ref[:half, :] = jnp.dot(mine_ref[...], weights, preferred_element_type=jnp.float32)
    acc_ref[half:, :] = jnp.dot(other_ref[...], weights, preferred_element_type=jnp.float32)


def queries_own(mine, other, wq):
    half, width = mine.shape
    nq = wq.shape[1]
    return pl.pallas_call(
        queries_own_kernel,
        in_specs=[WHOLE] * 3,
        out_specs=WHOLE,
        out_shape=shaped((2 * half, nq), jnp.float32),
        compiler_params=params(12),
        cost_estimate=cost(4 * half * width * nq, half * nq * 8),
        name="queries_own",
    )(mine, other, wq)


def queries_kernel(
    mine_ref, other_ref, acc_ref, wq_ref, cos_ref, sin_ref, wout_hbm, q_ref, wsend_ref, wlater_ref, acc, sems
):
    half, width = mine_ref.shape
    send = features(width, True).start
    loads = load_rows(wout_hbm.at[:, pl.ds(send, width // 2)], wsend_ref, sems.at[0], PIECES)
    loads += load_rows(wout_hbm.at[:, pl.ds(send + width // 2, width // 2)], wlater_ref, sems.at[1], PIECES)
    weights = wq_ref[features(width, True), :]
    acc[:half, :] = jnp.dot(mine_ref[...], weights, preferred_element_type=jnp.float32)
    acc[half:, :] = jnp.dot(other_ref[...], weights, preferred_element_type=jnp.float32)

    def finish(me):
        for part, which in ((slice(0, half), me), (slice(half, 2 * half), 1 - me)):
            at = slice(which * half, (which + 1) * half)
            for h in range(q_ref.shape[1] // HEAD):
                lanes = slice(h * HEAD, (h + 1) * HEAD)
                q_ref[at, lanes] = turn(acc_ref[part, lanes] + acc[part, lanes], cos_ref[at, :], sin_ref[at, :])

    for core in range(2):
        pl.when(lax.axis_index("tp") == core)(functools.partial(finish, core))
    for load in loads:
        load.wait()


def finish_queries(mine, other, acc, wq, tables, w_out):
    half, width = mine.shape
    nq = wq.shape[1]
    depth = w_out.shape[0]
    return pl.pallas_call(
        queries_kernel,
        in_specs=[WHOLE] * 6 + [HBM],
        out_specs=[WHOLE] * 3,
        out_shape=[
            shaped((2 * half, nq), jnp.bfloat16),
            shaped((depth, width // 2), w_out.dtype),
            shaped((depth, width // 2), w_out.dtype),
        ],
        scratch_shapes=[pltpu.VMEM((2 * half, nq), jnp.float32), pltpu.SemaphoreType.DMA((2, PIECES))],
        compiler_params=params(12),
        cost_estimate=cost(4 * half * width * nq, half * nq * 8),
        name="queries",
    )(mine, other, acc, wq, *tables, *in_hbm(w_out))


TILE = 128
SPAN = 512


def place_blocks(blocks, starts, keys, values):
    for block, start in zip(blocks, starts, strict=True):
        at = pl.ds(pl.multiple_of(start, block.shape[0]), block.shape[0])
        keys[:, at] = block[:, :HEAD].T
        values[at, :] = block[:, HEAD:]


def lanes_max(x):
    return jnp.broadcast_to(jnp.max(x, axis=1, keepdims=True), x.shape)


def weigh(scores, probs, at, first, count, top):
    scaled = top * EXP2_SCALE
    total = jnp.zeros((ROWS, LANES), jnp.float32)
    for j in range(0, count, WIDE):
        weights = []
        for i in range(j, j + WIDE, LANES):
            w = jnp.exp2(scores[at, first + i : first + i + LANES] * EXP2_SCALE - scaled)
            total = total + w
            weights.append(w)
        probs[at, first + j : first + j + WIDE] = jnp.concatenate(weights, axis=1).astype(jnp.bfloat16)
    return total


def attend_own_kernel(
    lengths_hbm, q_ref, mine_ref, other_ref, wout_hbm, acc_ref, tops_ref, sums_ref, wkeep_ref,
    keys, values, bias, scores, probs, lengths_ref, sems,
):
    load = pltpu.make_async_copy(lengths_hbm, lengths_ref, sems.at[PIECES])
    load.start()
    keeps = load_rows(wout_hbm.at[:, features(wkeep_ref.shape[1], False)], wkeep_ref, sems, PIECES)
    rows = q_ref.shape[0]
    half = rows // 2
    me = lax.axis_index("tp")
    place_blocks([mine_ref, other_ref], [me * half, (1 - me) * half], keys, values)
    load.wait()
    row = lax.broadcasted_iota(jnp.int32, (rows, LANES), 0)
    lane = lax.broadcasted_iota(jnp.int32, (rows, LANES), 1)
    begin = first_of_document(lengths_ref, lax.axis_index("dp") * rows, row)
    for j in range(0, rows, LANES):
        allowed = (lane + j >= begin) & (lane + j <= row)
        bias[:, j : j + LANES] = jnp.where(allowed, 0.0, -1e30)
    for h in range(q_ref.shape[1] // HEAD):
        for first, count in ((0, half), (half, rows)):
            scores[:, :count] = jnp.dot(
                q_ref[first : first + half, h * HEAD : (h + 1) * HEAD],
                keys[:, :count],
                preferred_element_type=jnp.float32,
            )
            out = h * rows + first

            def block(r, carry):
                at = block_rows(0, r)
                out_at = block_rows(out, r)
                top = jnp.full((ROWS, LANES), -1e30, jnp.float32)
                for j in range(0, count, LANES):
                    s = scores[at, j : j + LANES] + bias[block_rows(first, r), j : j + LANES]
                    scores[at, j : j + LANES] = s
                    top = jnp.maximum(top, s)
                top = lanes_max(top)
                tops_ref[out_at, :] = top
                sums_ref[out_at, :] = weigh(scores, probs, at, 0, count, top)
                return carry

            lax.fori_loop(0, half // ROWS, block, 0, unroll=True)
            acc_ref[out : out + half, :] = jnp.dot(
                probs[:, :count], values[:count, :], preferred_element_type=jnp.float32
            )
    for keep in keeps:
        keep.wait()


def attend_kernel(
    lengths_hbm, q_ref, third_ref, third_other_ref, block_ref, block_other_ref, acc_in, tops_in, sums_in,
    ctx_ref, keys, values, stacked, scores, probs, acc, sums, lengths_ref, sem,
):
    load = pltpu.make_async_copy(lengths_hbm, lengths_ref, sem)
    load.start()
    rows = q_ref.shape[0]
    half = rows // 2
    heads = q_ref.shape[1] // HEAD
    behind = keys.shape[1]
    me = lax.axis_index("tp")
    place_blocks(
        [third_ref, third_other_ref, block_ref, block_other_ref],
        [me * half, (1 - me) * half, rows * (2 - me), rows * (1 + me)],
        keys,
        values,
    )
    load.wait()
    start = -lax.axis_index("dp") * rows
    begin, end = start, jnp.int32(rows)
    for d in range(lengths_ref.shape[0] - 1):
        start = start + lengths_ref[d]
        begin = jnp.where(start <= 0, start, begin)
        end = jnp.where(start > 0, jnp.minimum(end, start), end)
    low = begin + behind
    lane = lax.broadcasted_iota(jnp.int32, (ROWS, LANES), 1)
    line = lax.broadcasted_iota(jnp.int32, (ROWS, LANES), 0)

    def alone(at, q_at, h):
        total = jnp.sum(sums_in[at, :], axis=1, keepdims=True)
        ctx_ref[q_at, h * HEAD : (h + 1) * HEAD] = (acc_in[at, :] / total).astype(jnp.bfloat16)

    def tile(t, carry):
        reached = (t * TILE < end) & (low < behind)

        @pl.when(jnp.logical_not(reached))
        def _():
            for h in range(heads):
                for r in range(TILE // ROWS):
                    alone(block_rows(h * rows + t * TILE, r), block_rows(t * TILE, r), h)

        def merge(first):
            for h in range(heads):
                stacked[h * TILE : (h + 1) * TILE, :] = q_ref[
                    pl.ds(pl.multiple_of(t * TILE, TILE), TILE), h * HEAD : (h + 1) * HEAD
                ]
            scores[:, first:] = jnp.dot(stacked[...], keys[:, first:], preferred_element_type=jnp.float32)
            for h in range(heads):
                for r in range(TILE // ROWS):
                    at = slice(h * TILE + r * ROWS, h * TILE + (r + 1) * ROWS)
                    state = block_rows(h * rows + t * TILE, r)
                    own_top = tops_in[state, :]
                    top = own_top
                    for j in range(first, behind, LANES):
                        s = scores[at, j : j + LANES]
                        if j < first + SPAN:
                            s = jnp.where(lane + j >= low, s, -1e30)
                            scores[at, j : j + LANES] = s
                        top = jnp.maximum(top, s)
                    top = lanes_max(top)
                    rescale = jnp.exp2((own_top - top) * EXP2_SCALE)
                    acc[at, :] = acc_in[state, :] * rescale
                    sums[at, :] = sums_in[state, :] * rescale + weigh(scores, probs, at, first, behind - first, top)
            acc[...] += jnp.dot(probs[:, first:], values[first:, :], preferred_element_type=jnp.float32)
            for h in range(heads):
                for r in range(TILE // ROWS):
                    at = slice(h * TILE + r * ROWS, h * TILE + (r + 1) * ROWS)
                    state = block_rows(h * rows + t * TILE, r)
                    merged = line + (t * TILE + r * ROWS) < end
                    total = jnp.sum(jnp.where(merged, sums[at, :], sums_in[state, :]), axis=1, keepdims=True)
                    context = jnp.where(merged, acc[at, :], acc_in[state, :]) / total
                    ctx_ref[block_rows(t * TILE, r), h * HEAD : (h + 1) * HEAD] = context.astype(jnp.bfloat16)

        for first in range(0, behind, SPAN):
            inside = (low >= first) & (low < first + SPAN)
            pl.when(reached & inside)(functools.partial(merge, first))
        return carry

    lax.fori_loop(0, rows // TILE, tile, 0)


def attend_own(lengths, queries, blocks, w_out):
    rows, width = queries.shape
    half = rows // 2
    heads = width // HEAD
    return pl.pallas_call(
        attend_own_kernel,
        in_specs=[HBM] + [WHOLE] * 3 + [HBM],
        out_specs=[WHOLE] * 4,
        scratch_shapes=[
            pltpu.VMEM((HEAD, rows), jnp.bfloat16),
            pltpu.VMEM((rows, HEAD), jnp.bfloat16),
            pltpu.VMEM((rows, rows), jnp.float32),
            pltpu.VMEM((half, rows), jnp.float32),
            pltpu.VMEM((half, rows), jnp.bfloat16),
            pltpu.SMEM(lengths.shape, lengths.dtype),
            pltpu.SemaphoreType.DMA((PIECES + 1,)),
        ],
        out_shape=[shaped((heads * rows, LANES), jnp.float32)] * 3
        + [shaped((w_out.shape[0], w_out.shape[1] // 2), w_out.dtype)],
        compiler_params=params(16),
        cost_estimate=SMALL,
        name="attend_own",
    )(*in_hbm(lengths), queries, *blocks, *in_hbm(w_out))


def attend(lengths, queries, blocks, state):
    rows, width = queries.shape
    heads = width // HEAD
    tall = heads * TILE
    places = sum(block.shape[0] for block in blocks)
    return pl.pallas_call(
        attend_kernel,
        in_specs=[HBM] + [WHOLE] * (1 + len(blocks) + len(state)),
        out_specs=WHOLE,
        scratch_shapes=[
            pltpu.VMEM((HEAD, places), jnp.bfloat16),
            pltpu.VMEM((places, HEAD), jnp.bfloat16),
            pltpu.VMEM((tall, HEAD), jnp.bfloat16),
            pltpu.VMEM((tall, places), jnp.float32),
            pltpu.VMEM((tall, places), jnp.bfloat16),
            pltpu.VMEM((tall, HEAD), jnp.float32),
            pltpu.VMEM((tall, LANES), jnp.float32),
            pltpu.SMEM(lengths.shape, lengths.dtype),
            pltpu.SemaphoreType.DMA,
        ],
        out_shape=shaped((rows, width), jnp.bfloat16),
        compiler_params=params(20),
        cost_estimate=SMALL,
        name="attend",
    )(*in_hbm(lengths), queries, *blocks, *state)


def term_kernel(context_ref, w_ref, term_ref):
    step = 1024
    for c in range(w_ref.shape[1] // step):
        part = slice(c * step, (c + 1) * step)
        term_ref[:, part] = jnp.dot(context_ref[...], w_ref[:, part], preferred_element_type=jnp.float32).astype(jnp.bfloat16)


def group_term(context, w):
    rows, depth = context.shape
    width = w.shape[1]
    return pl.pallas_call(
        term_kernel,
        in_specs=[WHOLE] * 2,
        out_specs=WHOLE,
        out_shape=shaped((rows, width), jnp.bfloat16),
        compiler_params=params(16),
        cost_estimate=SMALL,
        name="own_term",
    )(context, w)


def output_kernel(tokens_ref, term_ref, context_ref, w_ref, w_later_ref, out_hbm, out, sems):
    width = out.shape[1]
    half = width // 2
    chunks = sems.shape[0]
    step = width // chunks
    stores = []
    for c in range(chunks):
        here = slice(c * step, (c + 1) * step)
        weights = w_ref[:, here] if c < chunks // 2 else w_later_ref[:, c * step - half : (c + 1) * step - half]
        other = jnp.dot(context_ref[...], weights, preferred_element_type=jnp.float32).astype(jnp.bfloat16)
        total = tokens_ref[:, here].astype(jnp.float32) + term_ref[:, here].astype(jnp.float32) + other.astype(jnp.float32)
        out[:, here] = total.astype(jnp.bfloat16)
        stores.append(pltpu.make_async_copy(out.at[:, here], out_hbm.at[:, here], sems.at[c]))
        stores[c].start()
    for store in stores:
        store.wait()


def output(tokens, term, context, w, w_later):
    rows, width = tokens.shape
    depth = context.shape[1]
    return pl.pallas_call(
        output_kernel,
        in_specs=[WHOLE] * 5,
        out_specs=HBM,
        out_shape=shaped((rows, width), jnp.bfloat16),
        scratch_shapes=[pltpu.VMEM((rows, width), jnp.bfloat16), pltpu.SemaphoreType.DMA((8,))],
        compiler_params=params(20),
        cost_estimate=cost(2 * rows * width * depth, rows * width * 4),
        name="output",
    )(tokens, term, context, w, w_later)


def swap(value):
    return lax.ppermute(value, "tp", SWAP)


def onward(value, distances):
    count, cores = lax.axis_size("dp"), len(distances)
    pairs = [
        (source * cores + core, (source + distance) * cores + core)
        for core, distance in enumerate(distances)
        for source in range(count - distance)
    ]
    return lax.ppermute(value, ("dp", "tp"), pairs)


def local(tokens, norm_gain, lengths, w_query, w_key, w_value, w_out):
    rows = tokens.shape[0]
    frequency = 500000.0 ** (-jnp.arange(HEAD // 2, dtype=jnp.float32) * 2.0 / HEAD)
    frequency = jnp.concatenate([frequency, frequency])[None, :]

    sums, gain, tokens = squares(frequency, norm_gain.reshape(-1, LANES), tokens)
    sums_other = swap(sums)
    tables = rotary_tables(frequency, lengths, rows)
    sums_other, tables = lax.optimization_barrier((sums_other, tables))
    normed_other, inverse = normalize_other(tokens, sums, sums_other, gain)
    come_mine = swap(normed_other)
    normed_mine, kv_partial, wk, wv = normalize_own(tokens, gain, inverse, w_key, w_value)
    come_other = swap(normed_mine)
    come_mine, kv_partial = lax.optimization_barrier((come_mine, kv_partial))
    kv = finish_keys(come_mine, kv_partial, wk, wv, tables)
    assert (rows + MOST - 2) // rows == 3
    kv, normed_mine = lax.optimization_barrier((kv, normed_mine))
    third = onward(kv, (3, 3))
    kv_other = swap(kv)
    block = onward(join(kv, kv_other), (1, 2))
    partial = queries_own(normed_mine, normed_other, w_query)
    queries, w_send, w_later = finish_queries(come_mine, come_other, partial, w_query, tables, w_out)
    third, block, w_send = lax.optimization_barrier((third, block, w_send))
    w_other = swap(w_send)
    *state, w_mine = attend_own(lengths, queries, [kv, kv_other], w_out)
    third, block, state = lax.optimization_barrier((third, block, state))
    blocks = [third, swap(third), block, swap(block)]
    blocks, w_later, w_other = lax.optimization_barrier((blocks, w_later, w_other))
    w_other_later = swap(w_later)
    context = attend(lengths, queries, blocks, state)
    context_other = swap(context)
    term = group_term(context, w_mine)
    return output(tokens, term, context_other, w_other, w_other_later)


def solution(mesh):
    placed = (P(("grp", "dp"), "tp"), P("tp"), P("grp"), P(None, "tp"), P(), P(), P("tp", None))
    return jax.shard_map(
        local, mesh=mesh, in_specs=placed, out_specs=P(("grp", "dp"), "tp"), check_vma=False
    )
```

```python
import functools
import math

import jax
import jax.numpy as jnp
from jax import lax
from jax.experimental import pallas as pl
from jax.experimental.pallas import tpu as pltpu
from jax.sharding import PartitionSpec as P

HEAD = 128
MOST = 1536
LANES = 128
SWAP = [(0, 1), (1, 0)]
MIB = 1024 * 1024
PIECES = 8
EXP2_SCALE = math.log2(math.e) / HEAD**0.5

WHOLE = pl.BlockSpec(memory_space=pltpu.VMEM)
HBM = pl.BlockSpec(memory_space=pltpu.HBM)


def in_hbm(*arrays):
    return [pltpu.with_memory_space_constraint(array, pltpu.HBM) for array in arrays]


def params(mib):
    return pltpu.CompilerParams(vmem_limit_bytes=mib * MIB)


def cost(flops, moved):
    return pl.CostEstimate(flops=flops, bytes_accessed=moved, transcendentals=0)


SMALL = cost(1, 1)


def load_rows(source, destination, sems, count):
    rows = destination.shape[0] // count
    loads = [
        pltpu.make_async_copy(source.at[i * rows : (i + 1) * rows], destination.at[i * rows : (i + 1) * rows], sems.at[i])
        for i in range(count)
    ]
    for load in loads:
        load.start()
    return loads


def shaped(shape, dtype):
    return jax.ShapeDtypeStruct(shape, dtype)


def first_of_document(lengths_ref, first_here, row):
    start = -first_here
    begin = jnp.full(jnp.shape(row), start, jnp.int32)
    for d in range(lengths_ref.shape[0] - 1):
        start = start + lengths_ref[d]
        begin = jnp.where(row >= start, start, begin)
    return begin


ROWS = 64
WIDE = 256


def block_rows(start, r):
    return pl.ds(pl.multiple_of(start + r * ROWS, ROWS), ROWS)


def wide_slice(ref, at, j):
    wide = ref[at, j : j + WIDE].astype(jnp.float32)
    return [wide[:, i : i + LANES] for i in range(0, WIDE, LANES)]


def squares_kernel(frequency_ref, gain_hbm, tokens_hbm, sums_ref, gain_ref, tokens_ref, narrow, sems):
    rows, width = tokens_ref.shape
    chunks = sems.shape[0] - 1
    height = rows // chunks
    loads = [
        pltpu.make_async_copy(
            tokens_hbm.at[c * height : (c + 1) * height], tokens_ref.at[c * height : (c + 1) * height], sems.at[c]
        )
        for c in range(chunks)
    ]
    loads.append(pltpu.make_async_copy(gain_hbm, narrow, sems.at[chunks]))
    for load in loads:
        load.start()
    for c in range(chunks):
        loads[c].wait()
        for r in range(height // ROWS):
            at = slice(c * height + r * ROWS, c * height + (r + 1) * ROWS)
            total = jnp.zeros((ROWS, LANES), jnp.float32)
            for j in range(0, width, WIDE):
                for wide in wide_slice(tokens_ref, at, j):
                    total = total + wide * wide
            sums_ref[at, :] = total
    loads[chunks].wait()
    gain_ref[...] = narrow[...].astype(jnp.float32)


def squares(frequency, gain, tokens):
    rows, width = tokens.shape
    return pl.pallas_call(
        squares_kernel,
        in_specs=[WHOLE, HBM, HBM],
        out_specs=[WHOLE] * 3,
        out_shape=[
            shaped((rows, LANES), jnp.float32),
            shaped(gain.shape, jnp.float32),
            shaped(tokens.shape, tokens.dtype),
        ],
        scratch_shapes=[pltpu.VMEM(gain.shape, gain.dtype), pltpu.SemaphoreType.DMA((8 + 1,))],
        compiler_params=params(16),
        cost_estimate=cost(rows * width * 2, rows * width * 2),
        name="squares",
    )(frequency, *in_hbm(gain, tokens))


def sine_and_cosine(x):
    turns = jnp.floor(x * (2.0 / math.pi) + 0.5)
    r = ((x - turns * 1.5703125) - turns * 4.837512969970703125e-4) - turns * 7.54978995489188e-8
    z = r * r
    s = ((-1.9515295891e-4 * z + 8.3321608736e-3) * z - 1.6666654611e-1) * z * r + r
    c = ((2.443315711809948e-5 * z - 1.388731625493765e-3) * z + 4.166664568298827e-2) * z * z - 0.5 * z + 1.0
    quadrant = turns.astype(jnp.int32)
    odd = (quadrant & 1) == 1
    sine = jnp.where(odd, c, s)
    cosine = jnp.where(odd, s, c)
    sine = jnp.where((quadrant & 2) == 2, -sine, sine)
    cosine = jnp.where(((quadrant + 1) & 2) == 2, -cosine, cosine)
    return sine, cosine


def tables_kernel(
    frequency_ref, lengths_hbm, wk_hbm, wv_hbm, cos_ref, sin_ref, wk_ref, wv_ref, lengths_ref, sem, sems
):
    rows = cos_ref.shape[0]
    half = rows // 2
    load = pltpu.make_async_copy(lengths_hbm, lengths_ref, sem)
    load.start()
    loads = load_rows(wk_hbm, wk_ref, sems.at[0], PIECES) + load_rows(wv_hbm, wv_ref, sems.at[1], PIECES)
    lane = lax.broadcasted_iota(jnp.int32, (half, HEAD), 1)
    row = lax.broadcasted_iota(jnp.int32, (half, HEAD), 0) + jnp.where(lane < HEAD // 2, 0, half)
    low = lane < HEAD // 2
    load.wait()
    begin = first_of_document(lengths_ref, lax.axis_index("dp") * rows, row)
    sine, cosine = sine_and_cosine((row - begin).astype(jnp.float32) * frequency_ref[...])
    for table_ref, table, sign in ((cos_ref, cosine, 1.0), (sin_ref, sine, -1.0)):
        turned = pltpu.roll(table, HEAD // 2, 1)
        table_ref[:half, :] = jnp.where(low, sign * table, turned)
        table_ref[half:, :] = jnp.where(low, sign * turned, table)
    for load in loads:
        load.wait()


def rotary_tables(frequency, lengths, rows, wk, wv):
    return pl.pallas_call(
        tables_kernel,
        in_specs=[WHOLE, HBM, HBM, HBM],
        out_specs=[WHOLE] * 4,
        out_shape=[shaped((rows, HEAD), jnp.float32)] * 2 + [shaped(wk.shape, wk.dtype), shaped(wv.shape, wv.dtype)],
        scratch_shapes=[
            pltpu.SMEM(lengths.shape, lengths.dtype),
            pltpu.SemaphoreType.DMA,
            pltpu.SemaphoreType.DMA((2, PIECES)),
        ],
        compiler_params=params(16),
        cost_estimate=cost(rows * HEAD * 100, wk.size * 4),
        name="tables",
    )(frequency, *in_hbm(lengths, wk, wv))


def normalize(out_ref, tokens_ref, start, inverse_ref, gains_ref):
    count, width = out_ref.shape

    def block(r, carry):
        at = block_rows(start, r)
        inverse = inverse_ref[at, :]
        for j in range(0, width, WIDE):
            normed = []
            for i, wide in enumerate(wide_slice(tokens_ref, at, j)):
                gain_row = j // LANES + i
                normed.append(wide * inverse * gains_ref[gain_row : gain_row + 1, :])
            out_ref[block_rows(0, r), j : j + WIDE] = jnp.concatenate(normed, axis=1).astype(jnp.bfloat16)
        return carry

    lax.fori_loop(0, count // ROWS, block, 0)


def turn(x, cosine, sine):
    return (x * cosine + pltpu.roll(x, HEAD // 2, 1) * sine).astype(jnp.bfloat16)


def half_rows(rows, other):
    me = lax.axis_index("tp")
    half = rows // 2
    return pl.ds(pl.multiple_of((1 - me if other else me) * half, half), half)


def features(width, other):
    me = lax.axis_index("tp")
    return pl.ds(pl.multiple_of((1 - me if other else me) * width, width), width)


def both_weights(wk_ref, wv_ref, depth):
    return jnp.concatenate([wk_ref[depth, :], wv_ref[depth, :]], axis=1)


def normalize_other_kernel(tokens_ref, mine_ref, other_ref, gain_ref, normed_ref, inverse_ref):
    rows, width = tokens_ref.shape
    mean = jnp.sum(mine_ref[...] + other_ref[...], axis=1, keepdims=True) * (0.5 / width)
    inverse_ref[...] = jnp.broadcast_to(lax.rsqrt(mean + 1e-05), (rows, LANES))
    normalize(normed_ref, tokens_ref, half_rows(rows, True).start, inverse_ref, gain_ref)


def normalize_other(tokens, sums, sums_other, gain):
    rows, width = tokens.shape
    return pl.pallas_call(
        normalize_other_kernel,
        in_specs=[WHOLE] * 4,
        out_specs=[WHOLE] * 2,
        out_shape=[shaped((rows // 2, width), jnp.bfloat16), shaped((rows, LANES), jnp.float32)],
        compiler_params=params(12),
        cost_estimate=cost(rows * width * 2, rows * width * 2),
        name="normalize_other",
    )(tokens, sums, sums_other, gain)


def normalize_own_kernel(tokens_ref, gain_ref, inverse_ref, wk_ref, wv_ref, normed_ref, acc_ref):
    rows, width = tokens_ref.shape
    normalize(normed_ref, tokens_ref, half_rows(rows, False).start, inverse_ref, gain_ref)
    acc_ref[...] = jnp.dot(
        normed_ref[...], both_weights(wk_ref, wv_ref, features(width, False)), preferred_element_type=jnp.float32
    )


def normalize_own(tokens, gain, inverse, wk, wv):
    rows, width = tokens.shape
    return pl.pallas_call(
        normalize_own_kernel,
        in_specs=[WHOLE] * 5,
        out_specs=[WHOLE] * 2,
        out_shape=[shaped((rows // 2, width), jnp.bfloat16), shaped((rows // 2, 2 * HEAD), jnp.float32)],
        compiler_params=params(12),
        cost_estimate=cost(2 * rows * width * HEAD, wk.size * 4),
        name="normalize_own",
    )(tokens, gain, inverse, wk, wv)


def keys_kernel(normed_ref, acc_ref, wk_ref, wv_ref, cos_ref, sin_ref, kv_ref):
    half, width = normed_ref.shape
    here = half_rows(2 * half, False)
    total = acc_ref[...] + jnp.dot(
        normed_ref[...], both_weights(wk_ref, wv_ref, features(width, True)), preferred_element_type=jnp.float32
    )
    kv_ref[:, :HEAD] = turn(total[:, :HEAD], cos_ref[here, :], sin_ref[here, :])
    kv_ref[:, HEAD:] = total[:, HEAD:].astype(jnp.bfloat16)


def finish_keys(normed_come, acc, wk, wv, tables):
    return pl.pallas_call(
        keys_kernel,
        in_specs=[WHOLE] * 6,
        out_specs=WHOLE,
        out_shape=shaped(acc.shape, jnp.bfloat16),
        compiler_params=params(12),
        cost_estimate=cost(normed_come.size * 4 * HEAD, acc.size * 4),
        name="keys",
    )(normed_come, acc, wk, wv, *tables)


def join_kernel(mine_ref, other_ref, out_ref):
    rows = out_ref.shape[0]
    out_ref[half_rows(rows, False), :] = mine_ref[...]
    out_ref[half_rows(rows, True), :] = other_ref[...]


def join(mine, other):
    half, width = mine.shape
    return pl.pallas_call(
        join_kernel,
        in_specs=[WHOLE] * 2,
        out_specs=WHOLE,
        out_shape=shaped((2 * half, width), mine.dtype),
        compiler_params=params(8),
        cost_estimate=SMALL,
        name="join",
    )(mine, other)


def queries_own_kernel(mine_ref, other_ref, wq_ref, acc_ref):
    half, width = mine_ref.shape
    weights = wq_ref[features(width, False), :]
    acc_ref[:half, :] = jnp.dot(mine_ref[...], weights, preferred_element_type=jnp.float32)
    acc_ref[half:, :] = jnp.dot(other_ref[...], weights, preferred_element_type=jnp.float32)


def queries_own(mine, other, wq):
    half, width = mine.shape
    nq = wq.shape[1]
    return pl.pallas_call(
        queries_own_kernel,
        in_specs=[WHOLE] * 3,
        out_specs=WHOLE,
        out_shape=shaped((2 * half, nq), jnp.float32),
        compiler_params=params(12),
        cost_estimate=cost(4 * half * width * nq, half * nq * 8),
        name="queries_own",
    )(mine, other, wq)


def queries_kernel(
    mine_ref, other_ref, acc_ref, wq_ref, cos_ref, sin_ref, q_ref, acc
):
    half, width = mine_ref.shape
    weights = wq_ref[features(width, True), :]
    acc[:half, :] = jnp.dot(mine_ref[...], weights, preferred_element_type=jnp.float32)
    acc[half:, :] = jnp.dot(other_ref[...], weights, preferred_element_type=jnp.float32)

    def finish(me):
        for part, which in ((slice(0, half), me), (slice(half, 2 * half), 1 - me)):
            at = slice(which * half, (which + 1) * half)
            for h in range(q_ref.shape[1] // HEAD):
                lanes = slice(h * HEAD, (h + 1) * HEAD)
                q_ref[at, lanes] = turn(acc_ref[part, lanes] + acc[part, lanes], cos_ref[at, :], sin_ref[at, :])

    for core in range(2):
        pl.when(lax.axis_index("tp") == core)(functools.partial(finish, core))


def finish_queries(mine, other, acc, wq, tables):
    half, width = mine.shape
    nq = wq.shape[1]
    return pl.pallas_call(
        queries_kernel,
        in_specs=[WHOLE] * 6,
        out_specs=WHOLE,
        out_shape=shaped((2 * half, nq), jnp.bfloat16),
        scratch_shapes=[pltpu.VMEM((2 * half, nq), jnp.float32)],
        compiler_params=params(12),
        cost_estimate=cost(4 * half * width * nq, half * nq * 8),
        name="queries",
    )(mine, other, acc, wq, *tables)


TILE = 128
SPAN = 512


def place_blocks(blocks, starts, keys, values):
    for block, start in zip(blocks, starts, strict=True):
        at = pl.ds(pl.multiple_of(start, block.shape[0]), block.shape[0])
        keys[:, at] = block[:, :HEAD].T
        values[at, :] = block[:, HEAD:]


def lanes_max(x):
    return jnp.broadcast_to(jnp.max(x, axis=1, keepdims=True), x.shape)


def weigh(scores, probs, at, first, count, top):
    scaled = top * EXP2_SCALE
    total = jnp.zeros((ROWS, LANES), jnp.float32)
    for j in range(0, count, WIDE):
        weights = []
        for i in range(j, j + WIDE, LANES):
            w = jnp.exp2(scores[at, first + i : first + i + LANES] * EXP2_SCALE - scaled)
            total = total + w
            weights.append(w)
        probs[at, first + j : first + j + WIDE] = jnp.concatenate(weights, axis=1).astype(jnp.bfloat16)
    return total


def attend_own_kernel(
    lengths_hbm, q_ref, mine_ref, other_ref, wout_hbm, acc_ref, tops_ref, sums_ref, wsend_ref, wlater_ref, wkeep_ref,
    keys, values, bias, scores, probs, lengths_ref, sem, sems,
):
    load = pltpu.make_async_copy(lengths_hbm, lengths_ref, sem)
    load.start()
    width = wkeep_ref.shape[1]
    send = features(width, True).start
    weights = load_rows(wout_hbm.at[:, pl.ds(send, width // 2)], wsend_ref, sems.at[0], PIECES)
    weights += load_rows(wout_hbm.at[:, pl.ds(send + width // 2, width // 2)], wlater_ref, sems.at[1], PIECES)
    weights += load_rows(wout_hbm.at[:, features(width, False)], wkeep_ref, sems.at[2], PIECES)
    rows = q_ref.shape[0]
    half = rows // 2
    me = lax.axis_index("tp")
    place_blocks([mine_ref, other_ref], [me * half, (1 - me) * half], keys, values)
    load.wait()
    row = lax.broadcasted_iota(jnp.int32, (rows, LANES), 0)
    lane = lax.broadcasted_iota(jnp.int32, (rows, LANES), 1)
    begin = first_of_document(lengths_ref, lax.axis_index("dp") * rows, row)
    for j in range(0, rows, LANES):
        allowed = (lane + j >= begin) & (lane + j <= row)
        bias[:, j : j + LANES] = jnp.where(allowed, 0.0, -1e30)
    for h in range(q_ref.shape[1] // HEAD):
        for first, count in ((0, half), (half, rows)):
            scores[:, :count] = jnp.dot(
                q_ref[first : first + half, h * HEAD : (h + 1) * HEAD],
                keys[:, :count],
                preferred_element_type=jnp.float32,
            )
            out = h * rows + first

            def block(r, carry):
                at = block_rows(0, r)
                out_at = block_rows(out, r)
                top = jnp.full((ROWS, LANES), -1e30, jnp.float32)
                for j in range(0, count, LANES):
                    s = scores[at, j : j + LANES] + bias[block_rows(first, r), j : j + LANES]
                    scores[at, j : j + LANES] = s
                    top = jnp.maximum(top, s)
                top = lanes_max(top)
                tops_ref[out_at, :] = top
                sums_ref[out_at, :] = weigh(scores, probs, at, 0, count, top)
                return carry

            lax.fori_loop(0, half // ROWS, block, 0, unroll=True)
            acc_ref[out : out + half, :] = jnp.dot(
                probs[:, :count], values[:count, :], preferred_element_type=jnp.float32
            )
    for weight in weights:
        weight.wait()


def attend_kernel(
    lengths_hbm, q_ref, third_ref, third_other_ref, block_ref, block_other_ref, acc_in, tops_in, sums_in,
    ctx_ref, keys, values, stacked, scores, probs, acc, sums, lengths_ref, sem,
):
    load = pltpu.make_async_copy(lengths_hbm, lengths_ref, sem)
    load.start()
    rows = q_ref.shape[0]
    half = rows // 2
    heads = q_ref.shape[1] // HEAD
    behind = keys.shape[1]
    me = lax.axis_index("tp")
    place_blocks(
        [third_ref, third_other_ref, block_ref, block_other_ref],
        [me * half, (1 - me) * half, rows * (2 - me), rows * (1 + me)],
        keys,
        values,
    )
    load.wait()
    start = -lax.axis_index("dp") * rows
    begin, end = start, jnp.int32(rows)
    for d in range(lengths_ref.shape[0] - 1):
        start = start + lengths_ref[d]
        begin = jnp.where(start <= 0, start, begin)
        end = jnp.where(start > 0, jnp.minimum(end, start), end)
    low = begin + behind
    lane = lax.broadcasted_iota(jnp.int32, (ROWS, LANES), 1)
    line = lax.broadcasted_iota(jnp.int32, (ROWS, LANES), 0)

    def alone(at, q_at, h):
        total = jnp.sum(sums_in[at, :], axis=1, keepdims=True)
        ctx_ref[q_at, h * HEAD : (h + 1) * HEAD] = (acc_in[at, :] / total).astype(jnp.bfloat16)

    def tile(t, carry):
        reached = (t * TILE < end) & (low < behind)

        @pl.when(jnp.logical_not(reached))
        def _():
            for h in range(heads):
                for r in range(TILE // ROWS):
                    alone(block_rows(h * rows + t * TILE, r), block_rows(t * TILE, r), h)

        def merge(first):
            for h in range(heads):
                stacked[h * TILE : (h + 1) * TILE, :] = q_ref[
                    pl.ds(pl.multiple_of(t * TILE, TILE), TILE), h * HEAD : (h + 1) * HEAD
                ]
            scores[:, first:] = jnp.dot(stacked[...], keys[:, first:], preferred_element_type=jnp.float32)
            for h in range(heads):
                for r in range(TILE // ROWS):
                    at = slice(h * TILE + r * ROWS, h * TILE + (r + 1) * ROWS)
                    state = block_rows(h * rows + t * TILE, r)
                    own_top = tops_in[state, :]
                    top = own_top
                    for j in range(first, behind, LANES):
                        s = scores[at, j : j + LANES]
                        if j < first + SPAN:
                            s = jnp.where(lane + j >= low, s, -1e30)
                            scores[at, j : j + LANES] = s
                        top = jnp.maximum(top, s)
                    top = lanes_max(top)
                    rescale = jnp.exp2((own_top - top) * EXP2_SCALE)
                    acc[at, :] = acc_in[state, :] * rescale
                    sums[at, :] = sums_in[state, :] * rescale + weigh(scores, probs, at, first, behind - first, top)
            acc[...] += jnp.dot(probs[:, first:], values[first:, :], preferred_element_type=jnp.float32)
            for h in range(heads):
                for r in range(TILE // ROWS):
                    at = slice(h * TILE + r * ROWS, h * TILE + (r + 1) * ROWS)
                    state = block_rows(h * rows + t * TILE, r)
                    merged = line + (t * TILE + r * ROWS) < end
                    total = jnp.sum(jnp.where(merged, sums[at, :], sums_in[state, :]), axis=1, keepdims=True)
                    context = jnp.where(merged, acc[at, :], acc_in[state, :]) / total
                    ctx_ref[block_rows(t * TILE, r), h * HEAD : (h + 1) * HEAD] = context.astype(jnp.bfloat16)

        for first in range(0, behind, SPAN):
            inside = (low >= first) & (low < first + SPAN)
            pl.when(reached & inside)(functools.partial(merge, first))
        return carry

    lax.fori_loop(0, rows // TILE, tile, 0)


def attend_own(lengths, queries, blocks, w_out):
    rows, width = queries.shape
    half = rows // 2
    heads = width // HEAD
    return pl.pallas_call(
        attend_own_kernel,
        in_specs=[HBM] + [WHOLE] * 3 + [HBM],
        out_specs=[WHOLE] * 6,
        scratch_shapes=[
            pltpu.VMEM((HEAD, rows), jnp.bfloat16),
            pltpu.VMEM((rows, HEAD), jnp.bfloat16),
            pltpu.VMEM((rows, rows), jnp.float32),
            pltpu.VMEM((half, rows), jnp.float32),
            pltpu.VMEM((half, rows), jnp.bfloat16),
            pltpu.SMEM(lengths.shape, lengths.dtype),
            pltpu.SemaphoreType.DMA,
            pltpu.SemaphoreType.DMA((3, PIECES)),
        ],
        out_shape=[shaped((heads * rows, LANES), jnp.float32)] * 3
        + [shaped((w_out.shape[0], w_out.shape[1] // part), w_out.dtype) for part in (4, 4, 2)],
        compiler_params=params(16),
        cost_estimate=SMALL,
        name="attend_own",
    )(*in_hbm(lengths), queries, *blocks, *in_hbm(w_out))


def attend(lengths, queries, blocks, state):
    rows, width = queries.shape
    heads = width // HEAD
    tall = heads * TILE
    places = sum(block.shape[0] for block in blocks)
    return pl.pallas_call(
        attend_kernel,
        in_specs=[HBM] + [WHOLE] * (1 + len(blocks) + len(state)),
        out_specs=WHOLE,
        scratch_shapes=[
            pltpu.VMEM((HEAD, places), jnp.bfloat16),
            pltpu.VMEM((places, HEAD), jnp.bfloat16),
            pltpu.VMEM((tall, HEAD), jnp.bfloat16),
            pltpu.VMEM((tall, places), jnp.float32),
            pltpu.VMEM((tall, places), jnp.bfloat16),
            pltpu.VMEM((tall, HEAD), jnp.float32),
            pltpu.VMEM((tall, LANES), jnp.float32),
            pltpu.SMEM(lengths.shape, lengths.dtype),
            pltpu.SemaphoreType.DMA,
        ],
        out_shape=shaped((rows, width), jnp.bfloat16),
        compiler_params=params(20),
        cost_estimate=SMALL,
        name="attend",
    )(*in_hbm(lengths), queries, *blocks, *state)


def term_kernel(context_ref, w_ref, term_ref):
    step = 1024
    for c in range(w_ref.shape[1] // step):
        part = slice(c * step, (c + 1) * step)
        term_ref[:, part] = jnp.dot(context_ref[...], w_ref[:, part], preferred_element_type=jnp.float32).astype(jnp.bfloat16)


def group_term(context, w):
    rows, depth = context.shape
    width = w.shape[1]
    return pl.pallas_call(
        term_kernel,
        in_specs=[WHOLE] * 2,
        out_specs=WHOLE,
        out_shape=shaped((rows, width), jnp.bfloat16),
        compiler_params=params(16),
        cost_estimate=SMALL,
        name="own_term",
    )(context, w)


def output_kernel(tokens_ref, term_ref, context_ref, w_ref, w_later_ref, out_hbm, out, sems):
    width = out.shape[1]
    half = width // 2
    chunks = sems.shape[0]
    step = width // chunks
    stores = []
    for c in range(chunks):
        here = slice(c * step, (c + 1) * step)
        weights = w_ref[:, here] if c < chunks // 2 else w_later_ref[:, c * step - half : (c + 1) * step - half]
        other = jnp.dot(context_ref[...], weights, preferred_element_type=jnp.float32).astype(jnp.bfloat16)
        total = tokens_ref[:, here].astype(jnp.float32) + term_ref[:, here].astype(jnp.float32) + other.astype(jnp.float32)
        out[:, here] = total.astype(jnp.bfloat16)
        stores.append(pltpu.make_async_copy(out.at[:, here], out_hbm.at[:, here], sems.at[c]))
        stores[c].start()
    for store in stores:
        store.wait()


def output(tokens, term, context, w, w_later):
    rows, width = tokens.shape
    depth = context.shape[1]
    return pl.pallas_call(
        output_kernel,
        in_specs=[WHOLE] * 5,
        out_specs=HBM,
        out_shape=shaped((rows, width), jnp.bfloat16),
        scratch_shapes=[pltpu.VMEM((rows, width), jnp.bfloat16), pltpu.SemaphoreType.DMA((8,))],
        compiler_params=params(20),
        cost_estimate=cost(2 * rows * width * depth, rows * width * 4),
        name="output",
    )(tokens, term, context, w, w_later)


def swap(value):
    return lax.ppermute(value, "tp", SWAP)


def onward(value, distances):
    count, cores = lax.axis_size("dp"), len(distances)
    pairs = [
        (source * cores + core, (source + distance) * cores + core)
        for core, distance in enumerate(distances)
        for source in range(count - distance)
    ]
    return lax.ppermute(value, ("dp", "tp"), pairs)


def local(tokens, norm_gain, lengths, w_query, w_key, w_value, w_out):
    rows = tokens.shape[0]
    frequency = 500000.0 ** (-jnp.arange(HEAD // 2, dtype=jnp.float32) * 2.0 / HEAD)
    frequency = jnp.concatenate([frequency, frequency])[None, :]

    sums, gain, tokens = squares(frequency, norm_gain.reshape(-1, LANES), tokens)
    sums_other = swap(sums)
    *tables, wk, wv = rotary_tables(frequency, lengths, rows, w_key, w_value)
    sums_other, tables, wk, wv = lax.optimization_barrier((sums_other, tables, wk, wv))
    normed_other, inverse = normalize_other(tokens, sums, sums_other, gain)
    come_mine = swap(normed_other)
    normed_mine, kv_partial = normalize_own(tokens, gain, inverse, wk, wv)
    come_other = swap(normed_mine)
    come_mine, kv_partial = lax.optimization_barrier((come_mine, kv_partial))
    kv = finish_keys(come_mine, kv_partial, wk, wv, tables)
    assert (rows + MOST - 2) // rows == 3
    kv, normed_mine = lax.optimization_barrier((kv, normed_mine))
    third = onward(kv, (3, 3))
    kv_other = swap(kv)
    block = onward(join(kv, kv_other), (1, 2))
    partial = queries_own(normed_mine, normed_other, w_query)
    queries = finish_queries(come_mine, come_other, partial, w_query, tables)
    *state, w_send, w_later, w_mine = attend_own(lengths, queries, [kv, kv_other], w_out)
    third, block, state, w_send = lax.optimization_barrier((third, block, state, w_send))
    blocks = [third, swap(third), block, swap(block)]
    w_other = swap(w_send)
    blocks, w_later = lax.optimization_barrier((blocks, w_later))
    w_other_later = swap(w_later)
    context = attend(lengths, queries, blocks, state)
    context_other = swap(context)
    term = group_term(context, w_mine)
    return output(tokens, term, context_other, w_other, w_other_later)


def solution(mesh):
    placed = (P(("grp", "dp"), "tp"), P("tp"), P("grp"), P(None, "tp"), P(), P(), P("tp", None))
    return jax.shard_map(
        local, mesh=mesh, in_specs=placed, out_specs=P(("grp", "dp"), "tp"), check_vma=False
    )
```

```python
import functools
import math

import jax
import jax.numpy as jnp
from jax import lax
from jax.experimental import pallas as pl
from jax.experimental.pallas import tpu as pltpu
from jax.sharding import PartitionSpec as P

HEAD = 128
MOST = 1536
LANES = 128
SWAP = [(0, 1), (1, 0)]
MIB = 1024 * 1024
PIECES = 8
EXP2_SCALE = math.log2(math.e) / HEAD**0.5

WHOLE = pl.BlockSpec(memory_space=pltpu.VMEM)
HBM = pl.BlockSpec(memory_space=pltpu.HBM)


def in_hbm(*arrays):
    return [pltpu.with_memory_space_constraint(array, pltpu.HBM) for array in arrays]


def params(mib):
    return pltpu.CompilerParams(vmem_limit_bytes=mib * MIB)


def cost(flops, moved):
    return pl.CostEstimate(flops=flops, bytes_accessed=moved, transcendentals=0)


SMALL = cost(1, 1)
LARGE = cost(2 * 10**10, 1)


def load_rows(source, destination, sems, count):
    rows = destination.shape[0] // count
    loads = [
        pltpu.make_async_copy(source.at[i * rows : (i + 1) * rows], destination.at[i * rows : (i + 1) * rows], sems.at[i])
        for i in range(count)
    ]
    for load in loads:
        load.start()
    return loads


def shaped(shape, dtype):
    return jax.ShapeDtypeStruct(shape, dtype)


def first_of_document(lengths_ref, first_here, row):
    start = -first_here
    begin = jnp.full(jnp.shape(row), start, jnp.int32)
    for d in range(lengths_ref.shape[0] - 1):
        start = start + lengths_ref[d]
        begin = jnp.where(row >= start, start, begin)
    return begin


ROWS = 64
WIDE = 256


def block_rows(start, r):
    return pl.ds(pl.multiple_of(start + r * ROWS, ROWS), ROWS)


def wide_slice(ref, at, j):
    wide = ref[at, j : j + WIDE].astype(jnp.float32)
    return [wide[:, i : i + LANES] for i in range(0, WIDE, LANES)]


def squares_kernel(
    frequency_ref, gain_hbm, tokens_hbm, wk_hbm, wv_hbm, sums_ref, gain_ref, tokens_ref, wk_ref, wv_ref, narrow, sem, sems
):
    rows, width = tokens_ref.shape
    chunks = PIECES
    height = rows // chunks
    loads = load_rows(tokens_hbm, tokens_ref, sems.at[0], chunks)
    load = pltpu.make_async_copy(gain_hbm, narrow, sem)
    load.start()
    later = load_rows(wk_hbm, wk_ref, sems.at[1], PIECES) + load_rows(wv_hbm, wv_ref, sems.at[2], PIECES)
    for c in range(chunks):
        loads[c].wait()
        for r in range(height // ROWS):
            at = slice(c * height + r * ROWS, c * height + (r + 1) * ROWS)
            total = jnp.zeros((ROWS, LANES), jnp.float32)
            for j in range(0, width, WIDE):
                for wide in wide_slice(tokens_ref, at, j):
                    total = total + wide * wide
            sums_ref[at, :] = total
    load.wait()
    gain_ref[...] = narrow[...].astype(jnp.float32)
    for load in later:
        load.wait()


def squares(frequency, gain, tokens, wk, wv):
    rows, width = tokens.shape
    return pl.pallas_call(
        squares_kernel,
        in_specs=[WHOLE] + [HBM] * 4,
        out_specs=[WHOLE] * 5,
        out_shape=[
            shaped((rows, LANES), jnp.float32),
            shaped(gain.shape, jnp.float32),
            shaped(tokens.shape, tokens.dtype),
            shaped(wk.shape, wk.dtype),
            shaped(wv.shape, wv.dtype),
        ],
        scratch_shapes=[
            pltpu.VMEM(gain.shape, gain.dtype),
            pltpu.SemaphoreType.DMA,
            pltpu.SemaphoreType.DMA((3, PIECES)),
        ],
        compiler_params=params(16),
        cost_estimate=cost(rows * width * 2, rows * width * 2),
        name="squares",
    )(frequency, *in_hbm(gain, tokens, wk, wv))


def sine_and_cosine(x):
    turns = jnp.floor(x * (2.0 / math.pi) + 0.5)
    r = ((x - turns * 1.5703125) - turns * 4.837512969970703125e-4) - turns * 7.54978995489188e-8
    z = r * r
    s = ((-1.9515295891e-4 * z + 8.3321608736e-3) * z - 1.6666654611e-1) * z * r + r
    c = ((2.443315711809948e-5 * z - 1.388731625493765e-3) * z + 4.166664568298827e-2) * z * z - 0.5 * z + 1.0
    quadrant = turns.astype(jnp.int32)
    odd = (quadrant & 1) == 1
    sine = jnp.where(odd, c, s)
    cosine = jnp.where(odd, s, c)
    sine = jnp.where((quadrant & 2) == 2, -sine, sine)
    cosine = jnp.where(((quadrant + 1) & 2) == 2, -cosine, cosine)
    return sine, cosine


def tables_kernel(
    frequency_ref, lengths_hbm, wq_hbm, cos_ref, sin_ref, wq_ref, lengths_ref, sem, sems
):
    rows = cos_ref.shape[0]
    half = rows // 2
    load = pltpu.make_async_copy(lengths_hbm, lengths_ref, sem)
    load.start()
    loads = load_rows(wq_hbm.at[features(wq_ref.shape[0], False), :], wq_ref, sems, PIECES)
    lane = lax.broadcasted_iota(jnp.int32, (half, HEAD), 1)
    row = lax.broadcasted_iota(jnp.int32, (half, HEAD), 0) + jnp.where(lane < HEAD // 2, 0, half)
    low = lane < HEAD // 2
    load.wait()
    begin = first_of_document(lengths_ref, lax.axis_index("dp") * rows, row)
    sine, cosine = sine_and_cosine((row - begin).astype(jnp.float32) * frequency_ref[...])
    for table_ref, table, sign in ((cos_ref, cosine, 1.0), (sin_ref, sine, -1.0)):
        turned = pltpu.roll(table, HEAD // 2, 1)
        table_ref[:half, :] = jnp.where(low, sign * table, turned)
        table_ref[half:, :] = jnp.where(low, sign * turned, table)
    for load in loads:
        load.wait()


def rotary_tables(frequency, lengths, rows, wq):
    return pl.pallas_call(
        tables_kernel,
        in_specs=[WHOLE, HBM, HBM],
        out_specs=[WHOLE] * 3,
        out_shape=[shaped((rows, HEAD), jnp.float32)] * 2 + [shaped((wq.shape[0] // 2, wq.shape[1]), wq.dtype)],
        scratch_shapes=[
            pltpu.SMEM(lengths.shape, lengths.dtype),
            pltpu.SemaphoreType.DMA,
            pltpu.SemaphoreType.DMA((PIECES,)),
        ],
        compiler_params=params(16),
        cost_estimate=cost(rows * HEAD * 100, wq.size),
        name="tables",
    )(frequency, *in_hbm(lengths, wq))


def normalize(out_ref, tokens_ref, start, inverse_ref, gains_ref):
    count, width = out_ref.shape

    def block(r, carry):
        at = block_rows(start, r)
        inverse = inverse_ref[at, :]
        for j in range(0, width, WIDE):
            normed = []
            for i, wide in enumerate(wide_slice(tokens_ref, at, j)):
                gain_row = j // LANES + i
                normed.append(wide * inverse * gains_ref[gain_row : gain_row + 1, :])
            out_ref[block_rows(0, r), j : j + WIDE] = jnp.concatenate(normed, axis=1).astype(jnp.bfloat16)
        return carry

    lax.fori_loop(0, count // ROWS, block, 0)


def turn(x, cosine, sine):
    return (x * cosine + pltpu.roll(x, HEAD // 2, 1) * sine).astype(jnp.bfloat16)


def half_rows(rows, other):
    me = lax.axis_index("tp")
    half = rows // 2
    return pl.ds(pl.multiple_of((1 - me if other else me) * half, half), half)


def features(width, other):
    me = lax.axis_index("tp")
    return pl.ds(pl.multiple_of((1 - me if other else me) * width, width), width)


def both_weights(wk_ref, wv_ref, depth):
    return jnp.concatenate([wk_ref[depth, :], wv_ref[depth, :]], axis=1)


def normalize_other_kernel(tokens_ref, mine_ref, other_ref, gain_ref, normed_ref, inverse_ref):
    rows, width = tokens_ref.shape
    mean = jnp.sum(mine_ref[...] + other_ref[...], axis=1, keepdims=True) * (0.5 / width)
    inverse_ref[...] = jnp.broadcast_to(lax.rsqrt(mean + 1e-05), (rows, LANES))
    normalize(normed_ref, tokens_ref, half_rows(rows, True).start, inverse_ref, gain_ref)


def normalize_other(tokens, sums, sums_other, gain):
    rows, width = tokens.shape
    return pl.pallas_call(
        normalize_other_kernel,
        in_specs=[WHOLE] * 4,
        out_specs=[WHOLE] * 2,
        out_shape=[shaped((rows // 2, width), jnp.bfloat16), shaped((rows, LANES), jnp.float32)],
        compiler_params=params(12),
        cost_estimate=cost(rows * width * 2, rows * width * 2),
        name="normalize_other",
    )(tokens, sums, sums_other, gain)


def normalize_own_kernel(tokens_ref, gain_ref, inverse_ref, wk_ref, wv_ref, normed_ref, acc_ref):
    rows, width = tokens_ref.shape
    normalize(normed_ref, tokens_ref, half_rows(rows, False).start, inverse_ref, gain_ref)
    acc_ref[...] = jnp.dot(
        normed_ref[...], both_weights(wk_ref, wv_ref, features(width, False)), preferred_element_type=jnp.float32
    )


def normalize_own(tokens, gain, inverse, wk, wv):
    rows, width = tokens.shape
    return pl.pallas_call(
        normalize_own_kernel,
        in_specs=[WHOLE] * 5,
        out_specs=[WHOLE] * 2,
        out_shape=[shaped((rows // 2, width), jnp.bfloat16), shaped((rows // 2, 2 * HEAD), jnp.float32)],
        compiler_params=params(12),
        cost_estimate=cost(2 * rows * width * HEAD, wk.size * 4),
        name="normalize_own",
    )(tokens, gain, inverse, wk, wv)


def keys_kernel(normed_ref, acc_ref, wk_ref, wv_ref, cos_ref, sin_ref, kv_ref):
    half, width = normed_ref.shape
    here = half_rows(2 * half, False)
    total = acc_ref[...] + jnp.dot(
        normed_ref[...], both_weights(wk_ref, wv_ref, features(width, True)), preferred_element_type=jnp.float32
    )
    kv_ref[:, :HEAD] = turn(total[:, :HEAD], cos_ref[here, :], sin_ref[here, :])
    kv_ref[:, HEAD:] = total[:, HEAD:].astype(jnp.bfloat16)


def finish_keys(normed_come, acc, wk, wv, tables):
    return pl.pallas_call(
        keys_kernel,
        in_specs=[WHOLE] * 6,
        out_specs=WHOLE,
        out_shape=shaped(acc.shape, jnp.bfloat16),
        compiler_params=params(12),
        cost_estimate=cost(normed_come.size * 4 * HEAD, acc.size * 4),
        name="keys",
    )(normed_come, acc, wk, wv, *tables)


def join_kernel(mine_ref, other_ref, out_ref):
    rows = out_ref.shape[0]
    out_ref[half_rows(rows, False), :] = mine_ref[...]
    out_ref[half_rows(rows, True), :] = other_ref[...]


def join(mine, other):
    half, width = mine.shape
    return pl.pallas_call(
        join_kernel,
        in_specs=[WHOLE] * 2,
        out_specs=WHOLE,
        out_shape=shaped((2 * half, width), mine.dtype),
        compiler_params=params(8),
        cost_estimate=SMALL,
        name="join",
    )(mine, other)


def queries_own_kernel(mine_ref, other_ref, wq_ref, acc_ref):
    half = mine_ref.shape[0]
    weights = wq_ref[...]
    acc_ref[:half, :] = jnp.dot(mine_ref[...], weights, preferred_element_type=jnp.float32)
    acc_ref[half:, :] = jnp.dot(other_ref[...], weights, preferred_element_type=jnp.float32)


def queries_own(mine, other, wq):
    half, width = mine.shape
    nq = wq.shape[1]
    return pl.pallas_call(
        queries_own_kernel,
        in_specs=[WHOLE] * 3,
        out_specs=WHOLE,
        out_shape=shaped((2 * half, nq), jnp.float32),
        compiler_params=params(12),
        cost_estimate=cost(4 * half * width * nq, half * nq * 8),
        name="queries_own",
    )(mine, other, wq)


def queries_kernel(
    mine_ref, other_ref, acc_ref, wq_ref, cos_ref, sin_ref, q_ref, acc
):
    half, width = mine_ref.shape
    weights = wq_ref[features(width, True), :]
    acc[:half, :] = jnp.dot(mine_ref[...], weights, preferred_element_type=jnp.float32)
    acc[half:, :] = jnp.dot(other_ref[...], weights, preferred_element_type=jnp.float32)

    def finish(me):
        for part, which in ((slice(0, half), me), (slice(half, 2 * half), 1 - me)):
            at = slice(which * half, (which + 1) * half)
            for h in range(q_ref.shape[1] // HEAD):
                lanes = slice(h * HEAD, (h + 1) * HEAD)
                q_ref[at, lanes] = turn(acc_ref[part, lanes] + acc[part, lanes], cos_ref[at, :], sin_ref[at, :])

    for core in range(2):
        pl.when(lax.axis_index("tp") == core)(functools.partial(finish, core))


def finish_queries(mine, other, acc, wq, tables):
    half, width = mine.shape
    nq = wq.shape[1]
    return pl.pallas_call(
        queries_kernel,
        in_specs=[WHOLE] * 6,
        out_specs=WHOLE,
        out_shape=shaped((2 * half, nq), jnp.bfloat16),
        scratch_shapes=[pltpu.VMEM((2 * half, nq), jnp.float32)],
        compiler_params=params(12),
        cost_estimate=LARGE,
        name="queries",
    )(mine, other, acc, wq, *tables)


TILE = 128
SPAN = 512


def place_blocks(blocks, starts, keys, values):
    for block, start in zip(blocks, starts, strict=True):
        at = pl.ds(pl.multiple_of(start, block.shape[0]), block.shape[0])
        keys[:, at] = block[:, :HEAD].T
        values[at, :] = block[:, HEAD:]


def lanes_max(x):
    return jnp.broadcast_to(jnp.max(x, axis=1, keepdims=True), x.shape)


def weigh(scores, probs, at, first, count, top):
    scaled = top * EXP2_SCALE
    total = jnp.zeros((ROWS, LANES), jnp.float32)
    for j in range(0, count, WIDE):
        weights = []
        for i in range(j, j + WIDE, LANES):
            w = jnp.exp2(scores[at, first + i : first + i + LANES] * EXP2_SCALE - scaled)
            total = total + w
            weights.append(w)
        probs[at, first + j : first + j + WIDE] = jnp.concatenate(weights, axis=1).astype(jnp.bfloat16)
    return total


def attend_own_kernel(
    lengths_hbm, q_ref, mine_ref, other_ref, wout_hbm, acc_ref, tops_ref, sums_ref, wsend_ref, wlater_ref, wkeep_ref,
    keys, values, bias, scores, probs, lengths_ref, sem, sems,
):
    load = pltpu.make_async_copy(lengths_hbm, lengths_ref, sem)
    load.start()
    width = wkeep_ref.shape[1]
    send = features(width, True).start
    weights = load_rows(wout_hbm.at[:, pl.ds(send, width // 2)], wsend_ref, sems.at[0], PIECES)
    weights += load_rows(wout_hbm.at[:, pl.ds(send + width // 2, width // 2)], wlater_ref, sems.at[1], PIECES)
    weights += load_rows(wout_hbm.at[:, features(width, False)], wkeep_ref, sems.at[2], PIECES)
    rows = q_ref.shape[0]
    half = rows // 2
    me = lax.axis_index("tp")
    place_blocks([mine_ref, other_ref], [me * half, (1 - me) * half], keys, values)
    load.wait()
    row = lax.broadcasted_iota(jnp.int32, (rows, LANES), 0)
    lane = lax.broadcasted_iota(jnp.int32, (rows, LANES), 1)
    begin = first_of_document(lengths_ref, lax.axis_index("dp") * rows, row)
    for j in range(0, rows, LANES):
        allowed = (lane + j >= begin) & (lane + j <= row)
        bias[:, j : j + LANES] = jnp.where(allowed, 0.0, -1e30)
    for h in range(q_ref.shape[1] // HEAD):
        for first, count in ((0, half), (half, rows)):
            scores[:, :count] = jnp.dot(
                q_ref[first : first + half, h * HEAD : (h + 1) * HEAD],
                keys[:, :count],
                preferred_element_type=jnp.float32,
            )
            out = h * rows + first

            def block(r, carry):
                at = block_rows(0, r)
                out_at = block_rows(out, r)
                top = jnp.full((ROWS, LANES), -1e30, jnp.float32)
                for j in range(0, count, LANES):
                    s = scores[at, j : j + LANES] + bias[block_rows(first, r), j : j + LANES]
                    scores[at, j : j + LANES] = s
                    top = jnp.maximum(top, s)
                top = lanes_max(top)
                tops_ref[out_at, :] = top
                sums_ref[out_at, :] = weigh(scores, probs, at, 0, count, top)
                return carry

            lax.fori_loop(0, half // ROWS, block, 0, unroll=True)
            acc_ref[out : out + half, :] = jnp.dot(
                probs[:, :count], values[:count, :], preferred_element_type=jnp.float32
            )
    for weight in weights:
        weight.wait()


def attend_kernel(
    lengths_hbm, q_ref, third_ref, third_other_ref, block_ref, block_other_ref, acc_in, tops_in, sums_in,
    ctx_ref, keys, values, stacked, scores, probs, acc, sums, lengths_ref, sem,
):
    load = pltpu.make_async_copy(lengths_hbm, lengths_ref, sem)
    load.start()
    rows = q_ref.shape[0]
    half = rows // 2
    heads = q_ref.shape[1] // HEAD
    behind = keys.shape[1]
    me = lax.axis_index("tp")
    place_blocks(
        [third_ref, third_other_ref, block_ref, block_other_ref],
        [me * half, (1 - me) * half, rows * (2 - me), rows * (1 + me)],
        keys,
        values,
    )
    load.wait()
    start = -lax.axis_index("dp") * rows
    begin, end = start, jnp.int32(rows)
    for d in range(lengths_ref.shape[0] - 1):
        start = start + lengths_ref[d]
        begin = jnp.where(start <= 0, start, begin)
        end = jnp.where(start > 0, jnp.minimum(end, start), end)
    low = begin + behind
    lane = lax.broadcasted_iota(jnp.int32, (ROWS, LANES), 1)
    line = lax.broadcasted_iota(jnp.int32, (ROWS, LANES), 0)

    def alone(at, q_at, h):
        total = jnp.sum(sums_in[at, :], axis=1, keepdims=True)
        ctx_ref[q_at, h * HEAD : (h + 1) * HEAD] = (acc_in[at, :] / total).astype(jnp.bfloat16)

    def tile(t, carry):
        reached = (t * TILE < end) & (low < behind)

        @pl.when(jnp.logical_not(reached))
        def _():
            for h in range(heads):
                for r in range(TILE // ROWS):
                    alone(block_rows(h * rows + t * TILE, r), block_rows(t * TILE, r), h)

        def merge(first):
            for h in range(heads):
                stacked[h * TILE : (h + 1) * TILE, :] = q_ref[
                    pl.ds(pl.multiple_of(t * TILE, TILE), TILE), h * HEAD : (h + 1) * HEAD
                ]
            scores[:, first:] = jnp.dot(stacked[...], keys[:, first:], preferred_element_type=jnp.float32)
            for h in range(heads):
                for r in range(TILE // ROWS):
                    at = slice(h * TILE + r * ROWS, h * TILE + (r + 1) * ROWS)
                    state = block_rows(h * rows + t * TILE, r)
                    own_top = tops_in[state, :]
                    top = own_top
                    for j in range(first, behind, LANES):
                        s = scores[at, j : j + LANES]
                        if j < first + SPAN:
                            s = jnp.where(lane + j >= low, s, -1e30)
                            scores[at, j : j + LANES] = s
                        top = jnp.maximum(top, s)
                    top = lanes_max(top)
                    rescale = jnp.exp2((own_top - top) * EXP2_SCALE)
                    acc[at, :] = acc_in[state, :] * rescale
                    sums[at, :] = sums_in[state, :] * rescale + weigh(scores, probs, at, first, behind - first, top)
            acc[...] += jnp.dot(probs[:, first:], values[first:, :], preferred_element_type=jnp.float32)
            for h in range(heads):
                for r in range(TILE // ROWS):
                    at = slice(h * TILE + r * ROWS, h * TILE + (r + 1) * ROWS)
                    state = block_rows(h * rows + t * TILE, r)
                    merged = line + (t * TILE + r * ROWS) < end
                    total = jnp.sum(jnp.where(merged, sums[at, :], sums_in[state, :]), axis=1, keepdims=True)
                    context = jnp.where(merged, acc[at, :], acc_in[state, :]) / total
                    ctx_ref[block_rows(t * TILE, r), h * HEAD : (h + 1) * HEAD] = context.astype(jnp.bfloat16)

        for first in range(0, behind, SPAN):
            inside = (low >= first) & (low < first + SPAN)
            pl.when(reached & inside)(functools.partial(merge, first))
        return carry

    lax.fori_loop(0, rows // TILE, tile, 0)


def attend_own(lengths, queries, blocks, w_out):
    rows, width = queries.shape
    half = rows // 2
    heads = width // HEAD
    return pl.pallas_call(
        attend_own_kernel,
        in_specs=[HBM] + [WHOLE] * 3 + [HBM],
        out_specs=[WHOLE] * 6,
        scratch_shapes=[
            pltpu.VMEM((HEAD, rows), jnp.bfloat16),
            pltpu.VMEM((rows, HEAD), jnp.bfloat16),
            pltpu.VMEM((rows, rows), jnp.float32),
            pltpu.VMEM((half, rows), jnp.float32),
            pltpu.VMEM((half, rows), jnp.bfloat16),
            pltpu.SMEM(lengths.shape, lengths.dtype),
            pltpu.SemaphoreType.DMA,
            pltpu.SemaphoreType.DMA((3, PIECES)),
        ],
        out_shape=[shaped((heads * rows, LANES), jnp.float32)] * 3
        + [shaped((w_out.shape[0], w_out.shape[1] // part), w_out.dtype) for part in (4, 4, 2)],
        compiler_params=params(16),
        cost_estimate=SMALL,
        name="attend_own",
    )(*in_hbm(lengths), queries, *blocks, *in_hbm(w_out))


def attend(lengths, queries, blocks, state):
    rows, width = queries.shape
    heads = width // HEAD
    tall = heads * TILE
    places = sum(block.shape[0] for block in blocks)
    return pl.pallas_call(
        attend_kernel,
        in_specs=[HBM] + [WHOLE] * (1 + len(blocks) + len(state)),
        out_specs=WHOLE,
        scratch_shapes=[
            pltpu.VMEM((HEAD, places), jnp.bfloat16),
            pltpu.VMEM((places, HEAD), jnp.bfloat16),
            pltpu.VMEM((tall, HEAD), jnp.bfloat16),
            pltpu.VMEM((tall, places), jnp.float32),
            pltpu.VMEM((tall, places), jnp.bfloat16),
            pltpu.VMEM((tall, HEAD), jnp.float32),
            pltpu.VMEM((tall, LANES), jnp.float32),
            pltpu.SMEM(lengths.shape, lengths.dtype),
            pltpu.SemaphoreType.DMA,
        ],
        out_shape=shaped((rows, width), jnp.bfloat16),
        compiler_params=params(20),
        cost_estimate=SMALL,
        name="attend",
    )(*in_hbm(lengths), queries, *blocks, *state)


def term_kernel(context_ref, w_ref, term_ref):
    step = 1024
    for c in range(w_ref.shape[1] // step):
        part = slice(c * step, (c + 1) * step)
        term_ref[:, part] = jnp.dot(context_ref[...], w_ref[:, part], preferred_element_type=jnp.float32).astype(jnp.bfloat16)


def group_term(context, w):
    rows, depth = context.shape
    width = w.shape[1]
    return pl.pallas_call(
        term_kernel,
        in_specs=[WHOLE] * 2,
        out_specs=WHOLE,
        out_shape=shaped((rows, width), jnp.bfloat16),
        compiler_params=params(16),
        cost_estimate=SMALL,
        name="own_term",
    )(context, w)


def output_kernel(tokens_ref, term_ref, context_ref, w_ref, w_later_ref, out_hbm, out, sems):
    width = out.shape[1]
    half = width // 2
    chunks = sems.shape[0]
    step = width // chunks
    stores = []
    for c in range(chunks):
        here = slice(c * step, (c + 1) * step)
        weights = w_ref[:, here] if c < chunks // 2 else w_later_ref[:, c * step - half : (c + 1) * step - half]
        other = jnp.dot(context_ref[...], weights, preferred_element_type=jnp.float32).astype(jnp.bfloat16)
        total = tokens_ref[:, here].astype(jnp.float32) + term_ref[:, here].astype(jnp.float32) + other.astype(jnp.float32)
        out[:, here] = total.astype(jnp.bfloat16)
        stores.append(pltpu.make_async_copy(out.at[:, here], out_hbm.at[:, here], sems.at[c]))
        stores[c].start()
    for store in stores:
        store.wait()


def output(tokens, term, context, w, w_later):
    rows, width = tokens.shape
    depth = context.shape[1]
    return pl.pallas_call(
        output_kernel,
        in_specs=[WHOLE] * 5,
        out_specs=HBM,
        out_shape=shaped((rows, width), jnp.bfloat16),
        scratch_shapes=[pltpu.VMEM((rows, width), jnp.bfloat16), pltpu.SemaphoreType.DMA((8,))],
        compiler_params=params(20),
        cost_estimate=cost(2 * rows * width * depth, rows * width * 4),
        name="output",
    )(tokens, term, context, w, w_later)


def swap(value):
    return lax.ppermute(value, "tp", SWAP)


def onward(value, distances):
    count, cores = lax.axis_size("dp"), len(distances)
    pairs = [
        (source * cores + core, (source + distance) * cores + core)
        for core, distance in enumerate(distances)
        for source in range(count - distance)
    ]
    return lax.ppermute(value, ("dp", "tp"), pairs)


def local(tokens, norm_gain, lengths, w_query, w_key, w_value, w_out):
    rows = tokens.shape[0]
    frequency = 500000.0 ** (-jnp.arange(HEAD // 2, dtype=jnp.float32) * 2.0 / HEAD)
    frequency = jnp.concatenate([frequency, frequency])[None, :]

    sums, gain, tokens, wk, wv = squares(frequency, norm_gain.reshape(-1, LANES), tokens, w_key, w_value)
    sums_other = swap(sums)
    *tables, wq_own = rotary_tables(frequency, lengths, rows, w_query)
    sums_other, tables, wq_own = lax.optimization_barrier((sums_other, tables, wq_own))
    normed_other, inverse = normalize_other(tokens, sums, sums_other, gain)
    come_mine = swap(normed_other)
    normed_mine, kv_partial = normalize_own(tokens, gain, inverse, wk, wv)
    come_other = swap(normed_mine)
    partial = queries_own(normed_mine, normed_other, wq_own)
    come_mine, kv_partial, partial = lax.optimization_barrier((come_mine, kv_partial, partial))
    kv = finish_keys(come_mine, kv_partial, wk, wv, tables)
    assert (rows + MOST - 2) // rows == 3
    kv, partial = lax.optimization_barrier((kv, partial))
    third = onward(kv, (3, 3))
    kv_other = swap(kv)
    block = onward(join(kv, kv_other), (1, 2))
    queries = finish_queries(come_mine, come_other, partial, w_query, tables)
    *state, w_send, w_later, w_mine = attend_own(lengths, queries, [kv, kv_other], w_out)
    third, block, state, w_send = lax.optimization_barrier((third, block, state, w_send))
    blocks = [third, swap(third), block, swap(block)]
    w_other = swap(w_send)
    blocks, w_later = lax.optimization_barrier((blocks, w_later))
    w_other_later = swap(w_later)
    context = attend(lengths, queries, blocks, state)
    context_other = swap(context)
    term = group_term(context, w_mine)
    return output(tokens, term, context_other, w_other, w_other_later)


def solution(mesh):
    placed = (P(("grp", "dp"), "tp"), P("tp"), P("grp"), P(None, "tp"), P(), P(), P("tp", None))
    return jax.shard_map(
        local, mesh=mesh, in_specs=placed, out_specs=P(("grp", "dp"), "tp"), check_vma=False
    )
```

```python
import functools
import math

import jax
import jax.numpy as jnp
from jax import lax
from jax.experimental import pallas as pl
from jax.experimental.pallas import tpu as pltpu
from jax.sharding import PartitionSpec as P

HEAD = 128
MOST = 1536
LANES = 128
SWAP = [(0, 1), (1, 0)]
MIB = 1024 * 1024
PIECES = 8
EXP2_SCALE = math.log2(math.e) / HEAD**0.5

WHOLE = pl.BlockSpec(memory_space=pltpu.VMEM)
HBM = pl.BlockSpec(memory_space=pltpu.HBM)


def in_hbm(*arrays):
    return [pltpu.with_memory_space_constraint(array, pltpu.HBM) for array in arrays]


def params(mib):
    return pltpu.CompilerParams(vmem_limit_bytes=mib * MIB)


def cost(flops, moved):
    return pl.CostEstimate(flops=flops, bytes_accessed=moved, transcendentals=0)


SMALL = cost(1, 1)


def load_rows(source, destination, sems, count):
    rows = destination.shape[0] // count
    loads = [
        pltpu.make_async_copy(source.at[i * rows : (i + 1) * rows], destination.at[i * rows : (i + 1) * rows], sems.at[i])
        for i in range(count)
    ]
    for load in loads:
        load.start()
    return loads


def shaped(shape, dtype):
    return jax.ShapeDtypeStruct(shape, dtype)


def first_of_document(lengths_ref, first_here, row):
    start = -first_here
    begin = jnp.full(jnp.shape(row), start, jnp.int32)
    for d in range(lengths_ref.shape[0] - 1):
        start = start + lengths_ref[d]
        begin = jnp.where(row >= start, start, begin)
    return begin


ROWS = 64
WIDE = 256


def block_rows(start, r):
    return pl.ds(pl.multiple_of(start + r * ROWS, ROWS), ROWS)


def wide_slice(ref, at, j):
    wide = ref[at, j : j + WIDE].astype(jnp.float32)
    return [wide[:, i : i + LANES] for i in range(0, WIDE, LANES)]


def squares_kernel(frequency_ref, gain_hbm, tokens_hbm, sums_ref, gain_ref, tokens_ref, narrow, sems):
    rows, width = tokens_ref.shape
    chunks = sems.shape[0] - 1
    height = rows // chunks
    loads = [
        pltpu.make_async_copy(
            tokens_hbm.at[c * height : (c + 1) * height], tokens_ref.at[c * height : (c + 1) * height], sems.at[c]
        )
        for c in range(chunks)
    ]
    loads.append(pltpu.make_async_copy(gain_hbm, narrow, sems.at[chunks]))
    for load in loads:
        load.start()
    for c in range(chunks):
        loads[c].wait()
        for r in range(height // ROWS):
            at = slice(c * height + r * ROWS, c * height + (r + 1) * ROWS)
            total = jnp.zeros((ROWS, LANES), jnp.float32)
            for j in range(0, width, WIDE):
                for wide in wide_slice(tokens_ref, at, j):
                    total = total + wide * wide
            sums_ref[at, :] = total
    loads[chunks].wait()
    gain_ref[...] = narrow[...].astype(jnp.float32)


def squares(frequency, gain, tokens):
    rows, width = tokens.shape
    return pl.pallas_call(
        squares_kernel,
        in_specs=[WHOLE, HBM, HBM],
        out_specs=[WHOLE] * 3,
        out_shape=[
            shaped((rows, LANES), jnp.float32),
            shaped(gain.shape, jnp.float32),
            shaped(tokens.shape, tokens.dtype),
        ],
        scratch_shapes=[pltpu.VMEM(gain.shape, gain.dtype), pltpu.SemaphoreType.DMA((8 + 1,))],
        compiler_params=params(16),
        cost_estimate=cost(rows * width * 2, rows * width * 2),
        name="squares",
    )(frequency, *in_hbm(gain, tokens))


def sine_and_cosine(x):
    turns = jnp.floor(x * (2.0 / math.pi) + 0.5)
    r = ((x - turns * 1.5703125) - turns * 4.837512969970703125e-4) - turns * 7.54978995489188e-8
    z = r * r
    s = ((-1.9515295891e-4 * z + 8.3321608736e-3) * z - 1.6666654611e-1) * z * r + r
    c = ((2.443315711809948e-5 * z - 1.388731625493765e-3) * z + 4.166664568298827e-2) * z * z - 0.5 * z + 1.0
    quadrant = turns.astype(jnp.int32)
    odd = (quadrant & 1) == 1
    sine = jnp.where(odd, c, s)
    cosine = jnp.where(odd, s, c)
    sine = jnp.where((quadrant & 2) == 2, -sine, sine)
    cosine = jnp.where(((quadrant + 1) & 2) == 2, -cosine, cosine)
    return sine, cosine


def tables_kernel(frequency_ref, lengths_hbm, cos_ref, sin_ref, lengths_ref, sem):
    rows = cos_ref.shape[0]
    half = rows // 2
    load = pltpu.make_async_copy(lengths_hbm, lengths_ref, sem)
    load.start()
    lane = lax.broadcasted_iota(jnp.int32, (half, HEAD), 1)
    row = lax.broadcasted_iota(jnp.int32, (half, HEAD), 0) + jnp.where(lane < HEAD // 2, 0, half)
    low = lane < HEAD // 2
    load.wait()
    begin = first_of_document(lengths_ref, lax.axis_index("dp") * rows, row)
    sine, cosine = sine_and_cosine((row - begin).astype(jnp.float32) * frequency_ref[...])
    for table_ref, table, sign in ((cos_ref, cosine, 1.0), (sin_ref, sine, -1.0)):
        turned = pltpu.roll(table, HEAD // 2, 1)
        table_ref[:half, :] = jnp.where(low, sign * table, turned)
        table_ref[half:, :] = jnp.where(low, sign * turned, table)


def rotary_tables(frequency, lengths, rows):
    return pl.pallas_call(
        tables_kernel,
        in_specs=[WHOLE, HBM],
        out_specs=[WHOLE] * 2,
        out_shape=[shaped((rows, HEAD), jnp.float32)] * 2,
        scratch_shapes=[pltpu.SMEM(lengths.shape, lengths.dtype), pltpu.SemaphoreType.DMA],
        compiler_params=params(16),
        cost_estimate=cost(rows * HEAD * 100, rows * HEAD * 8),
        name="tables",
    )(frequency, *in_hbm(lengths))


def normalize(out_ref, tokens_ref, start, inverse_ref, gains_ref):
    count, width = out_ref.shape

    def block(r, carry):
        at = block_rows(start, r)
        inverse = inverse_ref[at, :]
        for j in range(0, width, WIDE):
            normed = []
            for i, wide in enumerate(wide_slice(tokens_ref, at, j)):
                gain_row = j // LANES + i
                normed.append(wide * inverse * gains_ref[gain_row : gain_row + 1, :])
            out_ref[block_rows(0, r), j : j + WIDE] = jnp.concatenate(normed, axis=1).astype(jnp.bfloat16)
        return carry

    lax.fori_loop(0, count // ROWS, block, 0)


def turn(x, cosine, sine):
    return (x * cosine + pltpu.roll(x, HEAD // 2, 1) * sine).astype(jnp.bfloat16)


def half_rows(rows, other):
    me = lax.axis_index("tp")
    half = rows // 2
    return pl.ds(pl.multiple_of((1 - me if other else me) * half, half), half)


def features(width, other):
    me = lax.axis_index("tp")
    return pl.ds(pl.multiple_of((1 - me if other else me) * width, width), width)


def both_weights(wk_ref, wv_ref, depth):
    return jnp.concatenate([wk_ref[depth, :], wv_ref[depth, :]], axis=1)


def normalize_other_kernel(tokens_ref, mine_ref, other_ref, gain_ref, normed_ref, inverse_ref):
    rows, width = tokens_ref.shape
    mean = jnp.sum(mine_ref[...] + other_ref[...], axis=1, keepdims=True) * (0.5 / width)
    inverse_ref[...] = jnp.broadcast_to(lax.rsqrt(mean + 1e-05), (rows, LANES))
    normalize(normed_ref, tokens_ref, half_rows(rows, True).start, inverse_ref, gain_ref)


def normalize_other(tokens, sums, sums_other, gain):
    rows, width = tokens.shape
    return pl.pallas_call(
        normalize_other_kernel,
        in_specs=[WHOLE] * 4,
        out_specs=[WHOLE] * 2,
        out_shape=[shaped((rows // 2, width), jnp.bfloat16), shaped((rows, LANES), jnp.float32)],
        compiler_params=params(12),
        cost_estimate=cost(rows * width * 2, rows * width * 2),
        name="normalize_other",
    )(tokens, sums, sums_other, gain)


def normalize_own_kernel(tokens_ref, gain_ref, inverse_ref, wk_hbm, wv_hbm, normed_ref, acc_ref, wk_ref, wv_ref, sems):
    rows, width = tokens_ref.shape
    loads = load_rows(wk_hbm, wk_ref, sems.at[0], PIECES) + load_rows(wv_hbm, wv_ref, sems.at[1], PIECES)
    normalize(normed_ref, tokens_ref, half_rows(rows, False).start, inverse_ref, gain_ref)
    for load in loads:
        load.wait()
    acc_ref[...] = jnp.dot(
        normed_ref[...], both_weights(wk_ref, wv_ref, features(width, False)), preferred_element_type=jnp.float32
    )


def normalize_own(tokens, gain, inverse, wk, wv):
    rows, width = tokens.shape
    return pl.pallas_call(
        normalize_own_kernel,
        in_specs=[WHOLE] * 3 + [HBM] * 2,
        out_specs=[WHOLE] * 4,
        out_shape=[
            shaped((rows // 2, width), jnp.bfloat16),
            shaped((rows // 2, 2 * HEAD), jnp.float32),
            shaped(wk.shape, wk.dtype),
            shaped(wv.shape, wv.dtype),
        ],
        scratch_shapes=[pltpu.SemaphoreType.DMA((2, PIECES))],
        compiler_params=params(12),
        cost_estimate=cost(2 * rows * width * HEAD, wk.size * 4),
        name="normalize_own",
    )(tokens, gain, inverse, *in_hbm(wk, wv))


def keys_kernel(normed_ref, acc_ref, wk_ref, wv_ref, cos_ref, sin_ref, kv_ref):
    half, width = normed_ref.shape
    here = half_rows(2 * half, False)
    total = acc_ref[...] + jnp.dot(
        normed_ref[...], both_weights(wk_ref, wv_ref, features(width, True)), preferred_element_type=jnp.float32
    )
    kv_ref[:, :HEAD] = turn(total[:, :HEAD], cos_ref[here, :], sin_ref[here, :])
    kv_ref[:, HEAD:] = total[:, HEAD:].astype(jnp.bfloat16)


def finish_keys(normed_come, acc, wk, wv, tables):
    return pl.pallas_call(
        keys_kernel,
        in_specs=[WHOLE] * 6,
        out_specs=WHOLE,
        out_shape=shaped(acc.shape, jnp.bfloat16),
        compiler_params=params(12),
        cost_estimate=cost(normed_come.size * 4 * HEAD, acc.size * 4),
        name="keys",
    )(normed_come, acc, wk, wv, *tables)


def join_kernel(mine_ref, other_ref, out_ref):
    rows = out_ref.shape[0]
    out_ref[half_rows(rows, False), :] = mine_ref[...]
    out_ref[half_rows(rows, True), :] = other_ref[...]


def join(mine, other):
    half, width = mine.shape
    return pl.pallas_call(
        join_kernel,
        in_specs=[WHOLE] * 2,
        out_specs=WHOLE,
        out_shape=shaped((2 * half, width), mine.dtype),
        compiler_params=params(8),
        cost_estimate=SMALL,
        name="join",
    )(mine, other)


def queries_own_kernel(mine_ref, other_ref, wq_ref, acc_ref):
    half, width = mine_ref.shape
    weights = wq_ref[features(width, False), :]
    acc_ref[:half, :] = jnp.dot(mine_ref[...], weights, preferred_element_type=jnp.float32)
    acc_ref[half:, :] = jnp.dot(other_ref[...], weights, preferred_element_type=jnp.float32)


def queries_own(mine, other, wq):
    half, width = mine.shape
    nq = wq.shape[1]
    return pl.pallas_call(
        queries_own_kernel,
        in_specs=[WHOLE] * 3,
        out_specs=WHOLE,
        out_shape=shaped((2 * half, nq), jnp.float32),
        compiler_params=params(12),
        cost_estimate=cost(4 * half * width * nq, half * nq * 8),
        name="queries_own",
    )(mine, other, wq)


def queries_kernel(
    mine_ref, other_ref, acc_ref, wq_ref, cos_ref, sin_ref, q_ref, acc
):
    half, width = mine_ref.shape
    weights = wq_ref[features(width, True), :]
    acc[:half, :] = jnp.dot(mine_ref[...], weights, preferred_element_type=jnp.float32)
    acc[half:, :] = jnp.dot(other_ref[...], weights, preferred_element_type=jnp.float32)

    def finish(me):
        for part, which in ((slice(0, half), me), (slice(half, 2 * half), 1 - me)):
            at = slice(which * half, (which + 1) * half)
            for h in range(q_ref.shape[1] // HEAD):
                lanes = slice(h * HEAD, (h + 1) * HEAD)
                q_ref[at, lanes] = turn(acc_ref[part, lanes] + acc[part, lanes], cos_ref[at, :], sin_ref[at, :])

    for core in range(2):
        pl.when(lax.axis_index("tp") == core)(functools.partial(finish, core))


def finish_queries(mine, other, acc, wq, tables):
    half, width = mine.shape
    nq = wq.shape[1]
    return pl.pallas_call(
        queries_kernel,
        in_specs=[WHOLE] * 6,
        out_specs=WHOLE,
        out_shape=shaped((2 * half, nq), jnp.bfloat16),
        scratch_shapes=[pltpu.VMEM((2 * half, nq), jnp.float32)],
        compiler_params=params(12),
        cost_estimate=cost(4 * half * width * nq, half * nq * 8),
        name="queries",
    )(mine, other, acc, wq, *tables)


TILE = 128
SPAN = 512


def place_blocks(blocks, starts, keys, values):
    for block, start in zip(blocks, starts, strict=True):
        at = pl.ds(pl.multiple_of(start, block.shape[0]), block.shape[0])
        keys[:, at] = block[:, :HEAD].T
        values[at, :] = block[:, HEAD:]


def lanes_max(x):
    return jnp.broadcast_to(jnp.max(x, axis=1, keepdims=True), x.shape)


def weigh(scores, probs, at, first, count, top):
    scaled = top * EXP2_SCALE
    total = jnp.zeros((ROWS, LANES), jnp.float32)
    for j in range(0, count, WIDE):
        weights = []
        for i in range(j, j + WIDE, LANES):
            w = jnp.exp2(scores[at, first + i : first + i + LANES] * EXP2_SCALE - scaled)
            total = total + w
            weights.append(w)
        probs[at, first + j : first + j + WIDE] = jnp.concatenate(weights, axis=1).astype(jnp.bfloat16)
    return total


def attend_own_kernel(
    lengths_hbm, q_ref, mine_ref, other_ref, wout_hbm, acc_ref, tops_ref, sums_ref, wsend_ref, wlater_ref, wkeep_ref,
    keys, values, bias, scores_even, scores_odd, probs_even, probs_odd, lengths_ref, sem, sems,
):
    load = pltpu.make_async_copy(lengths_hbm, lengths_ref, sem)
    load.start()
    width = wkeep_ref.shape[1]
    send = features(width, True).start
    weights = load_rows(wout_hbm.at[:, pl.ds(send, width // 2)], wsend_ref, sems.at[0], PIECES)
    weights += load_rows(wout_hbm.at[:, pl.ds(send + width // 2, width // 2)], wlater_ref, sems.at[1], PIECES)
    weights += load_rows(wout_hbm.at[:, features(width, False)], wkeep_ref, sems.at[2], PIECES)
    rows = q_ref.shape[0]
    half = rows // 2
    me = lax.axis_index("tp")
    place_blocks([mine_ref, other_ref], [me * half, (1 - me) * half], keys, values)
    load.wait()
    row = lax.broadcasted_iota(jnp.int32, (rows, LANES), 0)
    lane = lax.broadcasted_iota(jnp.int32, (rows, LANES), 1)
    begin = first_of_document(lengths_ref, lax.axis_index("dp") * rows, row)
    for j in range(0, rows, LANES):
        allowed = (lane + j >= begin) & (lane + j <= row)
        bias[:, j : j + LANES] = jnp.where(allowed, 0.0, -1e30)
    for h in range(q_ref.shape[1] // HEAD):
        for first, count, scores, probs in (
            (0, half, scores_even, probs_even),
            (half, rows, scores_odd, probs_odd),
        ):
            scores[:, :count] = jnp.dot(
                q_ref[first : first + half, h * HEAD : (h + 1) * HEAD],
                keys[:, :count],
                preferred_element_type=jnp.float32,
            )
            out = h * rows + first

            for r in range(0, half, ROWS):
                at = slice(r, r + ROWS)
                out_at = slice(out + r, out + r + ROWS)
                top = jnp.full((ROWS, LANES), -1e30, jnp.float32)
                for j in range(0, count, LANES):
                    s = scores[at, j : j + LANES] + bias[first + r : first + r + ROWS, j : j + LANES]
                    scores[at, j : j + LANES] = s
                    top = jnp.maximum(top, s)
                top = lanes_max(top)
                tops_ref[out_at, :] = top
                sums_ref[out_at, :] = weigh(scores, probs, at, 0, count, top)
            acc_ref[out : out + half, :] = jnp.dot(
                probs[:, :count], values[:count, :], preferred_element_type=jnp.float32
            )
    for weight in weights:
        weight.wait()


def attend_kernel(
    lengths_hbm, q_ref, third_ref, third_other_ref, block_ref, block_other_ref, acc_in, tops_in, sums_in,
    ctx_ref, keys, values, stacked, scores_even, scores_odd, probs_even, probs_odd, acc, sums, lengths_ref, sem,
):
    load = pltpu.make_async_copy(lengths_hbm, lengths_ref, sem)
    load.start()
    rows = q_ref.shape[0]
    half = rows // 2
    heads = q_ref.shape[1] // HEAD
    behind = keys.shape[1]
    me = lax.axis_index("tp")
    place_blocks(
        [third_ref, third_other_ref, block_ref, block_other_ref],
        [me * half, (1 - me) * half, rows * (2 - me), rows * (1 + me)],
        keys,
        values,
    )
    load.wait()
    start = -lax.axis_index("dp") * rows
    begin, end = start, jnp.int32(rows)
    for d in range(lengths_ref.shape[0] - 1):
        start = start + lengths_ref[d]
        begin = jnp.where(start <= 0, start, begin)
        end = jnp.where(start > 0, jnp.minimum(end, start), end)
    low = begin + behind
    lane = lax.broadcasted_iota(jnp.int32, (ROWS, LANES), 1)
    line = lax.broadcasted_iota(jnp.int32, (ROWS, LANES), 0)

    def alone(at, q_at, h):
        total = jnp.sum(sums_in[at, :], axis=1, keepdims=True)
        ctx_ref[q_at, h * HEAD : (h + 1) * HEAD] = (acc_in[at, :] / total).astype(jnp.bfloat16)

    def tile(t, carry):
        reached = (t * TILE < end) & (low < behind)

        @pl.when(jnp.logical_not(reached))
        def _():
            for h in range(heads):
                for r in range(TILE // ROWS):
                    alone(block_rows(h * rows + t * TILE, r), block_rows(t * TILE, r), h)

        def merge(first):
            for h in range(heads):
                stacked[h * TILE : (h + 1) * TILE, :] = q_ref[
                    pl.ds(pl.multiple_of(t * TILE, TILE), TILE), h * HEAD : (h + 1) * HEAD
                ]
            groups = ((0, scores_even, probs_even), (heads // 2, scores_odd, probs_odd))
            for group, scores, _ in groups:
                scores[:, first:] = jnp.dot(
                    stacked[group * TILE : (group + heads // 2) * TILE, :], keys[:, first:], preferred_element_type=jnp.float32
                )
            for group, scores, probs in groups:
                for h in range(group, group + heads // 2):
                    for r in range(0, TILE, ROWS):
                        at = slice((h - group) * TILE + r, (h - group) * TILE + r + ROWS)
                        out_at = slice(h * TILE + r, h * TILE + r + ROWS)
                        state = block_rows(h * rows + t * TILE, r // ROWS)
                        own_top = tops_in[state, :]
                        top = own_top
                        for j in range(first, behind, LANES):
                            s = scores[at, j : j + LANES]
                            if j < first + SPAN:
                                s = jnp.where(lane + j >= low, s, -1e30)
                                scores[at, j : j + LANES] = s
                            top = jnp.maximum(top, s)
                        top = lanes_max(top)
                        rescale = jnp.exp2((own_top - top) * EXP2_SCALE)
                        acc[out_at, :] = acc_in[state, :] * rescale
                        total = weigh(scores, probs, at, first, behind - first, top)
                        sums[out_at, :] = sums_in[state, :] * rescale + total
                out = slice(group * TILE, (group + heads // 2) * TILE)
                acc[out, :] += jnp.dot(probs[:, first:], values[first:, :], preferred_element_type=jnp.float32)
            for h in range(heads):
                for r in range(TILE // ROWS):
                    at = slice(h * TILE + r * ROWS, h * TILE + (r + 1) * ROWS)
                    state = block_rows(h * rows + t * TILE, r)
                    merged = line + (t * TILE + r * ROWS) < end
                    total = jnp.sum(jnp.where(merged, sums[at, :], sums_in[state, :]), axis=1, keepdims=True)
                    context = jnp.where(merged, acc[at, :], acc_in[state, :]) / total
                    ctx_ref[block_rows(t * TILE, r), h * HEAD : (h + 1) * HEAD] = context.astype(jnp.bfloat16)

        for first in range(0, behind, SPAN):
            inside = (low >= first) & (low < first + SPAN)
            pl.when(reached & inside)(functools.partial(merge, first))
        return carry

    lax.fori_loop(0, rows // TILE, tile, 0)


def attend_own(lengths, queries, blocks, w_out):
    rows, width = queries.shape
    half = rows // 2
    heads = width // HEAD
    return pl.pallas_call(
        attend_own_kernel,
        in_specs=[HBM] + [WHOLE] * 3 + [HBM],
        out_specs=[WHOLE] * 6,
        scratch_shapes=[
            pltpu.VMEM((HEAD, rows), jnp.bfloat16),
            pltpu.VMEM((rows, HEAD), jnp.bfloat16),
            pltpu.VMEM((rows, rows), jnp.float32),
            pltpu.VMEM((half, half), jnp.float32),
            pltpu.VMEM((half, rows), jnp.float32),
            pltpu.VMEM((half, half), jnp.bfloat16),
            pltpu.VMEM((half, rows), jnp.bfloat16),
            pltpu.SMEM(lengths.shape, lengths.dtype),
            pltpu.SemaphoreType.DMA,
            pltpu.SemaphoreType.DMA((3, PIECES)),
        ],
        out_shape=[shaped((heads * rows, LANES), jnp.float32)] * 3
        + [shaped((w_out.shape[0], w_out.shape[1] // part), w_out.dtype) for part in (4, 4, 2)],
        compiler_params=params(16),
        cost_estimate=SMALL,
        name="attend_own",
    )(*in_hbm(lengths), queries, *blocks, *in_hbm(w_out))


def attend(lengths, queries, blocks, state):
    rows, width = queries.shape
    heads = width // HEAD
    tall = heads * TILE
    places = sum(block.shape[0] for block in blocks)
    return pl.pallas_call(
        attend_kernel,
        in_specs=[HBM] + [WHOLE] * (1 + len(blocks) + len(state)),
        out_specs=WHOLE,
        scratch_shapes=[
            pltpu.VMEM((HEAD, places), jnp.bfloat16),
            pltpu.VMEM((places, HEAD), jnp.bfloat16),
            pltpu.VMEM((tall, HEAD), jnp.bfloat16),
            pltpu.VMEM((tall // 2, places), jnp.float32),
            pltpu.VMEM((tall // 2, places), jnp.float32),
            pltpu.VMEM((tall // 2, places), jnp.bfloat16),
            pltpu.VMEM((tall // 2, places), jnp.bfloat16),
            pltpu.VMEM((tall, HEAD), jnp.float32),
            pltpu.VMEM((tall, LANES), jnp.float32),
            pltpu.SMEM(lengths.shape, lengths.dtype),
            pltpu.SemaphoreType.DMA,
        ],
        out_shape=shaped((rows, width), jnp.bfloat16),
        compiler_params=params(20),
        cost_estimate=SMALL,
        name="attend",
    )(*in_hbm(lengths), queries, *blocks, *state)


def term_kernel(context_ref, w_ref, term_ref):
    step = 1024
    for c in range(w_ref.shape[1] // step):
        part = slice(c * step, (c + 1) * step)
        term_ref[:, part] = jnp.dot(context_ref[...], w_ref[:, part], preferred_element_type=jnp.float32).astype(jnp.bfloat16)


def group_term(context, w):
    rows, depth = context.shape
    width = w.shape[1]
    return pl.pallas_call(
        term_kernel,
        in_specs=[WHOLE] * 2,
        out_specs=WHOLE,
        out_shape=shaped((rows, width), jnp.bfloat16),
        compiler_params=params(16),
        cost_estimate=SMALL,
        name="own_term",
    )(context, w)


def output_kernel(tokens_ref, term_ref, context_ref, w_ref, w_later_ref, out_hbm, out, sems):
    width = out.shape[1]
    half = width // 2
    chunks = sems.shape[0]
    step = width // chunks
    stores = []
    for c in range(chunks):
        here = slice(c * step, (c + 1) * step)
        weights = w_ref[:, here] if c < chunks // 2 else w_later_ref[:, c * step - half : (c + 1) * step - half]
        other = jnp.dot(context_ref[...], weights, preferred_element_type=jnp.float32).astype(jnp.bfloat16)
        total = tokens_ref[:, here].astype(jnp.float32) + term_ref[:, here].astype(jnp.float32) + other.astype(jnp.float32)
        out[:, here] = total.astype(jnp.bfloat16)
        stores.append(pltpu.make_async_copy(out.at[:, here], out_hbm.at[:, here], sems.at[c]))
        stores[c].start()
    for store in stores:
        store.wait()


def output(tokens, term, context, w, w_later):
    rows, width = tokens.shape
    depth = context.shape[1]
    return pl.pallas_call(
        output_kernel,
        in_specs=[WHOLE] * 5,
        out_specs=HBM,
        out_shape=shaped((rows, width), jnp.bfloat16),
        scratch_shapes=[pltpu.VMEM((rows, width), jnp.bfloat16), pltpu.SemaphoreType.DMA((8,))],
        compiler_params=params(20),
        cost_estimate=cost(2 * rows * width * depth, rows * width * 4),
        name="output",
    )(tokens, term, context, w, w_later)


def swap(value):
    return lax.ppermute(value, "tp", SWAP)


def onward(value, distances):
    count, cores = lax.axis_size("dp"), len(distances)
    pairs = [
        (source * cores + core, (source + distance) * cores + core)
        for core, distance in enumerate(distances)
        for source in range(count - distance)
    ]
    return lax.ppermute(value, ("dp", "tp"), pairs)


def local(tokens, norm_gain, lengths, w_query, w_key, w_value, w_out):
    rows = tokens.shape[0]
    frequency = 500000.0 ** (-jnp.arange(HEAD // 2, dtype=jnp.float32) * 2.0 / HEAD)
    frequency = jnp.concatenate([frequency, frequency])[None, :]

    sums, gain, tokens = squares(frequency, norm_gain.reshape(-1, LANES), tokens)
    sums_other = swap(sums)
    tables = rotary_tables(frequency, lengths, rows)
    sums_other, tables = lax.optimization_barrier((sums_other, tables))
    normed_other, inverse = normalize_other(tokens, sums, sums_other, gain)
    come_mine = swap(normed_other)
    normed_mine, kv_partial, wk, wv = normalize_own(tokens, gain, inverse, w_key, w_value)
    come_other = swap(normed_mine)
    come_mine, kv_partial = lax.optimization_barrier((come_mine, kv_partial))
    kv = finish_keys(come_mine, kv_partial, wk, wv, tables)
    assert (rows + MOST - 2) // rows == 3
    kv, normed_mine = lax.optimization_barrier((kv, normed_mine))
    third = onward(kv, (3, 3))
    kv_other = swap(kv)
    block = onward(join(kv, kv_other), (1, 2))
    partial = queries_own(normed_mine, normed_other, w_query)
    queries = finish_queries(come_mine, come_other, partial, w_query, tables)
    *state, w_send, w_later, w_mine = attend_own(lengths, queries, [kv, kv_other], w_out)
    third, block, state, w_send = lax.optimization_barrier((third, block, state, w_send))
    blocks = [third, swap(third), block, swap(block)]
    w_other = swap(w_send)
    blocks, w_later = lax.optimization_barrier((blocks, w_later))
    w_other_later = swap(w_later)
    context = attend(lengths, queries, blocks, state)
    context_other = swap(context)
    term = group_term(context, w_mine)
    return output(tokens, term, context_other, w_other, w_other_later)


def solution(mesh):
    placed = (P(("grp", "dp"), "tp"), P("tp"), P("grp"), P(None, "tp"), P(), P(), P("tp", None))
    return jax.shard_map(
        local, mesh=mesh, in_specs=placed, out_specs=P(("grp", "dp"), "tp"), check_vma=False
    )
```

```python
import functools
import math

import jax
import jax.numpy as jnp
from jax import lax
from jax.experimental import pallas as pl
from jax.experimental.pallas import tpu as pltpu
from jax.sharding import PartitionSpec as P

HEAD = 128
MOST = 1536
LANES = 128
SWAP = [(0, 1), (1, 0)]
MIB = 1024 * 1024
PIECES = 8
EXP2_SCALE = math.log2(math.e) / HEAD**0.5

WHOLE = pl.BlockSpec(memory_space=pltpu.VMEM)
HBM = pl.BlockSpec(memory_space=pltpu.HBM)


def in_hbm(*arrays):
    return [pltpu.with_memory_space_constraint(array, pltpu.HBM) for array in arrays]


def params(mib):
    return pltpu.CompilerParams(vmem_limit_bytes=mib * MIB)


def cost(flops, moved):
    return pl.CostEstimate(flops=flops, bytes_accessed=moved, transcendentals=0)


SMALL = cost(1, 1)


def load_rows(source, destination, sems, count):
    rows = destination.shape[0] // count
    loads = [
        pltpu.make_async_copy(source.at[i * rows : (i + 1) * rows], destination.at[i * rows : (i + 1) * rows], sems.at[i])
        for i in range(count)
    ]
    for load in loads:
        load.start()
    return loads


def shaped(shape, dtype):
    return jax.ShapeDtypeStruct(shape, dtype)


def first_of_document(lengths_ref, first_here, row):
    start = -first_here
    begin = jnp.full(jnp.shape(row), start, jnp.int32)
    for d in range(lengths_ref.shape[0] - 1):
        start = start + lengths_ref[d]
        begin = jnp.where(row >= start, start, begin)
    return begin


ROWS = 64
WIDE = 256


def block_rows(start, r):
    return pl.ds(pl.multiple_of(start + r * ROWS, ROWS), ROWS)


def wide_slice(ref, at, j):
    wide = ref[at, j : j + WIDE].astype(jnp.float32)
    return [wide[:, i : i + LANES] for i in range(0, WIDE, LANES)]


def squares_kernel(frequency_ref, gain_hbm, tokens_hbm, sums_ref, gain_ref, tokens_ref, narrow, sems):
    rows, width = tokens_ref.shape
    chunks = sems.shape[0] - 1
    height = rows // chunks
    loads = [
        pltpu.make_async_copy(
            tokens_hbm.at[c * height : (c + 1) * height], tokens_ref.at[c * height : (c + 1) * height], sems.at[c]
        )
        for c in range(chunks)
    ]
    loads.append(pltpu.make_async_copy(gain_hbm, narrow, sems.at[chunks]))
    for load in loads:
        load.start()
    for c in range(chunks):
        loads[c].wait()
        for r in range(height // ROWS):
            at = slice(c * height + r * ROWS, c * height + (r + 1) * ROWS)
            total = jnp.zeros((ROWS, LANES), jnp.float32)
            for j in range(0, width, WIDE):
                for wide in wide_slice(tokens_ref, at, j):
                    total = total + wide * wide
            sums_ref[at, :] = total
    loads[chunks].wait()
    gain_ref[...] = narrow[...].astype(jnp.float32)


def squares(frequency, gain, tokens):
    rows, width = tokens.shape
    return pl.pallas_call(
        squares_kernel,
        in_specs=[WHOLE, HBM, HBM],
        out_specs=[WHOLE] * 3,
        out_shape=[
            shaped((rows, LANES), jnp.float32),
            shaped(gain.shape, jnp.float32),
            shaped(tokens.shape, tokens.dtype),
        ],
        scratch_shapes=[pltpu.VMEM(gain.shape, gain.dtype), pltpu.SemaphoreType.DMA((8 + 1,))],
        compiler_params=params(16),
        cost_estimate=cost(rows * width * 2, rows * width * 2),
        name="squares",
    )(frequency, *in_hbm(gain, tokens))


def sine_and_cosine(x):
    turns = jnp.floor(x * (2.0 / math.pi) + 0.5)
    r = ((x - turns * 1.5703125) - turns * 4.837512969970703125e-4) - turns * 7.54978995489188e-8
    z = r * r
    s = ((-1.9515295891e-4 * z + 8.3321608736e-3) * z - 1.6666654611e-1) * z * r + r
    c = ((2.443315711809948e-5 * z - 1.388731625493765e-3) * z + 4.166664568298827e-2) * z * z - 0.5 * z + 1.0
    quadrant = turns.astype(jnp.int32)
    odd = (quadrant & 1) == 1
    sine = jnp.where(odd, c, s)
    cosine = jnp.where(odd, s, c)
    sine = jnp.where((quadrant & 2) == 2, -sine, sine)
    cosine = jnp.where(((quadrant + 1) & 2) == 2, -cosine, cosine)
    return sine, cosine


def tables_kernel(frequency_ref, lengths_hbm, cos_ref, sin_ref, lengths_ref, sem):
    rows = cos_ref.shape[0]
    half = rows // 2
    load = pltpu.make_async_copy(lengths_hbm, lengths_ref, sem)
    load.start()
    lane = lax.broadcasted_iota(jnp.int32, (half, HEAD), 1)
    row = lax.broadcasted_iota(jnp.int32, (half, HEAD), 0) + jnp.where(lane < HEAD // 2, 0, half)
    low = lane < HEAD // 2
    load.wait()
    begin = first_of_document(lengths_ref, lax.axis_index("dp") * rows, row)
    sine, cosine = sine_and_cosine((row - begin).astype(jnp.float32) * frequency_ref[...])
    for table_ref, table, sign in ((cos_ref, cosine, 1.0), (sin_ref, sine, -1.0)):
        turned = pltpu.roll(table, HEAD // 2, 1)
        table_ref[:half, :] = jnp.where(low, sign * table, turned)
        table_ref[half:, :] = jnp.where(low, sign * turned, table)


def rotary_tables(frequency, lengths, rows):
    return pl.pallas_call(
        tables_kernel,
        in_specs=[WHOLE, HBM],
        out_specs=[WHOLE] * 2,
        out_shape=[shaped((rows, HEAD), jnp.float32)] * 2,
        scratch_shapes=[pltpu.SMEM(lengths.shape, lengths.dtype), pltpu.SemaphoreType.DMA],
        compiler_params=params(16),
        cost_estimate=cost(rows * HEAD * 100, rows * HEAD * 8),
        name="tables",
    )(frequency, *in_hbm(lengths))


def normalize(out_ref, tokens_ref, start, inverse_ref, gains_ref):
    count, width = out_ref.shape

    def block(r, carry):
        at = block_rows(start, r)
        inverse = inverse_ref[at, :]
        for j in range(0, width, WIDE):
            normed = []
            for i, wide in enumerate(wide_slice(tokens_ref, at, j)):
                gain_row = j // LANES + i
                normed.append(wide * inverse * gains_ref[gain_row : gain_row + 1, :])
            out_ref[block_rows(0, r), j : j + WIDE] = jnp.concatenate(normed, axis=1).astype(jnp.bfloat16)
        return carry

    lax.fori_loop(0, count // ROWS, block, 0)


def turn(x, cosine, sine):
    return (x * cosine + pltpu.roll(x, HEAD // 2, 1) * sine).astype(jnp.bfloat16)


def half_rows(rows, other):
    me = lax.axis_index("tp")
    half = rows // 2
    return pl.ds(pl.multiple_of((1 - me if other else me) * half, half), half)


def features(width, other):
    me = lax.axis_index("tp")
    return pl.ds(pl.multiple_of((1 - me if other else me) * width, width), width)


def both_weights(wk_ref, wv_ref, depth):
    return jnp.concatenate([wk_ref[depth, :], wv_ref[depth, :]], axis=1)


def normalize_other_kernel(tokens_ref, mine_ref, other_ref, gain_ref, normed_ref, inverse_ref):
    rows, width = tokens_ref.shape
    mean = jnp.sum(mine_ref[...] + other_ref[...], axis=1, keepdims=True) * (0.5 / width)
    inverse_ref[...] = jnp.broadcast_to(lax.rsqrt(mean + 1e-05), (rows, LANES))
    normalize(normed_ref, tokens_ref, half_rows(rows, True).start, inverse_ref, gain_ref)


def normalize_other(tokens, sums, sums_other, gain):
    rows, width = tokens.shape
    return pl.pallas_call(
        normalize_other_kernel,
        in_specs=[WHOLE] * 4,
        out_specs=[WHOLE] * 2,
        out_shape=[shaped((rows // 2, width), jnp.bfloat16), shaped((rows, LANES), jnp.float32)],
        compiler_params=params(12),
        cost_estimate=cost(rows * width * 2, rows * width * 2),
        name="normalize_other",
    )(tokens, sums, sums_other, gain)


def normalize_own_kernel(tokens_ref, gain_ref, inverse_ref, wk_hbm, wv_hbm, normed_ref, acc_ref, wk_ref, wv_ref, sems):
    rows, width = tokens_ref.shape
    loads = load_rows(wk_hbm, wk_ref, sems.at[0], PIECES) + load_rows(wv_hbm, wv_ref, sems.at[1], PIECES)
    normalize(normed_ref, tokens_ref, half_rows(rows, False).start, inverse_ref, gain_ref)
    for load in loads:
        load.wait()
    acc_ref[...] = jnp.dot(
        normed_ref[...], both_weights(wk_ref, wv_ref, features(width, False)), preferred_element_type=jnp.float32
    )


def normalize_own(tokens, gain, inverse, wk, wv):
    rows, width = tokens.shape
    return pl.pallas_call(
        normalize_own_kernel,
        in_specs=[WHOLE] * 3 + [HBM] * 2,
        out_specs=[WHOLE] * 4,
        out_shape=[
            shaped((rows // 2, width), jnp.bfloat16),
            shaped((rows // 2, 2 * HEAD), jnp.float32),
            shaped(wk.shape, wk.dtype),
            shaped(wv.shape, wv.dtype),
        ],
        scratch_shapes=[pltpu.SemaphoreType.DMA((2, PIECES))],
        compiler_params=params(12),
        cost_estimate=cost(2 * rows * width * HEAD, wk.size * 4),
        name="normalize_own",
    )(tokens, gain, inverse, *in_hbm(wk, wv))


def keys_kernel(normed_ref, acc_ref, wk_ref, wv_ref, cos_ref, sin_ref, kv_ref):
    half, width = normed_ref.shape
    here = half_rows(2 * half, False)
    total = acc_ref[...] + jnp.dot(
        normed_ref[...], both_weights(wk_ref, wv_ref, features(width, True)), preferred_element_type=jnp.float32
    )
    kv_ref[:, :HEAD] = turn(total[:, :HEAD], cos_ref[here, :], sin_ref[here, :])
    kv_ref[:, HEAD:] = total[:, HEAD:].astype(jnp.bfloat16)


def finish_keys(normed_come, acc, wk, wv, tables):
    return pl.pallas_call(
        keys_kernel,
        in_specs=[WHOLE] * 6,
        out_specs=WHOLE,
        out_shape=shaped(acc.shape, jnp.bfloat16),
        compiler_params=params(12),
        cost_estimate=cost(normed_come.size * 4 * HEAD, acc.size * 4),
        name="keys",
    )(normed_come, acc, wk, wv, *tables)


def join_kernel(mine_ref, other_ref, out_ref):
    rows = out_ref.shape[0]
    out_ref[half_rows(rows, False), :] = mine_ref[...]
    out_ref[half_rows(rows, True), :] = other_ref[...]


def join(mine, other):
    half, width = mine.shape
    return pl.pallas_call(
        join_kernel,
        in_specs=[WHOLE] * 2,
        out_specs=WHOLE,
        out_shape=shaped((2 * half, width), mine.dtype),
        compiler_params=params(8),
        cost_estimate=SMALL,
        name="join",
    )(mine, other)


def queries_own_kernel(mine_ref, other_ref, wq_ref, wout_ref, acc_ref, wsend_ref, wlater_ref):
    half, width = mine_ref.shape
    weights = wq_ref[features(width, False), :]
    acc_ref[:half, :] = jnp.dot(mine_ref[...], weights, preferred_element_type=jnp.float32)
    acc_ref[half:, :] = jnp.dot(other_ref[...], weights, preferred_element_type=jnp.float32)
    send = features(width, True).start
    wsend_ref[...] = wout_ref[:, pl.ds(send, width // 2)]
    wlater_ref[...] = wout_ref[:, pl.ds(send + width // 2, width // 2)]


def queries_own(mine, other, wq, w_out):
    half, width = mine.shape
    nq = wq.shape[1]
    part = shaped((w_out.shape[0], width // 2), w_out.dtype)
    return pl.pallas_call(
        queries_own_kernel,
        in_specs=[WHOLE] * 4,
        out_specs=[WHOLE] * 3,
        out_shape=[shaped((2 * half, nq), jnp.float32), part, part],
        compiler_params=params(12),
        cost_estimate=cost(10**10, 1),
        name="queries_own",
    )(mine, other, wq, w_out)


def queries_kernel(
    mine_ref, other_ref, acc_ref, wq_ref, cos_ref, sin_ref, q_ref, acc
):
    half, width = mine_ref.shape
    weights = wq_ref[features(width, True), :]
    acc[:half, :] = jnp.dot(mine_ref[...], weights, preferred_element_type=jnp.float32)
    acc[half:, :] = jnp.dot(other_ref[...], weights, preferred_element_type=jnp.float32)

    def finish(me):
        for part, which in ((slice(0, half), me), (slice(half, 2 * half), 1 - me)):
            at = slice(which * half, (which + 1) * half)
            for h in range(q_ref.shape[1] // HEAD):
                lanes = slice(h * HEAD, (h + 1) * HEAD)
                q_ref[at, lanes] = turn(acc_ref[part, lanes] + acc[part, lanes], cos_ref[at, :], sin_ref[at, :])

    for core in range(2):
        pl.when(lax.axis_index("tp") == core)(functools.partial(finish, core))


def finish_queries(mine, other, acc, wq, tables):
    half, width = mine.shape
    nq = wq.shape[1]
    return pl.pallas_call(
        queries_kernel,
        in_specs=[WHOLE] * 6,
        out_specs=WHOLE,
        out_shape=shaped((2 * half, nq), jnp.bfloat16),
        scratch_shapes=[pltpu.VMEM((2 * half, nq), jnp.float32)],
        compiler_params=params(12),
        cost_estimate=cost(4 * half * width * nq, half * nq * 8),
        name="queries",
    )(mine, other, acc, wq, *tables)


TILE = 128
SPAN = 512


def place_blocks(blocks, starts, keys, values):
    for block, start in zip(blocks, starts, strict=True):
        at = pl.ds(pl.multiple_of(start, block.shape[0]), block.shape[0])
        keys[:, at] = block[:, :HEAD].T
        values[at, :] = block[:, HEAD:]


def lanes_max(x):
    return jnp.broadcast_to(jnp.max(x, axis=1, keepdims=True), x.shape)


def weigh(scores, probs, at, first, count, top):
    scaled = top * EXP2_SCALE
    total = jnp.zeros((ROWS, LANES), jnp.float32)
    for j in range(0, count, WIDE):
        weights = []
        for i in range(j, j + WIDE, LANES):
            w = jnp.exp2(scores[at, first + i : first + i + LANES] * EXP2_SCALE - scaled)
            total = total + w
            weights.append(w)
        probs[at, first + j : first + j + WIDE] = jnp.concatenate(weights, axis=1).astype(jnp.bfloat16)
    return total


def attend_own_kernel(
    lengths_hbm, q_ref, mine_ref, other_ref, acc_ref, tops_ref, sums_ref,
    keys, values, bias, scores_even, scores_odd, probs_even, probs_odd, lengths_ref, sem,
):
    load = pltpu.make_async_copy(lengths_hbm, lengths_ref, sem)
    load.start()
    rows = q_ref.shape[0]
    half = rows // 2
    me = lax.axis_index("tp")
    place_blocks([mine_ref, other_ref], [me * half, (1 - me) * half], keys, values)
    load.wait()
    row = lax.broadcasted_iota(jnp.int32, (rows, LANES), 0)
    lane = lax.broadcasted_iota(jnp.int32, (rows, LANES), 1)
    begin = first_of_document(lengths_ref, lax.axis_index("dp") * rows, row)
    for j in range(0, rows, LANES):
        allowed = (lane + j >= begin) & (lane + j <= row)
        bias[:, j : j + LANES] = jnp.where(allowed, 0.0, -1e30)
    for h in range(q_ref.shape[1] // HEAD):
        for first, count, scores, probs in (
            (0, half, scores_even, probs_even),
            (half, rows, scores_odd, probs_odd),
        ):
            scores[:, :count] = jnp.dot(
                q_ref[first : first + half, h * HEAD : (h + 1) * HEAD],
                keys[:, :count],
                preferred_element_type=jnp.float32,
            )
            out = h * rows + first

            for r in range(0, half, ROWS):
                at = slice(r, r + ROWS)
                out_at = slice(out + r, out + r + ROWS)
                top = jnp.full((ROWS, LANES), -1e30, jnp.float32)
                for j in range(0, count, LANES):
                    s = scores[at, j : j + LANES] + bias[first + r : first + r + ROWS, j : j + LANES]
                    scores[at, j : j + LANES] = s
                    top = jnp.maximum(top, s)
                top = lanes_max(top)
                tops_ref[out_at, :] = top
                sums_ref[out_at, :] = weigh(scores, probs, at, 0, count, top)
            acc_ref[out : out + half, :] = jnp.dot(
                probs[:, :count], values[:count, :], preferred_element_type=jnp.float32
            )


def attend_kernel(
    lengths_hbm, q_ref, third_ref, third_other_ref, block_ref, block_other_ref, acc_in, tops_in, sums_in,
    ctx_ref, keys, values, stacked, scores_even, scores_odd, probs_even, probs_odd, acc, sums, lengths_ref, sem,
):
    load = pltpu.make_async_copy(lengths_hbm, lengths_ref, sem)
    load.start()
    rows = q_ref.shape[0]
    half = rows // 2
    heads = q_ref.shape[1] // HEAD
    behind = keys.shape[1]
    me = lax.axis_index("tp")
    load.wait()
    start = -lax.axis_index("dp") * rows
    begin, end = start, jnp.int32(rows)
    for d in range(lengths_ref.shape[0] - 1):
        start = start + lengths_ref[d]
        begin = jnp.where(start <= 0, start, begin)
        end = jnp.where(start > 0, jnp.minimum(end, start), end)
    low = begin + behind

    @pl.when(low < behind)
    def _():
        place_blocks(
            [third_ref, third_other_ref, block_ref, block_other_ref],
            [me * half, (1 - me) * half, rows * (2 - me), rows * (1 + me)],
            keys,
            values,
        )

    lane = lax.broadcasted_iota(jnp.int32, (ROWS, LANES), 1)
    line = lax.broadcasted_iota(jnp.int32, (ROWS, LANES), 0)

    def alone(at, q_at, h):
        total = jnp.sum(sums_in[at, :], axis=1, keepdims=True)
        ctx_ref[q_at, h * HEAD : (h + 1) * HEAD] = (acc_in[at, :] / total).astype(jnp.bfloat16)

    def tile(t, carry):
        reached = (t * TILE < end) & (low < behind)

        @pl.when(jnp.logical_not(reached))
        def _():
            for h in range(heads):
                for r in range(TILE // ROWS):
                    alone(block_rows(h * rows + t * TILE, r), block_rows(t * TILE, r), h)

        def merge(first):
            for h in range(heads):
                stacked[h * TILE : (h + 1) * TILE, :] = q_ref[
                    pl.ds(pl.multiple_of(t * TILE, TILE), TILE), h * HEAD : (h + 1) * HEAD
                ]
            groups = ((0, scores_even, probs_even), (heads // 2, scores_odd, probs_odd))
            for group, scores, _ in groups:
                scores[:, first:] = jnp.dot(
                    stacked[group * TILE : (group + heads // 2) * TILE, :], keys[:, first:], preferred_element_type=jnp.float32
                )
            for group, scores, probs in groups:
                for h in range(group, group + heads // 2):
                    for r in range(0, TILE, ROWS):
                        at = slice((h - group) * TILE + r, (h - group) * TILE + r + ROWS)
                        out_at = slice(h * TILE + r, h * TILE + r + ROWS)
                        state = block_rows(h * rows + t * TILE, r // ROWS)
                        own_top = tops_in[state, :]
                        top = own_top
                        for j in range(first, behind, LANES):
                            s = scores[at, j : j + LANES]
                            if j < first + SPAN:
                                s = jnp.where(lane + j >= low, s, -1e30)
                                scores[at, j : j + LANES] = s
                            top = jnp.maximum(top, s)
                        top = lanes_max(top)
                        rescale = jnp.exp2((own_top - top) * EXP2_SCALE)
                        acc[out_at, :] = acc_in[state, :] * rescale
                        total = weigh(scores, probs, at, first, behind - first, top)
                        sums[out_at, :] = sums_in[state, :] * rescale + total
                out = slice(group * TILE, (group + heads // 2) * TILE)
                acc[out, :] += jnp.dot(probs[:, first:], values[first:, :], preferred_element_type=jnp.float32)
            for h in range(heads):
                for r in range(TILE // ROWS):
                    at = slice(h * TILE + r * ROWS, h * TILE + (r + 1) * ROWS)
                    state = block_rows(h * rows + t * TILE, r)
                    merged = line + (t * TILE + r * ROWS) < end
                    total = jnp.sum(jnp.where(merged, sums[at, :], sums_in[state, :]), axis=1, keepdims=True)
                    context = jnp.where(merged, acc[at, :], acc_in[state, :]) / total
                    ctx_ref[block_rows(t * TILE, r), h * HEAD : (h + 1) * HEAD] = context.astype(jnp.bfloat16)

        for first in range(0, behind, SPAN):
            inside = (low >= first) & (low < first + SPAN)
            pl.when(reached & inside)(functools.partial(merge, first))
        return carry

    lax.fori_loop(0, rows // TILE, tile, 0)


def attend_own(lengths, queries, blocks):
    rows, width = queries.shape
    half = rows // 2
    heads = width // HEAD
    return pl.pallas_call(
        attend_own_kernel,
        in_specs=[HBM] + [WHOLE] * 3,
        out_specs=[WHOLE] * 3,
        scratch_shapes=[
            pltpu.VMEM((HEAD, rows), jnp.bfloat16),
            pltpu.VMEM((rows, HEAD), jnp.bfloat16),
            pltpu.VMEM((rows, rows), jnp.float32),
            pltpu.VMEM((half, half), jnp.float32),
            pltpu.VMEM((half, rows), jnp.float32),
            pltpu.VMEM((half, half), jnp.bfloat16),
            pltpu.VMEM((half, rows), jnp.bfloat16),
            pltpu.SMEM(lengths.shape, lengths.dtype),
            pltpu.SemaphoreType.DMA,
        ],
        out_shape=[shaped((heads * rows, LANES), jnp.float32)] * 3,
        compiler_params=params(16),
        cost_estimate=SMALL,
        name="attend_own",
    )(*in_hbm(lengths), queries, *blocks)


def attend(lengths, queries, blocks, state):
    rows, width = queries.shape
    heads = width // HEAD
    tall = heads * TILE
    places = sum(block.shape[0] for block in blocks)
    return pl.pallas_call(
        attend_kernel,
        in_specs=[HBM] + [WHOLE] * (1 + len(blocks) + len(state)),
        out_specs=WHOLE,
        scratch_shapes=[
            pltpu.VMEM((HEAD, places), jnp.bfloat16),
            pltpu.VMEM((places, HEAD), jnp.bfloat16),
            pltpu.VMEM((tall, HEAD), jnp.bfloat16),
            pltpu.VMEM((tall // 2, places), jnp.float32),
            pltpu.VMEM((tall // 2, places), jnp.float32),
            pltpu.VMEM((tall // 2, places), jnp.bfloat16),
            pltpu.VMEM((tall // 2, places), jnp.bfloat16),
            pltpu.VMEM((tall, HEAD), jnp.float32),
            pltpu.VMEM((tall, LANES), jnp.float32),
            pltpu.SMEM(lengths.shape, lengths.dtype),
            pltpu.SemaphoreType.DMA,
        ],
        out_shape=shaped((rows, width), jnp.bfloat16),
        compiler_params=params(20),
        cost_estimate=cost(12 * 10**9, 1),
        name="attend",
    )(*in_hbm(lengths), queries, *blocks, *state)


def term_kernel(context_ref, w_ref, term_ref):
    width = term_ref.shape[1]
    step = 1024
    for c in range(width // step):
        here = pl.ds(pl.multiple_of(lax.axis_index("tp") * width + c * step, step), step)
        term = jnp.dot(context_ref[...], w_ref[:, here], preferred_element_type=jnp.float32)
        term_ref[:, c * step : (c + 1) * step] = term.astype(jnp.bfloat16)


def group_term(context, w_out):
    rows, depth = context.shape
    width = w_out.shape[1] // 2
    return pl.pallas_call(
        term_kernel,
        in_specs=[WHOLE] * 2,
        out_specs=WHOLE,
        out_shape=shaped((rows, width), jnp.bfloat16),
        compiler_params=params(12),
        cost_estimate=SMALL,
        name="own_term",
    )(context, w_out)


def output_kernel(tokens_ref, term_ref, context_ref, w_ref, w_later_ref, out_hbm, out, sems):
    width = out.shape[1]
    half = width // 2
    chunks = sems.shape[0]
    step = width // chunks
    stores = []
    for c in range(chunks):
        here = slice(c * step, (c + 1) * step)
        weights = w_ref[:, here] if c < chunks // 2 else w_later_ref[:, c * step - half : (c + 1) * step - half]
        other = jnp.dot(context_ref[...], weights, preferred_element_type=jnp.float32).astype(jnp.bfloat16)
        total = tokens_ref[:, here].astype(jnp.float32) + term_ref[:, here].astype(jnp.float32) + other.astype(jnp.float32)
        out[:, here] = total.astype(jnp.bfloat16)
        stores.append(pltpu.make_async_copy(out.at[:, here], out_hbm.at[:, here], sems.at[c]))
        stores[c].start()
    for store in stores:
        store.wait()


def output(tokens, term, context, w, w_later):
    rows, width = tokens.shape
    depth = context.shape[1]
    return pl.pallas_call(
        output_kernel,
        in_specs=[WHOLE] * 5,
        out_specs=HBM,
        out_shape=shaped((rows, width), jnp.bfloat16),
        scratch_shapes=[pltpu.VMEM((rows, width), jnp.bfloat16), pltpu.SemaphoreType.DMA((8,))],
        compiler_params=params(20),
        cost_estimate=cost(2 * rows * width * depth, rows * width * 4),
        name="output",
    )(tokens, term, context, w, w_later)


def swap(value):
    return lax.ppermute(value, "tp", SWAP)


def onward(value, distances):
    count, cores = lax.axis_size("dp"), len(distances)
    pairs = [
        (source * cores + core, (source + distance) * cores + core)
        for core, distance in enumerate(distances)
        for source in range(count - distance)
    ]
    return lax.ppermute(value, ("dp", "tp"), pairs)


def local(tokens, norm_gain, lengths, w_query, w_key, w_value, w_out):
    rows = tokens.shape[0]
    frequency = 500000.0 ** (-jnp.arange(HEAD // 2, dtype=jnp.float32) * 2.0 / HEAD)
    frequency = jnp.concatenate([frequency, frequency])[None, :]

    sums, gain, tokens = squares(frequency, norm_gain.reshape(-1, LANES), tokens)
    sums_other = swap(sums)
    tables = rotary_tables(frequency, lengths, rows)
    sums_other, tables = lax.optimization_barrier((sums_other, tables))
    normed_other, inverse = normalize_other(tokens, sums, sums_other, gain)
    come_mine = swap(normed_other)
    normed_mine, kv_partial, wk, wv = normalize_own(tokens, gain, inverse, w_key, w_value)
    come_other = swap(normed_mine)
    come_mine, kv_partial = lax.optimization_barrier((come_mine, kv_partial))
    kv = finish_keys(come_mine, kv_partial, wk, wv, tables)
    assert (rows + MOST - 2) // rows == 3
    kv, normed_mine = lax.optimization_barrier((kv, normed_mine))
    third = onward(kv, (3, 3))
    kv_other = swap(kv)
    block = onward(join(kv, kv_other), (1, 2))
    partial, w_send, w_later = queries_own(normed_mine, normed_other, w_query, w_out)
    queries = finish_queries(come_mine, come_other, partial, w_query, tables)
    w_other, w_other_later = swap(w_send), swap(w_later)
    state = attend_own(lengths, queries, [kv, kv_other])
    third, block, state = lax.optimization_barrier((third, block, state))
    blocks = [third, swap(third), block, swap(block)]
    context = attend(lengths, queries, blocks, state)
    context_other = swap(context)
    term = group_term(context, w_out)
    return output(tokens, term, context_other, w_other, w_other_later)


def solution(mesh):
    placed = (P(("grp", "dp"), "tp"), P("tp"), P("grp"), P(None, "tp"), P(), P(), P("tp", None))
    return jax.shard_map(
        local, mesh=mesh, in_specs=placed, out_specs=P(("grp", "dp"), "tp"), check_vma=False
    )
```

```python
import functools
import math

import jax
import jax.numpy as jnp
from jax import lax
from jax.experimental import pallas as pl
from jax.experimental.pallas import tpu as pltpu
from jax.sharding import PartitionSpec as P

HEAD = 128
MOST = 1536
LANES = 128
SWAP = [(0, 1), (1, 0)]
MIB = 1024 * 1024
PIECES = 8
EXP2_SCALE = math.log2(math.e) / HEAD**0.5

WHOLE = pl.BlockSpec(memory_space=pltpu.VMEM)
HBM = pl.BlockSpec(memory_space=pltpu.HBM)


def in_hbm(*arrays):
    return [pltpu.with_memory_space_constraint(array, pltpu.HBM) for array in arrays]


def params(mib):
    return pltpu.CompilerParams(vmem_limit_bytes=mib * MIB)


def cost(flops, moved):
    return pl.CostEstimate(flops=flops, bytes_accessed=moved, transcendentals=0)


SMALL = cost(1, 1)


def load_rows(source, destination, sems, count):
    rows = destination.shape[0] // count
    loads = [
        pltpu.make_async_copy(source.at[i * rows : (i + 1) * rows], destination.at[i * rows : (i + 1) * rows], sems.at[i])
        for i in range(count)
    ]
    for load in loads:
        load.start()
    return loads


def shaped(shape, dtype):
    return jax.ShapeDtypeStruct(shape, dtype)


def first_of_document(lengths_ref, first_here, row):
    start = -first_here
    begin = jnp.full(jnp.shape(row), start, jnp.int32)
    for d in range(lengths_ref.shape[0] - 1):
        start = start + lengths_ref[d]
        begin = jnp.where(row >= start, start, begin)
    return begin


ROWS = 64
WIDE = 256


def block_rows(start, r):
    return pl.ds(pl.multiple_of(start + r * ROWS, ROWS), ROWS)


def wide_slice(ref, at, j):
    wide = ref[at, j : j + WIDE].astype(jnp.float32)
    return [wide[:, i : i + LANES] for i in range(0, WIDE, LANES)]


def squares_kernel(frequency_ref, gain_hbm, tokens_hbm, sums_ref, gain_ref, tokens_ref, narrow, sems):
    rows, width = tokens_ref.shape
    chunks = sems.shape[0] - 1
    height = rows // chunks
    loads = [
        pltpu.make_async_copy(
            tokens_hbm.at[c * height : (c + 1) * height], tokens_ref.at[c * height : (c + 1) * height], sems.at[c]
        )
        for c in range(chunks)
    ]
    loads.append(pltpu.make_async_copy(gain_hbm, narrow, sems.at[chunks]))
    for load in loads:
        load.start()
    for c in range(chunks):
        loads[c].wait()
        for r in range(height // ROWS):
            at = slice(c * height + r * ROWS, c * height + (r + 1) * ROWS)
            total = jnp.zeros((ROWS, LANES), jnp.float32)
            for j in range(0, width, WIDE):
                for wide in wide_slice(tokens_ref, at, j):
                    total = total + wide * wide
            sums_ref[at, :] = total
    loads[chunks].wait()
    gain_ref[...] = narrow[...].astype(jnp.float32)


def squares(frequency, gain, tokens):
    rows, width = tokens.shape
    return pl.pallas_call(
        squares_kernel,
        in_specs=[WHOLE, HBM, HBM],
        out_specs=[WHOLE] * 3,
        out_shape=[
            shaped((rows, LANES), jnp.float32),
            shaped(gain.shape, jnp.float32),
            shaped(tokens.shape, tokens.dtype),
        ],
        scratch_shapes=[pltpu.VMEM(gain.shape, gain.dtype), pltpu.SemaphoreType.DMA((8 + 1,))],
        compiler_params=params(16),
        cost_estimate=cost(rows * width * 2, rows * width * 2),
        name="squares",
    )(frequency, *in_hbm(gain, tokens))


def sine_and_cosine(x):
    turns = jnp.floor(x * (2.0 / math.pi) + 0.5)
    r = ((x - turns * 1.5703125) - turns * 4.837512969970703125e-4) - turns * 7.54978995489188e-8
    z = r * r
    s = ((-1.9515295891e-4 * z + 8.3321608736e-3) * z - 1.6666654611e-1) * z * r + r
    c = ((2.443315711809948e-5 * z - 1.388731625493765e-3) * z + 4.166664568298827e-2) * z * z - 0.5 * z + 1.0
    quadrant = turns.astype(jnp.int32)
    odd = (quadrant & 1) == 1
    sine = jnp.where(odd, c, s)
    cosine = jnp.where(odd, s, c)
    sine = jnp.where((quadrant & 2) == 2, -sine, sine)
    cosine = jnp.where(((quadrant + 1) & 2) == 2, -cosine, cosine)
    return sine, cosine


def tables_kernel(frequency_ref, lengths_hbm, cos_ref, sin_ref, lengths_ref, sem):
    rows = cos_ref.shape[0]
    half = rows // 2
    load = pltpu.make_async_copy(lengths_hbm, lengths_ref, sem)
    load.start()
    lane = lax.broadcasted_iota(jnp.int32, (half, HEAD), 1)
    row = lax.broadcasted_iota(jnp.int32, (half, HEAD), 0) + jnp.where(lane < HEAD // 2, 0, half)
    low = lane < HEAD // 2
    load.wait()
    begin = first_of_document(lengths_ref, lax.axis_index("dp") * rows, row)
    sine, cosine = sine_and_cosine((row - begin).astype(jnp.float32) * frequency_ref[...])
    for table_ref, table, sign in ((cos_ref, cosine, 1.0), (sin_ref, sine, -1.0)):
        turned = pltpu.roll(table, HEAD // 2, 1)
        table_ref[:half, :] = jnp.where(low, sign * table, turned)
        table_ref[half:, :] = jnp.where(low, sign * turned, table)


def rotary_tables(frequency, lengths, rows):
    return pl.pallas_call(
        tables_kernel,
        in_specs=[WHOLE, HBM],
        out_specs=[WHOLE] * 2,
        out_shape=[shaped((rows, HEAD), jnp.float32)] * 2,
        scratch_shapes=[pltpu.SMEM(lengths.shape, lengths.dtype), pltpu.SemaphoreType.DMA],
        compiler_params=params(16),
        cost_estimate=cost(rows * HEAD * 100, rows * HEAD * 8),
        name="tables",
    )(frequency, *in_hbm(lengths))


def normalize(out_ref, tokens_ref, start, inverse_ref, gains_ref):
    count, width = out_ref.shape

    def block(r, carry):
        at = block_rows(start, r)
        inverse = inverse_ref[at, :]
        for j in range(0, width, WIDE):
            normed = []
            for i, wide in enumerate(wide_slice(tokens_ref, at, j)):
                gain_row = j // LANES + i
                normed.append(wide * inverse * gains_ref[gain_row : gain_row + 1, :])
            out_ref[block_rows(0, r), j : j + WIDE] = jnp.concatenate(normed, axis=1).astype(jnp.bfloat16)
        return carry

    lax.fori_loop(0, count // ROWS, block, 0)


def turn(x, cosine, sine):
    return (x * cosine + pltpu.roll(x, HEAD // 2, 1) * sine).astype(jnp.bfloat16)


def half_rows(rows, other):
    me = lax.axis_index("tp")
    half = rows // 2
    return pl.ds(pl.multiple_of((1 - me if other else me) * half, half), half)


def features(width, other):
    me = lax.axis_index("tp")
    return pl.ds(pl.multiple_of((1 - me if other else me) * width, width), width)


def both_weights(wk_ref, wv_ref, depth):
    return jnp.concatenate([wk_ref[depth, :], wv_ref[depth, :]], axis=1)


def normalize_other_kernel(tokens_ref, mine_ref, other_ref, gain_ref, normed_ref, inverse_ref):
    rows, width = tokens_ref.shape
    mean = jnp.sum(mine_ref[...] + other_ref[...], axis=1, keepdims=True) * (0.5 / width)
    inverse_ref[...] = jnp.broadcast_to(lax.rsqrt(mean + 1e-05), (rows, LANES))
    normalize(normed_ref, tokens_ref, half_rows(rows, True).start, inverse_ref, gain_ref)


def normalize_other(tokens, sums, sums_other, gain):
    rows, width = tokens.shape
    return pl.pallas_call(
        normalize_other_kernel,
        in_specs=[WHOLE] * 4,
        out_specs=[WHOLE] * 2,
        out_shape=[shaped((rows // 2, width), jnp.bfloat16), shaped((rows, LANES), jnp.float32)],
        compiler_params=params(12),
        cost_estimate=cost(rows * width * 2, rows * width * 2),
        name="normalize_other",
    )(tokens, sums, sums_other, gain)


def normalize_own_kernel(tokens_ref, gain_ref, inverse_ref, wk_hbm, wv_hbm, normed_ref, acc_ref, wk_ref, wv_ref, sems):
    rows, width = tokens_ref.shape
    loads = load_rows(wk_hbm, wk_ref, sems.at[0], PIECES) + load_rows(wv_hbm, wv_ref, sems.at[1], PIECES)
    normalize(normed_ref, tokens_ref, half_rows(rows, False).start, inverse_ref, gain_ref)
    for load in loads:
        load.wait()
    acc_ref[...] = jnp.dot(
        normed_ref[...], both_weights(wk_ref, wv_ref, features(width, False)), preferred_element_type=jnp.float32
    )


def normalize_own(tokens, gain, inverse, wk, wv):
    rows, width = tokens.shape
    return pl.pallas_call(
        normalize_own_kernel,
        in_specs=[WHOLE] * 3 + [HBM] * 2,
        out_specs=[WHOLE] * 4,
        out_shape=[
            shaped((rows // 2, width), jnp.bfloat16),
            shaped((rows // 2, 2 * HEAD), jnp.float32),
            shaped(wk.shape, wk.dtype),
            shaped(wv.shape, wv.dtype),
        ],
        scratch_shapes=[pltpu.SemaphoreType.DMA((2, PIECES))],
        compiler_params=params(12),
        cost_estimate=cost(2 * rows * width * HEAD, wk.size * 4),
        name="normalize_own",
    )(tokens, gain, inverse, *in_hbm(wk, wv))


def keys_kernel(normed_ref, acc_ref, wk_ref, wv_ref, cos_ref, sin_ref, kv_ref):
    half, width = normed_ref.shape
    here = half_rows(2 * half, False)
    total = acc_ref[...] + jnp.dot(
        normed_ref[...], both_weights(wk_ref, wv_ref, features(width, True)), preferred_element_type=jnp.float32
    )
    kv_ref[:, :HEAD] = turn(total[:, :HEAD], cos_ref[here, :], sin_ref[here, :])
    kv_ref[:, HEAD:] = total[:, HEAD:].astype(jnp.bfloat16)


def finish_keys(normed_come, acc, wk, wv, tables):
    return pl.pallas_call(
        keys_kernel,
        in_specs=[WHOLE] * 6,
        out_specs=WHOLE,
        out_shape=shaped(acc.shape, jnp.bfloat16),
        compiler_params=params(12),
        cost_estimate=cost(normed_come.size * 4 * HEAD, acc.size * 4),
        name="keys",
    )(normed_come, acc, wk, wv, *tables)


def join_kernel(mine_ref, other_ref, out_ref):
    rows = out_ref.shape[0]
    out_ref[half_rows(rows, False), :] = mine_ref[...]
    out_ref[half_rows(rows, True), :] = other_ref[...]


def join(mine, other):
    half, width = mine.shape
    return pl.pallas_call(
        join_kernel,
        in_specs=[WHOLE] * 2,
        out_specs=WHOLE,
        out_shape=shaped((2 * half, width), mine.dtype),
        compiler_params=params(8),
        cost_estimate=SMALL,
        name="join",
    )(mine, other)


def queries_own_kernel(mine_ref, other_ref, wq_ref, wout_ref, acc_ref, wsend_ref, wlater_ref):
    half, width = mine_ref.shape
    weights = wq_ref[features(width, False), :]
    acc_ref[:half, :] = jnp.dot(mine_ref[...], weights, preferred_element_type=jnp.float32)
    acc_ref[half:, :] = jnp.dot(other_ref[...], weights, preferred_element_type=jnp.float32)
    send = features(width, True).start
    wsend_ref[...] = wout_ref[:, pl.ds(send, width // 2)]
    wlater_ref[...] = wout_ref[:, pl.ds(send + width // 2, width // 2)]


def queries_own(mine, other, wq, w_out):
    half, width = mine.shape
    nq = wq.shape[1]
    part = shaped((w_out.shape[0], width // 2), w_out.dtype)
    return pl.pallas_call(
        queries_own_kernel,
        in_specs=[WHOLE] * 4,
        out_specs=[WHOLE] * 3,
        out_shape=[shaped((2 * half, nq), jnp.float32), part, part],
        compiler_params=params(12),
        cost_estimate=cost(10**10, 1),
        name="queries_own",
    )(mine, other, wq, w_out)


def queries_kernel(
    mine_ref, other_ref, acc_ref, wq_ref, cos_ref, sin_ref, q_ref, acc
):
    half, width = mine_ref.shape
    weights = wq_ref[features(width, True), :]
    acc[:half, :] = jnp.dot(mine_ref[...], weights, preferred_element_type=jnp.float32)
    acc[half:, :] = jnp.dot(other_ref[...], weights, preferred_element_type=jnp.float32)

    def finish(me):
        for part, which in ((slice(0, half), me), (slice(half, 2 * half), 1 - me)):
            at = slice(which * half, (which + 1) * half)
            for h in range(q_ref.shape[1] // HEAD):
                lanes = slice(h * HEAD, (h + 1) * HEAD)
                q_ref[at, lanes] = turn(acc_ref[part, lanes] + acc[part, lanes], cos_ref[at, :], sin_ref[at, :])

    for core in range(2):
        pl.when(lax.axis_index("tp") == core)(functools.partial(finish, core))


def finish_queries(mine, other, acc, wq, tables):
    half, width = mine.shape
    nq = wq.shape[1]
    return pl.pallas_call(
        queries_kernel,
        in_specs=[WHOLE] * 6,
        out_specs=WHOLE,
        out_shape=shaped((2 * half, nq), jnp.bfloat16),
        scratch_shapes=[pltpu.VMEM((2 * half, nq), jnp.float32)],
        compiler_params=params(12),
        cost_estimate=cost(4 * half * width * nq, half * nq * 8),
        name="queries",
    )(mine, other, acc, wq, *tables)


TILE = 128
GROUPS = 2
SPAN = 256


def place_blocks(blocks, starts, keys, values):
    for block, start in zip(blocks, starts, strict=True):
        at = pl.ds(pl.multiple_of(start, block.shape[0]), block.shape[0])
        keys[:, at] = block[:, :HEAD].T
        values[at, :] = block[:, HEAD:]


def lanes_max(x):
    return jnp.broadcast_to(jnp.max(x, axis=1, keepdims=True), x.shape)


def weigh(scores, probs, at, first, count, top):
    scaled = top * EXP2_SCALE
    total = jnp.zeros((ROWS, LANES), jnp.float32)
    for j in range(0, count, WIDE):
        weights = []
        for i in range(j, j + WIDE, LANES):
            w = jnp.exp2(scores[at, first + i : first + i + LANES] * EXP2_SCALE - scaled)
            total = total + w
            weights.append(w)
        probs[at, first + j : first + j + WIDE] = jnp.concatenate(weights, axis=1).astype(jnp.bfloat16)
    return total


def attend_own_kernel(
    group, lengths_hbm, q_ref, mine_ref, other_ref, acc_ref, tops_ref, sums_ref,
    keys, values, bias, scores_even, scores_odd, probs_even, probs_odd, lengths_ref, sem,
):
    load = pltpu.make_async_copy(lengths_hbm, lengths_ref, sem)
    load.start()
    rows = q_ref.shape[0]
    half = rows // 2
    me = lax.axis_index("tp")
    place_blocks([mine_ref, other_ref], [me * half, (1 - me) * half], keys, values)
    load.wait()
    row = lax.broadcasted_iota(jnp.int32, (rows, LANES), 0)
    lane = lax.broadcasted_iota(jnp.int32, (rows, LANES), 1)
    begin = first_of_document(lengths_ref, lax.axis_index("dp") * rows, row)
    for j in range(0, rows, LANES):
        allowed = (lane + j >= begin) & (lane + j <= row)
        bias[:, j : j + LANES] = jnp.where(allowed, 0.0, -1e30)
    per = q_ref.shape[1] // HEAD // GROUPS
    for h in range(per):
        column = (group * per + h) * HEAD
        for first, count, scores, probs in (
            (0, half, scores_even, probs_even),
            (half, rows, scores_odd, probs_odd),
        ):
            scores[:, :count] = jnp.dot(
                q_ref[first : first + half, column : column + HEAD],
                keys[:, :count],
                preferred_element_type=jnp.float32,
            )
            out = h * rows + first

            for r in range(0, half, ROWS):
                at = slice(r, r + ROWS)
                out_at = slice(out + r, out + r + ROWS)
                top = jnp.full((ROWS, LANES), -1e30, jnp.float32)
                for j in range(0, count, LANES):
                    s = scores[at, j : j + LANES] + bias[first + r : first + r + ROWS, j : j + LANES]
                    scores[at, j : j + LANES] = s
                    top = jnp.maximum(top, s)
                top = lanes_max(top)
                tops_ref[out_at, :] = top
                sums_ref[out_at, :] = weigh(scores, probs, at, 0, count, top)
            acc_ref[out : out + half, :] = jnp.dot(
                probs[:, :count], values[:count, :], preferred_element_type=jnp.float32
            )


def attend_kernel(
    lengths_hbm, q_ref, third_ref, third_other_ref, block_ref, block_other_ref,
    acc_first, tops_first, sums_first, acc_second, tops_second, sums_second, ctx_ref, keys, values, stacked, scores_even, scores_odd, probs_even, probs_odd, acc, sums, lengths_ref, sem,
):
    load = pltpu.make_async_copy(lengths_hbm, lengths_ref, sem)
    load.start()
    rows = q_ref.shape[0]
    half = rows // 2
    heads = q_ref.shape[1] // HEAD
    behind = keys.shape[1]
    me = lax.axis_index("tp")
    load.wait()
    start = -lax.axis_index("dp") * rows
    begin, end = start, jnp.int32(rows)
    for d in range(lengths_ref.shape[0] - 1):
        start = start + lengths_ref[d]
        begin = jnp.where(start <= 0, start, begin)
        end = jnp.where(start > 0, jnp.minimum(end, start), end)
    low = begin + behind

    @pl.when(low < behind)
    def _():
        place_blocks(
            [third_ref, third_other_ref, block_ref, block_other_ref],
            [me * half, (1 - me) * half, rows * (2 - me), rows * (1 + me)],
            keys,
            values,
        )

    lane = lax.broadcasted_iota(jnp.int32, (ROWS, LANES), 1)
    line = lax.broadcasted_iota(jnp.int32, (ROWS, LANES), 0)

    per = heads // GROUPS
    states = ((acc_first, tops_first, sums_first), (acc_second, tops_second, sums_second))

    def own_state(h, t, r):
        return *states[h // per], block_rows(h % per * rows + t * TILE, r)

    def alone(t, r, h):
        acc_in, _, sums_in, at = own_state(h, t, r)
        total = jnp.sum(sums_in[at, :], axis=1, keepdims=True)
        ctx_ref[block_rows(t * TILE, r), h * HEAD : (h + 1) * HEAD] = (acc_in[at, :] / total).astype(jnp.bfloat16)

    def tile(t, carry):
        reached = (t * TILE < end) & (low < behind)

        @pl.when(jnp.logical_not(reached))
        def _():
            for h in range(heads):
                for r in range(TILE // ROWS):
                    alone(t, r, h)

        def merge(first):
            for h in range(heads):
                stacked[h * TILE : (h + 1) * TILE, :] = q_ref[
                    pl.ds(pl.multiple_of(t * TILE, TILE), TILE), h * HEAD : (h + 1) * HEAD
                ]
            groups = ((0, scores_even, probs_even), (heads // 2, scores_odd, probs_odd))
            for group, scores, _ in groups:
                scores[:, first:] = jnp.dot(
                    stacked[group * TILE : (group + heads // 2) * TILE, :], keys[:, first:], preferred_element_type=jnp.float32
                )
            for group, scores, probs in groups:
                for h in range(group, group + heads // 2):
                    for r in range(0, TILE, ROWS):
                        at = slice((h - group) * TILE + r, (h - group) * TILE + r + ROWS)
                        out_at = slice(h * TILE + r, h * TILE + r + ROWS)
                        acc_in, tops_in, sums_in, state = own_state(h, t, r // ROWS)
                        own_top = tops_in[state, :]
                        top = own_top
                        for j in range(first, behind, LANES):
                            s = scores[at, j : j + LANES]
                            if j < first + SPAN:
                                s = jnp.where(lane + j >= low, s, -1e30)
                                scores[at, j : j + LANES] = s
                            top = jnp.maximum(top, s)
                        top = lanes_max(top)
                        rescale = jnp.exp2((own_top - top) * EXP2_SCALE)
                        acc[out_at, :] = acc_in[state, :] * rescale
                        total = weigh(scores, probs, at, first, behind - first, top)
                        sums[out_at, :] = sums_in[state, :] * rescale + total
                out = slice(group * TILE, (group + heads // 2) * TILE)
                acc[out, :] += jnp.dot(probs[:, first:], values[first:, :], preferred_element_type=jnp.float32)
            for h in range(heads):
                for r in range(TILE // ROWS):
                    at = slice(h * TILE + r * ROWS, h * TILE + (r + 1) * ROWS)
                    acc_in, _, sums_in, state = own_state(h, t, r)
                    merged = line + (t * TILE + r * ROWS) < end
                    total = jnp.sum(jnp.where(merged, sums[at, :], sums_in[state, :]), axis=1, keepdims=True)
                    context = jnp.where(merged, acc[at, :], acc_in[state, :]) / total
                    ctx_ref[block_rows(t * TILE, r), h * HEAD : (h + 1) * HEAD] = context.astype(jnp.bfloat16)

        for first in range(0, behind, SPAN):
            inside = (low >= first) & (low < first + SPAN)
            pl.when(reached & inside)(functools.partial(merge, first))
        return carry

    lax.fori_loop(0, rows // TILE, tile, 0)


def attend_own(group, lengths, queries, blocks):
    rows, width = queries.shape
    half = rows // 2
    per = width // HEAD // GROUPS
    return pl.pallas_call(
        functools.partial(attend_own_kernel, group),
        in_specs=[HBM] + [WHOLE] * 3,
        out_specs=[WHOLE] * 3,
        scratch_shapes=[
            pltpu.VMEM((HEAD, rows), jnp.bfloat16),
            pltpu.VMEM((rows, HEAD), jnp.bfloat16),
            pltpu.VMEM((rows, rows), jnp.float32),
            pltpu.VMEM((half, half), jnp.float32),
            pltpu.VMEM((half, rows), jnp.float32),
            pltpu.VMEM((half, half), jnp.bfloat16),
            pltpu.VMEM((half, rows), jnp.bfloat16),
            pltpu.SMEM(lengths.shape, lengths.dtype),
            pltpu.SemaphoreType.DMA,
        ],
        out_shape=[shaped((per * rows, LANES), jnp.float32)] * 3,
        compiler_params=params(16),
        cost_estimate=SMALL,
        name="attend_own",
    )(*in_hbm(lengths), queries, *blocks)


def attend(lengths, queries, blocks, state):
    rows, width = queries.shape
    heads = width // HEAD
    tall = heads * TILE
    places = sum(block.shape[0] for block in blocks)
    return pl.pallas_call(
        attend_kernel,
        in_specs=[HBM] + [WHOLE] * (1 + len(blocks) + len(state)),
        out_specs=WHOLE,
        scratch_shapes=[
            pltpu.VMEM((HEAD, places), jnp.bfloat16),
            pltpu.VMEM((places, HEAD), jnp.bfloat16),
            pltpu.VMEM((tall, HEAD), jnp.bfloat16),
            pltpu.VMEM((tall // 2, places), jnp.float32),
            pltpu.VMEM((tall // 2, places), jnp.float32),
            pltpu.VMEM((tall // 2, places), jnp.bfloat16),
            pltpu.VMEM((tall // 2, places), jnp.bfloat16),
            pltpu.VMEM((tall, HEAD), jnp.float32),
            pltpu.VMEM((tall, LANES), jnp.float32),
            pltpu.SMEM(lengths.shape, lengths.dtype),
            pltpu.SemaphoreType.DMA,
        ],
        out_shape=shaped((rows, width), jnp.bfloat16),
        compiler_params=params(20),
        cost_estimate=cost(12 * 10**9, 1),
        name="attend",
    )(*in_hbm(lengths), queries, *blocks, *state)


def term_kernel(context_ref, w_ref, term_ref):
    width = term_ref.shape[1]
    step = 1024
    for c in range(width // step):
        here = pl.ds(pl.multiple_of(lax.axis_index("tp") * width + c * step, step), step)
        term = jnp.dot(context_ref[...], w_ref[:, here], preferred_element_type=jnp.float32)
        term_ref[:, c * step : (c + 1) * step] = term.astype(jnp.bfloat16)


def group_term(context, w_out):
    rows, depth = context.shape
    width = w_out.shape[1] // 2
    return pl.pallas_call(
        term_kernel,
        in_specs=[WHOLE] * 2,
        out_specs=WHOLE,
        out_shape=shaped((rows, width), jnp.bfloat16),
        compiler_params=params(12),
        cost_estimate=SMALL,
        name="own_term",
    )(context, w_out)


def output_kernel(tokens_ref, term_ref, context_ref, w_ref, w_later_ref, out_hbm, out, sems):
    width = out.shape[1]
    half = width // 2
    chunks = sems.shape[0]
    step = width // chunks
    stores = []
    for c in range(chunks):
        here = slice(c * step, (c + 1) * step)
        weights = w_ref[:, here] if c < chunks // 2 else w_later_ref[:, c * step - half : (c + 1) * step - half]
        other = jnp.dot(context_ref[...], weights, preferred_element_type=jnp.float32).astype(jnp.bfloat16)
        total = tokens_ref[:, here].astype(jnp.float32) + term_ref[:, here].astype(jnp.float32) + other.astype(jnp.float32)
        out[:, here] = total.astype(jnp.bfloat16)
        stores.append(pltpu.make_async_copy(out.at[:, here], out_hbm.at[:, here], sems.at[c]))
        stores[c].start()
    for store in stores:
        store.wait()


def output(tokens, term, context, w, w_later):
    rows, width = tokens.shape
    depth = context.shape[1]
    return pl.pallas_call(
        output_kernel,
        in_specs=[WHOLE] * 5,
        out_specs=HBM,
        out_shape=shaped((rows, width), jnp.bfloat16),
        scratch_shapes=[pltpu.VMEM((rows, width), jnp.bfloat16), pltpu.SemaphoreType.DMA((8,))],
        compiler_params=params(20),
        cost_estimate=cost(2 * rows * width * depth, rows * width * 4),
        name="output",
    )(tokens, term, context, w, w_later)


def swap(value):
    return lax.ppermute(value, "tp", SWAP)


def onward(value, distances):
    count, cores = lax.axis_size("dp"), len(distances)
    pairs = [
        (source * cores + core, (source + distance) * cores + core)
        for core, distance in enumerate(distances)
        for source in range(count - distance)
    ]
    return lax.ppermute(value, ("dp", "tp"), pairs)


def local(tokens, norm_gain, lengths, w_query, w_key, w_value, w_out):
    rows = tokens.shape[0]
    frequency = 500000.0 ** (-jnp.arange(HEAD // 2, dtype=jnp.float32) * 2.0 / HEAD)
    frequency = jnp.concatenate([frequency, frequency])[None, :]

    sums, gain, tokens = squares(frequency, norm_gain.reshape(-1, LANES), tokens)
    sums_other = swap(sums)
    tables = rotary_tables(frequency, lengths, rows)
    sums_other, tables = lax.optimization_barrier((sums_other, tables))
    normed_other, inverse = normalize_other(tokens, sums, sums_other, gain)
    come_mine = swap(normed_other)
    normed_mine, kv_partial, wk, wv = normalize_own(tokens, gain, inverse, w_key, w_value)
    come_other = swap(normed_mine)
    come_mine, kv_partial = lax.optimization_barrier((come_mine, kv_partial))
    kv = finish_keys(come_mine, kv_partial, wk, wv, tables)
    assert (rows + MOST - 2) // rows == 3
    kv, normed_mine = lax.optimization_barrier((kv, normed_mine))
    third = onward(kv, (3, 3))
    kv_other = swap(kv)
    block = onward(join(kv, kv_other), (1, 2))
    partial, w_send, w_later = queries_own(normed_mine, normed_other, w_query, w_out)
    queries = finish_queries(come_mine, come_other, partial, w_query, tables)
    w_other, w_other_later = swap(w_send), swap(w_later)
    state = attend_own(0, lengths, queries, [kv, kv_other])
    third, block, state = lax.optimization_barrier((third, block, state))
    blocks = [third, swap(third), block, swap(block)]
    state = [*state, *attend_own(1, lengths, queries, [kv, kv_other])]
    context = attend(lengths, queries, blocks, state)
    context_other = swap(context)
    term = group_term(context, w_out)
    return output(tokens, term, context_other, w_other, w_other_later)


def solution(mesh):
    placed = (P(("grp", "dp"), "tp"), P("tp"), P("grp"), P(None, "tp"), P(), P(), P("tp", None))
    return jax.shard_map(
        local, mesh=mesh, in_specs=placed, out_specs=P(("grp", "dp"), "tp"), check_vma=False
    )
```

```python
import functools
import math

import jax
import jax.numpy as jnp
from jax import lax
from jax.experimental import pallas as pl
from jax.experimental.pallas import tpu as pltpu
from jax.sharding import PartitionSpec as P

HEAD = 128
MOST = 1536
LANES = 128
SWAP = [(0, 1), (1, 0)]
MIB = 1024 * 1024
PIECES = 8
EXP2_SCALE = math.log2(math.e) / HEAD**0.5

WHOLE = pl.BlockSpec(memory_space=pltpu.VMEM)
HBM = pl.BlockSpec(memory_space=pltpu.HBM)


def in_hbm(*arrays):
    return [pltpu.with_memory_space_constraint(array, pltpu.HBM) for array in arrays]


def params(mib):
    return pltpu.CompilerParams(vmem_limit_bytes=mib * MIB)


def cost(flops, moved):
    return pl.CostEstimate(flops=flops, bytes_accessed=moved, transcendentals=0)


SMALL = cost(1, 1)


def load_rows(source, destination, sems, count):
    rows = destination.shape[0] // count
    loads = [
        pltpu.make_async_copy(source.at[i * rows : (i + 1) * rows], destination.at[i * rows : (i + 1) * rows], sems.at[i])
        for i in range(count)
    ]
    for load in loads:
        load.start()
    return loads


def shaped(shape, dtype):
    return jax.ShapeDtypeStruct(shape, dtype)


def first_of_document(lengths_ref, first_here, row):
    start = -first_here
    begin = jnp.full(jnp.shape(row), start, jnp.int32)
    for d in range(lengths_ref.shape[0] - 1):
        start = start + lengths_ref[d]
        begin = jnp.where(row >= start, start, begin)
    return begin


ROWS = 64
WIDE = 256


def block_rows(start, r):
    return pl.ds(pl.multiple_of(start + r * ROWS, ROWS), ROWS)


def wide_slice(ref, at, j):
    wide = ref[at, j : j + WIDE].astype(jnp.float32)
    return [wide[:, i : i + LANES] for i in range(0, WIDE, LANES)]


def squares_kernel(frequency_ref, gain_hbm, tokens_hbm, sums_ref, gain_ref, tokens_ref, narrow, sems):
    rows, width = tokens_ref.shape
    chunks = sems.shape[0] - 1
    height = rows // chunks
    loads = [
        pltpu.make_async_copy(
            tokens_hbm.at[c * height : (c + 1) * height], tokens_ref.at[c * height : (c + 1) * height], sems.at[c]
        )
        for c in range(chunks)
    ]
    loads.append(pltpu.make_async_copy(gain_hbm, narrow, sems.at[chunks]))
    for load in loads:
        load.start()
    for c in range(chunks):
        loads[c].wait()
        for r in range(height // ROWS):
            at = slice(c * height + r * ROWS, c * height + (r + 1) * ROWS)
            total = jnp.zeros((ROWS, LANES), jnp.float32)
            for j in range(0, width, WIDE):
                for wide in wide_slice(tokens_ref, at, j):
                    total = total + wide * wide
            sums_ref[at, :] = total
    loads[chunks].wait()
    gain_ref[...] = narrow[...].astype(jnp.float32)


def squares(frequency, gain, tokens):
    rows, width = tokens.shape
    return pl.pallas_call(
        squares_kernel,
        in_specs=[WHOLE, HBM, HBM],
        out_specs=[WHOLE] * 3,
        out_shape=[
            shaped((rows, LANES), jnp.float32),
            shaped(gain.shape, jnp.float32),
            shaped(tokens.shape, tokens.dtype),
        ],
        scratch_shapes=[pltpu.VMEM(gain.shape, gain.dtype), pltpu.SemaphoreType.DMA((8 + 1,))],
        compiler_params=params(16),
        cost_estimate=cost(rows * width * 2, rows * width * 2),
        name="squares",
    )(frequency, *in_hbm(gain, tokens))


def sine_and_cosine(x):
    turns = jnp.floor(x * (2.0 / math.pi) + 0.5)
    r = ((x - turns * 1.5703125) - turns * 4.837512969970703125e-4) - turns * 7.54978995489188e-8
    z = r * r
    s = ((-1.9515295891e-4 * z + 8.3321608736e-3) * z - 1.6666654611e-1) * z * r + r
    c = ((2.443315711809948e-5 * z - 1.388731625493765e-3) * z + 4.166664568298827e-2) * z * z - 0.5 * z + 1.0
    quadrant = turns.astype(jnp.int32)
    odd = (quadrant & 1) == 1
    sine = jnp.where(odd, c, s)
    cosine = jnp.where(odd, s, c)
    sine = jnp.where((quadrant & 2) == 2, -sine, sine)
    cosine = jnp.where(((quadrant + 1) & 2) == 2, -cosine, cosine)
    return sine, cosine


def tables_kernel(frequency_ref, lengths_hbm, cos_ref, sin_ref, lengths_ref, sem):
    rows = cos_ref.shape[0]
    half = rows // 2
    load = pltpu.make_async_copy(lengths_hbm, lengths_ref, sem)
    load.start()
    lane = lax.broadcasted_iota(jnp.int32, (half, HEAD), 1)
    row = lax.broadcasted_iota(jnp.int32, (half, HEAD), 0) + jnp.where(lane < HEAD // 2, 0, half)
    low = lane < HEAD // 2
    load.wait()
    begin = first_of_document(lengths_ref, lax.axis_index("dp") * rows, row)
    sine, cosine = sine_and_cosine((row - begin).astype(jnp.float32) * frequency_ref[...])
    for table_ref, table, sign in ((cos_ref, cosine, 1.0), (sin_ref, sine, -1.0)):
        turned = pltpu.roll(table, HEAD // 2, 1)
        table_ref[:half, :] = jnp.where(low, sign * table, turned)
        table_ref[half:, :] = jnp.where(low, sign * turned, table)


def rotary_tables(frequency, lengths, rows):
    return pl.pallas_call(
        tables_kernel,
        in_specs=[WHOLE, HBM],
        out_specs=[WHOLE] * 2,
        out_shape=[shaped((rows, HEAD), jnp.float32)] * 2,
        scratch_shapes=[pltpu.SMEM(lengths.shape, lengths.dtype), pltpu.SemaphoreType.DMA],
        compiler_params=params(16),
        cost_estimate=cost(rows * HEAD * 100, rows * HEAD * 8),
        name="tables",
    )(frequency, *in_hbm(lengths))


def normalize(out_ref, tokens_ref, start, inverse_ref, gains_ref):
    count, width = out_ref.shape

    def block(r, carry):
        at = block_rows(start, r)
        inverse = inverse_ref[at, :]
        for j in range(0, width, WIDE):
            normed = []
            for i, wide in enumerate(wide_slice(tokens_ref, at, j)):
                gain_row = j // LANES + i
                normed.append(wide * inverse * gains_ref[gain_row : gain_row + 1, :])
            out_ref[block_rows(0, r), j : j + WIDE] = jnp.concatenate(normed, axis=1).astype(jnp.bfloat16)
        return carry

    lax.fori_loop(0, count // ROWS, block, 0)


def turn(x, cosine, sine):
    return (x * cosine + pltpu.roll(x, HEAD // 2, 1) * sine).astype(jnp.bfloat16)


def half_rows(rows, other):
    me = lax.axis_index("tp")
    half = rows // 2
    return pl.ds(pl.multiple_of((1 - me if other else me) * half, half), half)


def features(width, other):
    me = lax.axis_index("tp")
    return pl.ds(pl.multiple_of((1 - me if other else me) * width, width), width)


def both_weights(wk_ref, wv_ref, depth):
    return jnp.concatenate([wk_ref[depth, :], wv_ref[depth, :]], axis=1)


def normalize_other_kernel(tokens_ref, mine_ref, other_ref, gain_ref, normed_ref, inverse_ref):
    rows, width = tokens_ref.shape
    mean = jnp.sum(mine_ref[...] + other_ref[...], axis=1, keepdims=True) * (0.5 / width)
    inverse_ref[...] = jnp.broadcast_to(lax.rsqrt(mean + 1e-05), (rows, LANES))
    normalize(normed_ref, tokens_ref, half_rows(rows, True).start, inverse_ref, gain_ref)


def normalize_other(tokens, sums, sums_other, gain):
    rows, width = tokens.shape
    return pl.pallas_call(
        normalize_other_kernel,
        in_specs=[WHOLE] * 4,
        out_specs=[WHOLE] * 2,
        out_shape=[shaped((rows // 2, width), jnp.bfloat16), shaped((rows, LANES), jnp.float32)],
        compiler_params=params(12),
        cost_estimate=cost(rows * width * 2, rows * width * 2),
        name="normalize_other",
    )(tokens, sums, sums_other, gain)


def normalize_own_kernel(tokens_ref, gain_ref, inverse_ref, wk_hbm, wv_hbm, normed_ref, acc_ref, wk_ref, wv_ref, sems):
    rows, width = tokens_ref.shape
    loads = load_rows(wk_hbm, wk_ref, sems.at[0], PIECES) + load_rows(wv_hbm, wv_ref, sems.at[1], PIECES)
    normalize(normed_ref, tokens_ref, half_rows(rows, False).start, inverse_ref, gain_ref)
    for load in loads:
        load.wait()
    acc_ref[...] = jnp.dot(
        normed_ref[...], both_weights(wk_ref, wv_ref, features(width, False)), preferred_element_type=jnp.float32
    )


def normalize_own(tokens, gain, inverse, wk, wv):
    rows, width = tokens.shape
    return pl.pallas_call(
        normalize_own_kernel,
        in_specs=[WHOLE] * 3 + [HBM] * 2,
        out_specs=[WHOLE] * 4,
        out_shape=[
            shaped((rows // 2, width), jnp.bfloat16),
            shaped((rows // 2, 2 * HEAD), jnp.float32),
            shaped(wk.shape, wk.dtype),
            shaped(wv.shape, wv.dtype),
        ],
        scratch_shapes=[pltpu.SemaphoreType.DMA((2, PIECES))],
        compiler_params=params(12),
        cost_estimate=cost(2 * rows * width * HEAD, wk.size * 4),
        name="normalize_own",
    )(tokens, gain, inverse, *in_hbm(wk, wv))


def keys_kernel(normed_ref, acc_ref, wk_ref, wv_ref, cos_ref, sin_ref, kv_ref):
    half, width = normed_ref.shape
    here = half_rows(2 * half, False)
    total = acc_ref[...] + jnp.dot(
        normed_ref[...], both_weights(wk_ref, wv_ref, features(width, True)), preferred_element_type=jnp.float32
    )
    kv_ref[:, :HEAD] = turn(total[:, :HEAD], cos_ref[here, :], sin_ref[here, :])
    kv_ref[:, HEAD:] = total[:, HEAD:].astype(jnp.bfloat16)


def finish_keys(normed_come, acc, wk, wv, tables):
    return pl.pallas_call(
        keys_kernel,
        in_specs=[WHOLE] * 6,
        out_specs=WHOLE,
        out_shape=shaped(acc.shape, jnp.bfloat16),
        compiler_params=params(12),
        cost_estimate=cost(normed_come.size * 4 * HEAD, acc.size * 4),
        name="keys",
    )(normed_come, acc, wk, wv, *tables)


def join_kernel(mine_ref, other_ref, out_ref):
    rows = out_ref.shape[0]
    out_ref[half_rows(rows, False), :] = mine_ref[...]
    out_ref[half_rows(rows, True), :] = other_ref[...]


def join(mine, other):
    half, width = mine.shape
    return pl.pallas_call(
        join_kernel,
        in_specs=[WHOLE] * 2,
        out_specs=WHOLE,
        out_shape=shaped((2 * half, width), mine.dtype),
        compiler_params=params(8),
        cost_estimate=SMALL,
        name="join",
    )(mine, other)


def queries_own_kernel(mine_ref, other_ref, wq_ref, wout_ref, acc_ref, wsend_ref, wlater_ref):
    half, width = mine_ref.shape
    weights = wq_ref[features(width, False), :]
    acc_ref[:half, :] = jnp.dot(mine_ref[...], weights, preferred_element_type=jnp.float32)
    acc_ref[half:, :] = jnp.dot(other_ref[...], weights, preferred_element_type=jnp.float32)
    send = features(width, True).start
    wsend_ref[...] = wout_ref[:, pl.ds(send, width // 2)]
    wlater_ref[...] = wout_ref[:, pl.ds(send + width // 2, width // 2)]


def queries_own(mine, other, wq, w_out):
    half, width = mine.shape
    nq = wq.shape[1]
    part = shaped((w_out.shape[0], width // 2), w_out.dtype)
    return pl.pallas_call(
        queries_own_kernel,
        in_specs=[WHOLE] * 4,
        out_specs=[WHOLE] * 3,
        out_shape=[shaped((2 * half, nq), jnp.float32), part, part],
        compiler_params=params(12),
        cost_estimate=cost(10**10, 1),
        name="queries_own",
    )(mine, other, wq, w_out)


def queries_kernel(
    mine_ref, other_ref, acc_ref, wq_ref, cos_ref, sin_ref, q_ref, acc
):
    half, width = mine_ref.shape
    weights = wq_ref[features(width, True), :]
    acc[:half, :] = jnp.dot(mine_ref[...], weights, preferred_element_type=jnp.float32)
    acc[half:, :] = jnp.dot(other_ref[...], weights, preferred_element_type=jnp.float32)

    def finish(me):
        for part, which in ((slice(0, half), me), (slice(half, 2 * half), 1 - me)):
            at = slice(which * half, (which + 1) * half)
            for h in range(q_ref.shape[1] // HEAD):
                lanes = slice(h * HEAD, (h + 1) * HEAD)
                q_ref[at, lanes] = turn(acc_ref[part, lanes] + acc[part, lanes], cos_ref[at, :], sin_ref[at, :])

    for core in range(2):
        pl.when(lax.axis_index("tp") == core)(functools.partial(finish, core))


def finish_queries(mine, other, acc, wq, tables):
    half, width = mine.shape
    nq = wq.shape[1]
    return pl.pallas_call(
        queries_kernel,
        in_specs=[WHOLE] * 6,
        out_specs=WHOLE,
        out_shape=shaped((2 * half, nq), jnp.bfloat16),
        scratch_shapes=[pltpu.VMEM((2 * half, nq), jnp.float32)],
        compiler_params=params(12),
        cost_estimate=cost(4 * half * width * nq, half * nq * 8),
        name="queries",
    )(mine, other, acc, wq, *tables)


TILE = 128
GROUPS = 2
SPAN = 256


def place_blocks(blocks, starts, keys, values):
    for block, start in zip(blocks, starts, strict=True):
        at = pl.ds(pl.multiple_of(start, block.shape[0]), block.shape[0])
        keys[:, at] = block[:, :HEAD].T
        values[at, :] = block[:, HEAD:]


def lanes_max(x):
    return jnp.broadcast_to(jnp.max(x, axis=1, keepdims=True), x.shape)


def weigh(scores, probs, at, first, count, top):
    scaled = top * EXP2_SCALE
    total = jnp.zeros((ROWS, LANES), jnp.float32)
    for j in range(0, count, WIDE):
        weights = []
        for i in range(j, j + WIDE, LANES):
            w = jnp.exp2(scores[at, first + i : first + i + LANES] * EXP2_SCALE - scaled)
            total = total + w
            weights.append(w)
        probs[at, first + j : first + j + WIDE] = jnp.concatenate(weights, axis=1).astype(jnp.bfloat16)
    return total


def attend_own_kernel(
    group, lengths_hbm, q_ref, mine_ref, other_ref, acc_ref, tops_ref, sums_ref,
    keys, values, bias, scores_even, scores_odd, probs_even, probs_odd, lengths_ref, sem,
):
    load = pltpu.make_async_copy(lengths_hbm, lengths_ref, sem)
    load.start()
    rows = q_ref.shape[0]
    half = rows // 2
    me = lax.axis_index("tp")
    place_blocks([mine_ref, other_ref], [me * half, (1 - me) * half], keys, values)
    load.wait()
    row = lax.broadcasted_iota(jnp.int32, (rows, LANES), 0)
    lane = lax.broadcasted_iota(jnp.int32, (rows, LANES), 1)
    begin = first_of_document(lengths_ref, lax.axis_index("dp") * rows, row)
    for j in range(0, rows, LANES):
        allowed = (lane + j >= begin) & (lane + j <= row)
        bias[:, j : j + LANES] = jnp.where(allowed, 0.0, -1e30)
    per = q_ref.shape[1] // HEAD // GROUPS
    for h in range(per):
        column = (group * per + h) * HEAD
        for first, count, scores, probs in (
            (0, half, scores_even, probs_even),
            (half, rows, scores_odd, probs_odd),
        ):
            scores[:, :count] = jnp.dot(
                q_ref[first : first + half, column : column + HEAD],
                keys[:, :count],
                preferred_element_type=jnp.float32,
            )
            out = h * rows + first

            for r in range(0, half, ROWS):
                at = slice(r, r + ROWS)
                out_at = slice(out + r, out + r + ROWS)
                top = jnp.full((ROWS, LANES), -1e30, jnp.float32)
                for j in range(0, count, LANES):
                    s = scores[at, j : j + LANES] + bias[first + r : first + r + ROWS, j : j + LANES]
                    scores[at, j : j + LANES] = s
                    top = jnp.maximum(top, s)
                top = lanes_max(top)
                tops_ref[out_at, :] = top
                sums_ref[out_at, :] = weigh(scores, probs, at, 0, count, top)
            acc_ref[out : out + half, :] = jnp.dot(
                probs[:, :count], values[:count, :], preferred_element_type=jnp.float32
            )


def attend_kernel(
    lengths_hbm, q_ref, third_ref, third_other_ref, block_ref, block_other_ref,
    acc_first, tops_first, sums_first, acc_second, tops_second, sums_second, ctx_ref, keys, values, stacked, scores_even, scores_odd, probs_even, probs_odd, acc, sums, lengths_ref, sem,
):
    load = pltpu.make_async_copy(lengths_hbm, lengths_ref, sem)
    load.start()
    rows = q_ref.shape[0]
    half = rows // 2
    heads = q_ref.shape[1] // HEAD
    behind = keys.shape[1]
    me = lax.axis_index("tp")
    load.wait()
    start = -lax.axis_index("dp") * rows
    begin, end = start, jnp.int32(rows)
    for d in range(lengths_ref.shape[0] - 1):
        start = start + lengths_ref[d]
        begin = jnp.where(start <= 0, start, begin)
        end = jnp.where(start > 0, jnp.minimum(end, start), end)
    low = begin + behind

    @pl.when(low < behind)
    def _():
        place_blocks(
            [third_ref, third_other_ref, block_ref, block_other_ref],
            [me * half, (1 - me) * half, rows * (2 - me), rows * (1 + me)],
            keys,
            values,
        )

    lane = lax.broadcasted_iota(jnp.int32, (ROWS, LANES), 1)
    line = lax.broadcasted_iota(jnp.int32, (ROWS, LANES), 0)

    per = heads // GROUPS
    states = ((acc_first, tops_first, sums_first), (acc_second, tops_second, sums_second))

    def own_state(h, t, r):
        return *states[h // per], block_rows(h % per * rows + t * TILE, r)

    def alone(t, r, h):
        acc_in, _, sums_in, at = own_state(h, t, r)
        total = jnp.sum(sums_in[at, :], axis=1, keepdims=True)
        ctx_ref[block_rows(t * TILE, r), h * HEAD : (h + 1) * HEAD] = (acc_in[at, :] / total).astype(jnp.bfloat16)

    def tile(t, carry):
        reached = (t * TILE < end) & (low < behind)

        @pl.when(jnp.logical_not(reached))
        def _():
            for h in range(heads):
                for r in range(TILE // ROWS):
                    alone(t, r, h)

        def merge(first):
            for h in range(heads):
                stacked[h * TILE : (h + 1) * TILE, :] = q_ref[
                    pl.ds(pl.multiple_of(t * TILE, TILE), TILE), h * HEAD : (h + 1) * HEAD
                ]
            groups = ((0, scores_even, probs_even), (heads // 2, scores_odd, probs_odd))
            for group, scores, _ in groups:
                scores[:, first:] = jnp.dot(
                    stacked[group * TILE : (group + heads // 2) * TILE, :], keys[:, first:], preferred_element_type=jnp.float32
                )
            for group, scores, probs in groups:
                for h in range(group, group + heads // 2):
                    for r in range(0, TILE, ROWS):
                        at = slice((h - group) * TILE + r, (h - group) * TILE + r + ROWS)
                        out_at = slice(h * TILE + r, h * TILE + r + ROWS)
                        acc_in, tops_in, sums_in, state = own_state(h, t, r // ROWS)
                        own_top = tops_in[state, :]
                        top = own_top
                        for j in range(first, behind, LANES):
                            s = scores[at, j : j + LANES]
                            if j < first + SPAN:
                                s = jnp.where(lane + j >= low, s, -1e30)
                                scores[at, j : j + LANES] = s
                            top = jnp.maximum(top, s)
                        top = lanes_max(top)
                        rescale = jnp.exp2((own_top - top) * EXP2_SCALE)
                        acc[out_at, :] = acc_in[state, :] * rescale
                        total = weigh(scores, probs, at, first, behind - first, top)
                        sums[out_at, :] = sums_in[state, :] * rescale + total
                out = slice(group * TILE, (group + heads // 2) * TILE)
                acc[out, :] += jnp.dot(probs[:, first:], values[first:, :], preferred_element_type=jnp.float32)
            for h in range(heads):
                for r in range(TILE // ROWS):
                    at = slice(h * TILE + r * ROWS, h * TILE + (r + 1) * ROWS)
                    acc_in, _, sums_in, state = own_state(h, t, r)
                    merged = line + (t * TILE + r * ROWS) < end
                    total = jnp.sum(jnp.where(merged, sums[at, :], sums_in[state, :]), axis=1, keepdims=True)
                    context = jnp.where(merged, acc[at, :], acc_in[state, :]) / total
                    ctx_ref[block_rows(t * TILE, r), h * HEAD : (h + 1) * HEAD] = context.astype(jnp.bfloat16)

        for first in range(0, behind, SPAN):
            inside = (low >= first) & (low < first + SPAN)
            pl.when(reached & inside)(functools.partial(merge, first))
        return carry

    lax.fori_loop(0, rows // TILE, tile, 0)


def attend_own(group, lengths, queries, blocks):
    rows, width = queries.shape
    half = rows // 2
    per = width // HEAD // GROUPS
    return pl.pallas_call(
        functools.partial(attend_own_kernel, group),
        in_specs=[HBM] + [WHOLE] * 3,
        out_specs=[WHOLE] * 3,
        scratch_shapes=[
            pltpu.VMEM((HEAD, rows), jnp.bfloat16),
            pltpu.VMEM((rows, HEAD), jnp.bfloat16),
            pltpu.VMEM((rows, rows), jnp.float32),
            pltpu.VMEM((half, half), jnp.float32),
            pltpu.VMEM((half, rows), jnp.float32),
            pltpu.VMEM((half, half), jnp.bfloat16),
            pltpu.VMEM((half, rows), jnp.bfloat16),
            pltpu.SMEM(lengths.shape, lengths.dtype),
            pltpu.SemaphoreType.DMA,
        ],
        out_shape=[shaped((per * rows, LANES), jnp.float32)] * 3,
        compiler_params=params(16),
        cost_estimate=SMALL,
        name="attend_own",
    )(*in_hbm(lengths), queries, *blocks)


def attend(lengths, queries, blocks, state):
    rows, width = queries.shape
    heads = width // HEAD
    tall = heads * TILE
    places = sum(block.shape[0] for block in blocks)
    return pl.pallas_call(
        attend_kernel,
        in_specs=[HBM] + [WHOLE] * (1 + len(blocks) + len(state)),
        out_specs=WHOLE,
        scratch_shapes=[
            pltpu.VMEM((HEAD, places), jnp.bfloat16),
            pltpu.VMEM((places, HEAD), jnp.bfloat16),
            pltpu.VMEM((tall, HEAD), jnp.bfloat16),
            pltpu.VMEM((tall // 2, places), jnp.float32),
            pltpu.VMEM((tall // 2, places), jnp.float32),
            pltpu.VMEM((tall // 2, places), jnp.bfloat16),
            pltpu.VMEM((tall // 2, places), jnp.bfloat16),
            pltpu.VMEM((tall, HEAD), jnp.float32),
            pltpu.VMEM((tall, LANES), jnp.float32),
            pltpu.SMEM(lengths.shape, lengths.dtype),
            pltpu.SemaphoreType.DMA,
        ],
        out_shape=shaped((rows, width), jnp.bfloat16),
        compiler_params=params(20),
        cost_estimate=cost(18 * 10**9, 1),
        name="attend",
    )(*in_hbm(lengths), queries, *blocks, *state)


def term_kernel(context_ref, w_ref, term_ref):
    width = term_ref.shape[1]
    step = 1024
    for c in range(width // step):
        here = pl.ds(pl.multiple_of(lax.axis_index("tp") * width + c * step, step), step)
        term = jnp.dot(context_ref[...], w_ref[:, here], preferred_element_type=jnp.float32)
        term_ref[:, c * step : (c + 1) * step] = term.astype(jnp.bfloat16)


def group_term(context, w_out):
    rows, depth = context.shape
    width = w_out.shape[1] // 2
    return pl.pallas_call(
        term_kernel,
        in_specs=[WHOLE] * 2,
        out_specs=WHOLE,
        out_shape=shaped((rows, width), jnp.bfloat16),
        compiler_params=params(12),
        cost_estimate=SMALL,
        name="own_term",
    )(context, w_out)


def output_kernel(tokens_ref, term_ref, context_ref, w_ref, w_later_ref, out_hbm, out, sems):
    width = out.shape[1]
    half = width // 2
    chunks = sems.shape[0]
    step = width // chunks
    stores = []
    for c in range(chunks):
        here = slice(c * step, (c + 1) * step)
        weights = w_ref[:, here] if c < chunks // 2 else w_later_ref[:, c * step - half : (c + 1) * step - half]
        other = jnp.dot(context_ref[...], weights, preferred_element_type=jnp.float32).astype(jnp.bfloat16)
        total = tokens_ref[:, here].astype(jnp.float32) + term_ref[:, here].astype(jnp.float32) + other.astype(jnp.float32)
        out[:, here] = total.astype(jnp.bfloat16)
        stores.append(pltpu.make_async_copy(out.at[:, here], out_hbm.at[:, here], sems.at[c]))
        stores[c].start()
    for store in stores:
        store.wait()


def output(tokens, term, context, w, w_later):
    rows, width = tokens.shape
    depth = context.shape[1]
    return pl.pallas_call(
        output_kernel,
        in_specs=[WHOLE] * 5,
        out_specs=HBM,
        out_shape=shaped((rows, width), jnp.bfloat16),
        scratch_shapes=[pltpu.VMEM((rows, width), jnp.bfloat16), pltpu.SemaphoreType.DMA((8,))],
        compiler_params=params(20),
        cost_estimate=cost(2 * rows * width * depth, rows * width * 4),
        name="output",
    )(tokens, term, context, w, w_later)


def swap(value):
    return lax.ppermute(value, "tp", SWAP)


def onward(value, distances):
    count, cores = lax.axis_size("dp"), len(distances)
    pairs = [
        (source * cores + core, (source + distance) * cores + core)
        for core, distance in enumerate(distances)
        for source in range(count - distance)
    ]
    return lax.ppermute(value, ("dp", "tp"), pairs)


def local(tokens, norm_gain, lengths, w_query, w_key, w_value, w_out):
    rows = tokens.shape[0]
    frequency = 500000.0 ** (-jnp.arange(HEAD // 2, dtype=jnp.float32) * 2.0 / HEAD)
    frequency = jnp.concatenate([frequency, frequency])[None, :]

    sums, gain, tokens = squares(frequency, norm_gain.reshape(-1, LANES), tokens)
    sums_other = swap(sums)
    tables = rotary_tables(frequency, lengths, rows)
    sums_other, tables = lax.optimization_barrier((sums_other, tables))
    normed_other, inverse = normalize_other(tokens, sums, sums_other, gain)
    come_mine = swap(normed_other)
    normed_mine, kv_partial, wk, wv = normalize_own(tokens, gain, inverse, w_key, w_value)
    come_other = swap(normed_mine)
    come_mine, kv_partial = lax.optimization_barrier((come_mine, kv_partial))
    kv = finish_keys(come_mine, kv_partial, wk, wv, tables)
    assert (rows + MOST - 2) // rows == 3
    kv, normed_mine = lax.optimization_barrier((kv, normed_mine))
    third = onward(kv, (3, 3))
    kv_other = swap(kv)
    block = onward(join(kv, kv_other), (1, 2))
    partial, w_send, w_later = queries_own(normed_mine, normed_other, w_query, w_out)
    queries = finish_queries(come_mine, come_other, partial, w_query, tables)
    w_other, w_other_later = swap(w_send), swap(w_later)
    state = attend_own(0, lengths, queries, [kv, kv_other])
    third, block, state = lax.optimization_barrier((third, block, state))
    blocks = [third, swap(third), block, swap(block)]
    state = [*state, *attend_own(1, lengths, queries, [kv, kv_other])]
    context = attend(lengths, queries, blocks, state)
    context_other = swap(context)
    term = group_term(context, w_out)
    return output(tokens, term, context_other, w_other, w_other_later)


def solution(mesh):
    placed = (P(("grp", "dp"), "tp"), P("tp"), P("grp"), P(None, "tp"), P(), P(), P("tp", None))
    return jax.shard_map(
        local, mesh=mesh, in_specs=placed, out_specs=P(("grp", "dp"), "tp"), check_vma=False
    )
```
